32 devices in a mesh: section: 8 (over z, core), rows: 4 (over y, x).
Axes of the slice: x: 2, y: 2, z: 4, core: 2. Of those that a mesh axis runs over, the one named last changes fastest.
Arguments:
- activations: bfloat16 [8, 16, 32, 768], P('section', 'rows'), may hold values from -6 to 6
- cotangent: bfloat16 [8, 16, 32, 3072], P('section', None, None, 'rows'), may hold values from -6 to 6
- proj_weight: bfloat16 [768, 3072], P('section', 'rows'), may hold values from -0.21875 to 0.21875
- kernel_taps: bfloat16 [49, 768], replicated, may hold values from -0.875 to 0.875
- ln_gain: float32 [768], replicated, may hold values from 0.1 to 1.9
- ln_shift: float32 [768], replicated, may hold values from -3 to 3
- heights: int32 [8], P('section'), may hold values from 8 to 16, as said below
- widths: int32 [8], P('section'), may hold values from 16 to 32, as said below
Outputs:
- input_grad: bfloat16 [8, 16, 32, 768], P('section', 'rows')
- weight_grad: float32 [768, 3072], P('section', 'rows')
The draws below stay inside these ranges and needn't reach their ends.
Inputs may be any that keep to these rules, and one draw needn't show every extreme that they name: `heights`: every image has at least half of 16 valid rows, and some image has all 16. `widths`: every image has at least half of 32 valid columns, and some image has all 32.
All inputs are finite; a program needn't handle non-finite values.
Results may differ from the reference program's by a relative error of at most 0.0049.
Values may be sent and summed in bfloat16 or wider, within the bound.
No kernel may reach another device: no remote copies, remote signals or barrier semaphores. Data moves between devices by JAX's collectives and lax.ppermute only.
A program may use at most 64 MiB of HBM per device.

```python
import jax
import jax.numpy as jnp
from jax import lax

C = 768
HID = 3072
KS = 7
WID = 32
HEIGHT = 16
IMAGES = 8


def draw_heights(key, part):
    first_key = jax.random.fold_in(key, 11)
    second_key = jax.random.fold_in(key, 12)
    values = jax.random.randint(first_key, (IMAGES,), HEIGHT // 2, HEIGHT + 1)
    chosen = jax.random.randint(second_key, (), 0, IMAGES)
    return jnp.where(jnp.arange(IMAGES) == chosen, HEIGHT, values).astype(jnp.int32)


def draw_widths(key, part):
    first_key = jax.random.fold_in(key, 21)
    second_key = jax.random.fold_in(key, 22)
    values = jax.random.randint(first_key, (IMAGES,), WID // 2, WID + 1)
    chosen = jax.random.randint(second_key, (), 0, IMAGES)
    return jnp.where(jnp.arange(IMAGES) == chosen, WID, values).astype(jnp.int32)


def block_levels(key, dims, pieces, least, top_value):
    factor_of = 1.0
    for dim, blocks in pieces:
        steps = jax.random.uniform(jax.random.fold_in(jax.random.fold_in(key, 6), dim), (blocks,), jnp.float32, least / len(pieces), top_value / len(pieces))
        factor_of = factor_of * jnp.repeat(jnp.exp(steps), dims[dim] // blocks).reshape((-1,) + (1,) * (len(dims) - 1 - dim))
    return factor_of


def gaussian(own_key, dims, width, reach, split=(), dtype=jnp.bfloat16):
    values = jax.random.normal(own_key, dims, jnp.float32) * width
    if len(split) > 0:
        values = block_levels(own_key, dims, split, -0.22, 0.18) * values
    return jnp.clip(values, min=-reach, max=reach).astype(dtype)


def setup_inputs(seed: int = 0) -> dict:
    key_list = jax.random.split(jax.random.key(seed), 9)
    return {
        "activations": gaussian(key_list[0], (IMAGES, HEIGHT, WID, C), 1.0, 6.0, ((0, 8), (1, 4))),
        "cotangent": gaussian(key_list[1], (IMAGES, HEIGHT, WID, HID), 1.0, 6.0, ((0, 8), (3, 4))),
        "proj_weight": gaussian(key_list[2], (C, HID), C ** -0.5, 0.21875, ((0, 8), (1, 4))),
        "kernel_taps": gaussian(key_list[3], (KS * KS, C), (KS * KS) ** -0.5, 0.875),
        "ln_gain": jnp.clip(1.0 + 0.18 * jax.random.normal(key_list[4], (C,), jnp.float32), 0.1, 1.9),
        "ln_shift": gaussian(key_list[5], (C,), 0.5, 3.0, (), jnp.float32),
        "heights": draw_heights(jax.random.fold_in(key_list[8], 71), 0),
        "widths": draw_widths(jax.random.fold_in(key_list[8], 71), 0),
    }


epsilon = 1e-06

def depth_conv(source, weights):
    padded = jnp.pad(source, ((3, 3), (3, 3), (0, 0)))
    height_all = source.shape[0]
    width_all = source.shape[1]
    running = jnp.zeros(source.shape, jnp.float32)
    for across in range(7):
        for along in range(7):
            running = running + weights[across * 7 + along] * padded[across:across + height_all, along:along + width_all]
    return running

def reference(activations, cotangent, proj_weight, kernel_taps, ln_gain, ln_shift, heights, widths):
    row_ids = lax.broadcasted_iota(jnp.int32, (HEIGHT, WID), 0)
    col_ids = lax.broadcasted_iota(jnp.int32, (HEIGHT, WID), 1)
    weights = kernel_taps.astype(jnp.float32)

    def one_image(summed, sample):
        image, grad_in, height_one, width_one = sample
        valid = ((row_ids < height_one) & (col_ids < width_one)).astype(jnp.float32)[:, :, None]
        masked = image.astype(jnp.float32) * valid
        mixed = depth_conv(masked, weights)
        centre = lax.optimization_barrier(jnp.mean(mixed, axis=-1, keepdims=True))
        variance = lax.optimization_barrier(jnp.mean((mixed - centre) ** 2, axis=-1, keepdims=True))
        inv_spread = 1.0 / jnp.sqrt(variance + epsilon)
        unit = (mixed - centre) * inv_spread
        normed = (unit * ln_gain + ln_shift).astype(jnp.bfloat16)
        live_grad = (grad_in.astype(jnp.float32) * valid).astype(jnp.bfloat16)
        normed_flat = normed.reshape(-1, C)
        grad_flat = live_grad.reshape(-1, HID)
        partial_value = jnp.dot(normed_flat.T, grad_flat, preferred_element_type=jnp.float32)
        grad_norm = jnp.dot(grad_flat, proj_weight.T, preferred_element_type=jnp.float32).reshape(HEIGHT, WID, C)
        scaled = grad_norm * ln_gain
        grad_mixed = inv_spread * (scaled - lax.optimization_barrier(jnp.mean(scaled, axis=-1, keepdims=True)) - unit * lax.optimization_barrier(jnp.mean(scaled * unit, axis=-1, keepdims=True)))
        grad_mixed = grad_mixed.astype(jnp.bfloat16).astype(jnp.float32)
        back = depth_conv(grad_mixed, weights[::-1]) * valid
        return (summed + partial_value, back.astype(jnp.bfloat16))
    summed, input_grad = lax.scan(one_image, jnp.zeros((C, HID), jnp.float32), (activations, cotangent, heights, widths))
    return (input_grad, summed / IMAGES)
```

```python
import jax
import jax.numpy as jnp
from jax import lax
from jax.sharding import PartitionSpec as P

epsilon = 1e-06


def padded_2(block, sides, width):
    for axis, dim in sides:
        count = lax.axis_size(axis)
        forward = [(i, i + 1) for i in range(count - 1)]
        backward = [(target, source) for source, target in forward]
        low = lax.ppermute(
            lax.slice_in_dim(block, block.shape[dim] - width, None, axis=dim), axis, forward
        )
        high = lax.ppermute(lax.slice_in_dim(block, 0, width, axis=dim), axis, backward)
        block = jnp.concatenate([low, block, high], axis=dim)
    return block


def spread_rows(source, weights):
    rows_dev = source.shape[1]
    width_dev = source.shape[2]
    padded = padded_2(source, (("rows", 1),), 3)
    padded = jnp.pad(padded, ((0, 0), (0, 0), (3, 3), (0, 0))).astype(jnp.float32)
    running = jnp.zeros(source.shape, jnp.float32)
    for across in range(7):
        for along in range(7):
            running = (
                running
                + weights[across * 7 + along]
                * padded[:, across : across + rows_dev, along : along + width_dev]
            )
    return running


def scatter_rows(partial):
    count = lax.axis_size("rows")
    pieces = partial.reshape(count, -1, partial.shape[-1])
    arrived = lax.all_to_all(
        pieces.astype(jnp.bfloat16), "rows", split_axis=0, concat_axis=0, tiled=True
    )
    return jnp.sum(arrived.astype(jnp.float32), axis=0)


def scatter_section(partial):
    count = lax.axis_size("section")
    me = lax.axis_index("section")
    hidden = partial.shape[1]
    pieces = partial.reshape(count // 2, 2, -1, hidden)
    parity = lax.rem(me, 2)
    mine = lax.dynamic_index_in_dim(pieces, parity, 1, keepdims=False)
    other = lax.dynamic_index_in_dim(pieces, 1 - parity, 1, keepdims=False).astype(jnp.bfloat16)
    swap = [(i, i ^ 1) for i in range(count)]
    pair = mine + lax.ppermute(other, "section", swap).astype(jnp.float32)
    groups = [[i for i in range(count) if i % 2 == p] for p in range(2)]
    arrived = lax.all_to_all(
        pair.astype(jnp.bfloat16),
        "section",
        split_axis=0,
        concat_axis=0,
        axis_index_groups=groups,
        tiled=True,
    )
    return jnp.sum(arrived.astype(jnp.float32), axis=0)


def local(activations, cotangent, proj_weight, kernel_taps, ln_gain, ln_shift, heights, widths):
    rows_dev = activations.shape[1]
    width_dev = activations.shape[2]
    chans = activations.shape[3]
    height_all = cotangent.shape[1]
    hidden_dev = cotangent.shape[3]
    offset_rows = lax.axis_index("rows") * rows_dev
    row_ids = lax.broadcasted_iota(jnp.int32, (height_all, width_dev), 0)
    col_ids = lax.broadcasted_iota(jnp.int32, (height_all, width_dev), 1)
    full_valid = ((row_ids < heights[0]) & (col_ids < widths[0])).astype(jnp.float32)
    own_valid = lax.dynamic_slice_in_dim(full_valid, offset_rows, rows_dev, 0)[None, :, :, None]
    weights = kernel_taps.astype(jnp.float32)
    proj_rows = lax.all_gather(proj_weight, "section", axis=0, tiled=True)
    masked = (activations.astype(jnp.float32) * own_valid).astype(jnp.bfloat16)
    mixed = spread_rows(masked, weights)
    centre = jnp.mean(mixed, axis=-1, keepdims=True)
    variance = jnp.mean((mixed - centre) ** 2, axis=-1, keepdims=True)
    inv_spread = 1.0 / jnp.sqrt(variance + epsilon)
    unit = (mixed - centre) * inv_spread
    normed = (unit * ln_gain + ln_shift).astype(jnp.bfloat16)
    normed_flat = normed.reshape(-1, chans)
    live_grad = (cotangent.astype(jnp.float32) * full_valid[None, :, :, None]).astype(jnp.bfloat16)
    grad_flat = live_grad.reshape(-1, hidden_dev)
    partial_value = lax.dot_general(
        lax.all_gather(normed_flat, "rows", axis=0, tiled=True),
        grad_flat,
        (((0,), (0,)), ((), ())),
        preferred_element_type=jnp.float32,
    )
    image_count = lax.axis_size("section") * activations.shape[0]
    proj_rows, partial_value = lax.optimization_barrier((proj_rows, partial_value))
    weight_grad = scatter_section(partial_value) / image_count
    grad_norm = scatter_rows(
        lax.dot_general(
            grad_flat, proj_rows, (((1,), (1,)), ((), ())), preferred_element_type=jnp.float32
        )
    )
    grad_norm = grad_norm.reshape(mixed.shape)
    scaled = grad_norm * ln_gain
    grad_mixed = inv_spread * (
        scaled
        - jnp.mean(scaled, axis=-1, keepdims=True)
        - unit * jnp.mean(scaled * unit, axis=-1, keepdims=True)
    )
    grad_mixed = grad_mixed.astype(jnp.bfloat16)
    back = spread_rows(grad_mixed, weights[::-1]) * own_valid
    return (back.astype(jnp.bfloat16), weight_grad)


def solution(mesh):
    in_specs = (
        P("section", "rows", None, None),
        P("section", None, None, "rows"),
        P("section", "rows"),
        P(),
        P(),
        P(),
        P("section"),
        P("section"),
    )
    out_specs = (P("section", "rows", None, None), P("section", "rows"))
    return jax.shard_map(local, mesh=mesh, in_specs=in_specs, out_specs=out_specs, check_vma=False)
```

```python
import functools

import jax
import jax.numpy as jnp
from jax import lax
from jax.experimental import pallas as pl
from jax.experimental.pallas import tpu as pltpu
from jax.sharding import PartitionSpec as P

epsilon = 1e-06
LANES = 128
SUBLANES = 8
VMEM_BYTES = 48 * 1024 * 1024


def tile_of(count):
    return 8 if count % 8 == 0 else 4 if count % 4 == 0 else 1


def widen_taps(taps_ref, wide_ref, lanes):
    for tap in range(taps_ref.shape[0]):
        row = taps_ref[tap : tap + 1, lanes]
        wide_ref[tap] = jnp.broadcast_to(row, (SUBLANES, LANES))


def conv_tile(source_ref, wide_ref, first, tile, width, flip):
    pieces = width // SUBLANES
    running = [jnp.zeros((pieces, SUBLANES, LANES), jnp.float32) for _ in range(tile)]
    for along in range(7):
        for row in range(tile + 6):
            shifted = source_ref[first + row, 5 + along : 5 + along + width, :]
            shifted = shifted.reshape(pieces, SUBLANES, LANES)
            for out in range(max(0, row - 6), min(tile, row + 1)):
                tap = (row - out) * 7 + along
                tap = 48 - tap if flip else tap
                running[out] = running[out] + wide_ref[tap][None] * shifted
    return [value.reshape(width, LANES) for value in running]


def forward_kernel(
    size_ref, act_ref, taps_ref, gain_ref, shift_ref,
    normed_ref, unit_ref, inv_ref,
    source, wide, mixed,
):
    height, width, chans = act_ref.shape
    blocks = chans // LANES
    rows_dev = unit_ref.shape[0] // width
    tile = tile_of(height)
    high, wid, band = size_ref[0], size_ref[1], size_ref[2]
    source[...] = jnp.zeros(source.shape, jnp.float32)
    columns = lax.broadcasted_iota(jnp.int32, (width, LANES), 0) < wid

    @pl.loop(0, blocks)
    def _(block):
        lanes = pl.ds(pl.multiple_of(block * LANES, LANES), LANES)
        widen_taps(taps_ref, wide, lanes)

        @pl.loop(0, height)
        def _(row):
            keep = columns & (row < high)
            value = act_ref[row, :, lanes].astype(jnp.float32)
            source[row + 3, 8 : 8 + width, :] = jnp.where(keep, value, 0.0)

        @pl.loop(0, height // tile)
        def _(step):
            first = step * tile
            for out, value in enumerate(conv_tile(source, wide, first, tile, width, False)):
                mixed[block, first + out] = value

    def normalise(row):
        values = [mixed[block, row] for block in range(blocks)]
        centre = sum(jnp.sum(v, axis=-1, keepdims=True) for v in values) / chans
        values = [v - centre for v in values]
        spread = sum(jnp.sum(v * v, axis=-1, keepdims=True) for v in values) / chans
        inv = 1.0 / jnp.sqrt(spread + epsilon)
        return [v * inv for v in values], inv

    @pl.loop(0, height)
    def _(row):
        units, inv = normalise(row)
        rows = pl.ds(pl.multiple_of(row * width, width), width)
        for block, unit in enumerate(units):
            lanes = slice(block * LANES, (block + 1) * LANES)
            normed_ref[rows, lanes] = (unit * gain_ref[:, lanes] + shift_ref[:, lanes]).astype(
                normed_ref.dtype
            )

    for row in range(rows_dev):
        units, inv = normalise(band * rows_dev + row)
        rows = slice(row * width, (row + 1) * width)
        inv_ref[rows, :] = jnp.broadcast_to(inv, (width, LANES))
        for block, unit in enumerate(units):
            unit_ref[rows, block * LANES : (block + 1) * LANES] = unit


def forward(sizes, act, taps, gain, shift, rows_dev):
    height, width, chans = act.shape
    vmem = pl.BlockSpec(memory_space=pltpu.VMEM)
    return pl.pallas_call(
        forward_kernel,
        out_shape=(
            jax.ShapeDtypeStruct((height * width, chans), jnp.bfloat16),
            jax.ShapeDtypeStruct((rows_dev * width, chans), jnp.float32),
            jax.ShapeDtypeStruct((rows_dev * width, LANES), jnp.float32),
        ),
        in_specs=[pl.BlockSpec(memory_space=pltpu.SMEM), vmem, vmem, vmem, vmem],
        out_specs=(vmem, vmem, vmem),
        scratch_shapes=[
            pltpu.VMEM((height + 6, width + 16, LANES), jnp.float32),
            pltpu.VMEM((taps.shape[0], SUBLANES, LANES), jnp.float32),
            pltpu.VMEM((chans // LANES, height, width, LANES), jnp.float32),
        ],
        compiler_params=pltpu.CompilerParams(vmem_limit_bytes=VMEM_BYTES),
        name="forward",
    )(sizes, act, taps, gain, shift)


def mixed_grad_kernel(parts_ref, unit_ref, inv_ref, gain_ref, out_ref):
    parts, pixels, chans = parts_ref.shape
    chunk = 32

    @pl.loop(0, pixels // chunk)
    def _(step):
        rows = pl.ds(pl.multiple_of(step * chunk, chunk), chunk)
        total = parts_ref[0, rows, :].astype(jnp.float32)
        for part in range(1, parts):
            total = total + parts_ref[part, rows, :].astype(jnp.float32)
        scaled = total * gain_ref[...]
        unit = unit_ref[rows, :]
        mean = jnp.sum(scaled, axis=-1, keepdims=True) / chans
        along = jnp.sum(scaled * unit, axis=-1, keepdims=True) / chans
        inv = inv_ref[rows, 0:1]
        out_ref[rows, :] = (inv * (scaled - mean - unit * along)).astype(out_ref.dtype)


def mixed_grad(parts, unit, inv, gain):
    vmem = pl.BlockSpec(memory_space=pltpu.VMEM)
    return pl.pallas_call(
        mixed_grad_kernel,
        out_shape=jax.ShapeDtypeStruct(parts.shape[1:], jnp.bfloat16),
        in_specs=[vmem] * 4,
        out_specs=vmem,
        compiler_params=pltpu.CompilerParams(vmem_limit_bytes=VMEM_BYTES),
        name="mixed_grad",
    )(parts, unit, inv, gain)


def backward_kernel(size_ref, low_ref, own_ref, high_ref, taps_ref, out_ref, source, wide):
    rows_dev, width, chans = own_ref.shape
    tile = tile_of(rows_dev)
    high, wid, band = size_ref[0], size_ref[1], size_ref[2]
    source[...] = jnp.zeros(source.shape, jnp.float32)
    columns = lax.broadcasted_iota(jnp.int32, (width, LANES), 0) < wid

    @pl.loop(0, chans // LANES)
    def _(block):
        lanes = pl.ds(pl.multiple_of(block * LANES, LANES), LANES)
        widen_taps(taps_ref, wide, lanes)
        for ref, start in ((low_ref, 0), (own_ref, 3), (high_ref, 3 + rows_dev)):
            for row in range(ref.shape[0]):
                source[start + row, 8 : 8 + width, :] = ref[row, :, lanes].astype(jnp.float32)
        for first in range(0, rows_dev, tile):
            for out, value in enumerate(conv_tile(source, wide, first, tile, width, True)):
                row = first + out
                keep = columns & (band * rows_dev + row < high)
                out_ref[row, :, lanes] = jnp.where(keep, value, 0.0).astype(out_ref.dtype)


def backward(sizes, low, own, high, taps):
    rows_dev, width, chans = own.shape
    vmem = pl.BlockSpec(memory_space=pltpu.VMEM)
    return pl.pallas_call(
        backward_kernel,
        out_shape=jax.ShapeDtypeStruct(own.shape, jnp.bfloat16),
        in_specs=[pl.BlockSpec(memory_space=pltpu.SMEM), vmem, vmem, vmem, vmem],
        out_specs=vmem,
        scratch_shapes=[
            pltpu.VMEM((rows_dev + 6, width + 16, LANES), jnp.float32),
            pltpu.VMEM((taps.shape[0], SUBLANES, LANES), jnp.float32),
        ],
        compiler_params=pltpu.CompilerParams(vmem_limit_bytes=VMEM_BYTES),
        name="backward",
    )(sizes, low, own, high, taps)


def parity_groups(count):
    return [[i for i in range(count) if i % 2 == p] for p in range(2)]


def gather_section(block):
    count = lax.axis_size("section")
    mine = lax.all_gather(
        block, "section", axis=0, axis_index_groups=parity_groups(count), tiled=False
    )
    other = lax.ppermute(mine, "section", [(i, i ^ 1) for i in range(count)])
    even = lax.rem(lax.axis_index("section"), 2) == 0
    low = jnp.where(even, mine, other)
    high = jnp.where(even, other, mine)
    return jnp.stack([low, high], axis=1).reshape(-1, block.shape[-1])


def scatter_rows(partial):
    count = lax.axis_size("rows")
    pieces = partial.reshape(count, -1, partial.shape[-1]).astype(jnp.bfloat16)
    return lax.all_to_all(pieces, "rows", split_axis=0, concat_axis=0, tiled=True)


def scatter_section(partial):
    count = lax.axis_size("section")
    hidden = partial.shape[1]
    pieces = partial.reshape(count // 2, 2, -1, hidden)
    parity = lax.rem(lax.axis_index("section"), 2)
    mine = lax.dynamic_index_in_dim(pieces, parity, 1, keepdims=False)
    other = lax.dynamic_index_in_dim(pieces, 1 - parity, 1, keepdims=False).astype(jnp.bfloat16)
    swap = [(i, i ^ 1) for i in range(count)]
    pair = mine + lax.ppermute(other, "section", swap).astype(jnp.float32)
    arrived = lax.all_to_all(
        pair.astype(jnp.bfloat16),
        "section",
        split_axis=0,
        concat_axis=0,
        axis_index_groups=parity_groups(count),
        tiled=True,
    )
    return jnp.sum(arrived.astype(jnp.float32), axis=0)


def local(activations, cotangent, proj_weight, kernel_taps, ln_gain, ln_shift, heights, widths):
    rows_dev, width_dev, chans = activations.shape[1:]
    height_all = cotangent.shape[1]
    hidden_dev = cotangent.shape[3]
    band = lax.axis_index("rows")
    sizes = jnp.concatenate([heights, widths, band[None].astype(jnp.int32)])
    taps = kernel_taps.astype(jnp.float32)
    gain = ln_gain[None]
    shift = ln_shift[None]

    proj_rows = gather_section(proj_weight)
    image = lax.all_gather(activations[0], "rows", axis=0, tiled=True)

    row_ids = lax.broadcasted_iota(jnp.int32, (height_all, width_dev), 0)
    col_ids = lax.broadcasted_iota(jnp.int32, (height_all, width_dev), 1)
    valid = ((row_ids < heights[0]) & (col_ids < widths[0])).astype(jnp.float32)
    live_grad = (cotangent[0].astype(jnp.float32) * valid[:, :, None]).astype(jnp.bfloat16)
    grad_flat = live_grad.reshape(-1, hidden_dev)

    normed, unit, inv = forward(sizes, image, taps, gain, shift, rows_dev)

    partial_grad = lax.dot_general(
        grad_flat, proj_rows, (((1,), (1,)), ((), ())), preferred_element_type=jnp.float32
    )
    parts = scatter_rows(partial_grad)

    partial_value = lax.dot_general(
        normed, grad_flat, (((0,), (0,)), ((), ())), preferred_element_type=jnp.float32
    )
    weight_grad = scatter_section(partial_value) / lax.axis_size("section")

    grad_mixed = mixed_grad(parts, unit, inv, gain).reshape(rows_dev, width_dev, chans)
    count = lax.axis_size("rows")
    low = lax.ppermute(grad_mixed[rows_dev - 3 :], "rows", [(i, i + 1) for i in range(count - 1)])
    high = lax.ppermute(grad_mixed[:3], "rows", [(i + 1, i) for i in range(count - 1)])
    back = backward(sizes, low, grad_mixed, high, taps)
    return (back[None], weight_grad)


def solution(mesh):
    in_specs = (
        P("section", "rows", None, None),
        P("section", None, None, "rows"),
        P("section", "rows"),
        P(),
        P(),
        P(),
        P("section"),
        P("section"),
    )
    out_specs = (P("section", "rows", None, None), P("section", "rows"))
    return jax.shard_map(local, mesh=mesh, in_specs=in_specs, out_specs=out_specs, check_vma=False)
```

```python
import functools

import jax
import jax.numpy as jnp
from jax import lax
from jax.experimental import pallas as pl
from jax.experimental.pallas import tpu as pltpu
from jax.sharding import PartitionSpec as P

epsilon = 1e-06
LANES = 128
SUBLANES = 8
VMEM_BYTES = 48 * 1024 * 1024


TILE = 4


def clear_margins(source, margin, rows, width):
    if margin:
        empty = jnp.zeros((margin,) + source.shape[1:], source.dtype)
        source[:margin] = empty
        source[margin + rows :] = empty
    sides = jnp.zeros((source.shape[0], 8, LANES), source.dtype)
    source[:, :8, :] = sides
    source[:, 8 + width :, :] = sides


def widen_taps(taps_ref, wide_ref, lanes):
    for tap in range(taps_ref.shape[0]):
        row = taps_ref[tap : tap + 1, lanes]
        wide_ref[tap] = jnp.broadcast_to(row, (SUBLANES, LANES))


def conv_tile(source_ref, wide_ref, first, tile, width, flip):
    stride = width // SUBLANES
    running = [[None] * stride for _ in range(tile)]
    for row in range(tile + 6):
        shifted = [
            source_ref[first + row, pl.ds(5 + k, SUBLANES, stride=stride), :]
            for k in range(stride + 6)
        ]
        for out in range(max(0, row - 6), min(tile, row + 1)):
            for along in range(7):
                tap = (row - out) * 7 + along
                weight = wide_ref[48 - tap if flip else tap]
                for i in range(stride):
                    term = weight * shifted[i + along]
                    before = running[out][i]
                    running[out][i] = term if before is None else before + term
    return running


def forward_kernel(
    size_ref, act_ref, taps_ref, gain_ref, shift_ref,
    normed_ref, unit_ref, inv_ref,
    source, wide, mixed, centres, spreads,
):
    height, width, chans = act_ref.shape
    blocks = chans // LANES
    stride = width // SUBLANES
    rows_dev = unit_ref.shape[0] // width
    tile = TILE
    high, wid, band = size_ref[0], size_ref[1], size_ref[2]
    clear_margins(source, 3, height, width)
    columns = lax.broadcasted_iota(jnp.int32, (width, LANES), 0) < wid

    @pl.loop(0, blocks)
    def _(block):
        lanes = pl.ds(pl.multiple_of(block * LANES, LANES), LANES)
        widen_taps(taps_ref, wide, lanes)

        @pl.loop(0, height // tile)
        def _(step):
            for i in range(tile):
                row = step * tile + i
                value = act_ref[row, :, lanes].astype(jnp.float32)
                source[row + 3, 8 : 8 + width, :] = jnp.where(columns & (row < high), value, 0.0)

        @pl.loop(0, height // tile)
        def _(step):
            first = step * tile
            for out, pieces in enumerate(conv_tile(source, wide, first, tile, width, False)):
                for i, value in enumerate(pieces):
                    mixed[block, first + out, pl.ds(i, SUBLANES, stride=stride), :] = value

    @pl.loop(0, height // tile)
    def _(step):
        rows = [step * tile + i for i in range(tile)]
        sums = [sum(mixed[block, row] for block in range(blocks)) for row in rows]
        for row, value in zip(rows, sums):
            centre = jnp.sum(value, axis=-1, keepdims=True) / chans
            centres[row] = jnp.broadcast_to(centre, (width, LANES))

    @pl.loop(0, height // tile)
    def _(step):
        rows = [step * tile + i for i in range(tile)]
        sums = []
        for row in rows:
            centre = centres[row]
            away = [mixed[block, row] - centre for block in range(blocks)]
            sums.append(sum(value * value for value in away))
        for row, value in zip(rows, sums):
            spread = jnp.sum(value, axis=-1, keepdims=True) / chans
            spreads[row] = jnp.broadcast_to(lax.rsqrt(spread + epsilon), (width, LANES))

    @pl.loop(0, height)
    def _(row):
        rows = pl.ds(pl.multiple_of(row * width, width), width)
        centre, inv = centres[row], spreads[row]
        for block in range(blocks):
            lanes = slice(block * LANES, (block + 1) * LANES)
            unit = (mixed[block, row] - centre) * inv
            normed_ref[rows, lanes] = (unit * gain_ref[:, lanes] + shift_ref[:, lanes]).astype(
                normed_ref.dtype
            )

    for i in range(rows_dev):
        row = band * rows_dev + i
        rows = slice(i * width, (i + 1) * width)
        centre, inv = centres[row], spreads[row]
        inv_ref[rows, :] = inv
        for block in range(blocks):
            lanes = slice(block * LANES, (block + 1) * LANES)
            unit_ref[rows, lanes] = (mixed[block, row] - centre) * inv


def forward(sizes, act, taps, gain, shift, rows_dev):
    height, width, chans = act.shape
    vmem = pl.BlockSpec(memory_space=pltpu.VMEM)
    return pl.pallas_call(
        forward_kernel,
        out_shape=(
            jax.ShapeDtypeStruct((height * width, chans), jnp.bfloat16),
            jax.ShapeDtypeStruct((rows_dev * width, chans), jnp.float32),
            jax.ShapeDtypeStruct((rows_dev * width, LANES), jnp.float32),
        ),
        in_specs=[pl.BlockSpec(memory_space=pltpu.SMEM), vmem, vmem, vmem, vmem],
        out_specs=(vmem, vmem, vmem),
        scratch_shapes=[
            pltpu.VMEM((height + 6, width + 16, LANES), jnp.float32),
            pltpu.VMEM((taps.shape[0], SUBLANES, LANES), jnp.float32),
            pltpu.VMEM((chans // LANES, height, width, LANES), jnp.float32),
            pltpu.VMEM((height, width, LANES), jnp.float32),
            pltpu.VMEM((height, width, LANES), jnp.float32),
        ],
        compiler_params=pltpu.CompilerParams(vmem_limit_bytes=VMEM_BYTES),
        name="forward",
    )(sizes, act, taps, gain, shift)


def mixed_grad_kernel(parts_ref, unit_ref, inv_ref, gain_ref, out_ref):
    parts, pixels, chans = parts_ref.shape
    chunk = 32

    @pl.loop(0, pixels // chunk)
    def _(step):
        rows = pl.ds(pl.multiple_of(step * chunk, chunk), chunk)
        total = parts_ref[0, rows, :].astype(jnp.float32)
        for part in range(1, parts):
            total = total + parts_ref[part, rows, :].astype(jnp.float32)
        scaled = total * gain_ref[...]
        unit = unit_ref[rows, :]
        mean = jnp.sum(scaled, axis=-1, keepdims=True) / chans
        along = jnp.sum(scaled * unit, axis=-1, keepdims=True) / chans
        inv = inv_ref[rows, 0:1]
        out_ref[rows, :] = (inv * (scaled - mean - unit * along)).astype(out_ref.dtype)


def mixed_grad(parts, unit, inv, gain):
    vmem = pl.BlockSpec(memory_space=pltpu.VMEM)
    return pl.pallas_call(
        mixed_grad_kernel,
        out_shape=jax.ShapeDtypeStruct(parts.shape[1:], jnp.bfloat16),
        in_specs=[vmem] * 4,
        out_specs=vmem,
        compiler_params=pltpu.CompilerParams(vmem_limit_bytes=VMEM_BYTES),
        name="mixed_grad",
    )(parts, unit, inv, gain)


def backward_kernel(size_ref, low_ref, own_ref, high_ref, taps_ref, out_ref, source, wide, result):
    rows_dev, width, chans = own_ref.shape
    stride = width // SUBLANES
    high, wid, band = size_ref[0], size_ref[1], size_ref[2]
    clear_margins(source, 0, rows_dev + 6, width)
    columns = lax.broadcasted_iota(jnp.int32, (width, LANES), 0) < wid

    @pl.loop(0, chans // LANES)
    def _(block):
        lanes = pl.ds(pl.multiple_of(block * LANES, LANES), LANES)
        widen_taps(taps_ref, wide, lanes)
        for ref, start in ((low_ref, 0), (own_ref, 3), (high_ref, 3 + rows_dev)):
            for row in range(ref.shape[0]):
                source[start + row, 8 : 8 + width, :] = ref[row, :, lanes].astype(jnp.float32)
        for first in range(0, rows_dev, TILE):
            for out, pieces in enumerate(conv_tile(source, wide, first, TILE, width, True)):
                for i, value in enumerate(pieces):
                    result[first + out, pl.ds(i, SUBLANES, stride=stride), :] = value
        for row in range(rows_dev):
            keep = columns & (band * rows_dev + row < high)
            out_ref[row, :, lanes] = jnp.where(keep, result[row], 0.0).astype(out_ref.dtype)


def backward(sizes, low, own, high, taps):
    rows_dev, width, chans = own.shape
    vmem = pl.BlockSpec(memory_space=pltpu.VMEM)
    return pl.pallas_call(
        backward_kernel,
        out_shape=jax.ShapeDtypeStruct(own.shape, jnp.bfloat16),
        in_specs=[pl.BlockSpec(memory_space=pltpu.SMEM), vmem, vmem, vmem, vmem],
        out_specs=vmem,
        scratch_shapes=[
            pltpu.VMEM((rows_dev + 6, width + 16, LANES), jnp.float32),
            pltpu.VMEM((taps.shape[0], SUBLANES, LANES), jnp.float32),
            pltpu.VMEM((rows_dev, width, LANES), jnp.float32),
        ],
        compiler_params=pltpu.CompilerParams(vmem_limit_bytes=VMEM_BYTES),
        name="backward",
    )(sizes, low, own, high, taps)


def project_kernel(parity_ref, grad_ref, mine_ref, other_ref, out_ref, whole):
    steps, band, _ = mine_ref.shape
    parity = parity_ref[0]
    for step in range(steps):
        for ref, core in ((mine_ref, parity), (other_ref, 1 - parity)):
            start = pl.multiple_of((2 * step + core) * band, 16)
            whole[pl.ds(start, band), :] = ref[step]
    for part in range(out_ref.shape[0]):
        out_ref[part] = lax.dot_general(
            grad_ref[part], whole[...], (((1,), (1,)), ((), ())), preferred_element_type=jnp.float32
        ).astype(out_ref.dtype)


def project(parity, grads, mine, other):
    bands, pixels, hidden = grads.shape
    steps, band, _ = mine.shape
    vmem = pl.BlockSpec(memory_space=pltpu.VMEM)
    return pl.pallas_call(
        project_kernel,
        out_shape=jax.ShapeDtypeStruct((bands, pixels, 2 * steps * band), jnp.bfloat16),
        in_specs=[pl.BlockSpec(memory_space=pltpu.SMEM), vmem, vmem, vmem],
        out_specs=vmem,
        scratch_shapes=[pltpu.VMEM((2 * steps * band, hidden), jnp.bfloat16)],
        compiler_params=pltpu.CompilerParams(vmem_limit_bytes=VMEM_BYTES),
        name="project",
    )(parity, grads, mine, other)


def outer_kernel(parity_ref, normed_ref, grad_ref, mine_ref, other_ref, whole):
    steps, band, _ = mine_ref.shape
    parity = parity_ref[0]
    whole[...] = lax.dot_general(
        normed_ref[...], grad_ref[...], (((0,), (0,)), ((), ())), preferred_element_type=jnp.float32
    )
    for step in range(steps):
        start = pl.multiple_of((2 * step + 1 - parity) * band, 16)
        other_ref[step] = whole[pl.ds(start, band), :].astype(other_ref.dtype)
        start = pl.multiple_of((2 * step + parity) * band, 16)
        mine_ref[step] = whole[pl.ds(start, band), :]


def outer(parity, normed, grad, count):
    chans, hidden = normed.shape[1], grad.shape[1]
    vmem = pl.BlockSpec(memory_space=pltpu.VMEM)
    halves = (count // 2, chans // count, hidden)
    return pl.pallas_call(
        outer_kernel,
        out_shape=(
            jax.ShapeDtypeStruct(halves, jnp.float32),
            jax.ShapeDtypeStruct(halves, jnp.bfloat16),
        ),
        in_specs=[pl.BlockSpec(memory_space=pltpu.SMEM), vmem, vmem],
        out_specs=(vmem, vmem),
        scratch_shapes=[pltpu.VMEM((chans, hidden), jnp.float32)],
        compiler_params=pltpu.CompilerParams(vmem_limit_bytes=VMEM_BYTES),
        name="outer",
    )(parity, normed, grad)


def parity_groups(count):
    return [[i for i in range(count) if i % 2 == p] for p in range(2)]


def swap_pairs(value):
    count = lax.axis_size("section")
    return lax.ppermute(value, "section", [(i, i ^ 1) for i in range(count)])


def gather_by_exchange(block, axis, groups=None):
    count = lax.axis_size(axis) if groups is None else len(groups[0])
    copies = jnp.broadcast_to(block[None], (count,) + block.shape)
    return lax.all_to_all(
        copies, axis, split_axis=0, concat_axis=0, axis_index_groups=groups, tiled=True
    )


def local(activations, cotangent, proj_weight, kernel_taps, ln_gain, ln_shift, heights, widths):
    rows_dev, width_dev, chans = activations.shape[1:]
    height_all = cotangent.shape[1]
    hidden_dev = cotangent.shape[3]
    bands = lax.axis_size("rows")
    count = lax.axis_size("section")
    band = lax.axis_index("rows")
    sizes = jnp.concatenate([heights, widths, band[None].astype(jnp.int32)])
    parity = lax.rem(lax.axis_index("section"), 2)[None].astype(jnp.int32)
    taps = kernel_taps.astype(jnp.float32)
    gain = ln_gain[None]
    shift = ln_shift[None]
    groups = parity_groups(count)

    proj_mine = gather_by_exchange(proj_weight, "section", groups)
    image = gather_by_exchange(activations[0], "rows").reshape(height_all, width_dev, chans)

    row_ids = lax.broadcasted_iota(jnp.int32, (height_all, width_dev), 0)
    col_ids = lax.broadcasted_iota(jnp.int32, (height_all, width_dev), 1)
    valid = ((row_ids < heights[0]) & (col_ids < widths[0])).astype(jnp.float32)
    live_grad = (cotangent[0].astype(jnp.float32) * valid[:, :, None]).astype(jnp.bfloat16)
    grad_flat = live_grad.reshape(-1, hidden_dev)

    normed, unit, inv = forward(sizes, image, taps, gain, shift, rows_dev)

    proj_other = swap_pairs(proj_mine)
    terms = project(parity, grad_flat.reshape(bands, -1, hidden_dev), proj_mine, proj_other)
    parts = lax.all_to_all(terms, "rows", split_axis=0, concat_axis=0, tiled=True)

    mine, other = outer(parity, normed, grad_flat, count)
    pair = (mine + swap_pairs(other).astype(jnp.float32)).astype(jnp.bfloat16)
    arrived = lax.all_to_all(
        pair, "section", split_axis=0, concat_axis=0, axis_index_groups=groups, tiled=True
    )
    weight_grad = jnp.sum(arrived.astype(jnp.float32), axis=0) / count

    grad_mixed = mixed_grad(parts, unit, inv, gain).reshape(rows_dev, width_dev, chans)
    low = lax.ppermute(grad_mixed[rows_dev - 3 :], "rows", [(i, i + 1) for i in range(bands - 1)])
    high = lax.ppermute(grad_mixed[:3], "rows", [(i + 1, i) for i in range(bands - 1)])
    back = backward(sizes, low, grad_mixed, high, taps)
    return (back[None], weight_grad)


def solution(mesh):
    in_specs = (
        P("section", "rows", None, None),
        P("section", None, None, "rows"),
        P("section", "rows"),
        P(),
        P(),
        P(),
        P("section"),
        P("section"),
    )
    out_specs = (P("section", "rows", None, None), P("section", "rows"))
    return jax.shard_map(local, mesh=mesh, in_specs=in_specs, out_specs=out_specs, check_vma=False)
```

```python
import functools

import jax
import jax.numpy as jnp
from jax import lax
from jax.experimental import pallas as pl
from jax.experimental.pallas import tpu as pltpu
from jax.sharding import PartitionSpec as P

epsilon = 1e-06
LANES = 128
SUBLANES = 8
VMEM_BYTES = 48 * 1024 * 1024


TILE = 4


def clear_margins(source, margin, rows, width):
    if margin:
        empty = jnp.zeros((margin,) + source.shape[1:], source.dtype)
        source[:margin] = empty
        source[margin + rows :] = empty
    sides = jnp.zeros((source.shape[0], 8, LANES), source.dtype)
    source[:, :8, :] = sides
    source[:, 8 + width :, :] = sides


def widen_taps(taps_ref, wide_ref, lanes):
    for tap in range(taps_ref.shape[0]):
        row = taps_ref[tap : tap + 1, lanes]
        wide_ref[tap] = jnp.broadcast_to(row, (SUBLANES, LANES))


def conv_tile(source_ref, wide_ref, first, tile, width, flip):
    stride = width // SUBLANES
    running = [[None] * stride for _ in range(tile)]
    for row in range(tile + 6):
        shifted = [
            source_ref[first + row, pl.ds(5 + k, SUBLANES, stride=stride), :]
            for k in range(stride + 6)
        ]
        for out in range(max(0, row - 6), min(tile, row + 1)):
            for along in range(7):
                tap = (row - out) * 7 + along
                weight = wide_ref[48 - tap if flip else tap]
                for i in range(stride):
                    term = weight * shifted[i + along]
                    before = running[out][i]
                    running[out][i] = term if before is None else before + term
    return running


def forward_kernel(
    size_ref, act_ref, taps_ref, gain_ref, shift_ref,
    normed_ref, unit_ref, inv_ref,
    source, wide, mixed, centres, spreads,
):
    height, width, chans = act_ref.shape
    blocks = chans // LANES
    stride = width // SUBLANES
    rows_dev = unit_ref.shape[0] // width
    tile = TILE
    high, wid, band = size_ref[0], size_ref[1], size_ref[2]
    clear_margins(source, 3, height, width)
    columns = lax.broadcasted_iota(jnp.int32, (width, LANES), 0) < wid

    @pl.loop(0, blocks)
    def _(block):
        lanes = pl.ds(pl.multiple_of(block * LANES, LANES), LANES)
        widen_taps(taps_ref, wide, lanes)

        @pl.loop(0, height // tile)
        def _(step):
            for i in range(tile):
                row = step * tile + i
                value = act_ref[row, :, lanes].astype(jnp.float32)
                source[row + 3, 8 : 8 + width, :] = jnp.where(columns & (row < high), value, 0.0)

        @pl.loop(0, height // tile)
        def _(step):
            first = step * tile
            for out, pieces in enumerate(conv_tile(source, wide, first, tile, width, False)):
                for i, value in enumerate(pieces):
                    mixed[block, first + out, pl.ds(i, SUBLANES, stride=stride), :] = value

    @pl.loop(0, height // tile)
    def _(step):
        rows = [step * tile + i for i in range(tile)]
        sums = [sum(mixed[block, row] for block in range(blocks)) for row in rows]
        for row, value in zip(rows, sums):
            centre = jnp.sum(value, axis=-1, keepdims=True) / chans
            centres[row] = jnp.broadcast_to(centre, (width, LANES))

    @pl.loop(0, height // tile)
    def _(step):
        rows = [step * tile + i for i in range(tile)]
        sums = []
        for row in rows:
            centre = centres[row]
            away = [mixed[block, row] - centre for block in range(blocks)]
            sums.append(sum(value * value for value in away))
        for row, value in zip(rows, sums):
            spread = jnp.sum(value, axis=-1, keepdims=True) / chans
            spreads[row] = jnp.broadcast_to(lax.rsqrt(spread + epsilon), (width, LANES))

    @pl.loop(0, height)
    def _(row):
        rows = pl.ds(pl.multiple_of(row * width, width), width)
        centre, inv = centres[row], spreads[row]
        for block in range(blocks):
            lanes = slice(block * LANES, (block + 1) * LANES)
            unit = (mixed[block, row] - centre) * inv
            normed_ref[rows, lanes] = (unit * gain_ref[:, lanes] + shift_ref[:, lanes]).astype(
                normed_ref.dtype
            )

    for i in range(rows_dev):
        row = band * rows_dev + i
        rows = slice(i * width, (i + 1) * width)
        centre, inv = centres[row], spreads[row]
        inv_ref[rows, :] = inv
        for block in range(blocks):
            lanes = slice(block * LANES, (block + 1) * LANES)
            unit_ref[rows, lanes] = (mixed[block, row] - centre) * inv


def forward(sizes, act, taps, gain, shift, rows_dev):
    height, width, chans = act.shape
    vmem = pl.BlockSpec(memory_space=pltpu.VMEM)
    return pl.pallas_call(
        forward_kernel,
        out_shape=(
            jax.ShapeDtypeStruct((height * width, chans), jnp.bfloat16),
            jax.ShapeDtypeStruct((rows_dev * width, chans), jnp.float32),
            jax.ShapeDtypeStruct((rows_dev * width, LANES), jnp.float32),
        ),
        in_specs=[pl.BlockSpec(memory_space=pltpu.SMEM), vmem, vmem, vmem, vmem],
        out_specs=(vmem, vmem, vmem),
        scratch_shapes=[
            pltpu.VMEM((height + 6, width + 16, LANES), jnp.float32),
            pltpu.VMEM((taps.shape[0], SUBLANES, LANES), jnp.float32),
            pltpu.VMEM((chans // LANES, height, width, LANES), jnp.float32),
            pltpu.VMEM((height, width, LANES), jnp.float32),
            pltpu.VMEM((height, width, LANES), jnp.float32),
        ],
        compiler_params=pltpu.CompilerParams(vmem_limit_bytes=VMEM_BYTES),
        name="forward",
    )(sizes, act, taps, gain, shift)


def mixed_grad_kernel(parts_ref, unit_ref, inv_ref, gain_ref, out_ref):
    parts, pixels, chans = parts_ref.shape
    chunk = 32

    @pl.loop(0, pixels // chunk)
    def _(step):
        rows = pl.ds(pl.multiple_of(step * chunk, chunk), chunk)
        total = parts_ref[0, rows, :].astype(jnp.float32)
        for part in range(1, parts):
            total = total + parts_ref[part, rows, :].astype(jnp.float32)
        scaled = total * gain_ref[...]
        unit = unit_ref[rows, :]
        mean = jnp.sum(scaled, axis=-1, keepdims=True) / chans
        along = jnp.sum(scaled * unit, axis=-1, keepdims=True) / chans
        inv = inv_ref[rows, 0:1]
        out_ref[rows, :] = (inv * (scaled - mean - unit * along)).astype(out_ref.dtype)


def mixed_grad(parts, unit, inv, gain):
    vmem = pl.BlockSpec(memory_space=pltpu.VMEM)
    return pl.pallas_call(
        mixed_grad_kernel,
        out_shape=jax.ShapeDtypeStruct(parts.shape[1:], jnp.bfloat16),
        in_specs=[vmem] * 4,
        out_specs=vmem,
        compiler_params=pltpu.CompilerParams(vmem_limit_bytes=VMEM_BYTES),
        name="mixed_grad",
    )(parts, unit, inv, gain)


def backward_kernel(size_ref, low_ref, own_ref, high_ref, taps_ref, out_ref, source, wide, result):
    rows_dev, width, chans = own_ref.shape
    stride = width // SUBLANES
    high, wid, band = size_ref[0], size_ref[1], size_ref[2]
    clear_margins(source, 0, rows_dev + 6, width)
    columns = lax.broadcasted_iota(jnp.int32, (width, LANES), 0) < wid

    @pl.loop(0, chans // LANES)
    def _(block):
        lanes = pl.ds(pl.multiple_of(block * LANES, LANES), LANES)
        widen_taps(taps_ref, wide, lanes)
        for ref, start in ((low_ref, 0), (own_ref, 3), (high_ref, 3 + rows_dev)):
            for row in range(ref.shape[0]):
                source[start + row, 8 : 8 + width, :] = ref[row, :, lanes].astype(jnp.float32)
        for first in range(0, rows_dev, TILE):
            for out, pieces in enumerate(conv_tile(source, wide, first, TILE, width, True)):
                for i, value in enumerate(pieces):
                    result[first + out, pl.ds(i, SUBLANES, stride=stride), :] = value
        for row in range(rows_dev):
            keep = columns & (band * rows_dev + row < high)
            out_ref[row, :, lanes] = jnp.where(keep, result[row], 0.0).astype(out_ref.dtype)


def backward(sizes, low, own, high, taps):
    rows_dev, width, chans = own.shape
    vmem = pl.BlockSpec(memory_space=pltpu.VMEM)
    return pl.pallas_call(
        backward_kernel,
        out_shape=jax.ShapeDtypeStruct(own.shape, jnp.bfloat16),
        in_specs=[pl.BlockSpec(memory_space=pltpu.SMEM), vmem, vmem, vmem, vmem],
        out_specs=vmem,
        scratch_shapes=[
            pltpu.VMEM((rows_dev + 6, width + 16, LANES), jnp.float32),
            pltpu.VMEM((taps.shape[0], SUBLANES, LANES), jnp.float32),
            pltpu.VMEM((rows_dev, width, LANES), jnp.float32),
        ],
        compiler_params=pltpu.CompilerParams(vmem_limit_bytes=VMEM_BYTES),
        name="backward",
    )(sizes, low, own, high, taps)


def project_kernel(grad_ref, proj_ref, out_ref):
    out_ref[...] = lax.dot_general(
        grad_ref[...], proj_ref[...], (((1,), (1,)), ((), ())), preferred_element_type=jnp.float32
    ).astype(out_ref.dtype)


def project(grad, proj):
    vmem = pl.BlockSpec(memory_space=pltpu.VMEM)
    return pl.pallas_call(
        project_kernel,
        out_shape=jax.ShapeDtypeStruct((grad.shape[0], proj.shape[0]), jnp.bfloat16),
        in_specs=[vmem, vmem],
        out_specs=vmem,
        compiler_params=pltpu.CompilerParams(vmem_limit_bytes=VMEM_BYTES),
        name="project",
    )(grad, proj)


def outer_kernel(where_ref, normed_ref, grad_ref, mine_ref, other_ref, whole):
    steps, band, _ = mine_ref.shape
    parity = where_ref[0]
    whole[...] = lax.dot_general(
        normed_ref[...], grad_ref[...], (((0,), (0,)), ((), ())), preferred_element_type=jnp.float32
    )
    for step in range(steps):
        start = pl.multiple_of((2 * step + 1 - parity) * band, 16)
        other_ref[step] = whole[pl.ds(start, band), :].astype(other_ref.dtype)
        start = pl.multiple_of((2 * step + parity) * band, 16)
        mine_ref[step] = whole[pl.ds(start, band), :]


def outer(where, normed, grad, count):
    chans, hidden = normed.shape[1], grad.shape[1]
    vmem = pl.BlockSpec(memory_space=pltpu.VMEM)
    halves = (count // 2, chans // count, hidden)
    return pl.pallas_call(
        outer_kernel,
        out_shape=(
            jax.ShapeDtypeStruct(halves, jnp.float32),
            jax.ShapeDtypeStruct(halves, jnp.bfloat16),
        ),
        in_specs=[pl.BlockSpec(memory_space=pltpu.SMEM), vmem, vmem],
        out_specs=(vmem, vmem),
        scratch_shapes=[pltpu.VMEM((chans, hidden), jnp.float32)],
        compiler_params=pltpu.CompilerParams(vmem_limit_bytes=VMEM_BYTES),
        name="outer",
    )(where, normed, grad)


def pair_sum_kernel(where_ref, mine_ref, other_ref, own_ref, *send_refs):
    steps = mine_ref.shape[0]
    place = where_ref[1]
    for index, ref in enumerate((own_ref,) + send_refs):
        step = partner(place, index, steps)
        total = mine_ref[step] + other_ref[step].astype(jnp.float32)
        ref[...] = total.astype(ref.dtype)


def pair_sum(where, mine, other):
    steps, band, hidden = mine.shape
    vmem = pl.BlockSpec(memory_space=pltpu.VMEM)
    return pl.pallas_call(
        pair_sum_kernel,
        out_shape=[jax.ShapeDtypeStruct((band, hidden), jnp.float32)]
        + [jax.ShapeDtypeStruct((band, hidden), jnp.bfloat16)] * (steps - 1),
        in_specs=[pl.BlockSpec(memory_space=pltpu.SMEM), vmem, vmem],
        out_specs=[vmem] * steps,
        compiler_params=pltpu.CompilerParams(vmem_limit_bytes=VMEM_BYTES),
        name="pair_sum",
    )(where, mine, other)


def partner(place, index, steps):
    if steps & (steps - 1) == 0:
        return place ^ index
    return (place + index) % steps


def swap_pairs(value):
    count = lax.axis_size("section")
    return lax.ppermute(value, "section", [(i, i ^ 1) for i in range(count)])


def scatter_pairs(where, mine, other):
    count = lax.axis_size("section")
    own, *sends = pair_sum(where, mine, swap_pairs(other))
    for index, send in enumerate(sends, 1):
        way = [(i, partner(i // 2, index, count // 2) * 2 + i % 2) for i in range(count)]
        own = own + lax.ppermute(send, "section", way).astype(jnp.float32)
    return own


def gather_by_exchange(block, axis):
    copies = jnp.broadcast_to(block[None], (lax.axis_size(axis),) + block.shape)
    return lax.all_to_all(copies, axis, split_axis=0, concat_axis=0, tiled=True)


def local(activations, cotangent, proj_weight, kernel_taps, ln_gain, ln_shift, heights, widths):
    rows_dev, width_dev, chans = activations.shape[1:]
    height_all = cotangent.shape[1]
    hidden_dev = cotangent.shape[3]
    bands = lax.axis_size("rows")
    count = lax.axis_size("section")
    band = lax.axis_index("rows")
    sizes = jnp.concatenate([heights, widths, band[None].astype(jnp.int32)])
    index = lax.axis_index("section")
    where = jnp.stack([lax.rem(index, 2), index // 2]).astype(jnp.int32)
    taps = kernel_taps.astype(jnp.float32)
    gain = ln_gain[None]
    shift = ln_shift[None]

    proj_rows = lax.all_gather(proj_weight, "section", axis=0, tiled=True)
    image = gather_by_exchange(activations[0], "rows").reshape(height_all, width_dev, chans)

    row_ids = lax.broadcasted_iota(jnp.int32, (height_all, width_dev), 0)
    col_ids = lax.broadcasted_iota(jnp.int32, (height_all, width_dev), 1)
    valid = ((row_ids < heights[0]) & (col_ids < widths[0])).astype(jnp.float32)
    live_grad = (cotangent[0].astype(jnp.float32) * valid[:, :, None]).astype(jnp.bfloat16)
    grad_flat = live_grad.reshape(-1, hidden_dev)

    normed, unit, inv = forward(sizes, image, taps, gain, shift, rows_dev)

    mine, other = outer(where, normed, grad_flat, count)
    terms = project(grad_flat, proj_rows).reshape(bands, -1, chans)
    parts = lax.all_to_all(terms, "rows", split_axis=0, concat_axis=0, tiled=True)
    weight_grad = scatter_pairs(where, mine, other) / count

    grad_mixed = mixed_grad(parts, unit, inv, gain).reshape(rows_dev, width_dev, chans)
    low = lax.ppermute(grad_mixed[rows_dev - 3 :], "rows", [(i, i + 1) for i in range(bands - 1)])
    high = lax.ppermute(grad_mixed[:3], "rows", [(i + 1, i) for i in range(bands - 1)])
    back = backward(sizes, low, grad_mixed, high, taps)
    return (back[None], weight_grad)


def solution(mesh):
    in_specs = (
        P("section", "rows", None, None),
        P("section", None, None, "rows"),
        P("section", "rows"),
        P(),
        P(),
        P(),
        P("section"),
        P("section"),
    )
    out_specs = (P("section", "rows", None, None), P("section", "rows"))
    return jax.shard_map(local, mesh=mesh, in_specs=in_specs, out_specs=out_specs, check_vma=False)
```

```python
import functools

import jax
import jax.numpy as jnp
from jax import lax
from jax.experimental import pallas as pl
from jax.experimental.pallas import tpu as pltpu
from jax.sharding import PartitionSpec as P

epsilon = 1e-06
LANES = 128
VECTOR = 240
SUBLANES = 8
VMEM_BYTES = 48 * 1024 * 1024


TILE = 4


def cost(operations, moved):
    return pl.CostEstimate(flops=operations, bytes_accessed=moved, transcendentals=0)


def clear_margins(source, margin, rows, width):
    if margin:
        empty = jnp.zeros((margin,) + source.shape[1:], source.dtype)
        source[:margin] = empty
        source[margin + rows :] = empty
    sides = jnp.zeros((source.shape[0], 8, LANES), source.dtype)
    source[:, :8, :] = sides
    source[:, 8 + width :, :] = sides


def widen_taps(taps_ref, wide_ref, lanes):
    for tap in range(taps_ref.shape[0]):
        row = taps_ref[tap : tap + 1, lanes]
        wide_ref[tap] = jnp.broadcast_to(row, (SUBLANES, LANES))


def conv_tile(source_ref, wide_ref, first, tile, width, flip):
    stride = width // SUBLANES
    running = [[None] * stride for _ in range(tile)]
    for row in range(tile + 6):
        shifted = [
            source_ref[first + row, pl.ds(5 + k, SUBLANES, stride=stride), :]
            for k in range(stride + 6)
        ]
        for out in range(max(0, row - 6), min(tile, row + 1)):
            for along in range(7):
                tap = (row - out) * 7 + along
                weight = wide_ref[48 - tap if flip else tap]
                for i in range(stride):
                    term = weight * shifted[i + along]
                    before = running[out][i]
                    running[out][i] = term if before is None else before + term
    return running


def forward_kernel(bands, size_ref, *refs):
    act_refs = refs[:bands]
    taps_ref, gain_ref, shift_ref, normed_ref, unit_ref, inv_ref = refs[bands : bands + 6]
    source, wide, mixed, centres, spreads = refs[bands + 6 :]
    rows_dev, width, chans = act_refs[0].shape
    height = rows_dev * bands
    blocks = chans // LANES
    stride = width // SUBLANES
    tile = TILE
    high, wid, band = size_ref[0], size_ref[1], size_ref[2]
    clear_margins(source, 3, height, width)
    columns = lax.broadcasted_iota(jnp.int32, (width, LANES), 0) < wid

    @pl.loop(0, blocks)
    def _(block):
        lanes = pl.ds(pl.multiple_of(block * LANES, LANES), LANES)
        widen_taps(taps_ref, wide, lanes)

        for index, act_ref in enumerate(act_refs):
            first = sender(band, index, bands) * rows_dev
            for i in range(rows_dev):
                row = first + i
                value = act_ref[i, :, lanes].astype(jnp.float32)
                source[row + 3, 8 : 8 + width, :] = jnp.where(columns & (row < high), value, 0.0)

        @pl.loop(0, height // tile)
        def _(step):
            first = step * tile
            for out, pieces in enumerate(conv_tile(source, wide, first, tile, width, False)):
                for i, value in enumerate(pieces):
                    mixed[block, first + out, pl.ds(i, SUBLANES, stride=stride), :] = value

    @pl.loop(0, height // tile)
    def _(step):
        rows = [step * tile + i for i in range(tile)]
        sums = [sum(mixed[block, row] for block in range(blocks)) for row in rows]
        for row, value in zip(rows, sums):
            centre = jnp.sum(value, axis=-1, keepdims=True) / chans
            centres[row] = jnp.broadcast_to(centre, (width, LANES))

    @pl.loop(0, height // tile)
    def _(step):
        rows = [step * tile + i for i in range(tile)]
        sums = []
        for row in rows:
            centre = centres[row]
            away = [mixed[block, row] - centre for block in range(blocks)]
            sums.append(sum(value * value for value in away))
        for row, value in zip(rows, sums):
            spread = jnp.sum(value, axis=-1, keepdims=True) / chans
            spreads[row] = jnp.broadcast_to(lax.rsqrt(spread + epsilon), (width, LANES))

    @pl.loop(0, height)
    def _(row):
        rows = pl.ds(pl.multiple_of(row * width, width), width)
        centre, inv = centres[row], spreads[row]
        for block in range(blocks):
            lanes = slice(block * LANES, (block + 1) * LANES)
            unit = (mixed[block, row] - centre) * inv
            normed_ref[rows, lanes] = (unit * gain_ref[:, lanes] + shift_ref[:, lanes]).astype(
                normed_ref.dtype
            )

    for i in range(rows_dev):
        row = band * rows_dev + i
        rows = slice(i * width, (i + 1) * width)
        centre, inv = centres[row], spreads[row]
        inv_ref[rows, :] = inv
        for block in range(blocks):
            lanes = slice(block * LANES, (block + 1) * LANES)
            unit_ref[rows, lanes] = (mixed[block, row] - centre) * inv


def forward(sizes, acts, taps, gain, shift):
    bands = len(acts)
    rows_dev, width, chans = acts[0].shape
    height = rows_dev * bands
    vmem = pl.BlockSpec(memory_space=pltpu.VMEM)
    return pl.pallas_call(
        functools.partial(forward_kernel, bands),
        out_shape=(
            jax.ShapeDtypeStruct((height * width, chans), jnp.bfloat16),
            jax.ShapeDtypeStruct((rows_dev * width, chans), jnp.float32),
            jax.ShapeDtypeStruct((rows_dev * width, LANES), jnp.float32),
        ),
        in_specs=[pl.BlockSpec(memory_space=pltpu.SMEM)] + [vmem] * (bands + 3),
        out_specs=(vmem, vmem, vmem),
        scratch_shapes=[
            pltpu.VMEM((height + 6, width + 16, LANES), jnp.float32),
            pltpu.VMEM((taps.shape[0], SUBLANES, LANES), jnp.float32),
            pltpu.VMEM((chans // LANES, height, width, LANES), jnp.float32),
            pltpu.VMEM((height, width, LANES), jnp.float32),
            pltpu.VMEM((height, width, LANES), jnp.float32),
        ],
        compiler_params=pltpu.CompilerParams(vmem_limit_bytes=VMEM_BYTES),
        cost_estimate=cost(VECTOR * height * width * chans * 49 * 2, 6 * height * width * chans),
        name="forward",
    )(sizes, *acts, taps, gain, shift)


def mixed_grad_kernel(bands, size_ref, *refs):
    own_ref, part_refs = refs[0], refs[1:bands]
    unit_ref, inv_ref, gain_ref, out_ref, first_ref, second_ref = refs[bands:]
    pixels, chans = own_ref.shape
    edge = first_ref.shape[0]
    chunk = 32

    @pl.loop(0, pixels // chunk)
    def _(step):
        rows = pl.ds(pl.multiple_of(step * chunk, chunk), chunk)
        total = own_ref[rows, :]
        for ref in part_refs:
            total = total + ref[rows, :].astype(jnp.float32)
        scaled = total * gain_ref[...]
        unit = unit_ref[rows, :]
        mean = jnp.sum(scaled, axis=-1, keepdims=True) / chans
        along = jnp.sum(scaled * unit, axis=-1, keepdims=True) / chans
        inv = inv_ref[rows, 0:1]
        out_ref[rows, :] = (inv * (scaled - mean - unit * along)).astype(out_ref.dtype)

    odd = lax.rem(size_ref[2], 2)
    start = pl.multiple_of((1 - odd) * (pixels - edge), 16)
    first_ref[...] = out_ref[pl.ds(start, edge), :]
    start = pl.multiple_of(odd * (pixels - edge), 16)
    second_ref[...] = out_ref[pl.ds(start, edge), :]


def mixed_grad(sizes, parts, unit, inv, gain, edge):
    bands = len(parts)
    pixels, chans = unit.shape
    vmem = pl.BlockSpec(memory_space=pltpu.VMEM)
    return pl.pallas_call(
        functools.partial(mixed_grad_kernel, bands),
        out_shape=(
            jax.ShapeDtypeStruct((pixels, chans), jnp.bfloat16),
            jax.ShapeDtypeStruct((edge, chans), jnp.bfloat16),
            jax.ShapeDtypeStruct((edge, chans), jnp.bfloat16),
        ),
        in_specs=[pl.BlockSpec(memory_space=pltpu.SMEM)] + [vmem] * (bands + 3),
        out_specs=(vmem, vmem, vmem),
        compiler_params=pltpu.CompilerParams(vmem_limit_bytes=VMEM_BYTES),
        cost_estimate=cost(VECTOR * pixels * chans * 10, 8 * pixels * chans),
        name="mixed_grad",
    )(sizes, *parts, unit, inv, gain)


def backward_kernel(size_ref, own_ref, first_ref, second_ref, taps_ref, out_ref, source, wide, result):
    rows_dev, width, chans = own_ref.shape
    stride = width // SUBLANES
    high, wid, band = size_ref[0], size_ref[1], size_ref[2]
    high_at = 3 + rows_dev
    clear_margins(source, 0, rows_dev + 6, width)
    columns = lax.broadcasted_iota(jnp.int32, (width, LANES), 0) < wid

    @pl.loop(0, chans // LANES)
    def _(block):
        lanes = pl.ds(pl.multiple_of(block * LANES, LANES), LANES)
        widen_taps(taps_ref, wide, lanes)
        odd = lax.rem(band, 2)
        places = ((own_ref, 3), (first_ref, (1 - odd) * high_at), (second_ref, odd * high_at))
        for ref, start in places:
            for row in range(ref.shape[0]):
                source[start + row, 8 : 8 + width, :] = ref[row, :, lanes].astype(jnp.float32)
        for first in range(0, rows_dev, TILE):
            for out, pieces in enumerate(conv_tile(source, wide, first, TILE, width, True)):
                for i, value in enumerate(pieces):
                    result[first + out, pl.ds(i, SUBLANES, stride=stride), :] = value
        for row in range(rows_dev):
            keep = columns & (band * rows_dev + row < high)
            out_ref[row, :, lanes] = jnp.where(keep, result[row], 0.0).astype(out_ref.dtype)


def backward(sizes, own, first, second, taps):
    rows_dev, width, chans = own.shape
    vmem = pl.BlockSpec(memory_space=pltpu.VMEM)
    return pl.pallas_call(
        backward_kernel,
        out_shape=jax.ShapeDtypeStruct(own.shape, jnp.bfloat16),
        in_specs=[pl.BlockSpec(memory_space=pltpu.SMEM), vmem, vmem, vmem, vmem],
        out_specs=vmem,
        scratch_shapes=[
            pltpu.VMEM((rows_dev + 6, width + 16, LANES), jnp.float32),
            pltpu.VMEM((taps.shape[0], SUBLANES, LANES), jnp.float32),
            pltpu.VMEM((rows_dev, width, LANES), jnp.float32),
        ],
        compiler_params=pltpu.CompilerParams(vmem_limit_bytes=VMEM_BYTES),
        cost_estimate=cost(VECTOR * own.size * 49 * 2, 4 * own.size),
        name="backward",
    )(sizes, own, first, second, taps)


def project_kernel(steps, bands, size_ref, where_ref, grad_ref, *refs):
    piece_refs, out_refs, (whole, result) = refs[: 2 * steps], refs[2 * steps : -2], refs[-2:]
    rows = piece_refs[0].shape[0]
    pixels = out_refs[0].shape[0]
    parity, place, band = where_ref[0], where_ref[1], size_ref[2]
    for index in range(steps):
        step = sender(place, index, steps)
        for ref, core in ((piece_refs[index], parity), (piece_refs[steps + index], 1 - parity)):
            start = pl.multiple_of((2 * step + core) * rows, 16)
            whole[pl.ds(start, rows), :] = ref[...]
    result[...] = lax.dot_general(
        grad_ref[...], whole[...], (((1,), (1,)), ((), ())), preferred_element_type=jnp.float32
    )
    for index, ref in enumerate(out_refs):
        start = pl.multiple_of(partner(band, index, bands) * pixels, 16)
        ref[...] = result[pl.ds(start, pixels), :].astype(ref.dtype)


def project(sizes, where, grad, pieces, bands):
    steps = len(pieces) // 2
    chans = len(pieces) * pieces[0].shape[0]
    pixels = grad.shape[0] // bands
    smem = pl.BlockSpec(memory_space=pltpu.SMEM)
    vmem = pl.BlockSpec(memory_space=pltpu.VMEM)
    return pl.pallas_call(
        functools.partial(project_kernel, steps, bands),
        out_shape=[jax.ShapeDtypeStruct((pixels, chans), jnp.float32)]
        + [jax.ShapeDtypeStruct((pixels, chans), jnp.bfloat16)] * (bands - 1),
        in_specs=[smem, smem] + [vmem] * (1 + len(pieces)),
        out_specs=[vmem] * bands,
        scratch_shapes=[
            pltpu.VMEM((chans, grad.shape[1]), jnp.bfloat16),
            pltpu.VMEM((grad.shape[0], chans), jnp.float32),
        ],
        compiler_params=pltpu.CompilerParams(vmem_limit_bytes=VMEM_BYTES),
        cost_estimate=cost(2 * grad.size * chans, 4 * grad.shape[0] * chans),
        name="project",
    )(sizes, where, grad, *pieces)


def outer_kernel(where_ref, normed_ref, grad_ref, mine_ref, other_ref, whole):
    steps, band, _ = mine_ref.shape
    parity = where_ref[0]
    whole[...] = lax.dot_general(
        normed_ref[...], grad_ref[...], (((0,), (0,)), ((), ())), preferred_element_type=jnp.float32
    )
    for step in range(steps):
        start = pl.multiple_of((2 * step + 1 - parity) * band, 16)
        other_ref[step] = whole[pl.ds(start, band), :].astype(other_ref.dtype)
        start = pl.multiple_of((2 * step + parity) * band, 16)
        mine_ref[step] = whole[pl.ds(start, band), :]


def outer(where, normed, grad, count):
    chans, hidden = normed.shape[1], grad.shape[1]
    vmem = pl.BlockSpec(memory_space=pltpu.VMEM)
    halves = (count // 2, chans // count, hidden)
    return pl.pallas_call(
        outer_kernel,
        out_shape=(
            jax.ShapeDtypeStruct(halves, jnp.float32),
            jax.ShapeDtypeStruct(halves, jnp.bfloat16),
        ),
        in_specs=[pl.BlockSpec(memory_space=pltpu.SMEM), vmem, vmem],
        out_specs=(vmem, vmem),
        scratch_shapes=[pltpu.VMEM((chans, hidden), jnp.float32)],
        compiler_params=pltpu.CompilerParams(vmem_limit_bytes=VMEM_BYTES),
        cost_estimate=cost(2 * grad.size * chans, 6 * chans * hidden),
        name="outer",
    )(where, normed, grad)


def pair_sum_kernel(where_ref, mine_ref, other_ref, own_ref, *send_refs):
    steps = mine_ref.shape[0]
    place = where_ref[1]
    for index, ref in enumerate((own_ref,) + send_refs):
        step = partner(place, index, steps)
        total = mine_ref[step] + other_ref[step].astype(jnp.float32)
        ref[...] = total.astype(ref.dtype)


def pair_sum(where, mine, other):
    steps, band, hidden = mine.shape
    vmem = pl.BlockSpec(memory_space=pltpu.VMEM)
    return pl.pallas_call(
        pair_sum_kernel,
        out_shape=[jax.ShapeDtypeStruct((band, hidden), jnp.float32)]
        + [jax.ShapeDtypeStruct((band, hidden), jnp.bfloat16)] * (steps - 1),
        in_specs=[pl.BlockSpec(memory_space=pltpu.SMEM), vmem, vmem],
        out_specs=[vmem] * steps,
        compiler_params=pltpu.CompilerParams(vmem_limit_bytes=VMEM_BYTES),
        cost_estimate=cost(VECTOR * mine.size * 2, 10 * mine.size),
        name="pair_sum",
    )(where, mine, other)


def partner(place, index, count):
    return place ^ index if count & (count - 1) == 0 else (place + index) % count


def sender(place, index, count):
    return place ^ index if count & (count - 1) == 0 else (place + count - index) % count


def swap_pairs(value):
    count = lax.axis_size("section")
    return lax.ppermute(value, "section", [(i, i ^ 1) for i in range(count)])


def send_rows(value, index):
    count = lax.axis_size("rows")
    return lax.ppermute(value, "rows", [(i, partner(i, index, count)) for i in range(count)])


def send_section(value, index):
    count = lax.axis_size("section")
    way = [(i, partner(i // 2, index, count // 2) * 2 + i % 2) for i in range(count)]
    return lax.ppermute(value, "section", way)


def swap_edges(first, second):
    count = lax.axis_size("rows")
    results = []
    for value, start in ((first, 0), (second, 1)):
        pairs = [(i, i + 1) for i in range(start, count - 1, 2)]
        results.append(lax.ppermute(value, "rows", pairs + [(b, a) for a, b in pairs]))
    return results


def local(activations, cotangent, proj_weight, kernel_taps, ln_gain, ln_shift, heights, widths):
    rows_dev, width_dev, chans = activations.shape[1:]
    height_all = cotangent.shape[1]
    hidden_dev = cotangent.shape[3]
    bands = lax.axis_size("rows")
    count = lax.axis_size("section")
    band = lax.axis_index("rows")
    sizes = jnp.concatenate([heights, widths, band[None].astype(jnp.int32)])
    index = lax.axis_index("section")
    where = jnp.stack([lax.rem(index, 2), index // 2]).astype(jnp.int32)
    taps = kernel_taps.astype(jnp.float32)
    gain = ln_gain[None]
    shift = ln_shift[None]

    steps = count // 2
    proj_mine = [proj_weight] + [send_section(proj_weight, i) for i in range(1, steps)]
    acts = [activations[0]] + [send_rows(activations[0], i) for i in range(1, bands)]
    proj_other = [swap_pairs(piece) for piece in proj_mine]

    row_ids = lax.broadcasted_iota(jnp.int32, (height_all, width_dev), 0)
    col_ids = lax.broadcasted_iota(jnp.int32, (height_all, width_dev), 1)
    valid = ((row_ids < heights[0]) & (col_ids < widths[0])).astype(jnp.float32)
    live_grad = (cotangent[0].astype(jnp.float32) * valid[:, :, None]).astype(jnp.bfloat16)
    grad_flat = live_grad.reshape(-1, hidden_dev)

    normed, unit, inv = forward(sizes, acts, taps, gain, shift)

    own, *terms = project(sizes, where, grad_flat, proj_mine + proj_other, bands)
    normed, terms = lax.optimization_barrier((normed, terms))
    mine, other = outer(where, normed, grad_flat, count)
    parts = [own] + [send_rows(term, i) for i, term in enumerate(terms, 1)]

    weight_grad, *sums = pair_sum(where, mine, swap_pairs(other))
    for i, value in enumerate(sums, 1):
        weight_grad = weight_grad + send_section(value, i).astype(jnp.float32)
    weight_grad = weight_grad / count

    grad_mixed, first, second = mixed_grad(sizes, parts, unit, inv, gain, 3 * width_dev)
    shape = (rows_dev, width_dev, chans)
    first, second = swap_edges(first, second)
    back = backward(
        sizes,
        grad_mixed.reshape(shape),
        first.reshape((3,) + shape[1:]),
        second.reshape((3,) + shape[1:]),
        taps,
    )
    return (back[None], weight_grad)


def solution(mesh):
    in_specs = (
        P("section", "rows", None, None),
        P("section", None, None, "rows"),
        P("section", "rows"),
        P(),
        P(),
        P(),
        P("section"),
        P("section"),
    )
    out_specs = (P("section", "rows", None, None), P("section", "rows"))
    return jax.shard_map(local, mesh=mesh, in_specs=in_specs, out_specs=out_specs, check_vma=False)
```

```python
import functools

import jax
import jax.numpy as jnp
from jax import lax
from jax.experimental import pallas as pl
from jax.experimental.pallas import tpu as pltpu
from jax.sharding import PartitionSpec as P

epsilon = 1e-06
LANES = 128
VECTOR = 240
SUBLANES = 8
VMEM_BYTES = 48 * 1024 * 1024


TILE = 4


def cost(operations, moved):
    return pl.CostEstimate(flops=operations, bytes_accessed=moved, transcendentals=0)


def clear_margins(source, margin, rows, width):
    if margin:
        empty = jnp.zeros((margin,) + source.shape[1:], source.dtype)
        source[:margin] = empty
        source[margin + rows :] = empty
    sides = jnp.zeros((source.shape[0], 8, LANES), source.dtype)
    source[:, :8, :] = sides
    source[:, 8 + width :, :] = sides


def widen_taps(taps_ref, wide_ref, lanes):
    for tap in range(taps_ref.shape[0]):
        row = taps_ref[tap : tap + 1, lanes]
        wide_ref[tap] = jnp.broadcast_to(row, (SUBLANES, LANES))


def conv_tile(source_ref, wide_ref, first, tile, width, flip):
    stride = width // SUBLANES
    running = [[None] * stride for _ in range(tile)]
    for row in range(tile + 6):
        shifted = [
            source_ref[first + row, pl.ds(5 + k, SUBLANES, stride=stride), :]
            for k in range(stride + 6)
        ]
        for out in range(max(0, row - 6), min(tile, row + 1)):
            for along in range(7):
                tap = (row - out) * 7 + along
                weight = wide_ref[48 - tap if flip else tap]
                for i in range(stride):
                    term = weight * shifted[i + along]
                    before = running[out][i]
                    running[out][i] = term if before is None else before + term
    return running


def forward_kernel(bands, size_ref, *refs):
    act_refs, (taps_ref, mixed, source, wide) = refs[:bands], refs[bands:]
    rows_dev, width, _ = act_refs[0].shape
    blocks, height = mixed.shape[:2]
    stride = width // SUBLANES
    high, wid, band = size_ref[0], size_ref[1], size_ref[2]
    clear_margins(source, 3, height, width)
    columns = lax.broadcasted_iota(jnp.int32, (width, LANES), 0) < wid

    @pl.loop(0, blocks)
    def _(block):
        lanes = pl.ds(pl.multiple_of(block * LANES, LANES), LANES)
        widen_taps(taps_ref, wide, lanes)

        for index, act_ref in enumerate(act_refs):
            first = sender(band, index, bands) * rows_dev
            for i in range(rows_dev):
                row = first + i
                value = act_ref[i, :, lanes].astype(jnp.float32)
                source[row + 3, 8 : 8 + width, :] = jnp.where(columns & (row < high), value, 0.0)

        @pl.loop(0, height // TILE)
        def _(step):
            first = step * TILE
            for out, pieces in enumerate(conv_tile(source, wide, first, TILE, width, False)):
                for i, value in enumerate(pieces):
                    mixed[block, first + out, pl.ds(i, SUBLANES, stride=stride), :] = value


def forward(sizes, acts, taps):
    bands = len(acts)
    rows_dev, width, chans = acts[0].shape
    height = rows_dev * bands
    vmem = pl.BlockSpec(memory_space=pltpu.VMEM)
    return pl.pallas_call(
        functools.partial(forward_kernel, bands),
        out_shape=jax.ShapeDtypeStruct((chans // LANES, height, width, LANES), jnp.float32),
        in_specs=[pl.BlockSpec(memory_space=pltpu.SMEM)] + [vmem] * (bands + 1),
        out_specs=vmem,
        scratch_shapes=[
            pltpu.VMEM((height + 6, width + 16, LANES), jnp.float32),
            pltpu.VMEM((taps.shape[0], SUBLANES, LANES), jnp.float32),
        ],
        compiler_params=pltpu.CompilerParams(vmem_limit_bytes=VMEM_BYTES),
        cost_estimate=cost(VECTOR * height * width * chans * 49 * 2, 6 * height * width * chans),
        name="forward",
    )(sizes, *acts, taps)


def normalise_kernel(
    size_ref, mixed, gain_ref, shift_ref, normed_ref, unit_ref, inv_ref, centres, spreads
):
    blocks, height, width, _ = mixed.shape
    chans = blocks * LANES
    rows_dev = unit_ref.shape[0] // width
    band = size_ref[2]

    @pl.loop(0, height // TILE)
    def _(step):
        rows = [step * TILE + i for i in range(TILE)]
        sums = [sum(mixed[block, row] for block in range(blocks)) for row in rows]
        for row, value in zip(rows, sums):
            centre = jnp.sum(value, axis=-1, keepdims=True) / chans
            centres[row] = jnp.broadcast_to(centre, (width, LANES))

    @pl.loop(0, height // TILE)
    def _(step):
        rows = [step * TILE + i for i in range(TILE)]
        sums = []
        for row in rows:
            centre = centres[row]
            away = [mixed[block, row] - centre for block in range(blocks)]
            sums.append(sum(value * value for value in away))
        for row, value in zip(rows, sums):
            spread = jnp.sum(value, axis=-1, keepdims=True) / chans
            spreads[row] = jnp.broadcast_to(lax.rsqrt(spread + epsilon), (width, LANES))

    @pl.loop(0, height)
    def _(row):
        rows = pl.ds(pl.multiple_of(row * width, width), width)
        centre, inv = centres[row], spreads[row]
        for block in range(blocks):
            lanes = slice(block * LANES, (block + 1) * LANES)
            unit = (mixed[block, row] - centre) * inv
            normed_ref[rows, lanes] = (unit * gain_ref[:, lanes] + shift_ref[:, lanes]).astype(
                normed_ref.dtype
            )

    for i in range(rows_dev):
        row = band * rows_dev + i
        rows = slice(i * width, (i + 1) * width)
        centre, inv = centres[row], spreads[row]
        inv_ref[rows, :] = inv
        for block in range(blocks):
            lanes = slice(block * LANES, (block + 1) * LANES)
            unit_ref[rows, lanes] = (mixed[block, row] - centre) * inv


def normalise(sizes, mixed, gain, shift, rows_dev):
    blocks, height, width, _ = mixed.shape
    chans = blocks * LANES
    vmem = pl.BlockSpec(memory_space=pltpu.VMEM)
    return pl.pallas_call(
        normalise_kernel,
        out_shape=(
            jax.ShapeDtypeStruct((height * width, chans), jnp.bfloat16),
            jax.ShapeDtypeStruct((rows_dev * width, chans), jnp.float32),
            jax.ShapeDtypeStruct((rows_dev * width, LANES), jnp.float32),
        ),
        in_specs=[pl.BlockSpec(memory_space=pltpu.SMEM)] + [vmem] * 3,
        out_specs=(vmem, vmem, vmem),
        scratch_shapes=[
            pltpu.VMEM((height, width, LANES), jnp.float32),
            pltpu.VMEM((height, width, LANES), jnp.float32),
        ],
        compiler_params=pltpu.CompilerParams(vmem_limit_bytes=VMEM_BYTES),
        cost_estimate=cost(VECTOR * mixed.size * 20, 6 * mixed.size),
        name="normalise",
    )(sizes, mixed, gain, shift)


def mixed_grad_kernel(bands, size_ref, *refs):
    own_ref, part_refs = refs[0], refs[1:bands]
    unit_ref, inv_ref, gain_ref, out_ref, first_ref, second_ref = refs[bands:]
    pixels, chans = own_ref.shape
    edge = first_ref.shape[0]
    chunk = 32

    @pl.loop(0, pixels // chunk)
    def _(step):
        rows = pl.ds(pl.multiple_of(step * chunk, chunk), chunk)
        total = own_ref[rows, :]
        for ref in part_refs:
            total = total + ref[rows, :].astype(jnp.float32)
        scaled = total * gain_ref[...]
        unit = unit_ref[rows, :]
        mean = jnp.sum(scaled, axis=-1, keepdims=True) / chans
        along = jnp.sum(scaled * unit, axis=-1, keepdims=True) / chans
        inv = inv_ref[rows, 0:1]
        out_ref[rows, :] = (inv * (scaled - mean - unit * along)).astype(out_ref.dtype)

    odd = lax.rem(size_ref[2], 2)
    start = pl.multiple_of((1 - odd) * (pixels - edge), 16)
    first_ref[...] = out_ref[pl.ds(start, edge), :]
    start = pl.multiple_of(odd * (pixels - edge), 16)
    second_ref[...] = out_ref[pl.ds(start, edge), :]


def mixed_grad(sizes, parts, unit, inv, gain, edge):
    bands = len(parts)
    pixels, chans = unit.shape
    vmem = pl.BlockSpec(memory_space=pltpu.VMEM)
    return pl.pallas_call(
        functools.partial(mixed_grad_kernel, bands),
        out_shape=(
            jax.ShapeDtypeStruct((pixels, chans), jnp.bfloat16),
            jax.ShapeDtypeStruct((edge, chans), jnp.bfloat16),
            jax.ShapeDtypeStruct((edge, chans), jnp.bfloat16),
        ),
        in_specs=[pl.BlockSpec(memory_space=pltpu.SMEM)] + [vmem] * (bands + 3),
        out_specs=(vmem, vmem, vmem),
        compiler_params=pltpu.CompilerParams(vmem_limit_bytes=VMEM_BYTES),
        cost_estimate=cost(VECTOR * pixels * chans * 10, 8 * pixels * chans),
        name="mixed_grad",
    )(sizes, *parts, unit, inv, gain)


def backward_kernel(size_ref, own_ref, first_ref, second_ref, taps_ref, out_ref, source, wide, result):
    rows_dev, width, chans = own_ref.shape
    stride = width // SUBLANES
    high, wid, band = size_ref[0], size_ref[1], size_ref[2]
    high_at = 3 + rows_dev
    clear_margins(source, 0, rows_dev + 6, width)
    columns = lax.broadcasted_iota(jnp.int32, (width, LANES), 0) < wid

    @pl.loop(0, chans // LANES)
    def _(block):
        lanes = pl.ds(pl.multiple_of(block * LANES, LANES), LANES)
        widen_taps(taps_ref, wide, lanes)
        odd = lax.rem(band, 2)
        places = ((own_ref, 3), (first_ref, (1 - odd) * high_at), (second_ref, odd * high_at))
        for ref, start in places:
            for row in range(ref.shape[0]):
                source[start + row, 8 : 8 + width, :] = ref[row, :, lanes].astype(jnp.float32)
        for first in range(0, rows_dev, TILE):
            for out, pieces in enumerate(conv_tile(source, wide, first, TILE, width, True)):
                for i, value in enumerate(pieces):
                    result[first + out, pl.ds(i, SUBLANES, stride=stride), :] = value
        for row in range(rows_dev):
            keep = columns & (band * rows_dev + row < high)
            out_ref[row, :, lanes] = jnp.where(keep, result[row], 0.0).astype(out_ref.dtype)


def backward(sizes, own, first, second, taps):
    rows_dev, width, chans = own.shape
    vmem = pl.BlockSpec(memory_space=pltpu.VMEM)
    return pl.pallas_call(
        backward_kernel,
        out_shape=jax.ShapeDtypeStruct(own.shape, jnp.bfloat16),
        in_specs=[pl.BlockSpec(memory_space=pltpu.SMEM), vmem, vmem, vmem, vmem],
        out_specs=vmem,
        scratch_shapes=[
            pltpu.VMEM((rows_dev + 6, width + 16, LANES), jnp.float32),
            pltpu.VMEM((taps.shape[0], SUBLANES, LANES), jnp.float32),
            pltpu.VMEM((rows_dev, width, LANES), jnp.float32),
        ],
        compiler_params=pltpu.CompilerParams(vmem_limit_bytes=VMEM_BYTES),
        cost_estimate=cost(VECTOR * own.size * 49 * 2, 4 * own.size),
        name="backward",
    )(sizes, own, first, second, taps)


def project_kernel(steps, bands, size_ref, where_ref, grad_ref, *refs):
    piece_refs, out_refs, (whole, result) = refs[: 2 * steps], refs[2 * steps : -2], refs[-2:]
    rows = piece_refs[0].shape[0]
    pixels = out_refs[0].shape[0]
    parity, place, band = where_ref[0], where_ref[1], size_ref[2]
    for index in range(steps):
        step = sender(place, index, steps)
        for ref, core in ((piece_refs[index], parity), (piece_refs[steps + index], 1 - parity)):
            start = pl.multiple_of((2 * step + core) * rows, 16)
            whole[pl.ds(start, rows), :] = ref[...]
    result[...] = lax.dot_general(
        grad_ref[...], whole[...], (((1,), (1,)), ((), ())), preferred_element_type=jnp.float32
    )
    for index, ref in enumerate(out_refs):
        start = pl.multiple_of(partner(band, index, bands) * pixels, 16)
        ref[...] = result[pl.ds(start, pixels), :].astype(ref.dtype)


def project(sizes, where, grad, pieces, bands):
    steps = len(pieces) // 2
    chans = len(pieces) * pieces[0].shape[0]
    pixels = grad.shape[0] // bands
    smem = pl.BlockSpec(memory_space=pltpu.SMEM)
    vmem = pl.BlockSpec(memory_space=pltpu.VMEM)
    return pl.pallas_call(
        functools.partial(project_kernel, steps, bands),
        out_shape=[jax.ShapeDtypeStruct((pixels, chans), jnp.float32)]
        + [jax.ShapeDtypeStruct((pixels, chans), jnp.bfloat16)] * (bands - 1),
        in_specs=[smem, smem] + [vmem] * (1 + len(pieces)),
        out_specs=[vmem] * bands,
        scratch_shapes=[
            pltpu.VMEM((chans, grad.shape[1]), jnp.bfloat16),
            pltpu.VMEM((grad.shape[0], chans), jnp.float32),
        ],
        compiler_params=pltpu.CompilerParams(vmem_limit_bytes=VMEM_BYTES),
        cost_estimate=cost(2 * grad.size * chans, 4 * grad.shape[0] * chans),
        name="project",
    )(sizes, where, grad, *pieces)


def split_halves(source, bit, keep_ref, send_ref):
    for piece in range(keep_ref.shape[0]):
        keep_ref[piece] = source(2 * piece + bit)
        send_ref[piece] = source(2 * piece + 1 - bit).astype(send_ref.dtype)


def outer_kernel(where_ref, normed_ref, grad_ref, keep_ref, send_ref, whole):
    band = keep_ref.shape[1]
    whole[...] = lax.dot_general(
        normed_ref[...], grad_ref[...], (((0,), (0,)), ((), ())), preferred_element_type=jnp.float32
    )

    def source(piece):
        return whole[pl.ds(pl.multiple_of(piece * band, 16), band), :]

    split_halves(source, where_ref[0], keep_ref, send_ref)


def fold_kernel(level, where_ref, held_ref, got_ref, keep_ref, send_ref):
    def source(piece):
        return held_ref[piece] + got_ref[piece].astype(jnp.float32)

    split_halves(source, lax.rem(where_ref[1] >> level - 1, 2), keep_ref, send_ref)


def halves(pieces, band, hidden):
    shape = (pieces // 2, band, hidden)
    return jax.ShapeDtypeStruct(shape, jnp.float32), jax.ShapeDtypeStruct(shape, jnp.bfloat16)


def outer(where, normed, grad, count):
    chans, hidden = normed.shape[1], grad.shape[1]
    vmem = pl.BlockSpec(memory_space=pltpu.VMEM)
    return pl.pallas_call(
        outer_kernel,
        out_shape=halves(count, chans // count, hidden),
        in_specs=[pl.BlockSpec(memory_space=pltpu.SMEM), vmem, vmem],
        out_specs=(vmem, vmem),
        scratch_shapes=[pltpu.VMEM((chans, hidden), jnp.float32)],
        compiler_params=pltpu.CompilerParams(vmem_limit_bytes=VMEM_BYTES),
        cost_estimate=cost(2 * grad.size * chans, 6 * chans * hidden),
        name="outer",
    )(where, normed, grad)


def fold(where, held, got, level):
    vmem = pl.BlockSpec(memory_space=pltpu.VMEM)
    return pl.pallas_call(
        functools.partial(fold_kernel, level),
        out_shape=halves(*held.shape),
        in_specs=[pl.BlockSpec(memory_space=pltpu.SMEM), vmem, vmem],
        out_specs=(vmem, vmem),
        compiler_params=pltpu.CompilerParams(vmem_limit_bytes=VMEM_BYTES),
        cost_estimate=cost(VECTOR * held.size * 2, 10 * held.size),
        name="fold",
    )(where, held, got)


def partner(place, index, count):
    return place ^ index if count & (count - 1) == 0 else (place + index) % count


def sender(place, index, count):
    return place ^ index if count & (count - 1) == 0 else (place + count - index) % count


def swap_pairs(value):
    count = lax.axis_size("section")
    return lax.ppermute(value, "section", [(i, i ^ 1) for i in range(count)])


def send_rows(value, index):
    count = lax.axis_size("rows")
    return lax.ppermute(value, "rows", [(i, partner(i, index, count)) for i in range(count)])


def send_section(value, index):
    count = lax.axis_size("section")
    way = [(i, partner(i // 2, index, count // 2) * 2 + i % 2) for i in range(count)]
    return lax.ppermute(value, "section", way)


def gather_pairs(block):
    steps = lax.axis_size("section") // 2
    if steps & (steps - 1):
        return [block] + [send_section(block, i) for i in range(1, steps)]
    pieces = {0: block}
    while len(pieces) < steps:
        far = steps // (2 * len(pieces))
        pieces |= {index ^ far: send_section(piece, far) for index, piece in pieces.items()}
    return [pieces[index] for index in range(steps)]


def scatter_section(where, keep, send):
    count = lax.axis_size("section")
    level = 0
    while True:
        way = [(i, i ^ 1 << level) for i in range(count)]
        got = lax.ppermute(send, "section", way)
        level += 1
        if keep.shape[0] % 2:
            break
        keep, send = fold(where, keep, got, level)
    rest = keep.shape[0]
    total = keep + got.astype(jnp.float32)
    if rest == 1:
        return total[0], send
    place = lax.axis_index("section") >> level
    result = lax.dynamic_index_in_dim(total, place, 0, keepdims=False)
    for shift in range(1, rest):
        piece = lax.dynamic_index_in_dim(total, (place + shift) % rest, 0, keepdims=False)
        way = [(i, (i + (shift << level)) % count) for i in range(count)]
        result = result + lax.ppermute(piece.astype(jnp.bfloat16), "section", way).astype(jnp.float32)
    return result, send


def after(value, *others):
    return lax.optimization_barrier((value, others))[0]


def swap_edges(first, second):
    count = lax.axis_size("rows")
    results = []
    for value, start in ((first, 0), (second, 1)):
        pairs = [(i, i + 1) for i in range(start, count - 1, 2)]
        results.append(lax.ppermute(value, "rows", pairs + [(b, a) for a, b in pairs]))
    return results


def local(activations, cotangent, proj_weight, kernel_taps, ln_gain, ln_shift, heights, widths):
    rows_dev, width_dev, chans = activations.shape[1:]
    height_all = cotangent.shape[1]
    hidden_dev = cotangent.shape[3]
    bands = lax.axis_size("rows")
    count = lax.axis_size("section")
    band = lax.axis_index("rows")
    sizes = jnp.concatenate([heights, widths, band[None].astype(jnp.int32)])
    index = lax.axis_index("section")
    where = jnp.stack([lax.rem(index, 2), index // 2]).astype(jnp.int32)
    taps = kernel_taps.astype(jnp.float32)
    gain = ln_gain[None]
    shift = ln_shift[None]

    acts = [activations[0]] + [send_rows(activations[0], i) for i in range(1, bands)]
    proj_mine = gather_pairs(proj_weight)
    row_ids = lax.broadcasted_iota(jnp.int32, (height_all, width_dev), 0)
    col_ids = lax.broadcasted_iota(jnp.int32, (height_all, width_dev), 1)
    valid = ((row_ids < heights[0]) & (col_ids < widths[0])).astype(jnp.float32)
    live_grad = (cotangent[0].astype(jnp.float32) * valid[:, :, None]).astype(jnp.bfloat16)
    grad_flat = live_grad.reshape(-1, hidden_dev)

    last = len(proj_mine) - 1
    proj_other = [swap_pairs(piece) for piece in proj_mine[:last]]
    mixed = forward(after(sizes, *proj_mine[1:last]), acts, taps)
    sizes_late = after(sizes, *proj_mine, *proj_other)
    normed, unit, inv = normalise(sizes_late, mixed, gain, shift, rows_dev)
    proj_other.append(swap_pairs(proj_mine[last]))

    keep, send = outer(where, normed, grad_flat, count)
    grads = after(grad_flat, keep)
    own, *terms = project(sizes, where, grads, proj_mine + proj_other, bands)
    parts = [send_rows(term, i) for i, term in enumerate(terms, 1)]

    weight_grad, sent = scatter_section(where, keep, send)
    weight_grad = weight_grad / count

    parts = [after(own, sent)] + parts
    grad_mixed, first, second = mixed_grad(sizes, parts, unit, inv, gain, 3 * width_dev)
    shape = (rows_dev, width_dev, chans)
    first, second = swap_edges(first, second)
    back = backward(
        sizes,
        grad_mixed.reshape(shape),
        first.reshape((3,) + shape[1:]),
        second.reshape((3,) + shape[1:]),
        taps,
    )
    return (back[None], weight_grad)


def solution(mesh):
    in_specs = (
        P("section", "rows", None, None),
        P("section", None, None, "rows"),
        P("section", "rows"),
        P(),
        P(),
        P(),
        P("section"),
        P("section"),
    )
    out_specs = (P("section", "rows", None, None), P("section", "rows"))
    return jax.shard_map(local, mesh=mesh, in_specs=in_specs, out_specs=out_specs, check_vma=False)
```

```python
import functools

import jax
import jax.numpy as jnp
from jax import lax
from jax.experimental import pallas as pl
from jax.experimental.pallas import tpu as pltpu
from jax.sharding import PartitionSpec as P

epsilon = 1e-06
LANES = 128
VECTOR = 240
SUBLANES = 8
VMEM_BYTES = 48 * 1024 * 1024


TILE = 4
GROUP = 8


def cost(operations, moved):
    return pl.CostEstimate(flops=operations, bytes_accessed=moved, transcendentals=0)


def cost(operations, moved):
    return pl.CostEstimate(flops=operations, bytes_accessed=moved, transcendentals=0)


def clear_sides(source, width):
    sides = jnp.zeros((source.shape[0], 8, LANES), source.dtype)
    source[:, :8, :] = sides
    source[:, 8 + width :, :] = sides


def conv_rows(source, positions, outs, wide_ref, lanes, width, flip):
    stride = width // SUBLANES
    running = {out: [None] * stride for out in outs}
    for row, position in enumerate(positions):
        users = [out for out in outs if 0 <= position - out <= 6]
        if not users:
            continue
        shifted = [
            source[row, pl.ds(5 + k, SUBLANES, stride=stride), :] for k in range(stride + 6)
        ]
        for out in users:
            for along in range(7):
                tap = (position - out) * 7 + along
                weight = wide_ref[48 - tap if flip else tap, :, lanes]
                for i in range(stride):
                    term = weight * shifted[i + along]
                    before = running[out][i]
                    running[out][i] = term if before is None else before + term
    return running


def forward_kernel(bands, indices, fresh, size_ref, *refs):
    act_refs = refs[: len(indices)]
    taps_ref, mixed, source = refs[len(indices)], refs[-2], refs[-1]
    rows_dev, width, _ = act_refs[0].shape
    blocks, height = mixed.shape[0], mixed.shape[1] - 6
    stride = width // SUBLANES
    high, wid, band = size_ref[0], size_ref[1], size_ref[2]
    joined = source.shape[0] // rows_dev
    clear_sides(source, width)
    columns = lax.broadcasted_iota(jnp.int32, (width, LANES), 0) < wid
    once = fresh and joined * rows_dev == source.shape[0] and len(indices) == joined
    firsts = [sender(band, index, bands) * rows_dev for index in indices]

    @pl.loop(0, blocks)
    def _(block):
        lanes = pl.ds(pl.multiple_of(block * LANES, LANES), LANES)
        if fresh:
            mixed[block] = jnp.zeros(mixed.shape[1:], mixed.dtype)
        for start in range(0, len(indices), joined):
            base = firsts[start]
            for first in firsts[start : start + joined]:
                base = jnp.minimum(base, first)
            for first, act_ref in zip(firsts[start:], act_refs[start : start + joined]):
                for i in range(rows_dev):
                    row = first + i
                    value = act_ref[i, :, lanes].astype(jnp.float32)
                    value = jnp.where(columns & (row < high), value, 0.0)
                    source[row - base, 8 : 8 + width, :] = value
            rows = joined * rows_dev
            for low in range(0, rows + 6, TILE):
                outs = range(low, min(low + TILE, rows + 6))
                positions = [i + 6 for i in range(rows)]
                running = conv_rows(source, positions, outs, taps_ref, lanes, width, False)
                for out, pieces in running.items():
                    for i, value in enumerate(pieces):
                        columns_of = pl.ds(i, SUBLANES, stride=stride)
                        if not once:
                            value = value + mixed[block, base + out, columns_of, :]
                        mixed[block, base + out, columns_of, :] = value


def forward(sizes, acts, indices, bands, taps, before=None):
    rows_dev, width, chans = acts[0].shape
    height = rows_dev * bands
    joined = 2 if bands & (bands - 1) == 0 else 1
    vmem = pl.BlockSpec(memory_space=pltpu.VMEM)
    extra = () if before is None else (before,)
    shape = (chans // LANES, height + 6, width, LANES)
    return pl.pallas_call(
        functools.partial(forward_kernel, bands, indices, before is None),
        out_shape=jax.ShapeDtypeStruct(shape, jnp.float32),
        in_specs=[pl.BlockSpec(memory_space=pltpu.SMEM)] + [vmem] * (len(acts) + 1 + len(extra)),
        out_specs=vmem,
        input_output_aliases={2 + len(acts): 0} if extra else {},
        scratch_shapes=[pltpu.VMEM((joined * rows_dev, width + 16, LANES), jnp.float32)],
        compiler_params=pltpu.CompilerParams(vmem_limit_bytes=VMEM_BYTES),
        cost_estimate=cost(3 * VECTOR * len(acts) * acts[0].size * 49 * 2, 6 * len(acts) * acts[0].size),
        name="forward",
    )(sizes, *acts, taps, *extra)


def normalise_kernel(
    size_ref, mixed, gain_ref, shift_ref, normed_ref, unit_ref, inv_ref, centres, spreads
):
    blocks, height, width, _ = mixed.shape
    height = height - 6
    chans = blocks * LANES
    rows_dev = unit_ref.shape[0] // width
    band = size_ref[2]

    @pl.loop(0, height // TILE)
    def _(step):
        rows = [step * TILE + i for i in range(TILE)]
        sums = [sum(mixed[block, row + 3] for block in range(blocks)) for row in rows]
        for row, value in zip(rows, sums):
            centre = jnp.sum(value, axis=-1, keepdims=True) / chans
            centres[row] = jnp.broadcast_to(centre, (width, LANES))

    @pl.loop(0, height // TILE)
    def _(step):
        rows = [step * TILE + i for i in range(TILE)]
        sums = []
        for row in rows:
            centre = centres[row]
            away = [mixed[block, row + 3] - centre for block in range(blocks)]
            sums.append(sum(value * value for value in away))
        for row, value in zip(rows, sums):
            spread = jnp.sum(value, axis=-1, keepdims=True) / chans
            spreads[row] = jnp.broadcast_to(lax.rsqrt(spread + epsilon), (width, LANES))

    @pl.loop(0, height)
    def _(row):
        rows = pl.ds(pl.multiple_of(row * width, width), width)
        centre, inv = centres[row], spreads[row]
        for block in range(blocks):
            lanes = slice(block * LANES, (block + 1) * LANES)
            unit = (mixed[block, row + 3] - centre) * inv
            normed_ref[rows, lanes] = (unit * gain_ref[:, lanes] + shift_ref[:, lanes]).astype(
                normed_ref.dtype
            )

    for i in range(rows_dev):
        row = band * rows_dev + i
        rows = slice(i * width, (i + 1) * width)
        centre, inv = centres[row], spreads[row]
        inv_ref[rows, :] = inv
        for block in range(blocks):
            lanes = slice(block * LANES, (block + 1) * LANES)
            unit_ref[rows, lanes] = (mixed[block, row + 3] - centre) * inv


def normalise(sizes, mixed, gain, shift, rows_dev):
    blocks, height, width, _ = mixed.shape
    height = height - 6
    chans = blocks * LANES
    vmem = pl.BlockSpec(memory_space=pltpu.VMEM)
    return pl.pallas_call(
        normalise_kernel,
        out_shape=(
            jax.ShapeDtypeStruct((height * width, chans), jnp.bfloat16),
            jax.ShapeDtypeStruct((rows_dev * width, chans), jnp.float32),
            jax.ShapeDtypeStruct((rows_dev * width, LANES), jnp.float32),
        ),
        in_specs=[pl.BlockSpec(memory_space=pltpu.SMEM)] + [vmem] * 3,
        out_specs=(vmem, vmem, vmem),
        scratch_shapes=[
            pltpu.VMEM((height, width, LANES), jnp.float32),
            pltpu.VMEM((height, width, LANES), jnp.float32),
        ],
        compiler_params=pltpu.CompilerParams(vmem_limit_bytes=VMEM_BYTES),
        cost_estimate=cost(1, 1),
        name="normalise",
    )(sizes, mixed, gain, shift)


def mixed_grad_kernel(bands, size_ref, *refs):
    own_ref, part_refs = refs[0], refs[1:bands]
    unit_ref, inv_ref, gain_ref, out_ref, first_ref, second_ref = refs[bands:]
    pixels, chans = own_ref.shape
    edge = first_ref.shape[0]
    chunk = 32

    @pl.loop(0, pixels // chunk)
    def _(step):
        rows = pl.ds(pl.multiple_of(step * chunk, chunk), chunk)
        total = own_ref[rows, :]
        for ref in part_refs:
            total = total + ref[rows, :].astype(jnp.float32)
        scaled = total * gain_ref[...]
        unit = unit_ref[rows, :]
        mean = jnp.sum(scaled, axis=-1, keepdims=True) / chans
        along = jnp.sum(scaled * unit, axis=-1, keepdims=True) / chans
        inv = inv_ref[rows, 0:1]
        out_ref[rows, :] = (inv * (scaled - mean - unit * along)).astype(out_ref.dtype)

    odd = lax.rem(size_ref[2], 2)
    start = pl.multiple_of((1 - odd) * (pixels - edge), 16)
    first_ref[...] = out_ref[pl.ds(start, edge), :]
    start = pl.multiple_of(odd * (pixels - edge), 16)
    second_ref[...] = out_ref[pl.ds(start, edge), :]


def mixed_grad(sizes, parts, unit, inv, gain, edge):
    bands = len(parts)
    pixels, chans = unit.shape
    vmem = pl.BlockSpec(memory_space=pltpu.VMEM)
    return pl.pallas_call(
        functools.partial(mixed_grad_kernel, bands),
        out_shape=(
            jax.ShapeDtypeStruct((pixels, chans), jnp.bfloat16),
            jax.ShapeDtypeStruct((edge, chans), jnp.bfloat16),
            jax.ShapeDtypeStruct((edge, chans), jnp.bfloat16),
        ),
        in_specs=[pl.BlockSpec(memory_space=pltpu.SMEM)] + [vmem] * (bands + 3),
        out_specs=(vmem, vmem, vmem),
        compiler_params=pltpu.CompilerParams(vmem_limit_bytes=VMEM_BYTES),
        cost_estimate=cost(1, 1),
        name="mixed_grad",
    )(sizes, *parts, unit, inv, gain)


def backward_own_kernel(own_ref, taps_ref, result, source):
    rows_dev, width, chans = own_ref.shape
    stride = width // SUBLANES
    clear_sides(source, width)

    @pl.loop(0, chans // LANES)
    def _(block):
        lanes = pl.ds(pl.multiple_of(block * LANES, LANES), LANES)
        for row in range(rows_dev):
            source[row, 8 : 8 + width, :] = own_ref[row, :, lanes].astype(jnp.float32)
        for low in range(0, rows_dev, TILE):
            outs = range(low, min(low + TILE, rows_dev))
            positions = [i + 3 for i in range(rows_dev)]
            running = conv_rows(source, positions, outs, taps_ref, lanes, width, True)
            for out, pieces in running.items():
                for i, value in enumerate(pieces):
                    result[block, out, pl.ds(i, SUBLANES, stride=stride), :] = value


def backward_own(own, taps):
    rows_dev, width, chans = own.shape
    vmem = pl.BlockSpec(memory_space=pltpu.VMEM)
    return pl.pallas_call(
        backward_own_kernel,
        out_shape=jax.ShapeDtypeStruct((chans // LANES, rows_dev, width, LANES), jnp.float32),
        in_specs=[vmem, vmem],
        out_specs=vmem,
        scratch_shapes=[pltpu.VMEM((rows_dev, width + 16, LANES), jnp.float32)],
        compiler_params=pltpu.CompilerParams(vmem_limit_bytes=VMEM_BYTES),
        cost_estimate=cost(VECTOR * own.size * 49, 4 * own.size),
        name="backward_own",
    )(own, taps)


def backward_kernel(size_ref, before_ref, first_ref, second_ref, taps_ref, out_ref, source, result):
    rows_dev, width, chans = out_ref.shape
    stride = width // SUBLANES
    high, wid, band = size_ref[0], size_ref[1], size_ref[2]
    odd = lax.rem(band, 2)
    clear_sides(source, width)
    columns = lax.broadcasted_iota(jnp.int32, (width, LANES), 0) < wid

    @pl.loop(0, chans // LANES)
    def _(block):
        lanes = pl.ds(pl.multiple_of(block * LANES, LANES), LANES)
        for ref, start in ((first_ref, (1 - odd) * 3), (second_ref, odd * 3)):
            for row in range(3):
                source[start + row, 8 : 8 + width, :] = ref[row, :, lanes].astype(jnp.float32)
        for low in range(0, rows_dev, TILE):
            outs = range(low, min(low + TILE, rows_dev))
            positions = [0, 1, 2] + [3 + rows_dev + i for i in range(3)]
            running = conv_rows(source, positions, outs, taps_ref, lanes, width, True)
            for out, pieces in running.items():
                for i, value in enumerate(pieces):
                    columns_of = pl.ds(i, SUBLANES, stride=stride)
                    if value is None:
                        value = jnp.zeros((SUBLANES, LANES), jnp.float32)
                    result[out, columns_of, :] = value + before_ref[block, out, columns_of, :]
        for row in range(rows_dev):
            keep = columns & (band * rows_dev + row < high)
            out_ref[row, :, lanes] = jnp.where(keep, result[row], 0.0).astype(out_ref.dtype)


def backward(sizes, before, first, second, taps):
    blocks, rows_dev, width, _ = before.shape
    vmem = pl.BlockSpec(memory_space=pltpu.VMEM)
    return pl.pallas_call(
        backward_kernel,
        out_shape=jax.ShapeDtypeStruct((rows_dev, width, blocks * LANES), jnp.bfloat16),
        in_specs=[pl.BlockSpec(memory_space=pltpu.SMEM), vmem, vmem, vmem, vmem],
        out_specs=vmem,
        scratch_shapes=[
            pltpu.VMEM((6, width + 16, LANES), jnp.float32),
            pltpu.VMEM((rows_dev, width, LANES), jnp.float32),
        ],
        compiler_params=pltpu.CompilerParams(vmem_limit_bytes=VMEM_BYTES),
        cost_estimate=cost(VECTOR * before.size * 49, 4 * before.size),
        name="backward",
    )(sizes, before, first, second, taps)


def project_kernel(steps, bands, size_ref, where_ref, grad_ref, *refs):
    piece_refs, out_refs, (whole, result) = refs[: 2 * steps], refs[2 * steps : -2], refs[-2:]
    rows = piece_refs[0].shape[0]
    pixels = out_refs[0].shape[0]
    parity, place, band = where_ref[0], where_ref[1], size_ref[2]
    for index in range(steps):
        step = sender(place, index, steps)
        for ref, core in ((piece_refs[index], parity), (piece_refs[steps + index], 1 - parity)):
            start = pl.multiple_of((2 * step + core) * rows, 16)
            whole[pl.ds(start, rows), :] = ref[...]
    result[...] = lax.dot_general(
        grad_ref[...], whole[...], (((1,), (1,)), ((), ())), preferred_element_type=jnp.float32
    )
    for index, ref in enumerate(out_refs):
        start = pl.multiple_of(partner(band, index, bands) * pixels, 16)
        ref[...] = result[pl.ds(start, pixels), :].astype(ref.dtype)


def project(sizes, where, grad, pieces, bands):
    steps = len(pieces) // 2
    chans = len(pieces) * pieces[0].shape[0]
    pixels = grad.shape[0] // bands
    smem = pl.BlockSpec(memory_space=pltpu.SMEM)
    vmem = pl.BlockSpec(memory_space=pltpu.VMEM)
    return pl.pallas_call(
        functools.partial(project_kernel, steps, bands),
        out_shape=[jax.ShapeDtypeStruct((pixels, chans), jnp.float32)]
        + [jax.ShapeDtypeStruct((pixels, chans), jnp.bfloat16)] * (bands - 1),
        in_specs=[smem, smem] + [vmem] * (1 + len(pieces)),
        out_specs=[vmem] * bands,
        scratch_shapes=[
            pltpu.VMEM((chans, grad.shape[1]), jnp.bfloat16),
            pltpu.VMEM((grad.shape[0], chans), jnp.float32),
        ],
        compiler_params=pltpu.CompilerParams(vmem_limit_bytes=VMEM_BYTES),
        cost_estimate=cost(1, 1),
        name="project",
    )(sizes, where, grad, *pieces)


def split_halves(source, bit, keep_ref, send_ref):
    for piece in range(keep_ref.shape[0]):
        keep_ref[piece] = source(2 * piece + bit)
        send_ref[piece] = source(2 * piece + 1 - bit).astype(send_ref.dtype)


def outer_kernel(where_ref, normed_ref, grad_ref, keep_ref, send_ref, whole):
    band = keep_ref.shape[1]
    whole[...] = lax.dot_general(
        normed_ref[...], grad_ref[...], (((0,), (0,)), ((), ())), preferred_element_type=jnp.float32
    )

    def source(piece):
        return whole[pl.ds(pl.multiple_of(piece * band, 16), band), :]

    split_halves(source, where_ref[0], keep_ref, send_ref)


def fold_kernel(level, where_ref, held_ref, got_ref, keep_ref, send_ref):
    def source(piece):
        return held_ref[piece] + got_ref[piece].astype(jnp.float32)

    split_halves(source, lax.rem(where_ref[1] >> level - 1, 2), keep_ref, send_ref)


def halves(pieces, band, hidden):
    shape = (pieces // 2, band, hidden)
    return jax.ShapeDtypeStruct(shape, jnp.float32), jax.ShapeDtypeStruct(shape, jnp.bfloat16)


def outer(where, normed, grad, count):
    chans, hidden = normed.shape[1], grad.shape[1]
    vmem = pl.BlockSpec(memory_space=pltpu.VMEM)
    return pl.pallas_call(
        outer_kernel,
        out_shape=halves(count, chans // count, hidden),
        in_specs=[pl.BlockSpec(memory_space=pltpu.SMEM), vmem, vmem],
        out_specs=(vmem, vmem),
        scratch_shapes=[pltpu.VMEM((chans, hidden), jnp.float32)],
        compiler_params=pltpu.CompilerParams(vmem_limit_bytes=VMEM_BYTES),
        cost_estimate=cost(1, 1),
        name="outer",
    )(where, normed, grad)


def fold(where, held, got, level):
    vmem = pl.BlockSpec(memory_space=pltpu.VMEM)
    return pl.pallas_call(
        functools.partial(fold_kernel, level),
        out_shape=halves(*held.shape),
        in_specs=[pl.BlockSpec(memory_space=pltpu.SMEM), vmem, vmem],
        out_specs=(vmem, vmem),
        compiler_params=pltpu.CompilerParams(vmem_limit_bytes=VMEM_BYTES),
        cost_estimate=cost(1, 1),
        name="fold",
    )(where, held, got)


def partner(place, index, count):
    return place ^ index if count & (count - 1) == 0 else (place + index) % count


def sender(place, index, count):
    return place ^ index if count & (count - 1) == 0 else (place + count - index) % count


def swap_pairs(value):
    count = lax.axis_size("section")
    return lax.ppermute(value, "section", [(i, i ^ 1) for i in range(count)])


def send_rows(value, index):
    count = lax.axis_size("rows")
    return lax.ppermute(value, "rows", [(i, partner(i, index, count)) for i in range(count)])


def send_section(value, index):
    count = lax.axis_size("section")
    way = [(i, partner(i // 2, index, count // 2) * 2 + i % 2) for i in range(count)]
    return lax.ppermute(value, "section", way)


def gather_pairs(block):
    steps = lax.axis_size("section") // 2
    if steps & (steps - 1):
        return [block] + [send_section(block, i) for i in range(1, steps)]
    pieces = {0: block}
    while len(pieces) < steps:
        far = steps // (2 * len(pieces))
        pieces |= {index ^ far: send_section(piece, far) for index, piece in pieces.items()}
    return [pieces[index] for index in range(steps)]


def scatter_section(where, keep, send):
    count = lax.axis_size("section")
    level, first_sent = 0, send
    while True:
        way = [(i, i ^ 1 << level) for i in range(count)]
        got = lax.ppermute(send, "section", way)
        level += 1
        if keep.shape[0] % 2:
            break
        keep, send = fold(where, keep, got, level)
        first_sent = send if level == 1 else first_sent
    rest = keep.shape[0]
    total = keep + got.astype(jnp.float32)
    if rest == 1:
        return total[0], first_sent
    place = lax.axis_index("section") >> level
    result = lax.dynamic_index_in_dim(total, place, 0, keepdims=False)
    for shift in range(1, rest):
        piece = lax.dynamic_index_in_dim(total, (place + shift) % rest, 0, keepdims=False)
        way = [(i, (i + (shift << level)) % count) for i in range(count)]
        result = result + lax.ppermute(piece.astype(jnp.bfloat16), "section", way).astype(jnp.float32)
    return result, first_sent


def after(value, *others):
    return lax.optimization_barrier((value, others))[0]


def swap_edges(first, second):
    count = lax.axis_size("rows")
    results = []
    for value, start in ((first, 0), (second, 1)):
        pairs = [(i, i + 1) for i in range(start, count - 1, 2)]
        results.append(lax.ppermute(value, "rows", pairs + [(b, a) for a, b in pairs]))
    return results


def local(activations, cotangent, proj_weight, kernel_taps, ln_gain, ln_shift, heights, widths):
    rows_dev, width_dev, chans = activations.shape[1:]
    height_all = cotangent.shape[1]
    hidden_dev = cotangent.shape[3]
    bands = lax.axis_size("rows")
    count = lax.axis_size("section")
    band = lax.axis_index("rows")
    sizes = jnp.concatenate([heights, widths, band[None].astype(jnp.int32)])
    index = lax.axis_index("section")
    where = jnp.stack([lax.rem(index, 2), index // 2]).astype(jnp.int32)
    taps = jnp.broadcast_to(
        kernel_taps.astype(jnp.float32)[:, None], (kernel_taps.shape[0], SUBLANES, chans)
    )
    gain = ln_gain[None]
    shift = ln_shift[None]

    acts = [activations[0]] + [send_rows(activations[0], i) for i in range(1, bands)]
    proj_mine = gather_pairs(proj_weight)
    row_ids = lax.broadcasted_iota(jnp.int32, (height_all, width_dev), 0)
    col_ids = lax.broadcasted_iota(jnp.int32, (height_all, width_dev), 1)
    valid = ((row_ids < heights[0]) & (col_ids < widths[0])).astype(jnp.float32)
    live_grad = (cotangent[0].astype(jnp.float32) * valid[:, :, None]).astype(jnp.bfloat16)
    grad_flat = live_grad.reshape(-1, hidden_dev)

    half = bands // 2
    indices = list(range(bands))
    mixed = forward(sizes, acts[:half], indices[:half], bands, taps)
    proj_other = [swap_pairs(after(piece, mixed)) for piece in proj_mine]
    sizes_there = after(sizes, *proj_mine, *proj_other[:-1])
    mixed = forward(sizes_there, acts[half:], indices[half:], bands, taps, mixed)

    normed, unit, inv = normalise(sizes, mixed, gain, shift, rows_dev)
    keep, send = outer(where, normed, grad_flat, count)
    grads = after(grad_flat, keep)
    own, *terms = project(sizes, where, grads, proj_mine + proj_other, bands)
    parts = [send_rows(term, i) for i, term in enumerate(terms, 1)]

    weight_grad, sent = scatter_section(where, keep, send)
    weight_grad = weight_grad / count

    parts = [after(own, sent)] + parts
    grad_mixed, first, second = mixed_grad(sizes, parts, unit, inv, gain, 3 * width_dev)
    shape = (rows_dev, width_dev, chans)
    first, second = swap_edges(first, second)
    before = backward_own(grad_mixed.reshape(shape), taps)
    edge_shape = (3,) + shape[1:]
    back = backward(sizes, before, first.reshape(edge_shape), second.reshape(edge_shape), taps)
    return (back[None], weight_grad)


def solution(mesh):
    in_specs = (
        P("section", "rows", None, None),
        P("section", None, None, "rows"),
        P("section", "rows"),
        P(),
        P(),
        P(),
        P("section"),
        P("section"),
    )
    out_specs = (P("section", "rows", None, None), P("section", "rows"))
    return jax.shard_map(local, mesh=mesh, in_specs=in_specs, out_specs=out_specs, check_vma=False)
```

```python
import functools

import jax
import jax.numpy as jnp
from jax import lax
from jax.experimental import pallas as pl
from jax.experimental.pallas import tpu as pltpu
from jax.sharding import PartitionSpec as P

epsilon = 1e-06
LANES = 128
VECTOR = 240
SUBLANES = 8
VMEM_BYTES = 48 * 1024 * 1024


TILE = 4

def cost(operations, moved):
    return pl.CostEstimate(flops=operations, bytes_accessed=moved, transcendentals=0)


def cost(operations, moved):
    return pl.CostEstimate(flops=operations, bytes_accessed=moved, transcendentals=0)


def clear_sides(source, width):
    sides = jnp.zeros((source.shape[0], 8, LANES), source.dtype)
    source[:, :8, :] = sides
    source[:, 8 + width :, :] = sides


def conv_rows(load, positions, outs, wide_ref, lanes, width, flip):
    stride = width // SUBLANES
    running = {out: [None] * stride for out in outs}
    for row, position in enumerate(positions):
        users = [out for out in outs if 0 <= position - out <= 6]
        if not users:
            continue
        shifted = [load(row, pl.ds(5 + k, SUBLANES, stride=stride)) for k in range(stride + 6)]
        for out in users:
            for along in range(7):
                tap = (position - out) * 7 + along
                weight = wide_ref[48 - tap if flip else tap, :, lanes]
                for i in range(stride):
                    term = weight * shifted[i + along]
                    before = running[out][i]
                    running[out][i] = term if before is None else before + term
    return running


def forward_kernel(bands, indices, fresh, size_ref, *refs):
    act_refs = refs[: len(indices)]
    taps_ref, mixed, source = refs[len(indices)], refs[-2], refs[-1]
    rows_dev, width, _ = act_refs[0].shape
    blocks, height = mixed.shape[0], mixed.shape[1] - 6
    stride = width // SUBLANES
    high, wid, band = size_ref[0], size_ref[1], size_ref[2]
    joined = source.shape[0] // rows_dev
    clear_sides(source, width)
    columns = lax.broadcasted_iota(jnp.int32, (width, LANES), 0) < wid
    once = fresh and joined * rows_dev == source.shape[0] and len(indices) == joined
    firsts = [sender(band, index, bands) * rows_dev for index in indices]

    @pl.loop(0, blocks)
    def _(block):
        lanes = pl.ds(pl.multiple_of(block * LANES, LANES), LANES)
        if fresh:
            mixed[block] = jnp.zeros(mixed.shape[1:], mixed.dtype)
        for start in range(0, len(indices), joined):
            base = firsts[start]
            for first in firsts[start : start + joined]:
                base = jnp.minimum(base, first)
            for first, act_ref in zip(firsts[start:], act_refs[start : start + joined]):
                for i in range(rows_dev):
                    row = first + i
                    value = act_ref[i, :, lanes].astype(jnp.float32)
                    value = jnp.where(columns & (row < high), value, 0.0)
                    source[row - base, 8 : 8 + width, :] = value
            rows = joined * rows_dev
            for low in range(0, rows + 6, TILE):
                outs = range(low, min(low + TILE, rows + 6))
                positions = [i + 6 for i in range(rows)]
                running = conv_rows(
                    lambda row, columns_of: source[row, columns_of, :],
                    positions, outs, taps_ref, lanes, width, False,
                )
                for out, pieces in running.items():
                    for i, value in enumerate(pieces):
                        columns_of = pl.ds(i, SUBLANES, stride=stride)
                        if not once:
                            value = value + mixed[block, base + out, columns_of, :]
                        mixed[block, base + out, columns_of, :] = value


def forward(sizes, acts, indices, bands, taps, before=None):
    rows_dev, width, chans = acts[0].shape
    height = rows_dev * bands
    joined = 2 if bands & (bands - 1) == 0 else 1
    vmem = pl.BlockSpec(memory_space=pltpu.VMEM)
    extra = () if before is None else (before,)
    shape = (chans // LANES, height + 6, width, LANES)
    return pl.pallas_call(
        functools.partial(forward_kernel, bands, indices, before is None),
        out_shape=jax.ShapeDtypeStruct(shape, jnp.float32),
        in_specs=[pl.BlockSpec(memory_space=pltpu.SMEM)] + [vmem] * (len(acts) + 1 + len(extra)),
        out_specs=vmem,
        input_output_aliases={2 + len(acts): 0} if extra else {},
        scratch_shapes=[pltpu.VMEM((joined * rows_dev, width + 16, LANES), jnp.float32)],
        compiler_params=pltpu.CompilerParams(vmem_limit_bytes=VMEM_BYTES),
        cost_estimate=cost(3 * VECTOR * len(acts) * acts[0].size * 49 * 2, 6 * len(acts) * acts[0].size),
        name="forward",
    )(sizes, *acts, taps, *extra)


def normalise_kernel(mixed, gain_ref, shift_ref, normed_ref, centres, spreads):
    blocks, height, width, _ = mixed.shape
    height = height - 6
    chans = blocks * LANES

    @pl.loop(0, height // TILE)
    def _(step):
        rows = [step * TILE + i for i in range(TILE)]
        sums = [sum(mixed[block, row + 3] for block in range(blocks)) for row in rows]
        for row, value in zip(rows, sums):
            centre = jnp.sum(value, axis=-1, keepdims=True) / chans
            centres[row] = jnp.broadcast_to(centre, (width, LANES))

    @pl.loop(0, height // TILE)
    def _(step):
        rows = [step * TILE + i for i in range(TILE)]
        sums = []
        for row in rows:
            centre = centres[row]
            away = [mixed[block, row + 3] - centre for block in range(blocks)]
            sums.append(sum(value * value for value in away))
        for row, value in zip(rows, sums):
            spread = jnp.sum(value, axis=-1, keepdims=True) / chans
            spreads[row] = jnp.broadcast_to(lax.rsqrt(spread + epsilon), (width, LANES))

    @pl.loop(0, height)
    def _(row):
        rows = pl.ds(pl.multiple_of(row * width, width), width)
        centre, inv = centres[row], spreads[row]
        for block in range(blocks):
            lanes = slice(block * LANES, (block + 1) * LANES)
            unit = (mixed[block, row + 3] - centre) * inv
            normed_ref[rows, lanes] = (unit * gain_ref[:, lanes] + shift_ref[:, lanes]).astype(
                normed_ref.dtype
            )


def normalise(mixed, gain, shift):
    blocks, height, width, _ = mixed.shape
    height = height - 6
    chans = blocks * LANES
    vmem = pl.BlockSpec(memory_space=pltpu.VMEM)
    return pl.pallas_call(
        normalise_kernel,
        out_shape=(
            jax.ShapeDtypeStruct((height * width, chans), jnp.bfloat16),
            jax.ShapeDtypeStruct((height, width, LANES), jnp.float32),
            jax.ShapeDtypeStruct((height, width, LANES), jnp.float32),
        ),
        in_specs=[vmem] * 3,
        out_specs=(vmem, vmem, vmem),
        compiler_params=pltpu.CompilerParams(vmem_limit_bytes=VMEM_BYTES),
        cost_estimate=cost(1, 1),
        name="normalise",
    )(mixed, gain, shift)


def project_kernel(steps, where_ref, grad_ref, mixed, centres, spreads, gain_ref, *refs):
    piece_refs, (out_ref, whole, result, means, alongs) = refs[: 2 * steps], refs[2 * steps :]
    band = piece_refs[0].shape[0]
    blocks, height, width, _ = mixed.shape
    height = height - 6
    chans = blocks * LANES
    parity, place = where_ref[0], where_ref[1]
    for index in range(steps):
        step = sender(place, index, steps)
        for ref, core in ((piece_refs[index], parity), (piece_refs[steps + index], 1 - parity)):
            start = pl.multiple_of((2 * step + core) * band, 16)
            whole[pl.ds(start, band), :] = ref[...]
    result[...] = lax.dot_general(
        grad_ref[...], whole[...], (((1,), (1,)), ((), ())), preferred_element_type=jnp.float32
    )

    def scaled_unit(row, block):
        rows = pl.ds(pl.multiple_of(row * width, width), width)
        lanes = slice(block * LANES, (block + 1) * LANES)
        scaled = result[rows, lanes] * gain_ref[:, lanes]
        return scaled, (mixed[block, row + 3] - centres[row]) * spreads[row]

    @pl.loop(0, height // TILE)
    def _(step):
        sums = []
        for i in range(TILE):
            row = step * TILE + i
            pairs = [scaled_unit(row, block) for block in range(blocks)]
            sums.append((row, sum(p[0] for p in pairs), sum(p[0] * p[1] for p in pairs)))
        for row, scaled, product in sums:
            mean = jnp.sum(scaled, axis=-1, keepdims=True) / chans
            means[row] = jnp.broadcast_to(mean, (width, LANES))
            along = jnp.sum(product, axis=-1, keepdims=True) / chans
            alongs[row] = jnp.broadcast_to(along, (width, LANES))

    @pl.loop(0, blocks)
    def _(block):
        clear_sides(out_ref.at[block], width)
        empty = jnp.zeros((3,) + out_ref.shape[2:], out_ref.dtype)
        out_ref[block, :3] = empty
        out_ref[block, 3 + height :] = empty

    @pl.loop(0, height)
    def _(row):
        mean, along, inv = means[row], alongs[row], spreads[row]
        for block in range(blocks):
            scaled, unit = scaled_unit(row, block)
            out_ref[block, row + 3, 8 : 8 + width, :] = inv * (scaled - mean - unit * along)


def project(where, grad, mixed, centres, spreads, gain, pieces):
    steps = len(pieces) // 2
    blocks, height, width, _ = mixed.shape
    chans = blocks * LANES
    vmem = pl.BlockSpec(memory_space=pltpu.VMEM)
    return pl.pallas_call(
        functools.partial(project_kernel, steps),
        out_shape=jax.ShapeDtypeStruct((blocks, height, width + 16, LANES), jnp.float32),
        in_specs=[pl.BlockSpec(memory_space=pltpu.SMEM)] + [vmem] * (5 + len(pieces)),
        out_specs=vmem,
        scratch_shapes=[
            pltpu.VMEM((chans, grad.shape[1]), jnp.bfloat16),
            pltpu.VMEM((grad.shape[0], chans), jnp.float32),
            pltpu.VMEM(centres.shape, jnp.float32),
            pltpu.VMEM(centres.shape, jnp.float32),
        ],
        compiler_params=pltpu.CompilerParams(vmem_limit_bytes=VMEM_BYTES),
        cost_estimate=cost(VECTOR * mixed.size * 12, 8 * mixed.size),
        name="project",
    )(where, grad, mixed, centres, spreads, gain, *pieces)


def backward_kernel(index, bands, size_ref, grad_ref, taps_ref, out_ref, result):
    rows_dev, width, chans = out_ref.shape
    stride = width // SUBLANES
    high, wid = size_ref[0], size_ref[1]
    first = partner(size_ref[2], index, bands) * rows_dev
    columns = lax.broadcasted_iota(jnp.int32, (width, LANES), 0) < wid

    @pl.loop(0, chans // LANES)
    def _(block):
        lanes = pl.ds(pl.multiple_of(block * LANES, LANES), LANES)
        for low in range(0, rows_dev, TILE):
            outs = range(low, min(low + TILE, rows_dev))
            running = conv_rows(
                lambda row, columns_of: grad_ref[block, first + row, columns_of, :],
                list(range(rows_dev + 6)), outs, taps_ref, lanes, width, True,
            )
            for out, pieces in running.items():
                for i, value in enumerate(pieces):
                    result[out, pl.ds(i, SUBLANES, stride=stride), :] = value
        for row in range(rows_dev):
            keep = columns & (first + row < high)
            out_ref[row, :, lanes] = jnp.where(keep, result[row], 0.0).astype(out_ref.dtype)


def backward(sizes, grad, taps, index, bands):
    blocks, height, width, _ = grad.shape
    rows_dev, width = (height - 6) // bands, width - 16
    vmem = pl.BlockSpec(memory_space=pltpu.VMEM)
    dtype = jnp.bfloat16 if index else jnp.float32
    return pl.pallas_call(
        functools.partial(backward_kernel, index, bands),
        out_shape=jax.ShapeDtypeStruct((rows_dev, width, blocks * LANES), dtype),
        in_specs=[pl.BlockSpec(memory_space=pltpu.SMEM), vmem, vmem],
        out_specs=vmem,
        scratch_shapes=[pltpu.VMEM((rows_dev, width, LANES), jnp.float32)],
        compiler_params=pltpu.CompilerParams(vmem_limit_bytes=VMEM_BYTES),
        cost_estimate=cost(VECTOR * rows_dev * width * blocks * LANES * 49 * 2, 1),
        name="backward",
    )(sizes, grad, taps)


def split_halves(source, bit, keep_ref, send_ref):
    for piece in range(keep_ref.shape[0]):
        keep_ref[piece] = source(2 * piece + bit)
        send_ref[piece] = source(2 * piece + 1 - bit).astype(send_ref.dtype)


def outer_kernel(where_ref, normed_ref, grad_ref, keep_ref, send_ref, whole):
    band = keep_ref.shape[1]
    whole[...] = lax.dot_general(
        normed_ref[...], grad_ref[...], (((0,), (0,)), ((), ())), preferred_element_type=jnp.float32
    )

    def source(piece):
        return whole[pl.ds(pl.multiple_of(piece * band, 16), band), :]

    split_halves(source, where_ref[0], keep_ref, send_ref)


def fold_kernel(level, where_ref, held_ref, got_ref, keep_ref, send_ref):
    def source(piece):
        return held_ref[piece] + got_ref[piece].astype(jnp.float32)

    split_halves(source, lax.rem(where_ref[1] >> level - 1, 2), keep_ref, send_ref)


def halves(pieces, band, hidden):
    shape = (pieces // 2, band, hidden)
    return jax.ShapeDtypeStruct(shape, jnp.float32), jax.ShapeDtypeStruct(shape, jnp.bfloat16)


def outer(where, normed, grad, count):
    chans, hidden = normed.shape[1], grad.shape[1]
    vmem = pl.BlockSpec(memory_space=pltpu.VMEM)
    return pl.pallas_call(
        outer_kernel,
        out_shape=halves(count, chans // count, hidden),
        in_specs=[pl.BlockSpec(memory_space=pltpu.SMEM), vmem, vmem],
        out_specs=(vmem, vmem),
        scratch_shapes=[pltpu.VMEM((chans, hidden), jnp.float32)],
        compiler_params=pltpu.CompilerParams(vmem_limit_bytes=VMEM_BYTES),
        cost_estimate=cost(1, 1),
        name="outer",
    )(where, normed, grad)


def fold(where, held, got, level):
    vmem = pl.BlockSpec(memory_space=pltpu.VMEM)
    return pl.pallas_call(
        functools.partial(fold_kernel, level),
        out_shape=halves(*held.shape),
        in_specs=[pl.BlockSpec(memory_space=pltpu.SMEM), vmem, vmem],
        out_specs=(vmem, vmem),
        compiler_params=pltpu.CompilerParams(vmem_limit_bytes=VMEM_BYTES),
        cost_estimate=cost(1, 1),
        name="fold",
    )(where, held, got)


def partner(place, index, count):
    return place ^ index if count & (count - 1) == 0 else (place + index) % count


def sender(place, index, count):
    return place ^ index if count & (count - 1) == 0 else (place + count - index) % count


def swap_pairs(value):
    count = lax.axis_size("section")
    return lax.ppermute(value, "section", [(i, i ^ 1) for i in range(count)])


def send_rows(value, index):
    count = lax.axis_size("rows")
    return lax.ppermute(value, "rows", [(i, partner(i, index, count)) for i in range(count)])


def send_section(value, index):
    count = lax.axis_size("section")
    way = [(i, partner(i // 2, index, count // 2) * 2 + i % 2) for i in range(count)]
    return lax.ppermute(value, "section", way)


def gather_pairs(block):
    steps = lax.axis_size("section") // 2
    if steps & (steps - 1):
        return [block] + [send_section(block, i) for i in range(1, steps)]
    pieces = {0: block}
    while len(pieces) < steps:
        far = steps // (2 * len(pieces))
        pieces |= {index ^ far: send_section(piece, far) for index, piece in pieces.items()}
    return [pieces[index] for index in range(steps)]


def scatter_section(where, keep, send):
    count = lax.axis_size("section")
    level, sends = 0, [send]
    while True:
        way = [(i, i ^ 1 << level) for i in range(count)]
        got = lax.ppermute(send, "section", way)
        level += 1
        if keep.shape[0] % 2:
            break
        keep, send = fold(where, keep, got, level)
        sends.append(send)
    rest = keep.shape[0]
    total = keep + got.astype(jnp.float32)
    if rest == 1:
        return total[0], sends
    place = lax.axis_index("section") >> level
    result = lax.dynamic_index_in_dim(total, place, 0, keepdims=False)
    for shift in range(1, rest):
        piece = lax.dynamic_index_in_dim(total, (place + shift) % rest, 0, keepdims=False)
        way = [(i, (i + (shift << level)) % count) for i in range(count)]
        result = result + lax.ppermute(piece.astype(jnp.bfloat16), "section", way).astype(jnp.float32)
    return result, sends


def after(value, *others):
    return lax.optimization_barrier((value, others))[0]


def gather_pairs(block):
    steps = lax.axis_size("section") // 2
    if steps & (steps - 1):
        return [block] + [send_section(block, i) for i in range(1, steps)]
    pieces = {0: block}
    while len(pieces) < steps:
        far = steps // (2 * len(pieces))
        pieces |= {index ^ far: send_section(piece, far) for index, piece in pieces.items()}
    return [pieces[index] for index in range(steps)]


def scatter_section(where, keep, send):
    count = lax.axis_size("section")
    level, sends = 0, [send]
    while True:
        way = [(i, i ^ 1 << level) for i in range(count)]
        got = lax.ppermute(send, "section", way)
        level += 1
        if keep.shape[0] % 2:
            break
        keep, send = fold(where, keep, got, level)
        sends.append(send)
    rest = keep.shape[0]
    total = keep + got.astype(jnp.float32)
    if rest == 1:
        return total[0], sends
    place = lax.axis_index("section") >> level
    result = lax.dynamic_index_in_dim(total, place, 0, keepdims=False)
    for shift in range(1, rest):
        piece = lax.dynamic_index_in_dim(total, (place + shift) % rest, 0, keepdims=False)
        way = [(i, (i + (shift << level)) % count) for i in range(count)]
        result = result + lax.ppermute(piece.astype(jnp.bfloat16), "section", way).astype(jnp.float32)
    return result, sends


def after(value, *others):
    return lax.optimization_barrier((value, others))[0]


def swap_edges(first, second):
    count = lax.axis_size("rows")
    results = []
    for value, start in ((first, 0), (second, 1)):
        pairs = [(i, i + 1) for i in range(start, count - 1, 2)]
        results.append(lax.ppermute(value, "rows", pairs + [(b, a) for a, b in pairs]))
    return results


def local(activations, cotangent, proj_weight, kernel_taps, ln_gain, ln_shift, heights, widths):
    rows_dev, width_dev, chans = activations.shape[1:]
    height_all = cotangent.shape[1]
    hidden_dev = cotangent.shape[3]
    bands = lax.axis_size("rows")
    count = lax.axis_size("section")
    band = lax.axis_index("rows")
    sizes = jnp.concatenate([heights, widths, band[None].astype(jnp.int32)])
    index = lax.axis_index("section")
    where = jnp.stack([lax.rem(index, 2), index // 2]).astype(jnp.int32)
    taps = jnp.broadcast_to(
        kernel_taps.astype(jnp.float32)[:, None], (kernel_taps.shape[0], SUBLANES, chans)
    )
    gain = ln_gain[None]
    shift = ln_shift[None]

    acts = [activations[0]] + [send_rows(activations[0], i) for i in range(1, bands)]
    proj_mine = gather_pairs(proj_weight)
    row_ids = lax.broadcasted_iota(jnp.int32, (height_all, width_dev), 0)
    col_ids = lax.broadcasted_iota(jnp.int32, (height_all, width_dev), 1)
    valid = ((row_ids < heights[0]) & (col_ids < widths[0])).astype(jnp.float32)
    live_grad = (cotangent[0].astype(jnp.float32) * valid[:, :, None]).astype(jnp.bfloat16)
    grad_flat = live_grad.reshape(-1, hidden_dev)

    half = bands // 2
    indices = list(range(bands))
    mixed = forward(sizes, acts[:half], indices[:half], bands, taps)
    proj_other = [swap_pairs(after(piece, mixed)) for piece in proj_mine]
    mixed = forward(after(sizes, *proj_mine), acts[half:], indices[half:], bands, taps, mixed)

    normed, centres, spreads = normalise(mixed, gain, shift)
    keep, send = outer(where, normed, grad_flat, count)
    weight_grad, sends = scatter_section(where, keep, send)
    weight_grad = weight_grad / count

    grads = after(grad_flat, keep)
    grad_mixed = project(where, grads, mixed, centres, spreads, gain, proj_mine + proj_other)
    sizes_sent = after(sizes, sends[min(1, len(sends) - 1)])
    sent = [
        send_rows(backward(sizes_sent, grad_mixed, taps, i, bands), i) for i in range(bands - 1, 0, -1)
    ]
    back = backward(after(sizes, sends[-1]), grad_mixed, taps, 0, bands)
    for value in sent:
        back = back + value.astype(jnp.float32)
    return (back.astype(jnp.bfloat16)[None], weight_grad)


def solution(mesh):
    in_specs = (
        P("section", "rows", None, None),
        P("section", None, None, "rows"),
        P("section", "rows"),
        P(),
        P(),
        P(),
        P("section"),
        P("section"),
    )
    out_specs = (P("section", "rows", None, None), P("section", "rows"))
    return jax.shard_map(local, mesh=mesh, in_specs=in_specs, out_specs=out_specs, check_vma=False)
```

```python
import functools

import jax
import jax.numpy as jnp
import numpy as np
from jax import lax
from jax.experimental import pallas as pl
from jax.experimental.pallas import tpu as pltpu
from jax.sharding import PartitionSpec as P

epsilon = 1e-06
LANES = 128
VECTOR = 240
SUBLANES = 8


TILE = 4

def cost(operations, moved):
    return pl.CostEstimate(flops=operations, bytes_accessed=moved, transcendentals=0)


def run(kernel, outs, args, scratch=(), estimate=None, aliases=None, name=None):
    held = [arg for arg in args if arg.ndim > 1] + list(outs) + list(scratch)
    taken = sum(int(np.prod(value.shape)) * jnp.dtype(value.dtype).itemsize for value in held)
    vmem = pl.BlockSpec(memory_space=pltpu.VMEM)
    smem = pl.BlockSpec(memory_space=pltpu.SMEM)
    return pl.pallas_call(
        kernel,
        out_shape=tuple(outs),
        in_specs=[smem if arg.ndim == 1 else vmem for arg in args],
        out_specs=tuple(vmem for _ in outs),
        scratch_shapes=[pltpu.VMEM(value.shape, value.dtype) for value in scratch],
        input_output_aliases=aliases or {},
        compiler_params=pltpu.CompilerParams(vmem_limit_bytes=taken + taken // 8 + (4 << 20)),
        cost_estimate=estimate or cost(1, 1),
        name=name,
    )(*args)


def f32(*shape):
    return jax.ShapeDtypeStruct(shape, jnp.float32)


def bf16(*shape):
    return jax.ShapeDtypeStruct(shape, jnp.bfloat16)


def clear_sides(source, width):
    sides = jnp.zeros((source.shape[0], 8, LANES), source.dtype)
    source[:, :8, :] = sides
    source[:, 8 + width :, :] = sides


def conv_rows(load, positions, outs, wide_ref, lanes, width, flip):
    stride = width // SUBLANES
    running = {out: [None] * stride for out in outs}
    for row, position in enumerate(positions):
        users = [out for out in outs if 0 <= position - out <= 6]
        if not users:
            continue
        shifted = [load(row, pl.ds(5 + k, SUBLANES, stride=stride)) for k in range(stride + 6)]
        for out in users:
            for along in range(7):
                tap = (position - out) * 7 + along
                weight = wide_ref[48 - tap if flip else tap, :, lanes]
                for i in range(stride):
                    term = weight * shifted[i + along]
                    before = running[out][i]
                    running[out][i] = term if before is None else before + term
    return running


def forward_kernel(bands, indices, fresh, size_ref, *refs):
    act_refs = refs[: len(indices)]
    taps_ref, mixed, source = refs[len(indices)], refs[-2], refs[-1]
    rows_dev, width, _ = act_refs[0].shape
    blocks, height = mixed.shape[0], mixed.shape[1] - 6
    stride = width // SUBLANES
    high, wid, band = size_ref[0], size_ref[1], size_ref[2]
    joined = source.shape[0] // rows_dev
    clear_sides(source, width)
    columns = lax.broadcasted_iota(jnp.int32, (width, LANES), 0) < wid
    once = fresh and joined * rows_dev == source.shape[0] and len(indices) == joined
    firsts = [sender(band, index, bands) * rows_dev for index in indices]

    @pl.loop(0, blocks)
    def _(block):
        lanes = pl.ds(pl.multiple_of(block * LANES, LANES), LANES)
        if fresh:
            mixed[block] = jnp.zeros(mixed.shape[1:], mixed.dtype)
        for start in range(0, len(indices), joined):
            base = firsts[start]
            for first in firsts[start : start + joined]:
                base = jnp.minimum(base, first)
            for first, act_ref in zip(firsts[start:], act_refs[start : start + joined]):
                for i in range(rows_dev):
                    row = first + i
                    value = act_ref[i, :, lanes].astype(jnp.float32)
                    value = jnp.where(columns & (row < high), value, 0.0)
                    source[row - base, 8 : 8 + width, :] = value
            rows = joined * rows_dev
            for low in range(0, rows + 6, TILE):
                outs = range(low, min(low + TILE, rows + 6))
                positions = [i + 6 for i in range(rows)]
                running = conv_rows(
                    lambda row, columns_of: source[row, columns_of, :],
                    positions, outs, taps_ref, lanes, width, False,
                )
                for out, pieces in running.items():
                    for i, value in enumerate(pieces):
                        columns_of = pl.ds(i, SUBLANES, stride=stride)
                        if not once:
                            value = value + mixed[block, base + out, columns_of, :]
                        mixed[block, base + out, columns_of, :] = value


def forward(sizes, acts, indices, bands, taps, before=None):
    rows_dev, width, chans = acts[0].shape
    joined = 2 if bands & (bands - 1) == 0 else 1
    extra = () if before is None else (before,)
    return run(
        functools.partial(forward_kernel, bands, indices, before is None),
        [f32(chans // LANES, rows_dev * bands + 6, width, LANES)],
        (sizes, *acts, taps, *extra),
        [f32(joined * rows_dev, width + 16, LANES)],
        cost(3 * VECTOR * len(acts) * acts[0].size * 49 * 2, 6 * len(acts) * acts[0].size),
        {2 + len(acts): 0} if extra else {},
        "forward",
    )[0]


def normalise_kernel(mixed, gain_ref, shift_ref, normed_ref, centres, spreads):
    blocks, height, width, _ = mixed.shape
    height = height - 6
    chans = blocks * LANES

    @pl.loop(0, height // TILE)
    def _(step):
        rows = [step * TILE + i for i in range(TILE)]
        sums = [sum(mixed[block, row + 3] for block in range(blocks)) for row in rows]
        for row, value in zip(rows, sums):
            centre = jnp.sum(value, axis=-1, keepdims=True) / chans
            centres[row] = jnp.broadcast_to(centre, (width, LANES))

    @pl.loop(0, height // TILE)
    def _(step):
        rows = [step * TILE + i for i in range(TILE)]
        sums = []
        for row in rows:
            centre = centres[row]
            away = [mixed[block, row + 3] - centre for block in range(blocks)]
            sums.append(sum(value * value for value in away))
        for row, value in zip(rows, sums):
            spread = jnp.sum(value, axis=-1, keepdims=True) / chans
            spreads[row] = jnp.broadcast_to(lax.rsqrt(spread + epsilon), (width, LANES))

    @pl.loop(0, height)
    def _(row):
        rows = pl.ds(pl.multiple_of(row * width, width), width)
        centre, inv = centres[row], spreads[row]
        for block in range(blocks):
            lanes = slice(block * LANES, (block + 1) * LANES)
            unit = (mixed[block, row + 3] - centre) * inv
            normed_ref[rows, lanes] = (unit * gain_ref[:, lanes] + shift_ref[:, lanes]).astype(
                normed_ref.dtype
            )


def normalise(mixed, gain, shift):
    blocks, height, width, _ = mixed.shape
    height = height - 6
    outs = [bf16(height * width, blocks * LANES)] + [f32(height, width, LANES)] * 2
    return run(normalise_kernel, outs, (mixed, gain, shift), name="normalise")


def project_kernel(groups, order, where_ref, grad_ref, mixed, centres, spreads, gain_ref, *refs):
    mine_refs, other_refs = refs[:groups], refs[groups : 2 * groups]
    out_ref, whole, result, means, alongs = refs[2 * groups :]
    size, band, _ = mine_refs[0].shape
    blocks, height, width, _ = mixed.shape
    height = height - 6
    chans = blocks * LANES
    parity, place = where_ref[0], where_ref[1]
    for refs_of, core in ((mine_refs, parity), (other_refs, 1 - parity)):
        for at, index in enumerate(order):
            step = sender(place, index, len(order))
            start = pl.multiple_of((2 * step + core) * band, 16)
            whole[pl.ds(start, band), :] = refs_of[at // size][at % size]
    result[...] = lax.dot_general(
        grad_ref[...], whole[...], (((1,), (1,)), ((), ())), preferred_element_type=jnp.float32
    )

    def scaled_unit(row, block):
        rows = pl.ds(pl.multiple_of(row * width, width), width)
        lanes = slice(block * LANES, (block + 1) * LANES)
        scaled = result[rows, lanes] * gain_ref[:, lanes]
        return scaled, (mixed[block, row + 3] - centres[row]) * spreads[row]

    @pl.loop(0, height // TILE)
    def _(step):
        sums = []
        for i in range(TILE):
            row = step * TILE + i
            pairs = [scaled_unit(row, block) for block in range(blocks)]
            sums.append((row, sum(p[0] for p in pairs), sum(p[0] * p[1] for p in pairs)))
        for row, scaled, product in sums:
            mean = jnp.sum(scaled, axis=-1, keepdims=True) / chans
            means[row] = jnp.broadcast_to(mean, (width, LANES))
            along = jnp.sum(product, axis=-1, keepdims=True) / chans
            alongs[row] = jnp.broadcast_to(along, (width, LANES))

    @pl.loop(0, blocks)
    def _(block):
        clear_sides(out_ref.at[block], width)
        empty = jnp.zeros((3,) + out_ref.shape[2:], out_ref.dtype)
        out_ref[block, :3] = empty
        out_ref[block, 3 + height :] = empty

    @pl.loop(0, height)
    def _(row):
        mean, along, inv = means[row], alongs[row], spreads[row]
        for block in range(blocks):
            scaled, unit = scaled_unit(row, block)
            out_ref[block, row + 3, 8 : 8 + width, :] = inv * (scaled - mean - unit * along)


def project(where, grad, mixed, centres, spreads, gain, mine, other, order):
    blocks, height, width, _ = mixed.shape
    chans = blocks * LANES
    return run(
        functools.partial(project_kernel, len(mine), order),
        [f32(blocks, height, width + 16, LANES)],
        (where, grad, mixed, centres, spreads, gain, *mine, *other),
        [bf16(chans, grad.shape[1]), f32(grad.shape[0], chans)] + [f32(*centres.shape)] * 2,
        cost(VECTOR * mixed.size * 12, 8 * mixed.size),
        name="project",
    )[0]


def backward_kernel(index, bands, size_ref, grad_ref, taps_ref, out_ref, result):
    rows_dev, width, chans = out_ref.shape
    stride = width // SUBLANES
    high, wid = size_ref[0], size_ref[1]
    first = partner(size_ref[2], index, bands) * rows_dev
    columns = lax.broadcasted_iota(jnp.int32, (width, LANES), 0) < wid

    @pl.loop(0, chans // LANES)
    def _(block):
        lanes = pl.ds(pl.multiple_of(block * LANES, LANES), LANES)
        for low in range(0, rows_dev, TILE):
            outs = range(low, min(low + TILE, rows_dev))
            running = conv_rows(
                lambda row, columns_of: grad_ref[block, first + row, columns_of, :],
                list(range(rows_dev + 6)), outs, taps_ref, lanes, width, True,
            )
            for out, pieces in running.items():
                for i, value in enumerate(pieces):
                    result[out, pl.ds(i, SUBLANES, stride=stride), :] = value
        for row in range(rows_dev):
            keep = columns & (first + row < high)
            out_ref[row, :, lanes] = jnp.where(keep, result[row], 0.0).astype(out_ref.dtype)


def backward(sizes, grad, taps, index, bands):
    blocks, height, width, _ = grad.shape
    rows_dev, width = (height - 6) // bands, width - 16
    shape = (rows_dev, width, blocks * LANES)
    return run(
        functools.partial(backward_kernel, index, bands),
        [bf16(*shape) if index else f32(*shape)],
        (sizes, grad, taps),
        [f32(rows_dev, width, LANES)],
        cost(VECTOR * rows_dev * width * blocks * LANES * 49 * 2, 1),
        name="backward",
    )[0]


def split_halves(source, bit, keep_ref, send_ref):
    for piece in range(keep_ref.shape[0]):
        keep_ref[piece] = source(2 * piece + bit)
        send_ref[piece] = source(2 * piece + 1 - bit).astype(send_ref.dtype)


def outer_kernel(where_ref, normed_ref, grad_ref, keep_ref, send_ref, whole):
    band = keep_ref.shape[1]
    whole[...] = lax.dot_general(
        normed_ref[...], grad_ref[...], (((0,), (0,)), ((), ())), preferred_element_type=jnp.float32
    )

    def source(piece):
        return whole[pl.ds(pl.multiple_of(piece * band, 16), band), :]

    split_halves(source, where_ref[0], keep_ref, send_ref)


def fold_kernel(level, where_ref, held_ref, got_ref, keep_ref, send_ref):
    def source(piece):
        return held_ref[piece] + got_ref[piece].astype(jnp.float32)

    split_halves(source, lax.rem(where_ref[1] >> level - 1, 2), keep_ref, send_ref)


def halves(pieces, band, hidden):
    return f32(pieces // 2, band, hidden), bf16(pieces // 2, band, hidden)


def outer(where, normed, grad, count):
    chans, hidden = normed.shape[1], grad.shape[1]
    outs = halves(count, chans // count, hidden)
    return run(outer_kernel, outs, (where, normed, grad), [f32(chans, hidden)], name="outer")


def fold(where, held, got, level):
    kernel = functools.partial(fold_kernel, level)
    return run(kernel, halves(*held.shape), (where, held, got), name="fold")


def partner(place, index, count):
    return place ^ index if count & (count - 1) == 0 else (place + index) % count


def sender(place, index, count):
    return place ^ index if count & (count - 1) == 0 else (place + count - index) % count


def swap_pairs(value):
    count = lax.axis_size("section")
    return lax.ppermute(value, "section", [(i, i ^ 1) for i in range(count)])


def send_rows(value, index):
    if index == 0:
        return value
    count = lax.axis_size("rows")
    return lax.ppermute(value, "rows", [(i, partner(i, index, count)) for i in range(count)])


def send_section(value, index):
    count = lax.axis_size("section")
    way = [(i, partner(i // 2, index, count // 2) * 2 + i % 2) for i in range(count)]
    return lax.ppermute(value, "section", way)


def gather_pairs(block):
    steps = lax.axis_size("section") // 2
    if steps & (steps - 1):
        sent = [send_section(block[None], i) for i in range(1, steps)]
        return [block[None]] + sent, list(range(steps))
    stack, order, half = block[None], [0], steps // 2
    while half > 1:
        stack = jnp.concatenate([stack, send_section(stack, half)])
        order = order + [index ^ half for index in order]
        half //= 2
    return [stack, send_section(stack, 1)], order + [index ^ 1 for index in order]


def scatter_section(where, keep, send):
    count = lax.axis_size("section")
    level, sends = 0, [send]
    while True:
        way = [(i, i ^ 1 << level) for i in range(count)]
        got = lax.ppermute(send, "section", way)
        level += 1
        if keep.shape[0] % 2:
            break
        keep, send = fold(where, keep, got, level)
        sends.append(send)
    rest = keep.shape[0]
    total = keep + got.astype(jnp.float32)
    if rest == 1:
        return total[0], sends
    place = lax.axis_index("section") >> level
    result = lax.dynamic_index_in_dim(total, place, 0, keepdims=False)
    for shift in range(1, rest):
        piece = lax.dynamic_index_in_dim(total, (place + shift) % rest, 0, keepdims=False)
        way = [(i, (i + (shift << level)) % count) for i in range(count)]
        result = result + lax.ppermute(piece.astype(jnp.bfloat16), "section", way).astype(jnp.float32)
    return result, sends


def after(value, *others):
    return lax.optimization_barrier((value, others))[0]


def local(activations, cotangent, proj_weight, kernel_taps, ln_gain, ln_shift, heights, widths):
    rows_dev, width_dev, chans = activations.shape[1:]
    height_all = cotangent.shape[1]
    hidden_dev = cotangent.shape[3]
    bands = lax.axis_size("rows")
    count = lax.axis_size("section")
    band = lax.axis_index("rows")
    sizes = jnp.concatenate([heights, widths, band[None].astype(jnp.int32)])
    index = lax.axis_index("section")
    where = jnp.stack([lax.rem(index, 2), index // 2]).astype(jnp.int32)
    taps = jnp.broadcast_to(
        kernel_taps.astype(jnp.float32)[:, None], (kernel_taps.shape[0], SUBLANES, chans)
    )
    gain = ln_gain[None]
    shift = ln_shift[None]

    acts = [activations[0]] + [send_rows(activations[0], i) for i in range(1, bands)]
    proj_mine, order = gather_pairs(proj_weight)
    row_ids = lax.broadcasted_iota(jnp.int32, (height_all, width_dev), 0)
    col_ids = lax.broadcasted_iota(jnp.int32, (height_all, width_dev), 1)
    valid = ((row_ids < heights[0]) & (col_ids < widths[0])).astype(jnp.float32)
    live_grad = (cotangent[0].astype(jnp.float32) * valid[:, :, None]).astype(jnp.bfloat16)
    grad_flat = live_grad.reshape(-1, hidden_dev)

    half = bands // 2
    indices = list(range(bands))
    mixed = forward(sizes, acts[:half], indices[:half], bands, taps)
    proj_other = [swap_pairs(after(stack, mixed)) for stack in proj_mine]
    mixed = forward(after(sizes, proj_mine[0]), acts[half:], indices[half:], bands, taps, mixed)

    normed, centres, spreads = normalise(mixed, gain, shift)
    keep, send = outer(where, normed, grad_flat, count)
    weight_grad, sends = scatter_section(where, keep, send)
    weight_grad = weight_grad / count

    grads = after(grad_flat, keep)
    grad_mixed = project(where, grads, mixed, centres, spreads, gain, proj_mine, proj_other, order)
    sent = []
    for i in range(bands - 1, -1, -1):
        ready = sends[min(1, len(sends) - 1)] if i > 1 else sends[-1]
        sent.append(send_rows(backward(after(sizes, ready), grad_mixed, taps, i, bands), i))
    back = sent.pop()
    for value in sent:
        back = back + value.astype(jnp.float32)
    return (back.astype(jnp.bfloat16)[None], weight_grad)


def solution(mesh):
    in_specs = (
        P("section", "rows", None, None),
        P("section", None, None, "rows"),
        P("section", "rows"),
        P(),
        P(),
        P(),
        P("section"),
        P("section"),
    )
    out_specs = (P("section", "rows", None, None), P("section", "rows"))
    return jax.shard_map(local, mesh=mesh, in_specs=in_specs, out_specs=out_specs, check_vma=False)
```

```python
import functools

import jax
import jax.numpy as jnp
import numpy as np
from jax import lax
from jax.experimental import pallas as pl
from jax.experimental.pallas import tpu as pltpu
from jax.sharding import PartitionSpec as P

epsilon = 1e-06
LANES = 128
VECTOR = 240
SUBLANES = 8


TILE = 4


def cost(operations, moved):
    return pl.CostEstimate(flops=operations, bytes_accessed=moved, transcendentals=0)


def run(kernel, outs, args, scratch=(), estimate=None, aliases=None, name=None):
    held = [arg for arg in args if arg.ndim > 1] + list(outs) + list(scratch)
    taken = sum(int(np.prod(value.shape)) * jnp.dtype(value.dtype).itemsize for value in held)
    vmem = pl.BlockSpec(memory_space=pltpu.VMEM)
    smem = pl.BlockSpec(memory_space=pltpu.SMEM)
    return pl.pallas_call(
        kernel,
        out_shape=tuple(outs),
        in_specs=[smem if arg.ndim == 1 else vmem for arg in args],
        out_specs=tuple(vmem for _ in outs),
        scratch_shapes=[pltpu.VMEM(value.shape, value.dtype) for value in scratch],
        input_output_aliases=aliases or {},
        compiler_params=pltpu.CompilerParams(vmem_limit_bytes=taken + taken // 8 + (4 << 20)),
        cost_estimate=estimate or cost(1, 1),
        name=name,
    )(*args)


def f32(*shape):
    return jax.ShapeDtypeStruct(shape, jnp.float32)


def bf16(*shape):
    return jax.ShapeDtypeStruct(shape, jnp.bfloat16)


def clear_sides(source, width):
    sides = jnp.zeros((source.shape[0], 8, LANES), source.dtype)
    source[:, :8, :] = sides
    source[:, 8 + width :, :] = sides


def conv_rows(load, positions, outs, wide_ref, lanes, width, flip):
    stride = width // SUBLANES
    running = {out: [None] * stride for out in outs}
    for row, position in enumerate(positions):
        users = [out for out in outs if 0 <= position - out <= 6]
        if not users:
            continue
        shifted = [load(row, pl.ds(5 + k, SUBLANES, stride=stride)) for k in range(stride + 6)]
        for out in users:
            for along in range(7):
                tap = (position - out) * 7 + along
                weight = wide_ref[48 - tap if flip else tap, :, lanes]
                for i in range(stride):
                    term = weight * shifted[i + along]
                    before = running[out][i]
                    running[out][i] = term if before is None else before + term
    return running


def forward_kernel(bands, indices, fresh, size_ref, *refs):
    act_refs = refs[: len(indices)]
    taps_ref, mixed, source = refs[len(indices)], refs[-2], refs[-1]
    rows_dev, width, _ = act_refs[0].shape
    blocks, height = mixed.shape[0], mixed.shape[1] - 6
    stride = width // SUBLANES
    high, wid, band = size_ref[0], size_ref[1], size_ref[2]
    joined = source.shape[0] // rows_dev
    clear_sides(source, width)
    columns = lax.broadcasted_iota(jnp.int32, (width, LANES), 0) < wid
    once = fresh and joined * rows_dev == source.shape[0] and len(indices) == joined
    firsts = [sender(band, index, bands) * rows_dev for index in indices]

    @pl.loop(0, blocks)
    def _(block):
        lanes = pl.ds(pl.multiple_of(block * LANES, LANES), LANES)
        if fresh:
            mixed[block] = jnp.zeros(mixed.shape[1:], mixed.dtype)
        for start in range(0, len(indices), joined):
            base = firsts[start]
            for first in firsts[start : start + joined]:
                base = jnp.minimum(base, first)
            for first, act_ref in zip(firsts[start:], act_refs[start : start + joined]):
                for i in range(rows_dev):
                    row = first + i
                    value = act_ref[i, :, lanes].astype(jnp.float32)
                    value = jnp.where(columns & (row < high), value, 0.0)
                    source[row - base, 8 : 8 + width, :] = value
            rows = joined * rows_dev
            for low in range(0, rows + 6, TILE):
                outs = range(low, min(low + TILE, rows + 6))
                positions = [i + 6 for i in range(rows)]
                running = conv_rows(
                    lambda row, columns_of: source[row, columns_of, :],
                    positions, outs, taps_ref, lanes, width, False,
                )
                for out, pieces in running.items():
                    for i, value in enumerate(pieces):
                        columns_of = pl.ds(i, SUBLANES, stride=stride)
                        if not once:
                            value = value + mixed[block, base + out, columns_of, :]
                        mixed[block, base + out, columns_of, :] = value


def forward(sizes, acts, indices, bands, taps, before=None):
    rows_dev, width, chans = acts[0].shape
    joined = 2 if bands & (bands - 1) == 0 else 1
    extra = () if before is None else (before,)
    return run(
        functools.partial(forward_kernel, bands, indices, before is None),
        [f32(chans // LANES, rows_dev * bands + 6, width, LANES)],
        (sizes, *acts, taps, *extra),
        [f32(joined * rows_dev, width + 16, LANES)],
        cost(3 * VECTOR * len(acts) * acts[0].size * 49 * 2, 6 * len(acts) * acts[0].size),
        {2 + len(acts): 0} if extra else {},
        "forward",
    )[0]


def normalise_kernel(mixed, gain_ref, shift_ref, normed_ref, centres, spreads):
    blocks, height, width, _ = mixed.shape
    height = height - 6
    chans = blocks * LANES

    @pl.loop(0, height // TILE)
    def _(step):
        rows = [step * TILE + i for i in range(TILE)]
        sums = [sum(mixed[block, row + 3] for block in range(blocks)) for row in rows]
        for row, value in zip(rows, sums):
            centre = jnp.sum(value, axis=-1, keepdims=True) / chans
            centres[row] = jnp.broadcast_to(centre, (width, LANES))

    @pl.loop(0, height // TILE)
    def _(step):
        rows = [step * TILE + i for i in range(TILE)]
        sums = []
        for row in rows:
            centre = centres[row]
            away = [mixed[block, row + 3] - centre for block in range(blocks)]
            sums.append(sum(value * value for value in away))
        for row, value in zip(rows, sums):
            spread = jnp.sum(value, axis=-1, keepdims=True) / chans
            spreads[row] = jnp.broadcast_to(lax.rsqrt(spread + epsilon), (width, LANES))

    @pl.loop(0, height)
    def _(row):
        rows = pl.ds(pl.multiple_of(row * width, width), width)
        centre, inv = centres[row], spreads[row]
        for block in range(blocks):
            lanes = slice(block * LANES, (block + 1) * LANES)
            unit = (mixed[block, row + 3] - centre) * inv
            normed_ref[rows, lanes] = (unit * gain_ref[:, lanes] + shift_ref[:, lanes]).astype(
                normed_ref.dtype
            )


def normalise(mixed, gain, shift):
    blocks, height, width, _ = mixed.shape
    height = height - 6
    outs = [bf16(height * width, blocks * LANES)] + [f32(height, width, LANES)] * 2
    return run(normalise_kernel, outs, (mixed, gain, shift), name="normalise")


def project_kernel(groups, order, where_ref, grad_ref, mixed, centres, spreads, gain_ref, *refs):
    mine_refs, other_refs = refs[:groups], refs[groups : 2 * groups]
    out_ref, whole, result, means, alongs = refs[2 * groups :]
    size, band, _ = mine_refs[0].shape
    blocks, height, width, _ = mixed.shape
    height = height - 6
    chans = blocks * LANES
    parity, place = where_ref[0], where_ref[1]
    for refs_of, core in ((mine_refs, parity), (other_refs, 1 - parity)):
        for at, index in enumerate(order):
            step = sender(place, index, len(order))
            start = pl.multiple_of((2 * step + core) * band, 16)
            whole[pl.ds(start, band), :] = refs_of[at // size][at % size]
    result[...] = lax.dot_general(
        grad_ref[...], whole[...], (((1,), (1,)), ((), ())), preferred_element_type=jnp.float32
    )

    def scaled_unit(row, block):
        rows = pl.ds(pl.multiple_of(row * width, width), width)
        lanes = slice(block * LANES, (block + 1) * LANES)
        scaled = result[rows, lanes] * gain_ref[:, lanes]
        return scaled, (mixed[block, row + 3] - centres[row]) * spreads[row]

    @pl.loop(0, height // TILE)
    def _(step):
        sums = []
        for i in range(TILE):
            row = step * TILE + i
            pairs = [scaled_unit(row, block) for block in range(blocks)]
            sums.append((row, sum(p[0] for p in pairs), sum(p[0] * p[1] for p in pairs)))
        for row, scaled, product in sums:
            mean = jnp.sum(scaled, axis=-1, keepdims=True) / chans
            means[row] = jnp.broadcast_to(mean, (width, LANES))
            along = jnp.sum(product, axis=-1, keepdims=True) / chans
            alongs[row] = jnp.broadcast_to(along, (width, LANES))

    @pl.loop(0, blocks)
    def _(block):
        clear_sides(out_ref.at[block], width)
        empty = jnp.zeros((3,) + out_ref.shape[2:], out_ref.dtype)
        out_ref[block, :3] = empty
        out_ref[block, 3 + height :] = empty

    @pl.loop(0, height)
    def _(row):
        mean, along, inv = means[row], alongs[row], spreads[row]
        for block in range(blocks):
            scaled, unit = scaled_unit(row, block)
            out_ref[block, row + 3, 8 : 8 + width, :] = inv * (scaled - mean - unit * along)


def project(where, grad, mixed, centres, spreads, gain, mine, other, order):
    blocks, height, width, _ = mixed.shape
    chans = blocks * LANES
    return run(
        functools.partial(project_kernel, len(mine), order),
        [f32(blocks, height, width + 16, LANES)],
        (where, grad, mixed, centres, spreads, gain, *mine, *other),
        [bf16(chans, grad.shape[1]), f32(grad.shape[0], chans)] + [f32(*centres.shape)] * 2,
        cost(VECTOR * mixed.size * 12, 8 * mixed.size),
        name="project",
    )[0]


def backward_kernel(index, bands, size_ref, grad_ref, taps_ref, out_ref, result):
    rows_dev, width, chans = out_ref.shape
    stride = width // SUBLANES
    high, wid = size_ref[0], size_ref[1]
    first = partner(size_ref[2], index, bands) * rows_dev
    columns = lax.broadcasted_iota(jnp.int32, (width, LANES), 0) < wid

    @pl.loop(0, chans // LANES)
    def _(block):
        lanes = pl.ds(pl.multiple_of(block * LANES, LANES), LANES)
        for low in range(0, rows_dev, TILE):
            outs = range(low, min(low + TILE, rows_dev))
            running = conv_rows(
                lambda row, columns_of: grad_ref[block, first + row, columns_of, :],
                list(range(rows_dev + 6)), outs, taps_ref, lanes, width, True,
            )
            for out, pieces in running.items():
                for i, value in enumerate(pieces):
                    result[out, pl.ds(i, SUBLANES, stride=stride), :] = value
        for row in range(rows_dev):
            keep = columns & (first + row < high)
            out_ref[row, :, lanes] = jnp.where(keep, result[row], 0.0).astype(out_ref.dtype)


def backward(sizes, grad, taps, index, bands):
    blocks, height, width, _ = grad.shape
    rows_dev, width = (height - 6) // bands, width - 16
    shape = (rows_dev, width, blocks * LANES)
    return run(
        functools.partial(backward_kernel, index, bands),
        [bf16(*shape) if index else f32(*shape)],
        (sizes, grad, taps),
        [f32(rows_dev, width, LANES)],
        cost(VECTOR * rows_dev * width * blocks * LANES * 49 * 2, 1),
        name="backward",
    )[0]


def split_halves(source, bit, keep_ref, send_ref):
    for piece in range(keep_ref.shape[0]):
        keep_ref[piece] = source(2 * piece + bit)
        send_ref[piece] = source(2 * piece + 1 - bit).astype(send_ref.dtype)


def outer_kernel(where_ref, normed_ref, grad_ref, keep_ref, send_ref, whole):
    band = keep_ref.shape[1]
    whole[...] = lax.dot_general(
        normed_ref[...], grad_ref[...], (((0,), (0,)), ((), ())), preferred_element_type=jnp.float32
    )

    def source(piece):
        return whole[pl.ds(pl.multiple_of(piece * band, 16), band), :]

    split_halves(source, where_ref[0], keep_ref, send_ref)


def fold_kernel(level, where_ref, held_ref, got_ref, keep_ref, send_ref):
    def source(piece):
        return held_ref[piece] + got_ref[piece].astype(jnp.float32)

    split_halves(source, lax.rem(where_ref[1] >> level - 1, 2), keep_ref, send_ref)


def halves(pieces, band, hidden):
    return f32(pieces // 2, band, hidden), bf16(pieces // 2, band, hidden)


def outer(where, normed, grad, count):
    chans, hidden = normed.shape[1], grad.shape[1]
    outs = halves(count, chans // count, hidden)
    return run(outer_kernel, outs, (where, normed, grad), [f32(chans, hidden)], name="outer")


def fold(where, held, got, level):
    kernel = functools.partial(fold_kernel, level)
    return run(kernel, halves(*held.shape), (where, held, got), name="fold")


def partner(place, index, count):
    return place ^ index if count & (count - 1) == 0 else (place + index) % count


def sender(place, index, count):
    return place ^ index if count & (count - 1) == 0 else (place + count - index) % count


def swap_pairs(value):
    count = lax.axis_size("section")
    return lax.ppermute(value, "section", [(i, i ^ 1) for i in range(count)])


def send_rows(value, index):
    if index == 0:
        return value
    count = lax.axis_size("rows")
    return lax.ppermute(value, "rows", [(i, partner(i, index, count)) for i in range(count)])


def send_section(value, index):
    count = lax.axis_size("section")
    way = [(i, partner(i // 2, index, count // 2) * 2 + i % 2) for i in range(count)]
    return lax.ppermute(value, "section", way)


def gather_pairs(block, first):
    steps = lax.axis_size("section") // 2
    if steps & (steps - 1):
        sent = [send_section(block[None], i) for i in range(1, steps)]
        return [block[None]] + sent, list(range(steps))
    stack, order, half = block[None], [0], steps // 2
    while half > 1:
        stack = jnp.concatenate([stack, after(send_section(stack, half), first)])
        order = order + [index ^ half for index in order]
        half //= 2
    return [stack, send_section(stack, 1)], order + [index ^ 1 for index in order]


def scatter_section(where, keep, send):
    count = lax.axis_size("section")
    level, sends = 0, [send]
    while True:
        way = [(i, i ^ 1 << level) for i in range(count)]
        got = lax.ppermute(send, "section", way)
        level += 1
        if keep.shape[0] % 2:
            break
        keep, send = fold(where, keep, got, level)
        sends.append(send)
    rest = keep.shape[0]
    total = keep + got.astype(jnp.float32)
    if rest == 1:
        return total[0], sends
    place = lax.axis_index("section") >> level
    result = lax.dynamic_index_in_dim(total, place, 0, keepdims=False)
    for shift in range(1, rest):
        piece = lax.dynamic_index_in_dim(total, (place + shift) % rest, 0, keepdims=False)
        way = [(i, (i + (shift << level)) % count) for i in range(count)]
        result = result + lax.ppermute(piece.astype(jnp.bfloat16), "section", way).astype(jnp.float32)
    return result, sends


def after(value, *others):
    return lax.optimization_barrier((value, others))[0]


def local(activations, cotangent, proj_weight, kernel_taps, ln_gain, ln_shift, heights, widths):
    rows_dev, width_dev, chans = activations.shape[1:]
    height_all = cotangent.shape[1]
    hidden_dev = cotangent.shape[3]
    bands = lax.axis_size("rows")
    count = lax.axis_size("section")
    band = lax.axis_index("rows")
    sizes = jnp.concatenate([heights, widths, band[None].astype(jnp.int32)])
    index = lax.axis_index("section")
    where = jnp.stack([lax.rem(index, 2), index // 2]).astype(jnp.int32)
    taps = jnp.broadcast_to(
        kernel_taps.astype(jnp.float32)[:, None], (kernel_taps.shape[0], SUBLANES, chans)
    )
    gain = ln_gain[None]
    shift = ln_shift[None]

    acts = [activations[0]] + [send_rows(activations[0], i) for i in range(1, bands)]
    row_ids = lax.broadcasted_iota(jnp.int32, (height_all, width_dev), 0)
    col_ids = lax.broadcasted_iota(jnp.int32, (height_all, width_dev), 1)
    valid = ((row_ids < heights[0]) & (col_ids < widths[0])).astype(jnp.float32)
    live_grad = (cotangent[0].astype(jnp.float32) * valid[:, :, None]).astype(jnp.bfloat16)
    grad_flat = live_grad.reshape(-1, hidden_dev)

    half = bands // 2
    indices = list(range(bands))
    mixed = forward(sizes, acts[:half], indices[:half], bands, taps)
    proj_mine, order = gather_pairs(proj_weight, mixed)
    mixed = forward(sizes, acts[half:], indices[half:], bands, taps, mixed)

    normed, centres, spreads = normalise(mixed, gain, shift)
    proj_other = [swap_pairs(after(stack, normed)) for stack in proj_mine]
    keep, send = outer(where, normed, after(grad_flat, *proj_mine), count)
    weight_grad, sends = scatter_section(where, keep, send)
    weight_grad = weight_grad / count

    grads = after(grad_flat, sends[min(1, len(sends) - 1)])
    grad_mixed = project(where, grads, mixed, centres, spreads, gain, proj_mine, proj_other, order)
    sent = []
    for i in range(bands - 1, -1, -1):
        ready = sends[min(1, len(sends) - 1)] if i > 1 else sends[-1]
        sent.append(send_rows(backward(after(sizes, ready), grad_mixed, taps, i, bands), i))
    back = sent.pop()
    for value in sent:
        back = back + value.astype(jnp.float32)
    return (back.astype(jnp.bfloat16)[None], weight_grad)


def solution(mesh):
    in_specs = (
        P("section", "rows", None, None),
        P("section", None, None, "rows"),
        P("section", "rows"),
        P(),
        P(),
        P(),
        P("section"),
        P("section"),
    )
    out_specs = (P("section", "rows", None, None), P("section", "rows"))
    return jax.shard_map(local, mesh=mesh, in_specs=in_specs, out_specs=out_specs, check_vma=False)
```

```python
import functools

import jax
import jax.numpy as jnp
import numpy as np
from jax import lax
from jax.experimental import pallas as pl
from jax.experimental.pallas import tpu as pltpu
from jax.sharding import PartitionSpec as P

epsilon = 1e-06
LANES = 128
VECTOR = 240
SUBLANES = 8


TILE = 4


def cost(operations, moved):
    return pl.CostEstimate(flops=operations, bytes_accessed=moved, transcendentals=0)


def run(kernel, outs, args, scratch=(), estimate=None, aliases=None, name=None):
    held = [arg for arg in args if arg.ndim > 1] + list(outs) + list(scratch)
    taken = sum(int(np.prod(value.shape)) * jnp.dtype(value.dtype).itemsize for value in held)
    vmem = pl.BlockSpec(memory_space=pltpu.VMEM)
    smem = pl.BlockSpec(memory_space=pltpu.SMEM)
    return pl.pallas_call(
        kernel,
        out_shape=tuple(outs),
        in_specs=[smem if arg.ndim == 1 else vmem for arg in args],
        out_specs=tuple(vmem for _ in outs),
        scratch_shapes=[pltpu.VMEM(value.shape, value.dtype) for value in scratch],
        input_output_aliases=aliases or {},
        compiler_params=pltpu.CompilerParams(vmem_limit_bytes=taken + taken // 8 + (4 << 20)),
        cost_estimate=estimate or cost(1, 1),
        name=name,
    )(*args)


def f32(*shape):
    return jax.ShapeDtypeStruct(shape, jnp.float32)


def bf16(*shape):
    return jax.ShapeDtypeStruct(shape, jnp.bfloat16)


def clear_sides(source, width):
    sides = jnp.zeros((source.shape[0], 8, LANES), source.dtype)
    source[:, :8, :] = sides
    source[:, 8 + width :, :] = sides


def conv_rows(load, positions, outs, wide_ref, lanes, width, flip):
    stride = width // SUBLANES
    running = {out: [None] * stride for out in outs}
    for row, position in enumerate(positions):
        users = [out for out in outs if 0 <= position - out <= 6]
        if not users:
            continue
        shifted = [load(row, pl.ds(5 + k, SUBLANES, stride=stride)) for k in range(stride + 6)]
        for out in users:
            for along in range(7):
                tap = (position - out) * 7 + along
                weight = wide_ref[48 - tap if flip else tap, :, lanes]
                for i in range(stride):
                    term = weight * shifted[i + along]
                    before = running[out][i]
                    running[out][i] = term if before is None else before + term
    return running


def forward_kernel(bands, indices, fresh, size_ref, *refs):
    act_refs = refs[: len(indices)]
    taps_ref, mixed, source = refs[len(indices)], refs[-2], refs[-1]
    rows_dev, width, _ = act_refs[0].shape
    blocks, height = mixed.shape[0], mixed.shape[1] - 6
    stride = width // SUBLANES
    high, wid, band = size_ref[0], size_ref[1], size_ref[2]
    joined = source.shape[0] // rows_dev
    clear_sides(source, width)
    columns = lax.broadcasted_iota(jnp.int32, (width, LANES), 0) < wid
    once = fresh and len(indices) == joined
    firsts = [sender(band, index, bands) * rows_dev for index in indices]

    @pl.loop(0, blocks)
    def _(block):
        lanes = pl.ds(pl.multiple_of(block * LANES, LANES), LANES)
        if fresh:
            mixed[block] = jnp.zeros(mixed.shape[1:], mixed.dtype)
        for start in range(0, len(indices), joined):
            base = firsts[start]
            for first in firsts[start : start + joined]:
                base = jnp.minimum(base, first)
            for first, act_ref in zip(firsts[start:], act_refs[start : start + joined]):
                for i in range(rows_dev):
                    row = first + i
                    value = act_ref[i, :, lanes].astype(jnp.float32)
                    value = jnp.where(columns & (row < high), value, 0.0)
                    source[row - base, 8 : 8 + width, :] = value
            rows = joined * rows_dev
            for low in range(0, rows + 6, TILE):
                outs = range(low, min(low + TILE, rows + 6))
                positions = [i + 6 for i in range(rows)]
                running = conv_rows(
                    lambda row, columns_of: source[row, columns_of, :],
                    positions, outs, taps_ref, lanes, width, False,
                )
                for out, pieces in running.items():
                    for i, value in enumerate(pieces):
                        columns_of = pl.ds(i, SUBLANES, stride=stride)
                        if not once:
                            value = value + mixed[block, base + out, columns_of, :]
                        mixed[block, base + out, columns_of, :] = value


def forward(sizes, acts, indices, bands, taps, before=None):
    rows_dev, width, chans = acts[0].shape
    joined = 2 if bands & (bands - 1) == 0 and len(indices) % 2 == 0 else 1
    extra = () if before is None else (before,)
    return run(
        functools.partial(forward_kernel, bands, indices, before is None),
        [f32(chans // LANES, rows_dev * bands + 6, width, LANES)],
        (sizes, *acts, taps, *extra),
        [f32(joined * rows_dev, width + 16, LANES)],
        cost(3 * VECTOR * len(acts) * acts[0].size * 49 * 2, 6 * len(acts) * acts[0].size),
        {2 + len(acts): 0} if extra else {},
        "forward",
    )[0]


def normalise_kernel(size_ref, mixed, wide_ref, normed_ref, centres, spreads):
    blocks, height, width, _ = mixed.shape
    height = height - 6
    chans = blocks * LANES
    high, wid = size_ref[0], size_ref[1]
    columns = lax.broadcasted_iota(jnp.int32, (width, LANES), 0) < wid

    @pl.loop(0, height // TILE)
    def _(step):
        rows = [step * TILE + i for i in range(TILE)]
        sums = [sum(mixed[block, row + 3] for block in range(blocks)) for row in rows]
        for row, value in zip(rows, sums):
            centre = jnp.sum(value, axis=-1, keepdims=True) / chans
            centres[row] = jnp.broadcast_to(centre, (width, LANES))

    @pl.loop(0, height // TILE)
    def _(step):
        rows = [step * TILE + i for i in range(TILE)]
        sums = []
        for row in rows:
            centre = centres[row]
            away = [mixed[block, row + 3] - centre for block in range(blocks)]
            sums.append(sum(value * value for value in away))
        for row, value in zip(rows, sums):
            spread = jnp.sum(value, axis=-1, keepdims=True) / chans
            spreads[row] = jnp.broadcast_to(lax.rsqrt(spread + epsilon), (width, LANES))

    @pl.loop(0, height)
    def _(row):
        rows = pl.ds(pl.multiple_of(row * width, width), width)
        centre, inv = centres[row], spreads[row]
        for block in range(blocks):
            lanes = slice(block * LANES, (block + 1) * LANES)
            unit = ((mixed[block, row + 3] - centre) * inv).reshape(-1, SUBLANES, LANES)
            value = unit * wide_ref[wide_ref.shape[0] - 2, :, lanes][None] + wide_ref[wide_ref.shape[0] - 1, :, lanes][None]
            value = jnp.where(columns & (row < high), value.reshape(width, LANES), 0.0)
            normed_ref[rows, lanes] = value.astype(normed_ref.dtype)


def normalise(sizes, mixed, wide):
    blocks, height, width, _ = mixed.shape
    height = height - 6
    outs = [bf16(height * width, blocks * LANES)] + [f32(height, width, LANES)] * 2
    return run(normalise_kernel, outs, (sizes, mixed, wide), name="normalise")


def project_kernel(groups, order, size_ref, where_ref, grad_ref, mixed, centres, spreads, wide_ref, *refs):
    mine_refs, other_refs = refs[:groups], refs[groups : 2 * groups]
    out_ref, whole, result, means, alongs = refs[2 * groups :]
    size, band, _ = mine_refs[0].shape
    blocks, height, width, _ = mixed.shape
    height = height - 6
    chans = blocks * LANES
    parity, place = where_ref[0], where_ref[1]
    high, wid = size_ref[0], size_ref[1]
    columns = lax.broadcasted_iota(jnp.int32, (width, LANES), 0) < wid
    for refs_of, core in ((mine_refs, parity), (other_refs, 1 - parity)):
        for at, index in enumerate(order):
            step = sender(place, index, len(order))
            start = pl.multiple_of((2 * step + core) * band, 16)
            whole[pl.ds(start, band), :] = refs_of[at // size][at % size]
    result[...] = lax.dot_general(
        grad_ref[...], whole[...], (((1,), (1,)), ((), ())), preferred_element_type=jnp.float32
    )

    def scaled_unit(row, block):
        rows = pl.ds(pl.multiple_of(row * width, width), width)
        lanes = slice(block * LANES, (block + 1) * LANES)
        scaled = result[rows, lanes].reshape(-1, SUBLANES, LANES)
        scaled = scaled * wide_ref[wide_ref.shape[0] - 2, :, lanes][None]
        scaled = scaled.reshape(width, LANES)
        return scaled, (mixed[block, row + 3] - centres[row]) * spreads[row]

    @pl.loop(0, height // TILE)
    def _(step):
        sums = []
        for i in range(TILE):
            row = step * TILE + i
            pairs = [scaled_unit(row, block) for block in range(blocks)]
            sums.append((row, sum(p[0] for p in pairs), sum(p[0] * p[1] for p in pairs)))
        for row, scaled, product in sums:
            mean = jnp.sum(scaled, axis=-1, keepdims=True) / chans
            means[row] = jnp.broadcast_to(mean, (width, LANES))
            along = jnp.sum(product, axis=-1, keepdims=True) / chans
            alongs[row] = jnp.broadcast_to(along, (width, LANES))

    @pl.loop(0, blocks)
    def _(block):
        clear_sides(out_ref.at[block], width)
        empty = jnp.zeros((3,) + out_ref.shape[2:], out_ref.dtype)
        out_ref[block, :3] = empty
        out_ref[block, 3 + height :] = empty

    @pl.loop(0, height)
    def _(row):
        mean, along = means[row], alongs[row]
        inv = jnp.where(columns & (row < high), spreads[row], 0.0)
        for block in range(blocks):
            scaled, unit = scaled_unit(row, block)
            out_ref[block, row + 3, 8 : 8 + width, :] = inv * (scaled - mean - unit * along)


def project(sizes, where, grad, mixed, centres, spreads, wide, mine, other, order):
    blocks, height, width, _ = mixed.shape
    chans = blocks * LANES
    return run(
        functools.partial(project_kernel, len(mine), order),
        [f32(blocks, height, width + 16, LANES)],
        (sizes, where, grad, mixed, centres, spreads, wide, *mine, *other),
        [bf16(chans, grad.shape[1]), f32(grad.shape[0], chans)] + [f32(*centres.shape)] * 2,
        cost(VECTOR * mixed.size * 12, 8 * mixed.size),
        name="project",
    )[0]


def backward_kernel(index, bands, size_ref, grad_ref, taps_ref, out_ref, result):
    rows_dev, width, chans = out_ref.shape
    stride = width // SUBLANES
    high, wid = size_ref[0], size_ref[1]
    first = partner(size_ref[2], index, bands) * rows_dev
    columns = lax.broadcasted_iota(jnp.int32, (width, LANES), 0) < wid

    @pl.loop(0, chans // LANES)
    def _(block):
        lanes = pl.ds(pl.multiple_of(block * LANES, LANES), LANES)
        for low in range(0, rows_dev, TILE):
            outs = range(low, min(low + TILE, rows_dev))
            running = conv_rows(
                lambda row, columns_of: grad_ref[block, first + row, columns_of, :],
                list(range(rows_dev + 6)), outs, taps_ref, lanes, width, True,
            )
            for out, pieces in running.items():
                for i, value in enumerate(pieces):
                    result[out, pl.ds(i, SUBLANES, stride=stride), :] = value
        for row in range(rows_dev):
            keep = columns & (first + row < high)
            out_ref[row, :, lanes] = jnp.where(keep, result[row], 0.0).astype(out_ref.dtype)


def backward(sizes, grad, taps, index, bands):
    blocks, height, width, _ = grad.shape
    rows_dev, width = (height - 6) // bands, width - 16
    shape = (rows_dev, width, blocks * LANES)
    return run(
        functools.partial(backward_kernel, index, bands),
        [bf16(*shape) if index else f32(*shape)],
        (sizes, grad, taps),
        [f32(rows_dev, width, LANES)],
        cost(VECTOR * rows_dev * width * blocks * LANES * 49 * 2, 1),
        name="backward",
    )[0]


def outer_kernel(where_ref, normed_ref, grad_ref, whole_ref, send_ref):
    pieces, band, hidden = whole_ref.shape
    whole_ref[...] = lax.dot_general(
        normed_ref[...], grad_ref[...], (((0,), (0,)), ((), ())), preferred_element_type=jnp.float32
    ).reshape(pieces, band, hidden)
    for piece in range(pieces // 2):
        send_ref[piece] = whole_ref[2 * piece + 1 - where_ref[0]].astype(send_ref.dtype)


def outer(where, normed, grad, count):
    chans, hidden = normed.shape[1], grad.shape[1]
    outs = [f32(count, chans // count, hidden), bf16(count // 2, chans // count, hidden)]
    return run(outer_kernel, outs, (where, normed, grad), name="outer")


def kept(where_ref, held_ref, got_ref, level, piece):
    held = held_ref[2 * piece + where_ref[0]] if level == 1 else held_ref[piece]
    return held + got_ref[piece].astype(jnp.float32)


def fold_kernel(level, where_ref, held_ref, got_ref, keep_ref, send_ref):
    bit = lax.rem(where_ref[1] >> level - 1, 2)
    for piece in range(keep_ref.shape[0]):
        keep_ref[piece] = kept(where_ref, held_ref, got_ref, level, 2 * piece + bit)
        sent = kept(where_ref, held_ref, got_ref, level, 2 * piece + 1 - bit)
        send_ref[piece] = sent.astype(send_ref.dtype)


def fold(where, held, got, level):
    pieces, band, hidden = got.shape
    outs = [f32(pieces // 2, band, hidden), bf16(pieces // 2, band, hidden)]
    return run(functools.partial(fold_kernel, level), outs, (where, held, got), name="fold")


def finish_kernel(count, parts, *refs):
    back_refs, weight_refs, (back_ref, weight_ref) = refs[:parts], refs[parts:-2], refs[-2:]

    def total(values):
        return sum(ref[...].astype(jnp.float32) for ref in values)

    back_ref[...] = total(back_refs).astype(back_ref.dtype)
    weight_ref[...] = total(weight_refs) / count


def finish(backs, weights, count):
    outs = [bf16(*backs[0].shape), f32(*weights[0].shape)]
    kernel = functools.partial(finish_kernel, count, len(backs))
    return run(kernel, outs, (*backs, *weights), name="finish")


def partner(place, index, count):
    return place ^ index if count & (count - 1) == 0 else (place + index) % count


def sender(place, index, count):
    return place ^ index if count & (count - 1) == 0 else (place + count - index) % count


def swap_pairs(value):
    count = lax.axis_size("section")
    return lax.ppermute(value, "section", [(i, i ^ 1) for i in range(count)])


def send_rows(value, index):
    if index == 0:
        return value
    count = lax.axis_size("rows")
    return lax.ppermute(value, "rows", [(i, partner(i, index, count)) for i in range(count)])


def send_section(value, index):
    count = lax.axis_size("section")
    way = [(i, partner(i // 2, index, count // 2) * 2 + i % 2) for i in range(count)]
    return lax.ppermute(value, "section", way)


def gather_pairs(block, first):
    steps = lax.axis_size("section") // 2
    if steps & (steps - 1):
        sent = [send_section(block[None], i) for i in range(1, steps)]
        return [block[None]] + sent, list(range(steps))
    far = {steps >> level: send_section(block[None], steps >> level) for level in range(1, steps.bit_length())}
    stack, order, near = [block[None]], [0], far.pop(1)
    for half, value in far.items():
        value = after(value, first)
        more = [value] + [send_section(piece, half) for piece in stack[1:]]
        stack, order = stack + more, order + [index ^ half for index in order]
    near = [near] + [send_section(piece, 1) for piece in stack[1:]]
    return [jnp.concatenate(stack), jnp.concatenate(near)], order + [index ^ 1 for index in order]


def scatter_section(where, keep, send):
    count = lax.axis_size("section")
    level, sends = 0, [send]
    while True:
        way = [(i, i ^ 1 << level) for i in range(count)]
        got = lax.ppermute(send, "section", way)
        level += 1
        if got.shape[0] % 2:
            break
        keep, send = fold(where, keep, got, level)
        sends.append(send)
    rest = keep.shape[0]
    if rest == 1:
        return [keep[0], got[0]], sends
    total = keep + got.astype(jnp.float32)
    place = lax.axis_index("section") >> level
    result = lax.dynamic_index_in_dim(total, place, 0, keepdims=False)
    for shift in range(1, rest):
        piece = lax.dynamic_index_in_dim(total, (place + shift) % rest, 0, keepdims=False)
        way = [(i, (i + (shift << level)) % count) for i in range(count)]
        result = result + lax.ppermute(piece.astype(jnp.bfloat16), "section", way).astype(jnp.float32)
    return [result], sends


def after(value, *others):
    return lax.optimization_barrier((value, others))[0]


def local(activations, cotangent, proj_weight, kernel_taps, ln_gain, ln_shift, heights, widths):
    rows_dev, width_dev, chans = activations.shape[1:]
    height_all = cotangent.shape[1]
    hidden_dev = cotangent.shape[3]
    bands = lax.axis_size("rows")
    count = lax.axis_size("section")
    band = lax.axis_index("rows")
    sizes = jnp.concatenate([heights, widths, band[None].astype(jnp.int32)])
    index = lax.axis_index("section")
    where = jnp.stack([lax.rem(index, 2), index // 2]).astype(jnp.int32)
    wide = jnp.concatenate([kernel_taps.astype(jnp.float32), ln_gain[None], ln_shift[None]])
    wide = jnp.broadcast_to(wide[:, None], (wide.shape[0], SUBLANES, chans))
    grad = cotangent.reshape(-1, hidden_dev)

    acts = [activations[0]] + [send_rows(activations[0], i) for i in range(1, bands)]
    half = bands // 2
    mixed = forward(sizes, acts[:1], range(1), bands, wide)
    mixed = forward(sizes, acts[1:half], range(1, half), bands, wide, mixed)
    proj_mine, order = gather_pairs(proj_weight, mixed)
    mixed = forward(sizes, acts[half:], range(half, bands), bands, wide, mixed)

    normed, centres, spreads = normalise(sizes, mixed, wide)
    whole, send = outer(where, normed, grad, count)
    weights, sends = scatter_section(where, whole, after(send, *proj_mine))

    proj_other = [swap_pairs(after(stack, normed)) for stack in proj_mine]
    grads = after(grad, sends[min(1, len(sends) - 1)])
    grad_mixed = project(sizes, where, grads, mixed, centres, spreads, wide, proj_mine, proj_other, order)
    backs = []
    for i in range(bands - 1, -1, -1):
        ready = sends[min(1, len(sends) - 1)] if i > 1 else sends[-1]
        backs.append(send_rows(backward(after(sizes, ready), grad_mixed, wide, i, bands), i))
    back, weight_grad = finish(backs, weights, count)
    return (back[None], weight_grad)


def solution(mesh):
    in_specs = (
        P("section", "rows", None, None),
        P("section", None, None, "rows"),
        P("section", "rows"),
        P(),
        P(),
        P(),
        P("section"),
        P("section"),
    )
    out_specs = (P("section", "rows", None, None), P("section", "rows"))
    return jax.shard_map(local, mesh=mesh, in_specs=in_specs, out_specs=out_specs, check_vma=False)
```

```python
import functools

import jax
import jax.numpy as jnp
import numpy as np
from jax import lax
from jax.experimental import pallas as pl
from jax.experimental.pallas import tpu as pltpu
from jax.sharding import PartitionSpec as P

epsilon = 1e-06
LANES = 128
VECTOR = 240
SUBLANES = 8


TILE = 4


def cost(operations, moved):
    return pl.CostEstimate(flops=operations, bytes_accessed=moved, transcendentals=0)


def run(kernel, outs, args, scratch=(), estimate=None, aliases=None, name=None):
    held = list(args) + list(outs) + list(scratch)
    taken = sum(int(np.prod(value.shape)) * jnp.dtype(value.dtype).itemsize for value in held)
    vmem = pl.BlockSpec(memory_space=pltpu.VMEM)
    smem = pl.BlockSpec(memory_space=pltpu.SMEM)
    return pl.pallas_call(
        kernel,
        out_shape=tuple(outs),
        in_specs=[smem if arg.dtype == jnp.int32 else vmem for arg in args],
        out_specs=tuple(vmem for _ in outs),
        scratch_shapes=[pltpu.VMEM(value.shape, value.dtype) for value in scratch],
        input_output_aliases=aliases or {},
        compiler_params=pltpu.CompilerParams(vmem_limit_bytes=taken + taken // 8 + (4 << 20)),
        cost_estimate=estimate or cost(1, 1),
        name=name,
    )(*args)


def f32(*shape):
    return jax.ShapeDtypeStruct(shape, jnp.float32)


def bf16(*shape):
    return jax.ShapeDtypeStruct(shape, jnp.bfloat16)


def prepare_kernel(high_ref, wid_ref, taps_ref, gain_ref, shift_ref, wide_ref, valid_ref):
    count, chans = taps_ref.shape
    taps = taps_ref[...].astype(jnp.float32)
    rows = [taps[tap : tap + 1] for tap in range(count)]
    for at, row in enumerate(rows + [gain_ref[...], shift_ref[...]]):
        wide_ref[at] = jnp.broadcast_to(row, (SUBLANES, chans))
    _, width, lanes = valid_ref.shape
    columns = lax.broadcasted_iota(jnp.int32, (width, lanes), 0) < wid_ref[0]

    @pl.loop(0, valid_ref.shape[0])
    def _(row):
        valid_ref[row] = jnp.where(columns & (row < high_ref[0]), 1.0, 0.0)


def prepare(heights, widths, taps, gain, shift, height, width):
    count, chans = taps.shape
    outs = [f32(count + 2, SUBLANES, chans), f32(height, width, LANES)]
    args = (heights, widths, taps, gain[None], shift[None])
    return run(prepare_kernel, outs, args, name="prepare")


def clear_sides(source, width):
    sides = jnp.zeros((source.shape[0], 8, LANES), source.dtype)
    source[:, :8, :] = sides
    source[:, 8 + width :, :] = sides


def conv_rows(load, positions, outs, wide_ref, lanes, width, flip):
    stride = width // SUBLANES
    running = {out: [None] * stride for out in outs}
    for row, position in enumerate(positions):
        users = [out for out in outs if 0 <= position - out <= 6]
        if not users:
            continue
        shifted = [load(row, pl.ds(5 + k, SUBLANES, stride=stride)) for k in range(stride + 6)]
        for out in users:
            for along in range(7):
                tap = (position - out) * 7 + along
                weight = wide_ref[48 - tap if flip else tap, :, lanes]
                for i in range(stride):
                    term = weight * shifted[i + along]
                    before = running[out][i]
                    running[out][i] = term if before is None else before + term
    return running


def forward_kernel(bands, indices, fresh, valid_ref, taps_ref, *refs):
    act_refs, (mixed, source) = refs[: len(indices)], refs[-2:]
    rows_dev, width, _ = act_refs[0].shape
    blocks, height = mixed.shape[0], mixed.shape[1] - 6
    stride = width // SUBLANES
    band = lax.axis_index("rows")
    joined = source.shape[0] // rows_dev
    clear_sides(source, width)
    once = fresh and len(indices) == joined
    firsts = [sender(band, index, bands) * rows_dev for index in indices]

    @pl.loop(0, blocks)
    def _(block):
        lanes = pl.ds(pl.multiple_of(block * LANES, LANES), LANES)
        if fresh:
            mixed[block] = jnp.zeros(mixed.shape[1:], mixed.dtype)
        for start in range(0, len(indices), joined):
            base = firsts[start]
            for first in firsts[start : start + joined]:
                base = jnp.minimum(base, first)
            for first, act_ref in zip(firsts[start:], act_refs[start : start + joined]):
                for i in range(rows_dev):
                    row = first + i
                    value = act_ref[i, :, lanes].astype(jnp.float32) * valid_ref[row]
                    source[row - base, 8 : 8 + width, :] = value
            rows = joined * rows_dev
            for low in range(0, rows + 6, TILE):
                outs = range(low, min(low + TILE, rows + 6))
                positions = [i + 6 for i in range(rows)]
                running = conv_rows(
                    lambda row, columns_of: source[row, columns_of, :],
                    positions, outs, taps_ref, lanes, width, False,
                )
                for out, pieces in running.items():
                    for i, value in enumerate(pieces):
                        columns_of = pl.ds(i, SUBLANES, stride=stride)
                        if not once:
                            value = value + mixed[block, base + out, columns_of, :]
                        mixed[block, base + out, columns_of, :] = value


def forward(valid, wide, acts, indices, bands, before=None):
    rows_dev, width, chans = acts[0].shape
    joined = 2 if bands & (bands - 1) == 0 and len(indices) % 2 == 0 else 1
    extra = () if before is None else (before,)
    return run(
        functools.partial(forward_kernel, bands, indices, before is None),
        [f32(chans // LANES, rows_dev * bands + 6, width, LANES)],
        (valid, wide, *acts, *extra),
        [f32(joined * rows_dev, width + 16, LANES)],
        cost(3 * VECTOR * len(acts) * acts[0].size * 49 * 2, 6 * len(acts) * acts[0].size),
        {2 + len(acts): 0} if extra else {},
        "forward",
    )[0]


def normalise_kernel(valid_ref, mixed, wide_ref, normed_ref, centres, spreads):
    blocks, height, width, _ = mixed.shape
    height = height - 6
    chans = blocks * LANES

    @pl.loop(0, height // TILE)
    def _(step):
        rows = [step * TILE + i for i in range(TILE)]
        sums = [sum(mixed[block, row + 3] for block in range(blocks)) for row in rows]
        for row, value in zip(rows, sums):
            centre = jnp.sum(value, axis=-1, keepdims=True) / chans
            centres[row] = jnp.broadcast_to(centre, (width, LANES))

    @pl.loop(0, height // TILE)
    def _(step):
        rows = [step * TILE + i for i in range(TILE)]
        sums = []
        for row in rows:
            centre = centres[row]
            away = [mixed[block, row + 3] - centre for block in range(blocks)]
            sums.append(sum(value * value for value in away))
        for row, value in zip(rows, sums):
            spread = jnp.sum(value, axis=-1, keepdims=True) / chans
            spreads[row] = jnp.broadcast_to(lax.rsqrt(spread + epsilon), (width, LANES))

    @pl.loop(0, height)
    def _(row):
        rows = pl.ds(pl.multiple_of(row * width, width), width)
        centre, inv = centres[row], spreads[row]
        for block in range(blocks):
            lanes = slice(block * LANES, (block + 1) * LANES)
            unit = ((mixed[block, row + 3] - centre) * inv).reshape(-1, SUBLANES, LANES)
            value = unit * wide_ref[wide_ref.shape[0] - 2, :, lanes][None] + wide_ref[wide_ref.shape[0] - 1, :, lanes][None]
            value = value.reshape(width, LANES) * valid_ref[row]
            normed_ref[rows, lanes] = value.astype(normed_ref.dtype)


def normalise(valid, mixed, wide):
    blocks, height, width, _ = mixed.shape
    height = height - 6
    outs = [bf16(height * width, blocks * LANES)] + [f32(height, width, LANES)] * 2
    return run(normalise_kernel, outs, (valid, mixed, wide), name="normalise")


def project_kernel(groups, order, valid_ref, grad_ref, mixed, centres, spreads, wide_ref, *refs):
    mine_refs, other_refs = refs[:groups], refs[groups : 2 * groups]
    out_ref, whole, result, means, alongs = refs[2 * groups :]
    size, band, _ = mine_refs[0].shape
    blocks, height, width, _ = mixed.shape
    height = height - 6
    chans = blocks * LANES
    parity, place = parity_and_place()
    for refs_of, core in ((mine_refs, parity), (other_refs, 1 - parity)):
        for at, index in enumerate(order):
            step = sender(place, index, len(order))
            start = pl.multiple_of((2 * step + core) * band, 16)
            whole[pl.ds(start, band), :] = refs_of[at // size][at % size]
    result[...] = lax.dot_general(
        grad_ref[...], whole[...], (((1,), (1,)), ((), ())), preferred_element_type=jnp.float32
    )

    def scaled_unit(row, block):
        rows = pl.ds(pl.multiple_of(row * width, width), width)
        lanes = slice(block * LANES, (block + 1) * LANES)
        scaled = result[rows, lanes].reshape(-1, SUBLANES, LANES)
        scaled = scaled * wide_ref[wide_ref.shape[0] - 2, :, lanes][None]
        scaled = scaled.reshape(width, LANES)
        return scaled, (mixed[block, row + 3] - centres[row]) * spreads[row]

    @pl.loop(0, height // TILE)
    def _(step):
        sums = []
        for i in range(TILE):
            row = step * TILE + i
            pairs = [scaled_unit(row, block) for block in range(blocks)]
            sums.append((row, sum(p[0] for p in pairs), sum(p[0] * p[1] for p in pairs)))
        for row, scaled, product in sums:
            mean = jnp.sum(scaled, axis=-1, keepdims=True) / chans
            means[row] = jnp.broadcast_to(mean, (width, LANES))
            along = jnp.sum(product, axis=-1, keepdims=True) / chans
            alongs[row] = jnp.broadcast_to(along, (width, LANES))

    @pl.loop(0, blocks)
    def _(block):
        clear_sides(out_ref.at[block], width)
        empty = jnp.zeros((3,) + out_ref.shape[2:], out_ref.dtype)
        out_ref[block, :3] = empty
        out_ref[block, 3 + height :] = empty

    @pl.loop(0, height)
    def _(row):
        mean, along = means[row], alongs[row]
        inv = spreads[row] * valid_ref[row]
        for block in range(blocks):
            scaled, unit = scaled_unit(row, block)
            out_ref[block, row + 3, 8 : 8 + width, :] = inv * (scaled - mean - unit * along)


def project(valid, grad, mixed, centres, spreads, wide, mine, other, order):
    blocks, height, width, _ = mixed.shape
    chans = blocks * LANES
    return run(
        functools.partial(project_kernel, len(mine), order),
        [f32(blocks, height, width + 16, LANES)],
        (valid, grad, mixed, centres, spreads, wide, *mine, *other),
        [bf16(chans, grad.shape[1]), f32(grad.shape[0], chans)] + [f32(*centres.shape)] * 2,
        cost(VECTOR * mixed.size * 12, 8 * mixed.size),
        name="project",
    )[0]


def backward_kernel(index, bands, valid_ref, grad_ref, taps_ref, out_ref, result):
    rows_dev, width, chans = out_ref.shape
    stride = width // SUBLANES
    first = partner(lax.axis_index("rows"), index, bands) * rows_dev

    @pl.loop(0, chans // LANES)
    def _(block):
        lanes = pl.ds(pl.multiple_of(block * LANES, LANES), LANES)
        for low in range(0, rows_dev, TILE):
            outs = range(low, min(low + TILE, rows_dev))
            running = conv_rows(
                lambda row, columns_of: grad_ref[block, first + row, columns_of, :],
                list(range(rows_dev + 6)), outs, taps_ref, lanes, width, True,
            )
            for out, pieces in running.items():
                for i, value in enumerate(pieces):
                    result[out, pl.ds(i, SUBLANES, stride=stride), :] = value
        for row in range(rows_dev):
            out_ref[row, :, lanes] = (result[row] * valid_ref[first + row]).astype(out_ref.dtype)


def backward(valid, grad, taps, index, bands):
    blocks, height, width, _ = grad.shape
    rows_dev, width = (height - 6) // bands, width - 16
    shape = (rows_dev, width, blocks * LANES)
    return run(
        functools.partial(backward_kernel, index, bands),
        [bf16(*shape) if index else f32(*shape)],
        (valid, grad, taps),
        [f32(rows_dev, width, LANES)],
        cost(VECTOR * rows_dev * width * blocks * LANES * 49 * 2, 1),
        name="backward",
    )[0]


def outer_kernel(normed_ref, grad_ref, whole_ref, send_ref):
    pieces, band, hidden = whole_ref.shape
    parity, _ = parity_and_place()
    whole_ref[...] = lax.dot_general(
        normed_ref[...], grad_ref[...], (((0,), (0,)), ((), ())), preferred_element_type=jnp.float32
    ).reshape(pieces, band, hidden)
    for piece in range(pieces // 2):
        send_ref[piece] = whole_ref[2 * piece + 1 - parity].astype(send_ref.dtype)


def outer(normed, grad, count):
    chans, hidden = normed.shape[1], grad.shape[1]
    outs = [f32(count, chans // count, hidden), bf16(count // 2, chans // count, hidden)]
    return run(outer_kernel, outs, (normed, grad), name="outer")


def kept(held_ref, got_ref, level, parity, piece):
    held = held_ref[2 * piece + parity] if level == 1 else held_ref[piece]
    return held + got_ref[piece].astype(jnp.float32)


def fold_kernel(level, held_ref, got_ref, keep_ref, send_ref):
    parity, place = parity_and_place()
    bit = lax.rem(place >> level - 1, 2)
    for piece in range(keep_ref.shape[0]):
        keep_ref[piece] = kept(held_ref, got_ref, level, parity, 2 * piece + bit)
        sent = kept(held_ref, got_ref, level, parity, 2 * piece + 1 - bit)
        send_ref[piece] = sent.astype(send_ref.dtype)


def fold(held, got, level):
    pieces, band, hidden = got.shape
    outs = [f32(pieces // 2, band, hidden), bf16(pieces // 2, band, hidden)]
    return run(functools.partial(fold_kernel, level), outs, (held, got), name="fold")


def finish_kernel(count, parts, *refs):
    back_refs, weight_refs, (back_ref, weight_ref) = refs[:parts], refs[parts:-2], refs[-2:]

    def total(values):
        return sum(ref[...].astype(jnp.float32) for ref in values)

    back_ref[...] = total(back_refs).astype(back_ref.dtype)
    weight_ref[...] = total(weight_refs) / count


def finish(backs, weights, count):
    outs = [bf16(*backs[0].shape), f32(*weights[0].shape)]
    kernel = functools.partial(finish_kernel, count, len(backs))
    return run(kernel, outs, (*backs, *weights), name="finish")


def parity_and_place():
    index = lax.axis_index("section")
    return lax.rem(index, 2), index // 2


def partner(place, index, count):
    return place ^ index if count & (count - 1) == 0 else (place + index) % count


def sender(place, index, count):
    return place ^ index if count & (count - 1) == 0 else (place + count - index) % count


def swap_pairs(value):
    count = lax.axis_size("section")
    return lax.ppermute(value, "section", [(i, i ^ 1) for i in range(count)])


def send_rows(value, index):
    if index == 0:
        return value
    count = lax.axis_size("rows")
    return lax.ppermute(value, "rows", [(i, partner(i, index, count)) for i in range(count)])


def send_section(value, index):
    count = lax.axis_size("section")
    way = [(i, partner(i // 2, index, count // 2) * 2 + i % 2) for i in range(count)]
    return lax.ppermute(value, "section", way)


def gather_pairs(block, first):
    steps = lax.axis_size("section") // 2
    if steps & (steps - 1):
        sent = [send_section(block[None], i) for i in range(1, steps)]
        return [block[None]] + sent, list(range(steps))
    stack, order, half = block[None], [0], steps // 2
    while half > 1:
        stack = jnp.concatenate([stack, after(send_section(stack, half), first)])
        order = order + [index ^ half for index in order]
        half //= 2
    return [stack, send_section(stack, 1)], order + [index ^ 1 for index in order]


def scatter_section(keep, send):
    count = lax.axis_size("section")
    level, sends = 0, [send]
    while True:
        way = [(i, i ^ 1 << level) for i in range(count)]
        got = lax.ppermute(send, "section", way)
        level += 1
        if got.shape[0] % 2:
            break
        keep, send = fold(keep, got, level)
        sends.append(send)
    rest = keep.shape[0]
    if rest == 1:
        return [keep[0], got[0]], sends
    total = keep + got.astype(jnp.float32)
    place = lax.axis_index("section") >> level
    result = lax.dynamic_index_in_dim(total, place, 0, keepdims=False)
    for shift in range(1, rest):
        piece = lax.dynamic_index_in_dim(total, (place + shift) % rest, 0, keepdims=False)
        way = [(i, (i + (shift << level)) % count) for i in range(count)]
        result = result + lax.ppermute(piece.astype(jnp.bfloat16), "section", way).astype(jnp.float32)
    return [result], sends


def after(value, *others):
    return lax.optimization_barrier((value, others))[0]


def local(activations, cotangent, proj_weight, kernel_taps, ln_gain, ln_shift, heights, widths):
    rows_dev, width_dev, chans = activations.shape[1:]
    height_all = cotangent.shape[1]
    hidden_dev = cotangent.shape[3]
    bands = lax.axis_size("rows")
    count = lax.axis_size("section")
    wide, valid = prepare(
        heights, widths, kernel_taps, ln_gain, ln_shift, height_all, width_dev
    )
    grad = cotangent.reshape(-1, hidden_dev)

    acts = [activations[0]] + [send_rows(activations[0], i) for i in range(1, bands)]
    half = bands // 2
    mixed = forward(valid, wide, acts[:half], range(half), bands)
    proj_mine, order = gather_pairs(proj_weight, mixed)
    mixed = forward(valid, wide, acts[half:], range(half, bands), bands, mixed)

    normed, centres, spreads = normalise(valid, mixed, wide)
    whole, send = outer(normed, grad, count)
    weights, sends = scatter_section(whole, after(send, *proj_mine))

    proj_other = [swap_pairs(after(stack, normed)) for stack in proj_mine]
    grads = after(grad, sends[min(1, len(sends) - 1)])
    grad_mixed = project(valid, grads, mixed, centres, spreads, wide, proj_mine, proj_other, order)
    backs = []
    for i in range(bands - 1, -1, -1):
        ready = sends[min(1, len(sends) - 1)] if i > 1 else sends[-1]
        backs.append(send_rows(backward(after(valid, ready), grad_mixed, wide, i, bands), i))
    back, weight_grad = finish(backs, weights, count)
    return (back[None], weight_grad)


def solution(mesh):
    in_specs = (
        P("section", "rows", None, None),
        P("section", None, None, "rows"),
        P("section", "rows"),
        P(),
        P(),
        P(),
        P("section"),
        P("section"),
    )
    out_specs = (P("section", "rows", None, None), P("section", "rows"))
    return jax.shard_map(local, mesh=mesh, in_specs=in_specs, out_specs=out_specs, check_vma=False)
```

```python
import functools

import jax
import jax.numpy as jnp
import numpy as np
from jax import lax
from jax.experimental import pallas as pl
from jax.experimental.pallas import tpu as pltpu
from jax.sharding import PartitionSpec as P

epsilon = 1e-06
LANES = 128
VECTOR = 240
SUBLANES = 8


TILE = 4


def cost(operations, moved):
    return pl.CostEstimate(flops=operations, bytes_accessed=moved, transcendentals=0)


def run(kernel, outs, args, scratch=(), estimate=None, aliases=None, name=None):
    held = list(args) + list(outs) + list(scratch)
    taken = sum(int(np.prod(value.shape)) * jnp.dtype(value.dtype).itemsize for value in held)
    vmem = pl.BlockSpec(memory_space=pltpu.VMEM)
    smem = pl.BlockSpec(memory_space=pltpu.SMEM)
    return pl.pallas_call(
        kernel,
        out_shape=tuple(outs),
        in_specs=[smem if arg.dtype == jnp.int32 else vmem for arg in args],
        out_specs=tuple(vmem for _ in outs),
        scratch_shapes=[pltpu.VMEM(value.shape, value.dtype) for value in scratch],
        input_output_aliases=aliases or {},
        compiler_params=pltpu.CompilerParams(vmem_limit_bytes=taken + taken // 8 + (4 << 20)),
        cost_estimate=estimate or cost(1, 1),
        name=name,
    )(*args)


def f32(*shape):
    return jax.ShapeDtypeStruct(shape, jnp.float32)


def bf16(*shape):
    return jax.ShapeDtypeStruct(shape, jnp.bfloat16)


def prepare_kernel(high_ref, wid_ref, taps_ref, wide_ref, valid_ref):
    count, chans = taps_ref.shape
    taps = taps_ref[...].astype(jnp.float32)
    for tap in range(count):
        wide_ref[tap] = jnp.broadcast_to(taps[tap : tap + 1], (SUBLANES, chans))
    _, width, lanes = valid_ref.shape
    columns = lax.broadcasted_iota(jnp.int32, (width, lanes), 0) < wid_ref[0]

    @pl.loop(0, valid_ref.shape[0])
    def _(row):
        valid_ref[row] = jnp.where(columns & (row < high_ref[0]), 1.0, 0.0)


def prepare(heights, widths, taps, height, width):
    count, chans = taps.shape
    outs = [f32(count, SUBLANES, chans), f32(height, width, LANES)]
    estimate = cost(VECTOR * 128 * taps.size, 1)
    return run(prepare_kernel, outs, (heights, widths, taps), estimate=estimate, name="prepare")


def clear_sides(source, width):
    sides = jnp.zeros((source.shape[0], 8, LANES), source.dtype)
    source[:, :8, :] = sides
    source[:, 8 + width :, :] = sides


def conv_rows(load, positions, outs, wide_ref, lanes, width, flip):
    stride = width // SUBLANES
    running = {out: [None] * stride for out in outs}
    for row, position in enumerate(positions):
        users = [out for out in outs if 0 <= position - out <= 6]
        if not users:
            continue
        shifted = [load(row, pl.ds(5 + k, SUBLANES, stride=stride)) for k in range(stride + 6)]
        for out in users:
            for along in range(7):
                tap = (position - out) * 7 + along
                weight = wide_ref[48 - tap if flip else tap, :, lanes]
                for i in range(stride):
                    term = weight * shifted[i + along]
                    before = running[out][i]
                    running[out][i] = term if before is None else before + term
    return running


def forward_kernel(bands, indices, fresh, valid_ref, taps_ref, *refs):
    act_refs, (mixed, source) = refs[: len(indices)], refs[-2:]
    rows_dev, width, _ = act_refs[0].shape
    blocks, height = mixed.shape[0], mixed.shape[1] - 6
    stride = width // SUBLANES
    band = lax.axis_index("rows")
    joined = source.shape[0] // rows_dev
    clear_sides(source, width)
    once = fresh and len(indices) == joined
    firsts = [sender(band, index, bands) * rows_dev for index in indices]

    @pl.loop(0, blocks)
    def _(block):
        lanes = pl.ds(pl.multiple_of(block * LANES, LANES), LANES)
        if fresh:
            mixed[block] = jnp.zeros(mixed.shape[1:], mixed.dtype)
        for start in range(0, len(indices), joined):
            base = firsts[start]
            for first in firsts[start : start + joined]:
                base = jnp.minimum(base, first)
            for first, act_ref in zip(firsts[start:], act_refs[start : start + joined]):
                for i in range(rows_dev):
                    row = first + i
                    value = act_ref[i, :, lanes].astype(jnp.float32) * valid_ref[row]
                    source[row - base, 8 : 8 + width, :] = value
            rows = joined * rows_dev
            for low in range(0, rows + 6, TILE):
                outs = range(low, min(low + TILE, rows + 6))
                positions = [i + 6 for i in range(rows)]
                running = conv_rows(
                    lambda row, columns_of: source[row, columns_of, :],
                    positions, outs, taps_ref, lanes, width, False,
                )
                for out, pieces in running.items():
                    for i, value in enumerate(pieces):
                        columns_of = pl.ds(i, SUBLANES, stride=stride)
                        if not once:
                            value = value + mixed[block, base + out, columns_of, :]
                        mixed[block, base + out, columns_of, :] = value


def forward(valid, wide, acts, indices, bands, before=None):
    rows_dev, width, chans = acts[0].shape
    joined = 2 if bands & (bands - 1) == 0 and len(indices) % 2 == 0 else 1
    extra = () if before is None else (before,)
    return run(
        functools.partial(forward_kernel, bands, indices, before is None),
        [f32(chans // LANES, rows_dev * bands + 6, width, LANES)],
        (valid, wide, *acts, *extra),
        [f32(joined * rows_dev, width + 16, LANES)],
        cost(3 * VECTOR * len(acts) * acts[0].size * 49 * 2, 6 * len(acts) * acts[0].size),
        {2 + len(acts): 0} if extra else {},
        "forward",
    )[0]


def normalise_kernel(valid_ref, mixed, gain_ref, shift_ref, normed_ref, centres, spreads):
    blocks, height, width, _ = mixed.shape
    height = height - 6
    chans = blocks * LANES

    @pl.loop(0, height // TILE)
    def _(step):
        rows = [step * TILE + i for i in range(TILE)]
        sums = [sum(mixed[block, row + 3] for block in range(blocks)) for row in rows]
        for row, value in zip(rows, sums):
            centre = jnp.sum(value, axis=-1, keepdims=True) / chans
            centres[row] = jnp.broadcast_to(centre, (width, LANES))

    @pl.loop(0, height // TILE)
    def _(step):
        rows = [step * TILE + i for i in range(TILE)]
        sums = []
        for row in rows:
            centre = centres[row]
            away = [mixed[block, row + 3] - centre for block in range(blocks)]
            sums.append(sum(value * value for value in away))
        for row, value in zip(rows, sums):
            spread = jnp.sum(value, axis=-1, keepdims=True) / chans
            spreads[row] = jnp.broadcast_to(lax.rsqrt(spread + epsilon), (width, LANES))

    @pl.loop(0, height)
    def _(row):
        rows = pl.ds(pl.multiple_of(row * width, width), width)
        centre, inv = centres[row], spreads[row]
        for block in range(blocks):
            lanes = slice(block * LANES, (block + 1) * LANES)
            unit = (mixed[block, row + 3] - centre) * inv
            value = unit * gain_ref[block : block + 1, :] + shift_ref[block : block + 1, :]
            value = value * valid_ref[row]
            normed_ref[rows, lanes] = value.astype(normed_ref.dtype)


def normalise(valid, mixed, gain, shift):
    blocks, height, width, _ = mixed.shape
    height = height - 6
    outs = [bf16(height * width, blocks * LANES)] + [f32(height, width, LANES)] * 2
    return run(normalise_kernel, outs, (valid, mixed, gain, shift), name="normalise")


def project_kernel(groups, order, valid_ref, grad_ref, mixed, centres, spreads, gain_ref, *refs):
    mine_refs, other_refs = refs[:groups], refs[groups : 2 * groups]
    out_ref, whole, result, means, alongs = refs[2 * groups :]
    band = mine_refs[0].shape[0]
    blocks, height, width, _ = mixed.shape
    height = height - 6
    chans = blocks * LANES
    parity, place = parity_and_place()
    for refs_of, core in ((mine_refs, parity), (other_refs, 1 - parity)):
        for at, index in enumerate(order):
            step = sender(place, index, len(order))
            start = pl.multiple_of((2 * step + core) * band, 16)
            whole[pl.ds(start, band), :] = refs_of[at][...]
    result[...] = lax.dot_general(
        grad_ref[...], whole[...], (((1,), (1,)), ((), ())), preferred_element_type=jnp.float32
    )

    def scaled_unit(row, block):
        rows = pl.ds(pl.multiple_of(row * width, width), width)
        lanes = slice(block * LANES, (block + 1) * LANES)
        scaled = result[rows, lanes] * gain_ref[block : block + 1, :]
        return scaled, (mixed[block, row + 3] - centres[row]) * spreads[row]

    @pl.loop(0, height // TILE)
    def _(step):
        sums = []
        for i in range(TILE):
            row = step * TILE + i
            pairs = [scaled_unit(row, block) for block in range(blocks)]
            sums.append((row, sum(p[0] for p in pairs), sum(p[0] * p[1] for p in pairs)))
        for row, scaled, product in sums:
            mean = jnp.sum(scaled, axis=-1, keepdims=True) / chans
            means[row] = jnp.broadcast_to(mean, (width, LANES))
            along = jnp.sum(product, axis=-1, keepdims=True) / chans
            alongs[row] = jnp.broadcast_to(along, (width, LANES))

    @pl.loop(0, blocks)
    def _(block):
        clear_sides(out_ref.at[block], width)
        empty = jnp.zeros((3,) + out_ref.shape[2:], out_ref.dtype)
        out_ref[block, :3] = empty
        out_ref[block, 3 + height :] = empty

    @pl.loop(0, height)
    def _(row):
        mean, along = means[row], alongs[row]
        inv = spreads[row] * valid_ref[row]
        for block in range(blocks):
            scaled, unit = scaled_unit(row, block)
            out_ref[block, row + 3, 8 : 8 + width, :] = inv * (scaled - mean - unit * along)


def project(valid, grad, mixed, centres, spreads, gain, mine, other, order):
    blocks, height, width, _ = mixed.shape
    chans = blocks * LANES
    return run(
        functools.partial(project_kernel, len(mine), order),
        [f32(blocks, height, width + 16, LANES)],
        (valid, grad, mixed, centres, spreads, gain, *mine, *other),
        [bf16(chans, grad.shape[1]), f32(grad.shape[0], chans)] + [f32(*centres.shape)] * 2,
        cost(VECTOR * mixed.size * 12, 8 * mixed.size),
        name="project",
    )[0]


def backward_kernel(index, bands, valid_ref, grad_ref, taps_ref, out_ref, result):
    rows_dev, width, chans = out_ref.shape
    stride = width // SUBLANES
    first = partner(lax.axis_index("rows"), index, bands) * rows_dev

    @pl.loop(0, chans // LANES)
    def _(block):
        lanes = pl.ds(pl.multiple_of(block * LANES, LANES), LANES)
        for low in range(0, rows_dev, TILE):
            outs = range(low, min(low + TILE, rows_dev))
            running = conv_rows(
                lambda row, columns_of: grad_ref[block, first + row, columns_of, :],
                list(range(rows_dev + 6)), outs, taps_ref, lanes, width, True,
            )
            for out, pieces in running.items():
                for i, value in enumerate(pieces):
                    result[out, pl.ds(i, SUBLANES, stride=stride), :] = value
        for row in range(rows_dev):
            out_ref[row, :, lanes] = (result[row] * valid_ref[first + row]).astype(out_ref.dtype)


def backward(valid, grad, taps, index, bands):
    blocks, height, width, _ = grad.shape
    rows_dev, width = (height - 6) // bands, width - 16
    shape = (rows_dev, width, blocks * LANES)
    return run(
        functools.partial(backward_kernel, index, bands),
        [bf16(*shape) if index else f32(*shape)],
        (valid, grad, taps),
        [f32(rows_dev, width, LANES)],
        cost(VECTOR * rows_dev * width * blocks * LANES * 49 * 2, 1),
        name="backward",
    )[0]


def outer_kernel(normed_ref, grad_ref, whole_ref, send_ref):
    pieces, band, hidden = whole_ref.shape
    parity, _ = parity_and_place()
    whole_ref[...] = lax.dot_general(
        normed_ref[...], grad_ref[...], (((0,), (0,)), ((), ())), preferred_element_type=jnp.float32
    ).reshape(pieces, band, hidden)
    for piece in range(pieces // 2):
        send_ref[piece] = whole_ref[2 * piece + 1 - parity].astype(send_ref.dtype)


def outer(normed, grad, count):
    chans, hidden = normed.shape[1], grad.shape[1]
    outs = [f32(count, chans // count, hidden), bf16(count // 2, chans // count, hidden)]
    return run(outer_kernel, outs, (normed, grad), name="outer")


def kept(held_ref, got_ref, level, parity, piece):
    held = held_ref[2 * piece + parity] if level == 1 else held_ref[piece]
    return held + got_ref[piece].astype(jnp.float32)


def fold_kernel(level, held_ref, got_ref, keep_ref, send_ref):
    parity, place = parity_and_place()
    bit = lax.rem(place >> level - 1, 2)
    for piece in range(keep_ref.shape[0]):
        keep_ref[piece] = kept(held_ref, got_ref, level, parity, 2 * piece + bit)
        sent = kept(held_ref, got_ref, level, parity, 2 * piece + 1 - bit)
        send_ref[piece] = sent.astype(send_ref.dtype)


def fold(held, got, level):
    pieces, band, hidden = got.shape
    outs = [f32(pieces // 2, band, hidden), bf16(pieces // 2, band, hidden)]
    return run(functools.partial(fold_kernel, level), outs, (held, got), name="fold")


def finish_kernel(count, parts, *refs):
    back_refs, weight_refs, (back_ref, weight_ref) = refs[:parts], refs[parts:-2], refs[-2:]

    def total(values):
        return sum(ref[...].astype(jnp.float32) for ref in values)

    back_ref[...] = total(back_refs).astype(back_ref.dtype)
    weight_ref[...] = total(weight_refs) / count


def finish(backs, weights, count):
    outs = [bf16(*backs[0].shape), f32(*weights[0].shape)]
    kernel = functools.partial(finish_kernel, count, len(backs))
    return run(kernel, outs, (*backs, *weights), name="finish")


def parity_and_place():
    index = lax.axis_index("section")
    return lax.rem(index, 2), index // 2


def partner(place, index, count):
    return place ^ index if count & (count - 1) == 0 else (place + index) % count


def sender(place, index, count):
    return place ^ index if count & (count - 1) == 0 else (place + count - index) % count


def swap_pairs(value):
    count = lax.axis_size("section")
    return lax.ppermute(value, "section", [(i, i ^ 1) for i in range(count)])


def send_rows(value, index):
    if index == 0:
        return value
    count = lax.axis_size("rows")
    return lax.ppermute(value, "rows", [(i, partner(i, index, count)) for i in range(count)])


def send_section(value, index):
    count = lax.axis_size("section")
    way = [(i, partner(i // 2, index, count // 2) * 2 + i % 2) for i in range(count)]
    return lax.ppermute(value, "section", way)


def gather_pairs(block, first):
    steps = lax.axis_size("section") // 2
    if steps & (steps - 1):
        return [block] + [send_section(block, i) for i in range(1, steps)], list(range(steps))
    pieces = {0: block}
    while len(pieces) < steps:
        far = steps // (2 * len(pieces))
        ready = {i: piece if i == 0 else after(piece, first) for i, piece in pieces.items()}
        pieces |= {i ^ far: send_section(piece, far) for i, piece in ready.items()}
    return list(pieces.values()), list(pieces)


def scatter_section(keep, send):
    count = lax.axis_size("section")
    level, sends = 0, [send]
    while True:
        way = [(i, i ^ 1 << level) for i in range(count)]
        got = lax.ppermute(send, "section", way)
        level += 1
        if got.shape[0] % 2:
            break
        keep, send = fold(keep, got, level)
        sends.append(send)
    rest = keep.shape[0]
    if rest == 1:
        return [keep[0], got[0]], sends
    total = keep + got.astype(jnp.float32)
    place = lax.axis_index("section") >> level
    result = lax.dynamic_index_in_dim(total, place, 0, keepdims=False)
    for shift in range(1, rest):
        piece = lax.dynamic_index_in_dim(total, (place + shift) % rest, 0, keepdims=False)
        way = [(i, (i + (shift << level)) % count) for i in range(count)]
        result = result + lax.ppermute(piece.astype(jnp.bfloat16), "section", way).astype(jnp.float32)
    return [result], sends


def after(value, *others):
    return lax.optimization_barrier((value, others))[0]


def local(activations, cotangent, proj_weight, kernel_taps, ln_gain, ln_shift, heights, widths):
    rows_dev, width_dev, chans = activations.shape[1:]
    height_all = cotangent.shape[1]
    hidden_dev = cotangent.shape[3]
    bands = lax.axis_size("rows")
    count = lax.axis_size("section")
    wide, valid = prepare(heights, widths, kernel_taps, height_all, width_dev)
    gain, shift = (value.reshape(chans // LANES, LANES) for value in (ln_gain, ln_shift))
    grad = cotangent.reshape(-1, hidden_dev)

    acts = [activations[0]] + [send_rows(activations[0], i) for i in range(1, bands)]
    half = bands // 2
    mixed = forward(valid, wide, acts[:half], range(half), bands)
    proj_mine, order = gather_pairs(proj_weight, mixed)
    mixed = forward(valid, wide, acts[half:], range(half, bands), bands, mixed)

    normed, centres, spreads = normalise(valid, mixed, gain, shift)
    whole, send = outer(normed, grad, count)
    weights, sends = scatter_section(whole, after(send, *proj_mine))

    proj_other = [swap_pairs(after(stack, normed)) for stack in proj_mine]
    grads = after(grad, sends[min(1, len(sends) - 1)])
    grad_mixed = project(valid, grads, mixed, centres, spreads, gain, proj_mine, proj_other, order)
    backs = []
    for i in range(bands - 1, -1, -1):
        ready = sends[min(1, len(sends) - 1)] if i > 1 else sends[-1]
        backs.append(send_rows(backward(after(valid, ready), grad_mixed, wide, i, bands), i))
    back, weight_grad = finish(backs, weights, count)
    return (back[None], weight_grad)


def solution(mesh):
    in_specs = (
        P("section", "rows", None, None),
        P("section", None, None, "rows"),
        P("section", "rows"),
        P(),
        P(),
        P(),
        P("section"),
        P("section"),
    )
    out_specs = (P("section", "rows", None, None), P("section", "rows"))
    return jax.shard_map(local, mesh=mesh, in_specs=in_specs, out_specs=out_specs, check_vma=False)
```

```python
import functools

import jax
import jax.numpy as jnp
import numpy as np
from jax import lax
from jax.experimental import pallas as pl
from jax.experimental.pallas import tpu as pltpu
from jax.sharding import PartitionSpec as P

epsilon = 1e-06
LANES = 128
VECTOR = 240
SUBLANES = 8


TILE = 4


def cost(operations, moved):
    return pl.CostEstimate(flops=operations, bytes_accessed=moved, transcendentals=0)


def run(kernel, outs, args, scratch=(), estimate=None, aliases=None, name=None):
    held = list(args) + list(outs) + list(scratch)
    taken = sum(int(np.prod(value.shape)) * jnp.dtype(value.dtype).itemsize for value in held)
    vmem = pl.BlockSpec(memory_space=pltpu.VMEM)
    smem = pl.BlockSpec(memory_space=pltpu.SMEM)
    return pl.pallas_call(
        kernel,
        out_shape=tuple(outs),
        in_specs=[smem if arg.dtype == jnp.int32 else vmem for arg in args],
        out_specs=tuple(vmem for _ in outs),
        scratch_shapes=[pltpu.VMEM(value.shape, value.dtype) for value in scratch],
        input_output_aliases=aliases or {},
        compiler_params=pltpu.CompilerParams(vmem_limit_bytes=taken + taken // 8 + (4 << 20)),
        cost_estimate=estimate or cost(1, 1),
        name=name,
    )(*args)


def f32(*shape):
    return jax.ShapeDtypeStruct(shape, jnp.float32)


def bf16(*shape):
    return jax.ShapeDtypeStruct(shape, jnp.bfloat16)


def begin_kernel(out_ref):
    out_ref[...] = jnp.zeros(out_ref.shape, out_ref.dtype)


def prepare_kernel(zero_ref, high_ref, wid_ref, taps_ref, wide_ref, valid_ref):
    count, chans = taps_ref.shape
    taps = taps_ref[...].astype(jnp.float32)
    for tap in range(count):
        wide_ref[tap] = jnp.broadcast_to(taps[tap : tap + 1], (SUBLANES, chans))
    _, width, lanes = valid_ref.shape
    columns = lax.broadcasted_iota(jnp.int32, (width, lanes), 0) < wid_ref[0]

    @pl.loop(0, valid_ref.shape[0])
    def _(row):
        valid_ref[row] = jnp.where(columns & (row < high_ref[0]), 1.0, 0.0) + zero_ref[0:1, :]


def prepare(heights, widths, taps, height, width):
    count, chans = taps.shape
    outs = [f32(count, SUBLANES, chans), f32(height, width, LANES)]
    estimate = cost(VECTOR * 128 * taps.size, 1)
    zero = run(begin_kernel, [f32(SUBLANES, LANES)], (), estimate=estimate, name="begin")[0]
    args = (zero, heights, widths, taps)
    return run(prepare_kernel, outs, args, name="prepare")


def clear_sides(source, width):
    sides = jnp.zeros((source.shape[0], 8, LANES), source.dtype)
    source[:, :8, :] = sides
    source[:, 8 + width :, :] = sides


def conv_rows(load, positions, outs, wide_ref, lanes, width, flip):
    stride = width // SUBLANES
    running = {out: [None] * stride for out in outs}
    for row, position in enumerate(positions):
        users = [out for out in outs if 0 <= position - out <= 6]
        if not users:
            continue
        shifted = [load(row, pl.ds(5 + k, SUBLANES, stride=stride)) for k in range(stride + 6)]
        for out in users:
            for along in range(7):
                tap = (position - out) * 7 + along
                weight = wide_ref[48 - tap if flip else tap, :, lanes]
                for i in range(stride):
                    term = weight * shifted[i + along]
                    before = running[out][i]
                    running[out][i] = term if before is None else before + term
    return running


def forward_kernel(bands, indices, fresh, valid_ref, taps_ref, *refs):
    act_refs, (mixed, source) = refs[: len(indices)], refs[-2:]
    rows_dev, width, _ = act_refs[0].shape
    blocks, height = mixed.shape[0], mixed.shape[1] - 6
    stride = width // SUBLANES
    band = lax.axis_index("rows")
    joined = source.shape[0] // rows_dev
    clear_sides(source, width)
    once = fresh and len(indices) == joined
    firsts = [sender(band, index, bands) * rows_dev for index in indices]

    @pl.loop(0, blocks)
    def _(block):
        lanes = pl.ds(pl.multiple_of(block * LANES, LANES), LANES)
        if fresh:
            mixed[block] = jnp.zeros(mixed.shape[1:], mixed.dtype)
        for start in range(0, len(indices), joined):
            base = firsts[start]
            for first in firsts[start : start + joined]:
                base = jnp.minimum(base, first)
            for first, act_ref in zip(firsts[start:], act_refs[start : start + joined]):
                for i in range(rows_dev):
                    row = first + i
                    value = act_ref[i, :, lanes].astype(jnp.float32) * valid_ref[row]
                    source[row - base, 8 : 8 + width, :] = value
            rows = joined * rows_dev
            for low in range(0, rows + 6, TILE):
                outs = range(low, min(low + TILE, rows + 6))
                positions = [i + 6 for i in range(rows)]
                running = conv_rows(
                    lambda row, columns_of: source[row, columns_of, :],
                    positions, outs, taps_ref, lanes, width, False,
                )
                for out, pieces in running.items():
                    for i, value in enumerate(pieces):
                        columns_of = pl.ds(i, SUBLANES, stride=stride)
                        if not once:
                            value = value + mixed[block, base + out, columns_of, :]
                        mixed[block, base + out, columns_of, :] = value


def forward(valid, wide, acts, indices, bands, before=None):
    rows_dev, width, chans = acts[0].shape
    joined = 2 if bands & (bands - 1) == 0 and len(indices) % 2 == 0 else 1
    extra = () if before is None else (before,)
    return run(
        functools.partial(forward_kernel, bands, indices, before is None),
        [f32(chans // LANES, rows_dev * bands + 6, width, LANES)],
        (valid, wide, *acts, *extra),
        [f32(joined * rows_dev, width + 16, LANES)],
        cost(3 * VECTOR * len(acts) * acts[0].size * 49 * 2, 6 * len(acts) * acts[0].size),
        {2 + len(acts): 0} if extra else {},
        "forward",
    )[0]


def normalise_kernel(valid_ref, mixed, gain_ref, shift_ref, normed_ref, centres, spreads):
    blocks, height, width, _ = mixed.shape
    height = height - 6
    chans = blocks * LANES

    @pl.loop(0, height // TILE)
    def _(step):
        rows = [step * TILE + i for i in range(TILE)]
        sums = [sum(mixed[block, row + 3] for block in range(blocks)) for row in rows]
        for row, value in zip(rows, sums):
            centre = jnp.sum(value, axis=-1, keepdims=True) / chans
            centres[row] = jnp.broadcast_to(centre, (width, LANES))

    @pl.loop(0, height // TILE)
    def _(step):
        rows = [step * TILE + i for i in range(TILE)]
        sums = []
        for row in rows:
            centre = centres[row]
            away = [mixed[block, row + 3] - centre for block in range(blocks)]
            sums.append(sum(value * value for value in away))
        for row, value in zip(rows, sums):
            spread = jnp.sum(value, axis=-1, keepdims=True) / chans
            spreads[row] = jnp.broadcast_to(lax.rsqrt(spread + epsilon), (width, LANES))

    @pl.loop(0, height)
    def _(row):
        rows = pl.ds(pl.multiple_of(row * width, width), width)
        centre, inv = centres[row], spreads[row]
        for block in range(blocks):
            lanes = slice(block * LANES, (block + 1) * LANES)
            unit = (mixed[block, row + 3] - centre) * inv
            value = unit * gain_ref[block : block + 1, :] + shift_ref[block : block + 1, :]
            value = value * valid_ref[row]
            normed_ref[rows, lanes] = value.astype(normed_ref.dtype)


def normalise(valid, mixed, gain, shift):
    blocks, height, width, _ = mixed.shape
    height = height - 6
    outs = [bf16(height * width, blocks * LANES)] + [f32(height, width, LANES)] * 2
    return run(normalise_kernel, outs, (valid, mixed, gain, shift), name="normalise")


def project_kernel(groups, order, valid_ref, grad_ref, mixed, centres, spreads, gain_ref, *refs):
    mine_refs, other_refs = refs[:groups], refs[groups : 2 * groups]
    out_ref, whole, result, means, alongs = refs[2 * groups :]
    band = mine_refs[0].shape[0]
    blocks, height, width, _ = mixed.shape
    height = height - 6
    chans = blocks * LANES
    parity, place = parity_and_place()
    for refs_of, core in ((mine_refs, parity), (other_refs, 1 - parity)):
        for at, index in enumerate(order):
            step = sender(place, index, len(order))
            start = pl.multiple_of((2 * step + core) * band, 16)
            whole[pl.ds(start, band), :] = refs_of[at][...]
    result[...] = lax.dot_general(
        grad_ref[...], whole[...], (((1,), (1,)), ((), ())), preferred_element_type=jnp.float32
    )

    def scaled_unit(row, block):
        rows = pl.ds(pl.multiple_of(row * width, width), width)
        lanes = slice(block * LANES, (block + 1) * LANES)
        scaled = result[rows, lanes] * gain_ref[block : block + 1, :]
        return scaled, (mixed[block, row + 3] - centres[row]) * spreads[row]

    @pl.loop(0, height // TILE)
    def _(step):
        sums = []
        for i in range(TILE):
            row = step * TILE + i
            pairs = [scaled_unit(row, block) for block in range(blocks)]
            sums.append((row, sum(p[0] for p in pairs), sum(p[0] * p[1] for p in pairs)))
        for row, scaled, product in sums:
            mean = jnp.sum(scaled, axis=-1, keepdims=True) / chans
            means[row] = jnp.broadcast_to(mean, (width, LANES))
            along = jnp.sum(product, axis=-1, keepdims=True) / chans
            alongs[row] = jnp.broadcast_to(along, (width, LANES))

    @pl.loop(0, blocks)
    def _(block):
        clear_sides(out_ref.at[block], width)
        empty = jnp.zeros((3,) + out_ref.shape[2:], out_ref.dtype)
        out_ref[block, :3] = empty
        out_ref[block, 3 + height :] = empty

    @pl.loop(0, height)
    def _(row):
        mean, along = means[row], alongs[row]
        inv = spreads[row] * valid_ref[row]
        for block in range(blocks):
            scaled, unit = scaled_unit(row, block)
            out_ref[block, row + 3, 8 : 8 + width, :] = inv * (scaled - mean - unit * along)


def project(valid, grad, mixed, centres, spreads, gain, mine, other, order):
    blocks, height, width, _ = mixed.shape
    chans = blocks * LANES
    return run(
        functools.partial(project_kernel, len(mine), order),
        [f32(blocks, height, width + 16, LANES)],
        (valid, grad, mixed, centres, spreads, gain, *mine, *other),
        [bf16(chans, grad.shape[1]), f32(grad.shape[0], chans)] + [f32(*centres.shape)] * 2,
        cost(VECTOR * mixed.size * 12, 8 * mixed.size),
        name="project",
    )[0]


def backward_kernel(index, bands, valid_ref, grad_ref, taps_ref, out_ref, result):
    rows_dev, width, chans = out_ref.shape
    stride = width // SUBLANES
    first = partner(lax.axis_index("rows"), index, bands) * rows_dev

    @pl.loop(0, chans // LANES)
    def _(block):
        lanes = pl.ds(pl.multiple_of(block * LANES, LANES), LANES)
        for low in range(0, rows_dev, TILE):
            outs = range(low, min(low + TILE, rows_dev))
            running = conv_rows(
                lambda row, columns_of: grad_ref[block, first + row, columns_of, :],
                list(range(rows_dev + 6)), outs, taps_ref, lanes, width, True,
            )
            for out, pieces in running.items():
                for i, value in enumerate(pieces):
                    result[out, pl.ds(i, SUBLANES, stride=stride), :] = value
        for row in range(rows_dev):
            out_ref[row, :, lanes] = (result[row] * valid_ref[first + row]).astype(out_ref.dtype)


def backward(valid, grad, taps, index, bands):
    blocks, height, width, _ = grad.shape
    rows_dev, width = (height - 6) // bands, width - 16
    shape = (rows_dev, width, blocks * LANES)
    return run(
        functools.partial(backward_kernel, index, bands),
        [bf16(*shape) if index else f32(*shape)],
        (valid, grad, taps),
        [f32(rows_dev, width, LANES)],
        cost(VECTOR * rows_dev * width * blocks * LANES * 49 * 2, 1),
        name="backward",
    )[0]


def outer_kernel(normed_ref, grad_ref, whole_ref, send_ref):
    pieces, band, hidden = whole_ref.shape
    parity, _ = parity_and_place()
    whole_ref[...] = lax.dot_general(
        normed_ref[...], grad_ref[...], (((0,), (0,)), ((), ())), preferred_element_type=jnp.float32
    ).reshape(pieces, band, hidden)
    for piece in range(pieces // 2):
        send_ref[piece] = whole_ref[2 * piece + 1 - parity].astype(send_ref.dtype)


def outer(normed, grad, count):
    chans, hidden = normed.shape[1], grad.shape[1]
    outs = [f32(count, chans // count, hidden), bf16(count // 2, chans // count, hidden)]
    return run(outer_kernel, outs, (normed, grad), name="outer")


def kept(held_ref, got_ref, level, parity, piece):
    held = held_ref[2 * piece + parity] if level == 1 else held_ref[piece]
    return held + got_ref[piece].astype(jnp.float32)


def fold_kernel(level, held_ref, got_ref, keep_ref, send_ref):
    parity, place = parity_and_place()
    bit = lax.rem(place >> level - 1, 2)
    for piece in range(keep_ref.shape[0]):
        keep_ref[piece] = kept(held_ref, got_ref, level, parity, 2 * piece + bit)
        sent = kept(held_ref, got_ref, level, parity, 2 * piece + 1 - bit)
        send_ref[piece] = sent.astype(send_ref.dtype)


def fold(held, got, level):
    pieces, band, hidden = got.shape
    outs = [f32(pieces // 2, band, hidden), bf16(pieces // 2, band, hidden)]
    return run(functools.partial(fold_kernel, level), outs, (held, got), name="fold")


def finish_kernel(count, parts, *refs):
    back_refs, weight_refs, (back_ref, weight_ref) = refs[:parts], refs[parts:-2], refs[-2:]

    def total(values):
        return sum(ref[...].astype(jnp.float32) for ref in values)

    back_ref[...] = total(back_refs).astype(back_ref.dtype)
    weight_ref[...] = total(weight_refs) / count


def finish(backs, weights, count):
    outs = [bf16(*backs[0].shape), f32(*weights[0].shape)]
    kernel = functools.partial(finish_kernel, count, len(backs))
    return run(kernel, outs, (*backs, *weights), name="finish")


def parity_and_place():
    index = lax.axis_index("section")
    return lax.rem(index, 2), index // 2


def partner(place, index, count):
    return place ^ index if count & (count - 1) == 0 else (place + index) % count


def sender(place, index, count):
    return place ^ index if count & (count - 1) == 0 else (place + count - index) % count


def swap_pairs(value):
    count = lax.axis_size("section")
    return lax.ppermute(value, "section", [(i, i ^ 1) for i in range(count)])


def send_rows(value, index):
    if index == 0:
        return value
    count = lax.axis_size("rows")
    return lax.ppermute(value, "rows", [(i, partner(i, index, count)) for i in range(count)])


def send_section(value, index):
    count = lax.axis_size("section")
    way = [(i, partner(i // 2, index, count // 2) * 2 + i % 2) for i in range(count)]
    return lax.ppermute(value, "section", way)


def gather_pairs(block, first):
    steps = lax.axis_size("section") // 2
    if steps & (steps - 1):
        return [block] + [send_section(block, i) for i in range(1, steps)], list(range(steps))
    pieces = {0: block}
    while len(pieces) < steps:
        far = steps // (2 * len(pieces))
        ready = {i: piece if i == 0 else after(piece, first) for i, piece in pieces.items()}
        pieces |= {i ^ far: send_section(piece, far) for i, piece in ready.items()}
    return list(pieces.values()), list(pieces)


def scatter_section(keep, send):
    count = lax.axis_size("section")
    level, sends = 0, [send]
    while True:
        way = [(i, i ^ 1 << level) for i in range(count)]
        got = lax.ppermute(send, "section", way)
        level += 1
        if got.shape[0] % 2:
            break
        keep, send = fold(keep, got, level)
        sends.append(send)
    rest = keep.shape[0]
    if rest == 1:
        return [keep[0], got[0]], sends
    total = keep + got.astype(jnp.float32)
    place = lax.axis_index("section") >> level
    result = lax.dynamic_index_in_dim(total, place, 0, keepdims=False)
    for shift in range(1, rest):
        piece = lax.dynamic_index_in_dim(total, (place + shift) % rest, 0, keepdims=False)
        way = [(i, (i + (shift << level)) % count) for i in range(count)]
        result = result + lax.ppermute(piece.astype(jnp.bfloat16), "section", way).astype(jnp.float32)
    return [result], sends


def after(value, *others):
    return lax.optimization_barrier((value, others))[0]


def local(activations, cotangent, proj_weight, kernel_taps, ln_gain, ln_shift, heights, widths):
    rows_dev, width_dev, chans = activations.shape[1:]
    height_all = cotangent.shape[1]
    hidden_dev = cotangent.shape[3]
    bands = lax.axis_size("rows")
    count = lax.axis_size("section")
    wide, valid = prepare(heights, widths, kernel_taps, height_all, width_dev)
    gain, shift = (value.reshape(chans // LANES, LANES) for value in (ln_gain, ln_shift))
    grad = cotangent.reshape(-1, hidden_dev)

    acts = [activations[0]] + [send_rows(activations[0], i) for i in range(1, bands)]
    half = bands // 2
    mixed = forward(valid, wide, acts[:half], range(half), bands)
    proj_mine, order = gather_pairs(proj_weight, mixed)
    mixed = forward(valid, wide, acts[half:], range(half, bands), bands, mixed)

    normed, centres, spreads = normalise(valid, mixed, gain, shift)
    whole, send = outer(normed, grad, count)
    weights, sends = scatter_section(whole, after(send, *proj_mine))

    proj_other = [swap_pairs(after(stack, normed)) for stack in proj_mine]
    grads = after(grad, sends[min(1, len(sends) - 1)])
    grad_mixed = project(valid, grads, mixed, centres, spreads, gain, proj_mine, proj_other, order)
    backs = []
    for i in [*range(2, bands), 1, 0]:
        ready = sends[min(1, len(sends) - 1)] if i > 1 else sends[-1]
        backs.append(send_rows(backward(after(valid, ready), grad_mixed, wide, i, bands), i))
    back, weight_grad = finish(backs, weights, count)
    return (back[None], weight_grad)


def solution(mesh):
    in_specs = (
        P("section", "rows", None, None),
        P("section", None, None, "rows"),
        P("section", "rows"),
        P(),
        P(),
        P(),
        P("section"),
        P("section"),
    )
    out_specs = (P("section", "rows", None, None), P("section", "rows"))
    return jax.shard_map(local, mesh=mesh, in_specs=in_specs, out_specs=out_specs, check_vma=False)
```

```python
import functools

import jax
import jax.numpy as jnp
import numpy as np
from jax import lax
from jax.experimental import pallas as pl
from jax.experimental.pallas import tpu as pltpu
from jax.sharding import PartitionSpec as P

epsilon = 1e-06
LANES = 128
VECTOR = 240
SUBLANES = 8


TILE = 4


def cost(operations, moved):
    return pl.CostEstimate(flops=operations, bytes_accessed=moved, transcendentals=0)


def run(kernel, outs, args, scratch=(), estimate=None, aliases=None, name=None):
    held = list(args) + list(outs) + list(scratch)
    taken = sum(int(np.prod(value.shape)) * jnp.dtype(value.dtype).itemsize for value in held)
    vmem = pl.BlockSpec(memory_space=pltpu.VMEM)
    smem = pl.BlockSpec(memory_space=pltpu.SMEM)
    return pl.pallas_call(
        kernel,
        out_shape=tuple(outs),
        in_specs=[smem if arg.dtype == jnp.int32 else vmem for arg in args],
        out_specs=tuple(vmem for _ in outs),
        scratch_shapes=[pltpu.VMEM(value.shape, value.dtype) for value in scratch],
        input_output_aliases=aliases or {},
        compiler_params=pltpu.CompilerParams(vmem_limit_bytes=taken + taken // 8 + (4 << 20)),
        cost_estimate=estimate or cost(1, 1),
        name=name,
    )(*args)


def f32(*shape):
    return jax.ShapeDtypeStruct(shape, jnp.float32)


def bf16(*shape):
    return jax.ShapeDtypeStruct(shape, jnp.bfloat16)


def begin_kernel(out_ref):
    out_ref[...] = jnp.zeros(out_ref.shape, out_ref.dtype)


def prepare_kernel(zero_ref, high_ref, wid_ref, taps_ref, act_ref, wide_ref, valid_ref):
    count, chans = taps_ref.shape
    taps = taps_ref[...].astype(jnp.float32)
    for tap in range(count):
        wide_ref[tap] = jnp.broadcast_to(taps[tap : tap + 1], (SUBLANES, chans))
    _, width, lanes = valid_ref.shape
    columns = lax.broadcasted_iota(jnp.int32, (width, lanes), 0) < wid_ref[0]

    @pl.loop(0, valid_ref.shape[0])
    def _(row):
        valid_ref[row] = jnp.where(columns & (row < high_ref[0]), 1.0, 0.0) + zero_ref[0:1, :]


def prepare(heights, widths, taps, act, height):
    count, chans = taps.shape
    outs = [f32(count, SUBLANES, chans), f32(height, act.shape[1], LANES)]
    estimate = cost(VECTOR * 128 * taps.size, 1)
    zero = run(begin_kernel, [f32(SUBLANES, LANES)], (), estimate=estimate, name="begin")[0]
    args = (zero, heights, widths, taps, act)
    return run(prepare_kernel, outs, args, name="prepare")


def clear_sides(source, width):
    sides = jnp.zeros((source.shape[0], 8, LANES), source.dtype)
    source[:, :8, :] = sides
    source[:, 8 + width :, :] = sides


def conv_rows(load, positions, outs, wide_ref, lanes, width, flip):
    stride = width // SUBLANES
    running = {out: [None] * stride for out in outs}
    for row, position in enumerate(positions):
        users = [out for out in outs if 0 <= position - out <= 6]
        if not users:
            continue
        shifted = [load(row, pl.ds(5 + k, SUBLANES, stride=stride)) for k in range(stride + 6)]
        for out in users:
            for along in range(7):
                tap = (position - out) * 7 + along
                weight = wide_ref[48 - tap if flip else tap, :, lanes]
                for i in range(stride):
                    term = weight * shifted[i + along]
                    before = running[out][i]
                    running[out][i] = term if before is None else before + term
    return running


def forward_kernel(bands, indices, fresh, valid_ref, taps_ref, *refs):
    act_refs, (mixed, source) = refs[: len(indices)], refs[-2:]
    rows_dev, width, _ = act_refs[0].shape
    blocks, height = mixed.shape[0], mixed.shape[1] - 6
    stride = width // SUBLANES
    band = lax.axis_index("rows")
    joined = source.shape[0] // rows_dev
    clear_sides(source, width)
    once = fresh and len(indices) == joined
    firsts = [sender(band, index, bands) * rows_dev for index in indices]

    @pl.loop(0, blocks)
    def _(block):
        lanes = pl.ds(pl.multiple_of(block * LANES, LANES), LANES)
        if fresh:
            mixed[block] = jnp.zeros(mixed.shape[1:], mixed.dtype)
        for start in range(0, len(indices), joined):
            base = firsts[start]
            for first in firsts[start : start + joined]:
                base = jnp.minimum(base, first)
            for first, act_ref in zip(firsts[start:], act_refs[start : start + joined]):
                for i in range(rows_dev):
                    row = first + i
                    value = act_ref[i, :, lanes].astype(jnp.float32) * valid_ref[row]
                    source[row - base, 8 : 8 + width, :] = value
            rows = joined * rows_dev
            for low in range(0, rows + 6, TILE):
                outs = range(low, min(low + TILE, rows + 6))
                positions = [i + 6 for i in range(rows)]
                running = conv_rows(
                    lambda row, columns_of: source[row, columns_of, :],
                    positions, outs, taps_ref, lanes, width, False,
                )
                for out, pieces in running.items():
                    for i, value in enumerate(pieces):
                        columns_of = pl.ds(i, SUBLANES, stride=stride)
                        if not once:
                            value = value + mixed[block, base + out, columns_of, :]
                        mixed[block, base + out, columns_of, :] = value


def forward(valid, wide, acts, indices, bands, before=None):
    rows_dev, width, chans = acts[0].shape
    joined = 2 if bands & (bands - 1) == 0 and len(indices) % 2 == 0 else 1
    extra = () if before is None else (before,)
    return run(
        functools.partial(forward_kernel, bands, indices, before is None),
        [f32(chans // LANES, rows_dev * bands + 6, width, LANES)],
        (valid, wide, *acts, *extra),
        [f32(joined * rows_dev, width + 16, LANES)],
        cost(1, 1) if extra else cost(3 * VECTOR * len(acts) * acts[0].size * 49 * 2, 1),
        {2 + len(acts): 0} if extra else {},
        "forward",
    )[0]


def normalise_kernel(valid_ref, mixed, gain_ref, shift_ref, normed_ref, centres, spreads):
    blocks, height, width, _ = mixed.shape
    height = height - 6
    chans = blocks * LANES

    @pl.loop(0, height // TILE)
    def _(step):
        rows = [step * TILE + i for i in range(TILE)]
        sums = [sum(mixed[block, row + 3] for block in range(blocks)) for row in rows]
        for row, value in zip(rows, sums):
            centre = jnp.sum(value, axis=-1, keepdims=True) / chans
            centres[row] = jnp.broadcast_to(centre, (width, LANES))

    @pl.loop(0, height // TILE)
    def _(step):
        rows = [step * TILE + i for i in range(TILE)]
        sums = []
        for row in rows:
            centre = centres[row]
            away = [mixed[block, row + 3] - centre for block in range(blocks)]
            sums.append(sum(value * value for value in away))
        for row, value in zip(rows, sums):
            spread = jnp.sum(value, axis=-1, keepdims=True) / chans
            spreads[row] = jnp.broadcast_to(lax.rsqrt(spread + epsilon), (width, LANES))

    @pl.loop(0, height)
    def _(row):
        rows = pl.ds(pl.multiple_of(row * width, width), width)
        centre, inv = centres[row], spreads[row]
        for block in range(blocks):
            lanes = slice(block * LANES, (block + 1) * LANES)
            unit = (mixed[block, row + 3] - centre) * inv
            value = unit * gain_ref[block : block + 1, :] + shift_ref[block : block + 1, :]
            value = value * valid_ref[row]
            normed_ref[rows, lanes] = value.astype(normed_ref.dtype)


def normalise(valid, mixed, gain, shift):
    blocks, height, width, _ = mixed.shape
    height = height - 6
    outs = [bf16(height * width, blocks * LANES)] + [f32(height, width, LANES)] * 2
    return run(normalise_kernel, outs, (valid, mixed, gain, shift), name="normalise")


def project_kernel(steps, valid_ref, grad_ref, mixed, centres, spreads, gain_ref, *refs):
    mine_refs, other_refs = refs[:steps], refs[steps : 2 * steps]
    out_ref, whole, result, means, alongs = refs[2 * steps :]
    band = mine_refs[0].shape[0]
    blocks, height, width, _ = mixed.shape
    height = height - 6
    chans = blocks * LANES
    parity, place = parity_and_place()
    for refs_of, core in ((mine_refs, parity), (other_refs, 1 - parity)):
        for index, ref in enumerate(refs_of):
            step = sender(place, index, steps)
            start = pl.multiple_of((2 * step + core) * band, 16)
            whole[pl.ds(start, band), :] = ref[...]
    result[...] = lax.dot_general(
        grad_ref[...], whole[...], (((1,), (1,)), ((), ())), preferred_element_type=jnp.float32
    )

    def scaled_unit(row, block):
        rows = pl.ds(pl.multiple_of(row * width, width), width)
        lanes = slice(block * LANES, (block + 1) * LANES)
        scaled = result[rows, lanes] * gain_ref[block : block + 1, :]
        return scaled, (mixed[block, row + 3] - centres[row]) * spreads[row]

    @pl.loop(0, height // TILE)
    def _(step):
        sums = []
        for i in range(TILE):
            row = step * TILE + i
            pairs = [scaled_unit(row, block) for block in range(blocks)]
            sums.append((row, sum(p[0] for p in pairs), sum(p[0] * p[1] for p in pairs)))
        for row, scaled, product in sums:
            mean = jnp.sum(scaled, axis=-1, keepdims=True) / chans
            means[row] = jnp.broadcast_to(mean, (width, LANES))
            along = jnp.sum(product, axis=-1, keepdims=True) / chans
            alongs[row] = jnp.broadcast_to(along, (width, LANES))

    @pl.loop(0, blocks)
    def _(block):
        clear_sides(out_ref.at[block], width)
        empty = jnp.zeros((3,) + out_ref.shape[2:], out_ref.dtype)
        out_ref[block, :3] = empty
        out_ref[block, 3 + height :] = empty

    @pl.loop(0, height)
    def _(row):
        mean, along = means[row], alongs[row]
        inv = spreads[row] * valid_ref[row]
        for block in range(blocks):
            scaled, unit = scaled_unit(row, block)
            out_ref[block, row + 3, 8 : 8 + width, :] = inv * (scaled - mean - unit * along)


def project(valid, grad, mixed, centres, spreads, gain, mine, other):
    blocks, height, width, _ = mixed.shape
    chans = blocks * LANES
    return run(
        functools.partial(project_kernel, len(mine)),
        [f32(blocks, height, width + 16, LANES)],
        (valid, grad, mixed, centres, spreads, gain, *mine, *other),
        [bf16(chans, grad.shape[1]), f32(grad.shape[0], chans)] + [f32(*centres.shape)] * 2,
        cost(VECTOR * mixed.size * 12, 8 * mixed.size),
        name="project",
    )[0]


def backward_kernel(index, bands, valid_ref, grad_ref, taps_ref, out_ref, result):
    rows_dev, width, chans = out_ref.shape
    stride = width // SUBLANES
    first = partner(lax.axis_index("rows"), index, bands) * rows_dev

    @pl.loop(0, chans // LANES)
    def _(block):
        lanes = pl.ds(pl.multiple_of(block * LANES, LANES), LANES)
        for low in range(0, rows_dev, TILE):
            outs = range(low, min(low + TILE, rows_dev))
            running = conv_rows(
                lambda row, columns_of: grad_ref[block, first + row, columns_of, :],
                list(range(rows_dev + 6)), outs, taps_ref, lanes, width, True,
            )
            for out, pieces in running.items():
                for i, value in enumerate(pieces):
                    result[out, pl.ds(i, SUBLANES, stride=stride), :] = value
        for row in range(rows_dev):
            out_ref[row, :, lanes] = (result[row] * valid_ref[first + row]).astype(out_ref.dtype)


def backward(valid, grad, taps, index, bands):
    blocks, height, width, _ = grad.shape
    rows_dev, width = (height - 6) // bands, width - 16
    shape = (rows_dev, width, blocks * LANES)
    return run(
        functools.partial(backward_kernel, index, bands),
        [bf16(*shape) if index else f32(*shape)],
        (valid, grad, taps),
        [f32(rows_dev, width, LANES)],
        cost(VECTOR * rows_dev * width * blocks * LANES * 49 * 2, 1),
        name="backward",
    )[0]


def outer_kernel(normed_ref, grad_ref, whole_ref, send_ref):
    pieces, band, hidden = whole_ref.shape
    parity, _ = parity_and_place()
    whole_ref[...] = lax.dot_general(
        normed_ref[...], grad_ref[...], (((0,), (0,)), ((), ())), preferred_element_type=jnp.float32
    ).reshape(pieces, band, hidden)
    for piece in range(pieces // 2):
        send_ref[piece] = whole_ref[2 * piece + 1 - parity].astype(send_ref.dtype)


def outer(normed, grad, count):
    chans, hidden = normed.shape[1], grad.shape[1]
    outs = [f32(count, chans // count, hidden), bf16(count // 2, chans // count, hidden)]
    return run(outer_kernel, outs, (normed, grad), name="outer")


def kept(held_ref, got_ref, level, parity, piece):
    held = held_ref[2 * piece + parity] if level == 1 else held_ref[piece]
    return held + got_ref[piece].astype(jnp.float32)


def fold_kernel(level, held_ref, got_ref, keep_ref, send_ref):
    parity, place = parity_and_place()
    bit = lax.rem(place >> level - 1, 2)
    for piece in range(keep_ref.shape[0]):
        keep_ref[piece] = kept(held_ref, got_ref, level, parity, 2 * piece + bit)
        sent = kept(held_ref, got_ref, level, parity, 2 * piece + 1 - bit)
        send_ref[piece] = sent.astype(send_ref.dtype)


def fold(held, got, level):
    pieces, band, hidden = got.shape
    outs = [f32(pieces // 2, band, hidden), bf16(pieces // 2, band, hidden)]
    return run(functools.partial(fold_kernel, level), outs, (held, got), name="fold")


def finish_kernel(count, parts, *refs):
    back_refs, weight_refs, (back_ref, weight_ref) = refs[:parts], refs[parts:-2], refs[-2:]

    def total(values):
        return sum(ref[...].astype(jnp.float32) for ref in values)

    back_ref[...] = total(back_refs).astype(back_ref.dtype)
    weight_ref[...] = total(weight_refs) / count


def finish(backs, weights, count):
    outs = [bf16(*backs[0].shape), f32(*weights[0].shape)]
    kernel = functools.partial(finish_kernel, count, len(backs))
    return run(kernel, outs, (*backs, *weights), name="finish")


def parity_and_place():
    index = lax.axis_index("section")
    return lax.rem(index, 2), index // 2


def partner(place, index, count):
    return place ^ index if count & (count - 1) == 0 else (place + index) % count


def sender(place, index, count):
    return place ^ index if count & (count - 1) == 0 else (place + count - index) % count


def swap_pairs(value):
    count = lax.axis_size("section")
    return lax.ppermute(value, "section", [(i, i ^ 1) for i in range(count)])


def send_rows(value, index):
    if index == 0:
        return value
    count = lax.axis_size("rows")
    return lax.ppermute(value, "rows", [(i, partner(i, index, count)) for i in range(count)])


def send_section(value, index):
    count = lax.axis_size("section")
    way = [(i, partner(i // 2, index, count // 2) * 2 + i % 2) for i in range(count)]
    return lax.ppermute(value, "section", way)


def gather_pairs(block):
    steps = lax.axis_size("section") // 2
    return [block] + [send_section(block, index) for index in range(1, steps)]


def scatter_section(keep, send):
    count = lax.axis_size("section")
    level, sends = 0, [send]
    while True:
        way = [(i, i ^ 1 << level) for i in range(count)]
        got = lax.ppermute(send, "section", way)
        level += 1
        if got.shape[0] % 2:
            break
        keep, send = fold(keep, got, level)
        sends.append(send)
    rest = keep.shape[0]
    if rest == 1:
        return [keep[0], got[0]], sends
    total = keep + got.astype(jnp.float32)
    place = lax.axis_index("section") >> level
    result = lax.dynamic_index_in_dim(total, place, 0, keepdims=False)
    for shift in range(1, rest):
        piece = lax.dynamic_index_in_dim(total, (place + shift) % rest, 0, keepdims=False)
        way = [(i, (i + (shift << level)) % count) for i in range(count)]
        result = result + lax.ppermute(piece.astype(jnp.bfloat16), "section", way).astype(jnp.float32)
    return [result], sends


def after(value, *others):
    return lax.optimization_barrier((value, others))[0]


def local(activations, cotangent, proj_weight, kernel_taps, ln_gain, ln_shift, heights, widths):
    rows_dev, width_dev, chans = activations.shape[1:]
    height_all = cotangent.shape[1]
    hidden_dev = cotangent.shape[3]
    bands = lax.axis_size("rows")
    count = lax.axis_size("section")
    wide, valid = prepare(heights, widths, kernel_taps, activations[0], height_all)
    gain, shift = (value.reshape(chans // LANES, LANES) for value in (ln_gain, ln_shift))
    grad = cotangent.reshape(-1, hidden_dev)

    acts = [activations[0]] + [send_rows(activations[0], i) for i in range(1, bands)]
    half = bands // 2
    mixed = forward(valid, wide, acts[:half], range(half), bands)
    mixed = forward(valid, wide, acts[half:], range(half, bands), bands, mixed)
    proj_mine = gather_pairs(proj_weight)

    normed, centres, spreads = normalise(valid, mixed, gain, shift)
    whole, send = outer(normed, grad, count)
    weights, sends = scatter_section(whole, after(send, *proj_mine))

    proj_other = [swap_pairs(after(stack, normed)) for stack in proj_mine]
    grads = after(grad, sends[min(1, len(sends) - 1)])
    grad_mixed = project(valid, grads, mixed, centres, spreads, gain, proj_mine, proj_other)
    backs = []
    for i in [*range(2, bands), 1, 0]:
        ready = sends[min(1, len(sends) - 1)] if i > 1 else sends[-1]
        backs.append(send_rows(backward(after(valid, ready), grad_mixed, wide, i, bands), i))
    back, weight_grad = finish(backs, weights, count)
    return (back[None], weight_grad)


def solution(mesh):
    in_specs = (
        P("section", "rows", None, None),
        P("section", None, None, "rows"),
        P("section", "rows"),
        P(),
        P(),
        P(),
        P("section"),
        P("section"),
    )
    out_specs = (P("section", "rows", None, None), P("section", "rows"))
    return jax.shard_map(local, mesh=mesh, in_specs=in_specs, out_specs=out_specs, check_vma=False)
```

```python
import functools

import jax
import jax.numpy as jnp
import numpy as np
from jax import lax
from jax.experimental import pallas as pl
from jax.experimental.pallas import tpu as pltpu
from jax.sharding import PartitionSpec as P

epsilon = 1e-06
LANES = 128
VECTOR = 240
SUBLANES = 8


TILE = 4


def cost(operations, moved):
    return pl.CostEstimate(flops=operations, bytes_accessed=moved, transcendentals=0)


def run(kernel, outs, args, scratch=(), estimate=None, aliases=None, name=None):
    held = list(args) + list(outs) + list(scratch)
    taken = sum(int(np.prod(value.shape)) * jnp.dtype(value.dtype).itemsize for value in held)
    vmem = pl.BlockSpec(memory_space=pltpu.VMEM)
    smem = pl.BlockSpec(memory_space=pltpu.SMEM)
    return pl.pallas_call(
        kernel,
        out_shape=tuple(outs),
        in_specs=[smem if arg.dtype == jnp.int32 else vmem for arg in args],
        out_specs=tuple(vmem for _ in outs),
        scratch_shapes=[pltpu.VMEM(value.shape, value.dtype) for value in scratch],
        input_output_aliases=aliases or {},
        compiler_params=pltpu.CompilerParams(vmem_limit_bytes=taken + taken // 8 + (4 << 20)),
        cost_estimate=estimate or cost(1, 1),
        name=name,
    )(*args)


def f32(*shape):
    return jax.ShapeDtypeStruct(shape, jnp.float32)


def bf16(*shape):
    return jax.ShapeDtypeStruct(shape, jnp.bfloat16)


def begin_kernel(out_ref):
    out_ref[...] = jnp.zeros(out_ref.shape, out_ref.dtype)


def prepare_kernel(zero_ref, high_ref, wid_ref, taps_ref, act_ref, wide_ref, valid_ref):
    count, chans = taps_ref.shape
    taps = taps_ref[...].astype(jnp.float32)
    for tap in range(count):
        wide_ref[tap] = jnp.broadcast_to(taps[tap : tap + 1], (SUBLANES, chans))
    _, width, lanes = valid_ref.shape
    columns = lax.broadcasted_iota(jnp.int32, (width, lanes), 0) < wid_ref[0]

    @pl.loop(0, valid_ref.shape[0])
    def _(row):
        valid_ref[row] = jnp.where(columns & (row < high_ref[0]), 1.0, 0.0) + zero_ref[0:1, :]


def prepare(heights, widths, taps, act, height):
    count, chans = taps.shape
    outs = [f32(count, SUBLANES, chans), f32(height, act.shape[1], LANES)]
    estimate = cost(VECTOR * 128 * taps.size, 1)
    zero = run(begin_kernel, [f32(SUBLANES, LANES)], (), estimate=estimate, name="begin")[0]
    args = (zero, heights, widths, taps, act)
    return run(prepare_kernel, outs, args, name="prepare")


def clear_sides(source, width):
    sides = jnp.zeros((source.shape[0], 8, LANES), source.dtype)
    source[:, :8, :] = sides
    source[:, 8 + width :, :] = sides


def conv_rows(load, positions, outs, wide_ref, lanes, width, flip):
    stride = width // SUBLANES
    running = {out: [None] * stride for out in outs}
    for row, position in enumerate(positions):
        users = [out for out in outs if 0 <= position - out <= 6]
        if not users:
            continue
        shifted = [load(row, pl.ds(5 + k, SUBLANES, stride=stride)) for k in range(stride + 6)]
        for out in users:
            for along in range(7):
                tap = (position - out) * 7 + along
                weight = wide_ref[48 - tap if flip else tap, :, lanes]
                for i in range(stride):
                    term = weight * shifted[i + along]
                    before = running[out][i]
                    running[out][i] = term if before is None else before + term
    return running


def forward_kernel(bands, indices, fresh, valid_ref, taps_ref, *refs):
    act_refs, (mixed, source) = refs[: len(indices)], refs[-2:]
    rows_dev, width, _ = act_refs[0].shape
    blocks, height = mixed.shape[0], mixed.shape[1] - 6
    stride = width // SUBLANES
    band = lax.axis_index("rows")
    joined = source.shape[0] // rows_dev
    clear_sides(source, width)
    once = fresh and len(indices) == joined
    firsts = [sender(band, index, bands) * rows_dev for index in indices]

    @pl.loop(0, blocks)
    def _(block):
        lanes = pl.ds(pl.multiple_of(block * LANES, LANES), LANES)
        if fresh:
            mixed[block] = jnp.zeros(mixed.shape[1:], mixed.dtype)
        for start in range(0, len(indices), joined):
            base = firsts[start]
            for first in firsts[start : start + joined]:
                base = jnp.minimum(base, first)
            for first, act_ref in zip(firsts[start:], act_refs[start : start + joined]):
                for i in range(rows_dev):
                    row = first + i
                    value = act_ref[i, :, lanes].astype(jnp.float32) * valid_ref[row]
                    source[row - base, 8 : 8 + width, :] = value
            rows = joined * rows_dev
            for low in range(0, rows + 6, TILE):
                outs = range(low, min(low + TILE, rows + 6))
                positions = [i + 6 for i in range(rows)]
                running = conv_rows(
                    lambda row, columns_of: source[row, columns_of, :],
                    positions, outs, taps_ref, lanes, width, False,
                )
                for out, pieces in running.items():
                    for i, value in enumerate(pieces):
                        columns_of = pl.ds(i, SUBLANES, stride=stride)
                        if not once:
                            value = value + mixed[block, base + out, columns_of, :]
                        mixed[block, base + out, columns_of, :] = value


def forward(valid, wide, acts, indices, bands, before=None):
    rows_dev, width, chans = acts[0].shape
    joined = 2 if bands & (bands - 1) == 0 and len(indices) % 2 == 0 else 1
    extra = () if before is None else (before,)
    return run(
        functools.partial(forward_kernel, bands, indices, before is None),
        [f32(chans // LANES, rows_dev * bands + 6, width, LANES)],
        (valid, wide, *acts, *extra),
        [f32(joined * rows_dev, width + 16, LANES)],
        cost(1, 1) if extra else cost(3 * VECTOR * len(acts) * acts[0].size * 49 * 2, 1),
        {2 + len(acts): 0} if extra else {},
        "forward",
    )[0]


def normalise_kernel(valid_ref, mixed, gain_ref, shift_ref, normed_ref, centres, spreads):
    blocks, height, width, _ = mixed.shape
    height = height - 6
    chans = blocks * LANES

    @pl.loop(0, height // TILE)
    def _(step):
        rows = [step * TILE + i for i in range(TILE)]
        sums = [sum(mixed[block, row + 3] for block in range(blocks)) for row in rows]
        for row, value in zip(rows, sums):
            centre = jnp.sum(value, axis=-1, keepdims=True) / chans
            centres[row] = jnp.broadcast_to(centre, (width, LANES))

    @pl.loop(0, height // TILE)
    def _(step):
        rows = [step * TILE + i for i in range(TILE)]
        sums = []
        for row in rows:
            centre = centres[row]
            away = [mixed[block, row + 3] - centre for block in range(blocks)]
            sums.append(sum(value * value for value in away))
        for row, value in zip(rows, sums):
            spread = jnp.sum(value, axis=-1, keepdims=True) / chans
            spreads[row] = jnp.broadcast_to(lax.rsqrt(spread + epsilon), (width, LANES))

    @pl.loop(0, height)
    def _(row):
        rows = pl.ds(pl.multiple_of(row * width, width), width)
        centre, inv = centres[row], spreads[row]
        for block in range(blocks):
            lanes = slice(block * LANES, (block + 1) * LANES)
            unit = (mixed[block, row + 3] - centre) * inv
            value = unit * gain_ref[block : block + 1, :] + shift_ref[block : block + 1, :]
            value = value * valid_ref[row]
            normed_ref[rows, lanes] = value.astype(normed_ref.dtype)


def normalise(valid, mixed, gain, shift):
    blocks, height, width, _ = mixed.shape
    height = height - 6
    outs = [bf16(height * width, blocks * LANES)] + [f32(height, width, LANES)] * 2
    return run(normalise_kernel, outs, (valid, mixed, gain, shift), name="normalise")


def project_kernel(steps, valid_ref, grad_ref, mixed, centres, spreads, gain_ref, *refs):
    mine_refs, other_refs = refs[:steps], refs[steps : 2 * steps]
    out_ref, whole, result, means, alongs = refs[2 * steps :]
    band = mine_refs[0].shape[0]
    blocks, height, width, _ = mixed.shape
    height = height - 6
    chans = blocks * LANES
    parity, place = parity_and_place()
    for refs_of, core in ((mine_refs, parity), (other_refs, 1 - parity)):
        for index, ref in enumerate(refs_of):
            step = sender(place, index, steps)
            start = pl.multiple_of((2 * step + core) * band, 16)
            whole[pl.ds(start, band), :] = ref[...]
    result[...] = lax.dot_general(
        grad_ref[...], whole[...], (((1,), (1,)), ((), ())), preferred_element_type=jnp.float32
    )

    def scaled_unit(row, block):
        rows = pl.ds(pl.multiple_of(row * width, width), width)
        lanes = slice(block * LANES, (block + 1) * LANES)
        scaled = result[rows, lanes] * gain_ref[block : block + 1, :]
        return scaled, (mixed[block, row + 3] - centres[row]) * spreads[row]

    @pl.loop(0, height // TILE)
    def _(step):
        sums = []
        for i in range(TILE):
            row = step * TILE + i
            pairs = [scaled_unit(row, block) for block in range(blocks)]
            sums.append((row, sum(p[0] for p in pairs), sum(p[0] * p[1] for p in pairs)))
        for row, scaled, product in sums:
            mean = jnp.sum(scaled, axis=-1, keepdims=True) / chans
            means[row] = jnp.broadcast_to(mean, (width, LANES))
            along = jnp.sum(product, axis=-1, keepdims=True) / chans
            alongs[row] = jnp.broadcast_to(along, (width, LANES))

    @pl.loop(0, blocks)
    def _(block):
        clear_sides(out_ref.at[block], width)
        empty = jnp.zeros((3,) + out_ref.shape[2:], out_ref.dtype)
        out_ref[block, :3] = empty
        out_ref[block, 3 + height :] = empty

    @pl.loop(0, height)
    def _(row):
        mean, along = means[row], alongs[row]
        inv = spreads[row] * valid_ref[row]
        for block in range(blocks):
            scaled, unit = scaled_unit(row, block)
            out_ref[block, row + 3, 8 : 8 + width, :] = inv * (scaled - mean - unit * along)


def project(valid, grad, mixed, centres, spreads, gain, mine, other):
    blocks, height, width, _ = mixed.shape
    chans = blocks * LANES
    return run(
        functools.partial(project_kernel, len(mine)),
        [f32(blocks, height, width + 16, LANES)],
        (valid, grad, mixed, centres, spreads, gain, *mine, *other),
        [bf16(chans, grad.shape[1]), f32(grad.shape[0], chans)] + [f32(*centres.shape)] * 2,
        cost(VECTOR * mixed.size * 12, 8 * mixed.size),
        name="project",
    )[0]


def backward_kernel(index, bands, valid_ref, grad_ref, taps_ref, out_ref, result):
    rows_dev, width, chans = out_ref.shape
    stride = width // SUBLANES
    first = partner(lax.axis_index("rows"), index, bands) * rows_dev

    @pl.loop(0, chans // LANES)
    def _(block):
        lanes = pl.ds(pl.multiple_of(block * LANES, LANES), LANES)
        for low in range(0, rows_dev, TILE):
            outs = range(low, min(low + TILE, rows_dev))
            running = conv_rows(
                lambda row, columns_of: grad_ref[block, first + row, columns_of, :],
                list(range(rows_dev + 6)), outs, taps_ref, lanes, width, True,
            )
            for out, pieces in running.items():
                for i, value in enumerate(pieces):
                    result[out, pl.ds(i, SUBLANES, stride=stride), :] = value
        for row in range(rows_dev):
            out_ref[row, :, lanes] = (result[row] * valid_ref[first + row]).astype(out_ref.dtype)


def backward(valid, grad, taps, index, bands):
    blocks, height, width, _ = grad.shape
    rows_dev, width = (height - 6) // bands, width - 16
    shape = (rows_dev, width, blocks * LANES)
    return run(
        functools.partial(backward_kernel, index, bands),
        [bf16(*shape) if index else f32(*shape)],
        (valid, grad, taps),
        [f32(rows_dev, width, LANES)],
        cost(VECTOR * rows_dev * width * blocks * LANES * 49 * 2, 1),
        name="backward",
    )[0]


def outer_kernel(normed_ref, grad_ref, whole_ref, send_ref):
    pieces, band, hidden = whole_ref.shape
    parity, _ = parity_and_place()
    whole_ref[...] = lax.dot_general(
        normed_ref[...], grad_ref[...], (((0,), (0,)), ((), ())), preferred_element_type=jnp.float32
    ).reshape(pieces, band, hidden)
    for piece in range(pieces // 2):
        send_ref[piece] = whole_ref[2 * piece + 1 - parity].astype(send_ref.dtype)


def outer(normed, grad, count):
    chans, hidden = normed.shape[1], grad.shape[1]
    outs = [f32(count, chans // count, hidden), bf16(count // 2, chans // count, hidden)]
    return run(outer_kernel, outs, (normed, grad), name="outer")


def kept(held_ref, got_ref, level, parity, piece):
    held = held_ref[2 * piece + parity] if level == 1 else held_ref[piece]
    return held + got_ref[piece].astype(jnp.float32)


def fold_kernel(level, held_ref, got_ref, keep_ref, send_ref):
    parity, place = parity_and_place()
    bit = lax.rem(place >> level - 1, 2)
    for piece in range(keep_ref.shape[0]):
        keep_ref[piece] = kept(held_ref, got_ref, level, parity, 2 * piece + bit)
        sent = kept(held_ref, got_ref, level, parity, 2 * piece + 1 - bit)
        send_ref[piece] = sent.astype(send_ref.dtype)


def fold(held, got, level):
    pieces, band, hidden = got.shape
    outs = [f32(pieces // 2, band, hidden), bf16(pieces // 2, band, hidden)]
    return run(functools.partial(fold_kernel, level), outs, (held, got), name="fold")


def finish_kernel(count, parts, *refs):
    back_refs, weight_refs, (back_ref, weight_ref) = refs[:parts], refs[parts:-2], refs[-2:]

    def total(values):
        return sum(ref[...].astype(jnp.float32) for ref in values)

    back_ref[...] = total(back_refs).astype(back_ref.dtype)
    weight_ref[...] = total(weight_refs) / count


def finish(backs, weights, count):
    outs = [bf16(*backs[0].shape), f32(*weights[0].shape)]
    kernel = functools.partial(finish_kernel, count, len(backs))
    return run(kernel, outs, (*backs, *weights), name="finish")


def parity_and_place():
    index = lax.axis_index("section")
    return lax.rem(index, 2), index // 2


def partner(place, index, count):
    return place ^ index if count & (count - 1) == 0 else (place + index) % count


def sender(place, index, count):
    return place ^ index if count & (count - 1) == 0 else (place + count - index) % count


def swap_pairs(value):
    count = lax.axis_size("section")
    return lax.ppermute(value, "section", [(i, i ^ 1) for i in range(count)])


def send_rows(value, index):
    if index == 0:
        return value
    count = lax.axis_size("rows")
    return lax.ppermute(value, "rows", [(i, partner(i, index, count)) for i in range(count)])


def send_section(value, index):
    count = lax.axis_size("section")
    way = [(i, partner(i // 2, index, count // 2) * 2 + i % 2) for i in range(count)]
    return lax.ppermute(value, "section", way)


def gather_pairs(block, first):
    steps = lax.axis_size("section") // 2
    late = after(block, first)
    sent = [send_section(block if i == steps // 2 else late, i) for i in range(1, steps)]
    return [block] + sent


def scatter_section(keep, send):
    count = lax.axis_size("section")
    level, sends = 0, [send]
    while True:
        way = [(i, i ^ 1 << level) for i in range(count)]
        got = lax.ppermute(send, "section", way)
        level += 1
        if got.shape[0] % 2:
            break
        keep, send = fold(keep, got, level)
        sends.append(send)
    rest = keep.shape[0]
    if rest == 1:
        return [keep[0], got[0]], sends
    total = keep + got.astype(jnp.float32)
    place = lax.axis_index("section") >> level
    result = lax.dynamic_index_in_dim(total, place, 0, keepdims=False)
    for shift in range(1, rest):
        piece = lax.dynamic_index_in_dim(total, (place + shift) % rest, 0, keepdims=False)
        way = [(i, (i + (shift << level)) % count) for i in range(count)]
        result = result + lax.ppermute(piece.astype(jnp.bfloat16), "section", way).astype(jnp.float32)
    return [result], sends


def after(value, *others):
    return lax.optimization_barrier((value, others))[0]


def local(activations, cotangent, proj_weight, kernel_taps, ln_gain, ln_shift, heights, widths):
    rows_dev, width_dev, chans = activations.shape[1:]
    height_all = cotangent.shape[1]
    hidden_dev = cotangent.shape[3]
    bands = lax.axis_size("rows")
    count = lax.axis_size("section")
    wide, valid = prepare(heights, widths, kernel_taps, activations[0], height_all)
    gain, shift = (value.reshape(chans // LANES, LANES) for value in (ln_gain, ln_shift))
    grad = cotangent.reshape(-1, hidden_dev)

    late = after(activations[0], valid)
    acts = [activations[0]] + [send_rows(activations[0], i) for i in range(1, bands - 1)]
    acts = acts + [send_rows(late, bands - 1)] if bands > 1 else acts
    half = bands // 2
    mixed = forward(valid, wide, acts[:half], range(half), bands)
    proj_mine = gather_pairs(proj_weight, mixed)
    valid_then = after(valid, proj_mine[count // 4])
    mixed = forward(valid_then, wide, acts[half:], range(half, bands), bands, mixed)

    normed, centres, spreads = normalise(valid, mixed, gain, shift)
    whole, send = outer(normed, grad, count)
    weights, sends = scatter_section(whole, after(send, *proj_mine))

    proj_other = [swap_pairs(after(stack, normed)) for stack in proj_mine]
    grads = after(grad, sends[min(1, len(sends) - 1)])
    grad_mixed = project(valid, grads, mixed, centres, spreads, gain, proj_mine, proj_other)
    backs = []
    for i in [*range(2, bands), 1, 0]:
        ready = sends[min(1, len(sends) - 1)] if i > 1 else sends[-1]
        backs.append(send_rows(backward(after(valid, ready), grad_mixed, wide, i, bands), i))
    back, weight_grad = finish(backs, weights, count)
    return (back[None], weight_grad)


def solution(mesh):
    in_specs = (
        P("section", "rows", None, None),
        P("section", None, None, "rows"),
        P("section", "rows"),
        P(),
        P(),
        P(),
        P("section"),
        P("section"),
    )
    out_specs = (P("section", "rows", None, None), P("section", "rows"))
    return jax.shard_map(local, mesh=mesh, in_specs=in_specs, out_specs=out_specs, check_vma=False)
```

```python
import functools

import jax
import jax.numpy as jnp
import numpy as np
from jax import lax
from jax.experimental import pallas as pl
from jax.experimental.pallas import tpu as pltpu
from jax.sharding import PartitionSpec as P

epsilon = 1e-06
LANES = 128
VECTOR = 240
SUBLANES = 8


TILE = 4


def cost(operations, moved):
    return pl.CostEstimate(flops=operations, bytes_accessed=moved, transcendentals=0)


def run(kernel, outs, args, scratch=(), estimate=None, aliases=None, name=None):
    held = list(args) + list(outs) + list(scratch)
    taken = sum(int(np.prod(value.shape)) * jnp.dtype(value.dtype).itemsize for value in held)
    vmem = pl.BlockSpec(memory_space=pltpu.VMEM)
    smem = pl.BlockSpec(memory_space=pltpu.SMEM)
    return pl.pallas_call(
        kernel,
        out_shape=tuple(outs),
        in_specs=[smem if arg.dtype == jnp.int32 else vmem for arg in args],
        out_specs=tuple(vmem for _ in outs),
        scratch_shapes=[pltpu.VMEM(value.shape, value.dtype) for value in scratch],
        input_output_aliases=aliases or {},
        compiler_params=pltpu.CompilerParams(vmem_limit_bytes=taken + taken // 8 + (4 << 20)),
        cost_estimate=estimate or cost(1, 1),
        name=name,
    )(*args)


def f32(*shape):
    return jax.ShapeDtypeStruct(shape, jnp.float32)


def bf16(*shape):
    return jax.ShapeDtypeStruct(shape, jnp.bfloat16)


def begin_kernel(out_ref):
    out_ref[...] = jnp.zeros(out_ref.shape, out_ref.dtype)


def prepare_kernel(zero_ref, high_ref, wid_ref, taps_ref, act_ref, wide_ref, valid_ref):
    count, chans = taps_ref.shape
    taps = taps_ref[...].astype(jnp.float32)
    for tap in range(count):
        wide_ref[tap] = jnp.broadcast_to(taps[tap : tap + 1], (SUBLANES, chans))
    _, width, lanes = valid_ref.shape
    columns = lax.broadcasted_iota(jnp.int32, (width, lanes), 0) < wid_ref[0]

    @pl.loop(0, valid_ref.shape[0])
    def _(row):
        valid_ref[row] = jnp.where(columns & (row < high_ref[0]), 1.0, 0.0) + zero_ref[0:1, :]


def prepare(heights, widths, taps, act, height):
    count, chans = taps.shape
    outs = [f32(count, SUBLANES, chans), f32(height, act.shape[1], LANES)]
    estimate = cost(VECTOR * 128 * taps.size, 1)
    zero = run(begin_kernel, [f32(SUBLANES, LANES)], (), estimate=estimate, name="begin")[0]
    args = (zero, heights, widths, taps, act)
    return run(prepare_kernel, outs, args, name="prepare")


def clear_sides(source, width):
    sides = jnp.zeros((source.shape[0], 8, LANES), source.dtype)
    source[:, :8, :] = sides
    source[:, 8 + width :, :] = sides


def conv_rows(load, positions, outs, wide_ref, lanes, width, flip):
    stride = width // SUBLANES
    running = {out: [None] * stride for out in outs}
    for row, position in enumerate(positions):
        users = [out for out in outs if 0 <= position - out <= 6]
        if not users:
            continue
        shifted = [load(row, pl.ds(5 + k, SUBLANES, stride=stride)) for k in range(stride + 6)]
        for out in users:
            for along in range(7):
                tap = (position - out) * 7 + along
                weight = wide_ref[48 - tap if flip else tap, :, lanes]
                for i in range(stride):
                    term = weight * shifted[i + along]
                    before = running[out][i]
                    running[out][i] = term if before is None else before + term
    return running


def forward_kernel(bands, indices, fresh, valid_ref, taps_ref, *refs):
    act_refs, (mixed, source) = refs[: len(indices)], refs[-2:]
    rows_dev, width, _ = act_refs[0].shape
    blocks, height = mixed.shape[0], mixed.shape[1] - 6
    stride = width // SUBLANES
    band = lax.axis_index("rows")
    joined = source.shape[0] // rows_dev
    clear_sides(source, width)
    once = fresh and len(indices) == joined
    firsts = [sender(band, index, bands) * rows_dev for index in indices]

    @pl.loop(0, blocks)
    def _(block):
        lanes = pl.ds(pl.multiple_of(block * LANES, LANES), LANES)
        if fresh:
            mixed[block] = jnp.zeros(mixed.shape[1:], mixed.dtype)
        for start in range(0, len(indices), joined):
            base = firsts[start]
            for first in firsts[start : start + joined]:
                base = jnp.minimum(base, first)
            for first, act_ref in zip(firsts[start:], act_refs[start : start + joined]):
                for i in range(rows_dev):
                    row = first + i
                    value = act_ref[i, :, lanes].astype(jnp.float32) * valid_ref[row]
                    source[row - base, 8 : 8 + width, :] = value
            rows = joined * rows_dev
            for low in range(0, rows + 6, TILE):
                outs = range(low, min(low + TILE, rows + 6))
                positions = [i + 6 for i in range(rows)]
                running = conv_rows(
                    lambda row, columns_of: source[row, columns_of, :],
                    positions, outs, taps_ref, lanes, width, False,
                )
                for out, pieces in running.items():
                    for i, value in enumerate(pieces):
                        columns_of = pl.ds(i, SUBLANES, stride=stride)
                        if not once:
                            value = value + mixed[block, base + out, columns_of, :]
                        mixed[block, base + out, columns_of, :] = value


def forward(valid, wide, acts, indices, bands, before=None):
    rows_dev, width, chans = acts[0].shape
    joined = 2 if bands & (bands - 1) == 0 and len(indices) % 2 == 0 else 1
    extra = () if before is None else (before,)
    return run(
        functools.partial(forward_kernel, bands, indices, before is None),
        [f32(chans // LANES, rows_dev * bands + 6, width, LANES)],
        (valid, wide, *acts, *extra),
        [f32(joined * rows_dev, width + 16, LANES)],
        cost(1, 1) if extra else cost(3 * VECTOR * len(acts) * acts[0].size * 49 * 2, 1),
        {2 + len(acts): 0} if extra else {},
        "forward",
    )[0]


def normalise_kernel(valid_ref, mixed, gain_ref, shift_ref, normed_ref, centres, spreads):
    blocks, height, width, _ = mixed.shape
    height = height - 6
    chans = blocks * LANES

    @pl.loop(0, height // TILE)
    def _(step):
        rows = [step * TILE + i for i in range(TILE)]
        sums = [sum(mixed[block, row + 3] for block in range(blocks)) for row in rows]
        for row, value in zip(rows, sums):
            centre = jnp.sum(value, axis=-1, keepdims=True) / chans
            centres[row] = jnp.broadcast_to(centre, (width, LANES))

    @pl.loop(0, height // TILE)
    def _(step):
        rows = [step * TILE + i for i in range(TILE)]
        sums = []
        for row in rows:
            centre = centres[row]
            away = [mixed[block, row + 3] - centre for block in range(blocks)]
            sums.append(sum(value * value for value in away))
        for row, value in zip(rows, sums):
            spread = jnp.sum(value, axis=-1, keepdims=True) / chans
            spreads[row] = jnp.broadcast_to(lax.rsqrt(spread + epsilon), (width, LANES))

    @pl.loop(0, height)
    def _(row):
        rows = pl.ds(pl.multiple_of(row * width, width), width)
        centre, inv = centres[row], spreads[row]
        for block in range(blocks):
            lanes = slice(block * LANES, (block + 1) * LANES)
            unit = (mixed[block, row + 3] - centre) * inv
            value = unit * gain_ref[block : block + 1, :] + shift_ref[block : block + 1, :]
            value = value * valid_ref[row]
            normed_ref[rows, lanes] = value.astype(normed_ref.dtype)


def normalise(valid, mixed, gain, shift):
    blocks, height, width, _ = mixed.shape
    height = height - 6
    outs = [bf16(height * width, blocks * LANES)] + [f32(height, width, LANES)] * 2
    return run(normalise_kernel, outs, (valid, mixed, gain, shift), name="normalise")


def project_kernel(valid_ref, grad_ref, mixed, centres, spreads, gain_ref, *refs):
    mine_ref, other_ref, out_ref, whole, result, means, alongs = refs
    steps, band, _ = mine_ref.shape
    blocks, height, width, _ = mixed.shape
    height = height - 6
    chans = blocks * LANES
    parity, place = parity_and_place()
    for ref, core in ((mine_ref, parity), (other_ref, 1 - parity)):
        for index in range(steps):
            step = sender(place, index, steps)
            start = pl.multiple_of((2 * step + core) * band, 16)
            whole[pl.ds(start, band), :] = ref[index]
    result[...] = lax.dot_general(
        grad_ref[...], whole[...], (((1,), (1,)), ((), ())), preferred_element_type=jnp.float32
    )

    def scaled_unit(row, block):
        rows = pl.ds(pl.multiple_of(row * width, width), width)
        lanes = slice(block * LANES, (block + 1) * LANES)
        scaled = result[rows, lanes] * gain_ref[block : block + 1, :]
        return scaled, (mixed[block, row + 3] - centres[row]) * spreads[row]

    @pl.loop(0, height // TILE)
    def _(step):
        sums = []
        for i in range(TILE):
            row = step * TILE + i
            pairs = [scaled_unit(row, block) for block in range(blocks)]
            sums.append((row, sum(p[0] for p in pairs), sum(p[0] * p[1] for p in pairs)))
        for row, scaled, product in sums:
            mean = jnp.sum(scaled, axis=-1, keepdims=True) / chans
            means[row] = jnp.broadcast_to(mean, (width, LANES))
            along = jnp.sum(product, axis=-1, keepdims=True) / chans
            alongs[row] = jnp.broadcast_to(along, (width, LANES))

    @pl.loop(0, blocks)
    def _(block):
        clear_sides(out_ref.at[block], width)
        empty = jnp.zeros((3,) + out_ref.shape[2:], out_ref.dtype)
        out_ref[block, :3] = empty
        out_ref[block, 3 + height :] = empty

    @pl.loop(0, height)
    def _(row):
        mean, along = means[row], alongs[row]
        inv = spreads[row] * valid_ref[row]
        for block in range(blocks):
            scaled, unit = scaled_unit(row, block)
            out_ref[block, row + 3, 8 : 8 + width, :] = inv * (scaled - mean - unit * along)


def project(valid, grad, mixed, centres, spreads, gain, mine, other):
    blocks, height, width, _ = mixed.shape
    chans = blocks * LANES
    return run(
        project_kernel,
        [f32(blocks, height, width + 16, LANES)],
        (valid, grad, mixed, centres, spreads, gain, mine, other),
        [bf16(chans, grad.shape[1]), f32(grad.shape[0], chans)] + [f32(*centres.shape)] * 2,
        cost(VECTOR * mixed.size * 12, 8 * mixed.size),
        name="project",
    )[0]


def backward_kernel(index, bands, valid_ref, grad_ref, taps_ref, out_ref, result):
    rows_dev, width, chans = out_ref.shape
    stride = width // SUBLANES
    first = partner(lax.axis_index("rows"), index, bands) * rows_dev

    @pl.loop(0, chans // LANES)
    def _(block):
        lanes = pl.ds(pl.multiple_of(block * LANES, LANES), LANES)
        for low in range(0, rows_dev, TILE):
            outs = range(low, min(low + TILE, rows_dev))
            running = conv_rows(
                lambda row, columns_of: grad_ref[block, first + row, columns_of, :],
                list(range(rows_dev + 6)), outs, taps_ref, lanes, width, True,
            )
            for out, pieces in running.items():
                for i, value in enumerate(pieces):
                    result[out, pl.ds(i, SUBLANES, stride=stride), :] = value
        for row in range(rows_dev):
            out_ref[row, :, lanes] = (result[row] * valid_ref[first + row]).astype(out_ref.dtype)


def backward(valid, grad, taps, index, bands):
    blocks, height, width, _ = grad.shape
    rows_dev, width = (height - 6) // bands, width - 16
    shape = (rows_dev, width, blocks * LANES)
    return run(
        functools.partial(backward_kernel, index, bands),
        [bf16(*shape) if index else f32(*shape)],
        (valid, grad, taps),
        [f32(rows_dev, width, LANES)],
        cost(VECTOR * rows_dev * width * blocks * LANES * 49 * 2, 1),
        name="backward",
    )[0]


def outer_kernel(normed_ref, grad_ref, whole_ref, send_ref):
    pieces, band, hidden = whole_ref.shape
    parity, _ = parity_and_place()
    whole_ref[...] = lax.dot_general(
        normed_ref[...], grad_ref[...], (((0,), (0,)), ((), ())), preferred_element_type=jnp.float32
    ).reshape(pieces, band, hidden)
    for piece in range(pieces // 2):
        send_ref[piece] = whole_ref[2 * piece + 1 - parity].astype(send_ref.dtype)


def outer(normed, grad, count):
    chans, hidden = normed.shape[1], grad.shape[1]
    outs = [f32(count, chans // count, hidden), bf16(count // 2, chans // count, hidden)]
    return run(outer_kernel, outs, (normed, grad), name="outer")


def kept(held_ref, got_ref, level, parity, piece):
    held = held_ref[2 * piece + parity] if level == 1 else held_ref[piece]
    return held + got_ref[piece].astype(jnp.float32)


def fold_kernel(level, held_ref, got_ref, keep_ref, send_ref):
    parity, place = parity_and_place()
    bit = lax.rem(place >> level - 1, 2)
    for piece in range(keep_ref.shape[0]):
        keep_ref[piece] = kept(held_ref, got_ref, level, parity, 2 * piece + bit)
        sent = kept(held_ref, got_ref, level, parity, 2 * piece + 1 - bit)
        send_ref[piece] = sent.astype(send_ref.dtype)


def fold(held, got, level):
    pieces, band, hidden = got.shape
    outs = [f32(pieces // 2, band, hidden), bf16(pieces // 2, band, hidden)]
    return run(functools.partial(fold_kernel, level), outs, (held, got), name="fold")


def finish_kernel(count, parts, *refs):
    back_refs, weight_refs, (back_ref, weight_ref) = refs[:parts], refs[parts:-2], refs[-2:]

    def total(values):
        return sum(ref[...].astype(jnp.float32) for ref in values)

    back_ref[...] = total(back_refs).astype(back_ref.dtype)
    weight_ref[...] = total(weight_refs) / count


def finish(backs, weights, count):
    outs = [bf16(*backs[0].shape), f32(*weights[0].shape)]
    kernel = functools.partial(finish_kernel, count, len(backs))
    return run(kernel, outs, (*backs, *weights), name="finish")


def parity_and_place():
    index = lax.axis_index("section")
    return lax.rem(index, 2), index // 2


def partner(place, index, count):
    return place ^ index if count & (count - 1) == 0 else (place + index) % count


def sender(place, index, count):
    return place ^ index if count & (count - 1) == 0 else (place + count - index) % count


def swap_pairs(value):
    count = lax.axis_size("section")
    return lax.ppermute(value, "section", [(i, i ^ 1) for i in range(count)])


def send_rows(value, index):
    if index == 0:
        return value
    count = lax.axis_size("rows")
    return lax.ppermute(value, "rows", [(i, partner(i, index, count)) for i in range(count)])


def send_section(value, index):
    count = lax.axis_size("section")
    way = [(i, partner(i // 2, index, count // 2) * 2 + i % 2) for i in range(count)]
    return lax.ppermute(value, "section", way)


def stack_kernel(*refs):
    for index, ref in enumerate(refs[:-1]):
        refs[-1][index] = ref[...]


def stack(pieces):
    return run(stack_kernel, [bf16(len(pieces), *pieces[0].shape)], pieces, name="stack")[0]


def send_pieces(block):
    steps = lax.axis_size("section") // 2
    if steps & (steps - 1):
        return {index: send_section(block, index) for index in range(1, steps)}
    return {1 << level: send_section(block, 1 << level) for level in range(steps.bit_length() - 1)}


def gather_pairs(block, sent, first):
    steps = lax.axis_size("section") // 2
    pieces = {0: block}
    for index in sorted(sent, reverse=True):
        if steps & (steps - 1):
            pieces[index] = sent[index]
            continue
        passed = {i ^ index: send_section(after(v, first), index) for i, v in pieces.items() if i}
        pieces = pieces | {index: sent[index]} | passed
    return [pieces[index] for index in range(steps)]


def scatter_section(keep, send):
    count = lax.axis_size("section")
    level, sends = 0, [send]
    while True:
        way = [(i, i ^ 1 << level) for i in range(count)]
        got = lax.ppermute(send, "section", way)
        level += 1
        if got.shape[0] % 2:
            break
        keep, send = fold(keep, got, level)
        sends.append(send)
    rest = keep.shape[0]
    if rest == 1:
        return [keep[0], got[0]], sends
    total = keep + got.astype(jnp.float32)
    place = lax.axis_index("section") >> level
    result = lax.dynamic_index_in_dim(total, place, 0, keepdims=False)
    for shift in range(1, rest):
        piece = lax.dynamic_index_in_dim(total, (place + shift) % rest, 0, keepdims=False)
        way = [(i, (i + (shift << level)) % count) for i in range(count)]
        result = result + lax.ppermute(piece.astype(jnp.bfloat16), "section", way).astype(jnp.float32)
    return [result], sends


def after(value, *others):
    return lax.optimization_barrier((value, others))[0]


def local(activations, cotangent, proj_weight, kernel_taps, ln_gain, ln_shift, heights, widths):
    rows_dev, width_dev, chans = activations.shape[1:]
    height_all = cotangent.shape[1]
    hidden_dev = cotangent.shape[3]
    bands = lax.axis_size("rows")
    count = lax.axis_size("section")
    wide, valid = prepare(heights, widths, kernel_taps, activations[0], height_all)
    gain, shift = (value.reshape(chans // LANES, LANES) for value in (ln_gain, ln_shift))
    grad = cotangent.reshape(-1, hidden_dev)

    acts = [activations[0]] + [send_rows(activations[0], i) for i in range(1, bands)]
    half = bands // 2
    mixed = forward(valid, wide, acts[:half], range(half), bands)
    sent = send_pieces(proj_weight)
    mixed = forward(after(valid, sent[1]), wide, acts[half:], range(half, bands), bands, mixed)
    proj_mine = stack(gather_pairs(proj_weight, sent, mixed))

    normed, centres, spreads = normalise(valid, mixed, gain, shift)
    whole, send = outer(normed, grad, count)
    weights, sends = scatter_section(whole, send)

    proj_other = swap_pairs(proj_mine)
    grads = after(grad, sends[min(1, len(sends) - 1)])
    grad_mixed = project(valid, grads, mixed, centres, spreads, gain, proj_mine, proj_other)
    backs = []
    for i in [*range(2, bands), 1, 0]:
        ready = sends[min(1, len(sends) - 1)] if i > 1 else sends[-1]
        backs.append(send_rows(backward(after(valid, ready), grad_mixed, wide, i, bands), i))
    back, weight_grad = finish(backs, weights, count)
    return (back[None], weight_grad)


def solution(mesh):
    in_specs = (
        P("section", "rows", None, None),
        P("section", None, None, "rows"),
        P("section", "rows"),
        P(),
        P(),
        P(),
        P("section"),
        P("section"),
    )
    out_specs = (P("section", "rows", None, None), P("section", "rows"))
    return jax.shard_map(local, mesh=mesh, in_specs=in_specs, out_specs=out_specs, check_vma=False)
```

```python
import functools

import jax
import jax.numpy as jnp
import numpy as np
from jax import lax
from jax.experimental import pallas as pl
from jax.experimental.pallas import tpu as pltpu
from jax.sharding import PartitionSpec as P

epsilon = 1e-06
LANES = 128
VECTOR = 240
SUBLANES = 8


TILE = 4


def cost(operations, moved):
    return pl.CostEstimate(flops=operations, bytes_accessed=moved, transcendentals=0)


def run(kernel, outs, args, scratch=(), estimate=None, aliases=None, name=None):
    held = list(args) + list(outs) + list(scratch)
    taken = sum(int(np.prod(value.shape)) * jnp.dtype(value.dtype).itemsize for value in held)
    vmem = pl.BlockSpec(memory_space=pltpu.VMEM)
    smem = pl.BlockSpec(memory_space=pltpu.SMEM)
    return pl.pallas_call(
        kernel,
        out_shape=tuple(outs),
        in_specs=[smem if arg.dtype == jnp.int32 else vmem for arg in args],
        out_specs=tuple(vmem for _ in outs),
        scratch_shapes=[pltpu.VMEM(value.shape, value.dtype) for value in scratch],
        input_output_aliases=aliases or {},
        compiler_params=pltpu.CompilerParams(vmem_limit_bytes=taken + taken // 8 + (4 << 20)),
        cost_estimate=estimate or cost(1, 1),
        name=name,
    )(*args)


def f32(*shape):
    return jax.ShapeDtypeStruct(shape, jnp.float32)


def bf16(*shape):
    return jax.ShapeDtypeStruct(shape, jnp.bfloat16)


def begin_kernel(out_ref):
    out_ref[...] = jnp.zeros(out_ref.shape, out_ref.dtype)


def prepare_kernel(zero_ref, high_ref, wid_ref, taps_ref, act_ref, wide_ref, valid_ref):
    count, chans = taps_ref.shape
    taps = taps_ref[...].astype(jnp.float32)
    for tap in range(count):
        wide_ref[tap] = jnp.broadcast_to(taps[tap : tap + 1], (SUBLANES, chans))
    _, width, lanes = valid_ref.shape
    columns = lax.broadcasted_iota(jnp.int32, (width, lanes), 0) < wid_ref[0]

    @pl.loop(0, valid_ref.shape[0])
    def _(row):
        valid_ref[row] = jnp.where(columns & (row < high_ref[0]), 1.0, 0.0) + zero_ref[0:1, :]


def prepare(heights, widths, taps, act, height):
    count, chans = taps.shape
    outs = [f32(count, SUBLANES, chans), f32(height, act.shape[1], LANES)]
    estimate = cost(VECTOR * 128 * taps.size, 1)
    zero = run(begin_kernel, [f32(SUBLANES, LANES)], (), estimate=estimate, name="begin")[0]
    args = (zero, heights, widths, taps, act)
    return run(prepare_kernel, outs, args, name="prepare")


def clear_sides(source, width):
    sides = jnp.zeros((source.shape[0], 8, LANES), source.dtype)
    source[:, :8, :] = sides
    source[:, 8 + width :, :] = sides


def conv_rows(load, positions, outs, wide_ref, lanes, width, flip):
    stride = width // SUBLANES
    running = {out: [None] * stride for out in outs}
    for row, position in enumerate(positions):
        users = [out for out in outs if 0 <= position - out <= 6]
        if not users:
            continue
        shifted = [load(row, pl.ds(5 + k, SUBLANES, stride=stride)) for k in range(stride + 6)]
        for out in users:
            for along in range(7):
                tap = (position - out) * 7 + along
                weight = wide_ref[48 - tap if flip else tap, :, lanes]
                for i in range(stride):
                    term = weight * shifted[i + along]
                    before = running[out][i]
                    running[out][i] = term if before is None else before + term
    return running


def forward_kernel(bands, indices, fresh, valid_ref, taps_ref, *refs):
    act_refs, (mixed, source) = refs[: len(indices)], refs[-2:]
    rows_dev, width, _ = act_refs[0].shape
    blocks, height = mixed.shape[0], mixed.shape[1] - 6
    stride = width // SUBLANES
    band = lax.axis_index("rows")
    joined = source.shape[0] // rows_dev
    clear_sides(source, width)
    once = fresh and len(indices) == joined
    firsts = [sender(band, index, bands) * rows_dev for index in indices]

    @pl.loop(0, blocks)
    def _(block):
        lanes = pl.ds(pl.multiple_of(block * LANES, LANES), LANES)
        if fresh:
            mixed[block] = jnp.zeros(mixed.shape[1:], mixed.dtype)
        for start in range(0, len(indices), joined):
            base = firsts[start]
            for first in firsts[start : start + joined]:
                base = jnp.minimum(base, first)
            for first, act_ref in zip(firsts[start:], act_refs[start : start + joined]):
                for i in range(rows_dev):
                    row = first + i
                    value = act_ref[i, :, lanes].astype(jnp.float32) * valid_ref[row]
                    source[row - base, 8 : 8 + width, :] = value
            rows = joined * rows_dev
            for low in range(0, rows + 6, TILE):
                outs = range(low, min(low + TILE, rows + 6))
                positions = [i + 6 for i in range(rows)]
                running = conv_rows(
                    lambda row, columns_of: source[row, columns_of, :],
                    positions, outs, taps_ref, lanes, width, False,
                )
                for out, pieces in running.items():
                    for i, value in enumerate(pieces):
                        columns_of = pl.ds(i, SUBLANES, stride=stride)
                        if not once:
                            value = value + mixed[block, base + out, columns_of, :]
                        mixed[block, base + out, columns_of, :] = value


def forward(valid, wide, acts, indices, bands, before=None):
    rows_dev, width, chans = acts[0].shape
    joined = 2 if bands & (bands - 1) == 0 and len(indices) % 2 == 0 else 1
    extra = () if before is None else (before,)
    return run(
        functools.partial(forward_kernel, bands, indices, before is None),
        [f32(chans // LANES, rows_dev * bands + 6, width, LANES)],
        (valid, wide, *acts, *extra),
        [f32(joined * rows_dev, width + 16, LANES)],
        cost(1, 1) if extra else cost(3 * VECTOR * len(acts) * acts[0].size * 49 * 2, 1),
        {2 + len(acts): 0} if extra else {},
        "forward",
    )[0]


def normalise_kernel(valid_ref, mixed, gain_ref, shift_ref, normed_ref, centres, spreads):
    blocks, height, width, _ = mixed.shape
    height = height - 6
    chans = blocks * LANES

    @pl.loop(0, height // TILE)
    def _(step):
        rows = [step * TILE + i for i in range(TILE)]
        sums = [sum(mixed[block, row + 3] for block in range(blocks)) for row in rows]
        for row, value in zip(rows, sums):
            centre = jnp.sum(value, axis=-1, keepdims=True) / chans
            centres[row] = jnp.broadcast_to(centre, (width, LANES))

    @pl.loop(0, height // TILE)
    def _(step):
        rows = [step * TILE + i for i in range(TILE)]
        sums = []
        for row in rows:
            centre = centres[row]
            away = [mixed[block, row + 3] - centre for block in range(blocks)]
            sums.append(sum(value * value for value in away))
        for row, value in zip(rows, sums):
            spread = jnp.sum(value, axis=-1, keepdims=True) / chans
            spreads[row] = jnp.broadcast_to(lax.rsqrt(spread + epsilon), (width, LANES))

    @pl.loop(0, height)
    def _(row):
        rows = pl.ds(pl.multiple_of(row * width, width), width)
        centre, inv = centres[row], spreads[row]
        for block in range(blocks):
            lanes = slice(block * LANES, (block + 1) * LANES)
            unit = (mixed[block, row + 3] - centre) * inv
            value = unit * gain_ref[block : block + 1, :] + shift_ref[block : block + 1, :]
            value = value * valid_ref[row]
            normed_ref[rows, lanes] = value.astype(normed_ref.dtype)


def normalise(valid, mixed, gain, shift):
    blocks, height, width, _ = mixed.shape
    height = height - 6
    outs = [bf16(height * width, blocks * LANES)] + [f32(height, width, LANES)] * 2
    return run(normalise_kernel, outs, (valid, mixed, gain, shift), name="normalise")


def project_kernel(valid_ref, grad_ref, mixed, centres, spreads, gain_ref, *refs):
    mine_ref, other_ref, out_ref, whole, result, means, alongs = refs
    steps, band, _ = mine_ref.shape
    blocks, height, width, _ = mixed.shape
    height = height - 6
    chans = blocks * LANES
    parity, place = parity_and_place()
    for ref, core in ((mine_ref, parity), (other_ref, 1 - parity)):
        for index in range(steps):
            step = sender(place, index, steps)
            start = pl.multiple_of((2 * step + core) * band, 16)
            whole[pl.ds(start, band), :] = ref[index]
    result[...] = lax.dot_general(
        grad_ref[...], whole[...], (((1,), (1,)), ((), ())), preferred_element_type=jnp.float32
    )

    def scaled_unit(row, block):
        rows = pl.ds(pl.multiple_of(row * width, width), width)
        lanes = slice(block * LANES, (block + 1) * LANES)
        scaled = result[rows, lanes] * gain_ref[block : block + 1, :]
        return scaled, (mixed[block, row + 3] - centres[row]) * spreads[row]

    @pl.loop(0, height // TILE)
    def _(step):
        sums = []
        for i in range(TILE):
            row = step * TILE + i
            pairs = [scaled_unit(row, block) for block in range(blocks)]
            sums.append((row, sum(p[0] for p in pairs), sum(p[0] * p[1] for p in pairs)))
        for row, scaled, product in sums:
            mean = jnp.sum(scaled, axis=-1, keepdims=True) / chans
            means[row] = jnp.broadcast_to(mean, (width, LANES))
            along = jnp.sum(product, axis=-1, keepdims=True) / chans
            alongs[row] = jnp.broadcast_to(along, (width, LANES))

    @pl.loop(0, blocks)
    def _(block):
        clear_sides(out_ref.at[block], width)
        empty = jnp.zeros((3,) + out_ref.shape[2:], out_ref.dtype)
        out_ref[block, :3] = empty
        out_ref[block, 3 + height :] = empty

    @pl.loop(0, height)
    def _(row):
        mean, along = means[row], alongs[row]
        inv = spreads[row] * valid_ref[row]
        for block in range(blocks):
            scaled, unit = scaled_unit(row, block)
            out_ref[block, row + 3, 8 : 8 + width, :] = inv * (scaled - mean - unit * along)


def project(valid, grad, mixed, centres, spreads, gain, mine, other):
    blocks, height, width, _ = mixed.shape
    chans = blocks * LANES
    return run(
        project_kernel,
        [f32(blocks, height, width + 16, LANES)],
        (valid, grad, mixed, centres, spreads, gain, mine, other),
        [bf16(chans, grad.shape[1]), f32(grad.shape[0], chans)] + [f32(*centres.shape)] * 2,
        cost(VECTOR * mixed.size * 12, 8 * mixed.size),
        name="project",
    )[0]


def backward_kernel(index, bands, valid_ref, grad_ref, taps_ref, out_ref, result):
    rows_dev, width, chans = out_ref.shape
    stride = width // SUBLANES
    first = partner(lax.axis_index("rows"), index, bands) * rows_dev

    @pl.loop(0, chans // LANES)
    def _(block):
        lanes = pl.ds(pl.multiple_of(block * LANES, LANES), LANES)
        for low in range(0, rows_dev, TILE):
            outs = range(low, min(low + TILE, rows_dev))
            running = conv_rows(
                lambda row, columns_of: grad_ref[block, first + row, columns_of, :],
                list(range(rows_dev + 6)), outs, taps_ref, lanes, width, True,
            )
            for out, pieces in running.items():
                for i, value in enumerate(pieces):
                    result[out, pl.ds(i, SUBLANES, stride=stride), :] = value
        for row in range(rows_dev):
            out_ref[row, :, lanes] = (result[row] * valid_ref[first + row]).astype(out_ref.dtype)


def backward(valid, grad, taps, index, bands):
    blocks, height, width, _ = grad.shape
    rows_dev, width = (height - 6) // bands, width - 16
    shape = (rows_dev, width, blocks * LANES)
    return run(
        functools.partial(backward_kernel, index, bands),
        [bf16(*shape) if index else f32(*shape)],
        (valid, grad, taps),
        [f32(rows_dev, width, LANES)],
        cost(VECTOR * rows_dev * width * blocks * LANES * 49 * 2, 1),
        name="backward",
    )[0]


def outer_kernel(normed_ref, grad_ref, whole_ref, send_ref):
    pieces, band, hidden = whole_ref.shape
    parity, _ = parity_and_place()
    whole_ref[...] = lax.dot_general(
        normed_ref[...], grad_ref[...], (((0,), (0,)), ((), ())), preferred_element_type=jnp.float32
    ).reshape(pieces, band, hidden)
    for piece in range(pieces // 2):
        send_ref[piece] = whole_ref[2 * piece + 1 - parity].astype(send_ref.dtype)


def outer(normed, grad, count):
    chans, hidden = normed.shape[1], grad.shape[1]
    outs = [f32(count, chans // count, hidden), bf16(count // 2, chans // count, hidden)]
    return run(outer_kernel, outs, (normed, grad), name="outer")


def kept(held_ref, got_ref, level, parity, piece):
    held = held_ref[2 * piece + parity] if level == 1 else held_ref[piece]
    return held + got_ref[piece].astype(jnp.float32)


def fold_kernel(level, held_ref, got_ref, keep_ref, send_ref):
    parity, place = parity_and_place()
    bit = lax.rem(place >> level - 1, 2)
    for piece in range(keep_ref.shape[0]):
        keep_ref[piece] = kept(held_ref, got_ref, level, parity, 2 * piece + bit)
        sent = kept(held_ref, got_ref, level, parity, 2 * piece + 1 - bit)
        send_ref[piece] = sent.astype(send_ref.dtype)


def fold(held, got, level):
    pieces, band, hidden = got.shape
    outs = [f32(pieces // 2, band, hidden), bf16(pieces // 2, band, hidden)]
    return run(functools.partial(fold_kernel, level), outs, (held, got), name="fold")


def finish_kernel(count, parts, *refs):
    back_refs, weight_refs, (back_ref, weight_ref) = refs[:parts], refs[parts:-2], refs[-2:]

    def total(values):
        return sum(ref[...].astype(jnp.float32) for ref in values)

    back_ref[...] = total(back_refs).astype(back_ref.dtype)
    weight_ref[...] = total(weight_refs) / count


def finish(backs, weights, count):
    outs = [bf16(*backs[0].shape), f32(*weights[0].shape)]
    kernel = functools.partial(finish_kernel, count, len(backs))
    return run(kernel, outs, (*backs, *weights), name="finish")


def parity_and_place():
    index = lax.axis_index("section")
    return lax.rem(index, 2), index // 2


def partner(place, index, count):
    return place ^ index if count & (count - 1) == 0 else (place + index) % count


def sender(place, index, count):
    return place ^ index if count & (count - 1) == 0 else (place + count - index) % count


def swap_pairs(value):
    count = lax.axis_size("section")
    return lax.ppermute(value, "section", [(i, i ^ 1) for i in range(count)])


def send_rows(value, index):
    if index == 0:
        return value
    count = lax.axis_size("rows")
    return lax.ppermute(value, "rows", [(i, partner(i, index, count)) for i in range(count)])


def send_section(value, index):
    count = lax.axis_size("section")
    way = [(i, partner(i // 2, index, count // 2) * 2 + i % 2) for i in range(count)]
    return lax.ppermute(value, "section", way)


def stack_kernel(*refs):
    for index, ref in enumerate(refs[:-1]):
        refs[-1][index] = ref[...]


def stack(pieces):
    return run(stack_kernel, [bf16(len(pieces), *pieces[0].shape)], pieces, name="stack")[0]


def send_pieces(block):
    steps = lax.axis_size("section") // 2
    if steps & (steps - 1):
        return {index: send_section(block, index) for index in range(1, steps)}
    return {1 << level: send_section(block, 1 << level) for level in range(steps.bit_length() - 1)}


def gather_pairs(block, sent, first):
    steps = lax.axis_size("section") // 2
    pieces = {0: block}
    for index in sorted(sent, reverse=True):
        if steps & (steps - 1):
            pieces[index] = sent[index]
            continue
        passed = {i ^ index: send_section(after(v, first), index) for i, v in pieces.items() if i}
        pieces = pieces | {index: sent[index]} | passed
    return [pieces[index] for index in range(steps)]


def scatter_section(keep, send):
    count = lax.axis_size("section")
    level, sends = 0, [send]
    while True:
        way = [(i, i ^ 1 << level) for i in range(count)]
        got = lax.ppermute(send, "section", way)
        level += 1
        if got.shape[0] % 2:
            break
        keep, send = fold(keep, got, level)
        sends.append(send)
    rest = keep.shape[0]
    if rest == 1:
        return [keep[0], got[0]], sends
    total = keep + got.astype(jnp.float32)
    place = lax.axis_index("section") >> level
    result = lax.dynamic_index_in_dim(total, place, 0, keepdims=False)
    for shift in range(1, rest):
        piece = lax.dynamic_index_in_dim(total, (place + shift) % rest, 0, keepdims=False)
        way = [(i, (i + (shift << level)) % count) for i in range(count)]
        result = result + lax.ppermute(piece.astype(jnp.bfloat16), "section", way).astype(jnp.float32)
    return [result], sends


def after(value, *others):
    return lax.optimization_barrier((value, others))[0]


def local(activations, cotangent, proj_weight, kernel_taps, ln_gain, ln_shift, heights, widths):
    rows_dev, width_dev, chans = activations.shape[1:]
    height_all = cotangent.shape[1]
    hidden_dev = cotangent.shape[3]
    bands = lax.axis_size("rows")
    count = lax.axis_size("section")
    wide, valid = prepare(heights, widths, kernel_taps, activations[0], height_all)
    gain, shift = (value.reshape(chans // LANES, LANES) for value in (ln_gain, ln_shift))
    grad = cotangent.reshape(-1, hidden_dev)

    acts = [activations[0]] + [send_rows(activations[0], i) for i in range(1, bands)]
    half = bands // 2
    mixed = forward(valid, wide, acts[:half], range(half), bands)
    sent = send_pieces(proj_weight)
    mixed = forward(valid, wide, acts[half:], range(half, bands), bands, mixed)
    proj_mine = stack(gather_pairs(proj_weight, sent, mixed))

    normed, centres, spreads = normalise(after(valid, sent[1]), mixed, gain, shift)
    whole, send = outer(normed, grad, count)
    weights, sends = scatter_section(whole, send)

    proj_other = swap_pairs(proj_mine)
    grads = after(grad, sends[min(1, len(sends) - 1)])
    grad_mixed = project(valid, grads, mixed, centres, spreads, gain, proj_mine, proj_other)
    backs = []
    for i in [*range(2, bands), 1, 0]:
        ready = sends[min(1, len(sends) - 1)] if i > 1 else sends[-1]
        backs.append(send_rows(backward(after(valid, ready), grad_mixed, wide, i, bands), i))
    back, weight_grad = finish(backs, weights, count)
    return (back[None], weight_grad)


def solution(mesh):
    in_specs = (
        P("section", "rows", None, None),
        P("section", None, None, "rows"),
        P("section", "rows"),
        P(),
        P(),
        P(),
        P("section"),
        P("section"),
    )
    out_specs = (P("section", "rows", None, None), P("section", "rows"))
    return jax.shard_map(local, mesh=mesh, in_specs=in_specs, out_specs=out_specs, check_vma=False)
```

```python
import functools

import jax
import jax.numpy as jnp
import numpy as np
from jax import lax
from jax.experimental import pallas as pl
from jax.experimental.pallas import tpu as pltpu
from jax.sharding import PartitionSpec as P

epsilon = 1e-06
LANES = 128
VECTOR = 240
SUBLANES = 8


TILE = 4


def cost(operations, moved):
    return pl.CostEstimate(flops=operations, bytes_accessed=moved, transcendentals=0)


def run(kernel, outs, args, scratch=(), estimate=None, aliases=None, name=None):
    held = list(args) + list(outs) + list(scratch)
    taken = sum(int(np.prod(value.shape)) * jnp.dtype(value.dtype).itemsize for value in held)
    vmem = pl.BlockSpec(memory_space=pltpu.VMEM)
    smem = pl.BlockSpec(memory_space=pltpu.SMEM)
    return pl.pallas_call(
        kernel,
        out_shape=tuple(outs),
        in_specs=[smem if arg.dtype == jnp.int32 else vmem for arg in args],
        out_specs=tuple(vmem for _ in outs),
        scratch_shapes=[pltpu.VMEM(value.shape, value.dtype) for value in scratch],
        input_output_aliases=aliases or {},
        compiler_params=pltpu.CompilerParams(vmem_limit_bytes=taken + taken // 8 + (4 << 20)),
        cost_estimate=estimate or cost(1, 1),
        name=name,
    )(*args)


def f32(*shape):
    return jax.ShapeDtypeStruct(shape, jnp.float32)


def bf16(*shape):
    return jax.ShapeDtypeStruct(shape, jnp.bfloat16)


def begin_kernel(out_ref):
    out_ref[...] = jnp.zeros(out_ref.shape, out_ref.dtype)


def prepare_kernel(zero_ref, high_ref, wid_ref, taps_ref, act_ref, wide_ref, valid_ref):
    count, chans = taps_ref.shape
    taps = taps_ref[...].astype(jnp.float32)
    for tap in range(count):
        wide_ref[tap] = jnp.broadcast_to(taps[tap : tap + 1], (SUBLANES, chans))
    _, width, lanes = valid_ref.shape
    columns = lax.broadcasted_iota(jnp.int32, (width, lanes), 0) < wid_ref[0]

    @pl.loop(0, valid_ref.shape[0])
    def _(row):
        valid_ref[row] = jnp.where(columns & (row < high_ref[0]), 1.0, 0.0) + zero_ref[0:1, :]


def prepare(heights, widths, taps, act, height):
    count, chans = taps.shape
    outs = [f32(count, SUBLANES, chans), f32(height, act.shape[1], LANES)]
    estimate = cost(VECTOR * 128 * taps.size, 1)
    zero = run(begin_kernel, [f32(SUBLANES, LANES)], (), estimate=estimate, name="begin")[0]
    args = (zero, heights, widths, taps, act)
    return run(prepare_kernel, outs, args, name="prepare")


def clear_sides(source, width):
    sides = jnp.zeros((source.shape[0], 8, LANES), source.dtype)
    source[:, :8, :] = sides
    source[:, 8 + width :, :] = sides


def conv_rows(load, positions, outs, wide_ref, lanes, width, flip):
    stride = width // SUBLANES
    running = {out: [None] * stride for out in outs}
    for row, position in enumerate(positions):
        users = [out for out in outs if 0 <= position - out <= 6]
        if not users:
            continue
        shifted = [load(row, pl.ds(5 + k, SUBLANES, stride=stride)) for k in range(stride + 6)]
        for out in users:
            for along in range(7):
                tap = (position - out) * 7 + along
                weight = wide_ref[48 - tap if flip else tap, :, lanes]
                for i in range(stride):
                    term = weight * shifted[i + along]
                    before = running[out][i]
                    running[out][i] = term if before is None else before + term
    return running


def forward_kernel(bands, indices, fresh, valid_ref, taps_ref, *refs):
    act_refs, (mixed, source) = refs[: len(indices)], refs[-2:]
    rows_dev, width, _ = act_refs[0].shape
    blocks, height = mixed.shape[0], mixed.shape[1] - 6
    stride = width // SUBLANES
    band = lax.axis_index("rows")
    joined = source.shape[0] // rows_dev
    clear_sides(source, width)
    once = fresh and len(indices) == joined
    firsts = [sender(band, index, bands) * rows_dev for index in indices]

    @pl.loop(0, blocks)
    def _(block):
        lanes = pl.ds(pl.multiple_of(block * LANES, LANES), LANES)
        if fresh:
            mixed[block] = jnp.zeros(mixed.shape[1:], mixed.dtype)
        for start in range(0, len(indices), joined):
            base = firsts[start]
            for first in firsts[start : start + joined]:
                base = jnp.minimum(base, first)
            for first, act_ref in zip(firsts[start:], act_refs[start : start + joined]):
                for i in range(rows_dev):
                    row = first + i
                    value = act_ref[i, :, lanes].astype(jnp.float32) * valid_ref[row]
                    source[row - base, 8 : 8 + width, :] = value
            rows = joined * rows_dev
            for low in range(0, rows + 6, TILE):
                outs = range(low, min(low + TILE, rows + 6))
                positions = [i + 6 for i in range(rows)]
                running = conv_rows(
                    lambda row, columns_of: source[row, columns_of, :],
                    positions, outs, taps_ref, lanes, width, False,
                )
                for out, pieces in running.items():
                    for i, value in enumerate(pieces):
                        columns_of = pl.ds(i, SUBLANES, stride=stride)
                        if not once:
                            value = value + mixed[block, base + out, columns_of, :]
                        mixed[block, base + out, columns_of, :] = value


def forward(valid, wide, acts, indices, bands, before=None):
    rows_dev, width, chans = acts[0].shape
    joined = 2 if bands & (bands - 1) == 0 and len(indices) % 2 == 0 else 1
    extra = () if before is None else (before,)
    return run(
        functools.partial(forward_kernel, bands, indices, before is None),
        [f32(chans // LANES, rows_dev * bands + 6, width, LANES)],
        (valid, wide, *acts, *extra),
        [f32(joined * rows_dev, width + 16, LANES)],
        cost(1, 1) if extra else cost(3 * VECTOR * len(acts) * acts[0].size * 49 * 2, 1),
        {2 + len(acts): 0} if extra else {},
        "forward",
    )[0]


def rows_at_once(height):
    return 2 * TILE if height % (2 * TILE) == 0 else TILE


def normalise_kernel(valid_ref, mixed, gain_ref, shift_ref, normed_ref, centres, spreads):
    blocks, height, width, _ = mixed.shape
    height = height - 6
    chans = blocks * LANES
    many = rows_at_once(height)

    @pl.loop(0, height // many)
    def _(step):
        rows = [step * many + i for i in range(many)]
        sums = [sum(mixed[block, row + 3] for block in range(blocks)) for row in rows]
        for row, value in zip(rows, sums):
            centre = jnp.sum(value, axis=-1, keepdims=True) / chans
            centres[row] = jnp.broadcast_to(centre, (width, LANES))

    @pl.loop(0, height // many)
    def _(step):
        rows = [step * many + i for i in range(many)]
        sums = []
        for row in rows:
            centre = centres[row]
            away = [mixed[block, row + 3] - centre for block in range(blocks)]
            sums.append(sum(value * value for value in away))
        for row, value in zip(rows, sums):
            spread = jnp.sum(value, axis=-1, keepdims=True) / chans
            spreads[row] = jnp.broadcast_to(lax.rsqrt(spread + epsilon), (width, LANES))

    @pl.loop(0, height, unroll=2)
    def _(row):
        rows = pl.ds(pl.multiple_of(row * width, width), width)
        centre, inv = centres[row], spreads[row]
        for block in range(blocks):
            lanes = slice(block * LANES, (block + 1) * LANES)
            unit = (mixed[block, row + 3] - centre) * inv
            value = unit * gain_ref[block : block + 1, :] + shift_ref[block : block + 1, :]
            value = value * valid_ref[row]
            normed_ref[rows, lanes] = value.astype(normed_ref.dtype)


def normalise(valid, mixed, gain, shift):
    blocks, height, width, _ = mixed.shape
    height = height - 6
    outs = [bf16(height * width, blocks * LANES)] + [f32(height, width, LANES)] * 2
    return run(normalise_kernel, outs, (valid, mixed, gain, shift), name="normalise")


def project_kernel(valid_ref, grad_ref, mixed, centres, spreads, gain_ref, *refs):
    mine_ref, other_ref, out_ref, whole, result, means, alongs = refs
    steps, band, _ = mine_ref.shape
    blocks, height, width, _ = mixed.shape
    height = height - 6
    chans = blocks * LANES
    parity, place = parity_and_place()
    for ref, core in ((mine_ref, parity), (other_ref, 1 - parity)):
        for index in range(steps):
            step = sender(place, index, steps)
            start = pl.multiple_of((2 * step + core) * band, 16)
            whole[pl.ds(start, band), :] = ref[index]
    result[...] = lax.dot_general(
        grad_ref[...], whole[...], (((1,), (1,)), ((), ())), preferred_element_type=jnp.float32
    )

    def scaled_unit(row, block):
        rows = pl.ds(pl.multiple_of(row * width, width), width)
        lanes = slice(block * LANES, (block + 1) * LANES)
        scaled = result[rows, lanes] * gain_ref[block : block + 1, :]
        return scaled, (mixed[block, row + 3] - centres[row]) * spreads[row]

    many = rows_at_once(height)

    @pl.loop(0, height // many)
    def _(step):
        sums = []
        for i in range(many):
            row = step * many + i
            pairs = [scaled_unit(row, block) for block in range(blocks)]
            sums.append((row, sum(p[0] for p in pairs), sum(p[0] * p[1] for p in pairs)))
        for row, scaled, product in sums:
            mean = jnp.sum(scaled, axis=-1, keepdims=True) / chans
            means[row] = jnp.broadcast_to(mean, (width, LANES))
            along = jnp.sum(product, axis=-1, keepdims=True) / chans
            alongs[row] = jnp.broadcast_to(along, (width, LANES))

    @pl.loop(0, blocks)
    def _(block):
        clear_sides(out_ref.at[block], width)
        empty = jnp.zeros((3,) + out_ref.shape[2:], out_ref.dtype)
        out_ref[block, :3] = empty
        out_ref[block, 3 + height :] = empty

    @pl.loop(0, height, unroll=2)
    def _(row):
        mean, along = means[row], alongs[row]
        inv = spreads[row] * valid_ref[row]
        for block in range(blocks):
            scaled, unit = scaled_unit(row, block)
            out_ref[block, row + 3, 8 : 8 + width, :] = inv * (scaled - mean - unit * along)


def project(valid, grad, mixed, centres, spreads, gain, mine, other):
    blocks, height, width, _ = mixed.shape
    chans = blocks * LANES
    return run(
        project_kernel,
        [f32(blocks, height, width + 16, LANES)],
        (valid, grad, mixed, centres, spreads, gain, mine, other),
        [bf16(chans, grad.shape[1]), f32(grad.shape[0], chans)] + [f32(*centres.shape)] * 2,
        cost(VECTOR * mixed.size * 12, 8 * mixed.size),
        name="project",
    )[0]


def backward_kernel(index, bands, valid_ref, grad_ref, taps_ref, out_ref, result):
    rows_dev, width, chans = out_ref.shape
    stride = width // SUBLANES
    first = partner(lax.axis_index("rows"), index, bands) * rows_dev

    @pl.loop(0, chans // LANES)
    def _(block):
        lanes = pl.ds(pl.multiple_of(block * LANES, LANES), LANES)
        for low in range(0, rows_dev, TILE):
            outs = range(low, min(low + TILE, rows_dev))
            running = conv_rows(
                lambda row, columns_of: grad_ref[block, first + row, columns_of, :],
                list(range(rows_dev + 6)), outs, taps_ref, lanes, width, True,
            )
            for out, pieces in running.items():
                for i, value in enumerate(pieces):
                    result[out, pl.ds(i, SUBLANES, stride=stride), :] = value
        for row in range(rows_dev):
            out_ref[row, :, lanes] = (result[row] * valid_ref[first + row]).astype(out_ref.dtype)


def backward(valid, grad, taps, index, bands):
    blocks, height, width, _ = grad.shape
    rows_dev, width = (height - 6) // bands, width - 16
    shape = (rows_dev, width, blocks * LANES)
    return run(
        functools.partial(backward_kernel, index, bands),
        [bf16(*shape) if index else f32(*shape)],
        (valid, grad, taps),
        [f32(rows_dev, width, LANES)],
        cost(VECTOR * rows_dev * width * blocks * LANES * 49 * 2, 1),
        name="backward",
    )[0]


def outer_kernel(normed_ref, grad_ref, whole_ref, send_ref):
    pieces, band, hidden = whole_ref.shape
    parity, _ = parity_and_place()
    whole_ref[...] = lax.dot_general(
        normed_ref[...], grad_ref[...], (((0,), (0,)), ((), ())), preferred_element_type=jnp.float32
    ).reshape(pieces, band, hidden)
    for piece in range(pieces // 2):
        send_ref[piece] = whole_ref[2 * piece + 1 - parity].astype(send_ref.dtype)


def outer(normed, grad, count):
    chans, hidden = normed.shape[1], grad.shape[1]
    outs = [f32(count, chans // count, hidden), bf16(count // 2, chans // count, hidden)]
    return run(outer_kernel, outs, (normed, grad), name="outer")


def kept(held_ref, got_ref, level, parity, piece):
    held = held_ref[2 * piece + parity] if level == 1 else held_ref[piece]
    return held + got_ref[piece].astype(jnp.float32)


def fold_kernel(level, held_ref, got_ref, keep_ref, send_ref):
    parity, place = parity_and_place()
    bit = lax.rem(place >> level - 1, 2)
    for piece in range(keep_ref.shape[0]):
        keep_ref[piece] = kept(held_ref, got_ref, level, parity, 2 * piece + bit)
        sent = kept(held_ref, got_ref, level, parity, 2 * piece + 1 - bit)
        send_ref[piece] = sent.astype(send_ref.dtype)


def fold(held, got, level):
    pieces, band, hidden = got.shape
    outs = [f32(pieces // 2, band, hidden), bf16(pieces // 2, band, hidden)]
    return run(functools.partial(fold_kernel, level), outs, (held, got), name="fold")


def finish_kernel(count, parts, *refs):
    back_refs, weight_refs, (back_ref, weight_ref) = refs[:parts], refs[parts:-2], refs[-2:]

    def total(values):
        return sum(ref[...].astype(jnp.float32) for ref in values)

    back_ref[...] = total(back_refs).astype(back_ref.dtype)
    weight_ref[...] = total(weight_refs) / count


def finish(backs, weights, count):
    outs = [bf16(*backs[0].shape), f32(*weights[0].shape)]
    kernel = functools.partial(finish_kernel, count, len(backs))
    return run(kernel, outs, (*backs, *weights), name="finish")


def parity_and_place():
    index = lax.axis_index("section")
    return lax.rem(index, 2), index // 2


def partner(place, index, count):
    return place ^ index if count & (count - 1) == 0 else (place + index) % count


def sender(place, index, count):
    return place ^ index if count & (count - 1) == 0 else (place + count - index) % count


def swap_pairs(value):
    count = lax.axis_size("section")
    return lax.ppermute(value, "section", [(i, i ^ 1) for i in range(count)])


def send_rows(value, index):
    if index == 0:
        return value
    count = lax.axis_size("rows")
    return lax.ppermute(value, "rows", [(i, partner(i, index, count)) for i in range(count)])


def send_section(value, index):
    count = lax.axis_size("section")
    way = [(i, partner(i // 2, index, count // 2) * 2 + i % 2) for i in range(count)]
    return lax.ppermute(value, "section", way)


def stack_kernel(*refs):
    for index, ref in enumerate(refs[:-1]):
        refs[-1][index] = ref[...]


def stack(pieces):
    return run(stack_kernel, [bf16(len(pieces), *pieces[0].shape)], pieces, name="stack")[0]


def send_pieces(block):
    steps = lax.axis_size("section") // 2
    if steps & (steps - 1):
        return {index: send_section(block, index) for index in range(1, steps)}
    return {1 << level: send_section(block, 1 << level) for level in range(steps.bit_length() - 1)}


def gather_pairs(block, sent, first):
    steps = lax.axis_size("section") // 2
    pieces = {0: block}
    for index in sorted(sent, reverse=True):
        if steps & (steps - 1):
            pieces[index] = sent[index]
            continue
        passed = {i ^ index: send_section(after(v, first), index) for i, v in pieces.items() if i}
        pieces = pieces | {index: sent[index]} | passed
    return [pieces[index] for index in range(steps)]


def scatter_section(keep, send):
    count = lax.axis_size("section")
    level, sends = 0, [send]
    while True:
        way = [(i, i ^ 1 << level) for i in range(count)]
        got = lax.ppermute(send, "section", way)
        level += 1
        if got.shape[0] % 2:
            break
        keep, send = fold(keep, got, level)
        sends.append(send)
    rest = keep.shape[0]
    if rest == 1:
        return [keep[0], got[0]], sends
    total = keep + got.astype(jnp.float32)
    place = lax.axis_index("section") >> level
    result = lax.dynamic_index_in_dim(total, place, 0, keepdims=False)
    for shift in range(1, rest):
        piece = lax.dynamic_index_in_dim(total, (place + shift) % rest, 0, keepdims=False)
        way = [(i, (i + (shift << level)) % count) for i in range(count)]
        result = result + lax.ppermute(piece.astype(jnp.bfloat16), "section", way).astype(jnp.float32)
    return [result], sends


def after(value, *others):
    return lax.optimization_barrier((value, others))[0]


def local(activations, cotangent, proj_weight, kernel_taps, ln_gain, ln_shift, heights, widths):
    rows_dev, width_dev, chans = activations.shape[1:]
    height_all = cotangent.shape[1]
    hidden_dev = cotangent.shape[3]
    bands = lax.axis_size("rows")
    count = lax.axis_size("section")
    wide, valid = prepare(heights, widths, kernel_taps, activations[0], height_all)
    gain, shift = (value.reshape(chans // LANES, LANES) for value in (ln_gain, ln_shift))
    grad = cotangent.reshape(-1, hidden_dev)

    acts = [activations[0]] + [send_rows(activations[0], i) for i in range(1, bands)]
    half = bands // 2
    mixed = forward(valid, wide, acts[:half], range(half), bands)
    sent = send_pieces(proj_weight)
    mixed = forward(valid, wide, acts[half:], range(half, bands), bands, mixed)
    proj_mine = stack(gather_pairs(proj_weight, sent, mixed))

    normed, centres, spreads = normalise(after(valid, sent[1]), mixed, gain, shift)
    whole, send = outer(normed, grad, count)
    weights, sends = scatter_section(whole, send)

    proj_other = swap_pairs(proj_mine)
    grads = after(grad, sends[min(1, len(sends) - 1)])
    grad_mixed = project(valid, grads, mixed, centres, spreads, gain, proj_mine, proj_other)
    backs = []
    for i in [*range(2, bands), 1, 0]:
        ready = sends[min(1, len(sends) - 1)] if i > 1 else sends[-1]
        backs.append(send_rows(backward(after(valid, ready), grad_mixed, wide, i, bands), i))
    back, weight_grad = finish(backs, weights, count)
    return (back[None], weight_grad)


def solution(mesh):
    in_specs = (
        P("section", "rows", None, None),
        P("section", None, None, "rows"),
        P("section", "rows"),
        P(),
        P(),
        P(),
        P("section"),
        P("section"),
    )
    out_specs = (P("section", "rows", None, None), P("section", "rows"))
    return jax.shard_map(local, mesh=mesh, in_specs=in_specs, out_specs=out_specs, check_vma=False)
```

```python
import functools

import jax
import jax.numpy as jnp
import numpy as np
from jax import lax
from jax.experimental import pallas as pl
from jax.experimental.pallas import tpu as pltpu
from jax.sharding import PartitionSpec as P

epsilon = 1e-06
LANES = 128
VECTOR = 240
SUBLANES = 8


TILE = 4


def cost(operations, moved):
    return pl.CostEstimate(flops=operations, bytes_accessed=moved, transcendentals=0)


def run(kernel, outs, args, scratch=(), estimate=None, aliases=None, name=None):
    held = list(args) + list(outs) + list(scratch)
    taken = sum(int(np.prod(value.shape)) * jnp.dtype(value.dtype).itemsize for value in held)
    vmem = pl.BlockSpec(memory_space=pltpu.VMEM)
    smem = pl.BlockSpec(memory_space=pltpu.SMEM)
    return pl.pallas_call(
        kernel,
        out_shape=tuple(outs),
        in_specs=[smem if arg.dtype == jnp.int32 else vmem for arg in args],
        out_specs=tuple(vmem for _ in outs),
        scratch_shapes=[pltpu.VMEM(value.shape, value.dtype) for value in scratch],
        input_output_aliases=aliases or {},
        compiler_params=pltpu.CompilerParams(vmem_limit_bytes=taken + taken // 8 + (4 << 20)),
        cost_estimate=estimate or cost(1, 1),
        name=name,
    )(*args)


def f32(*shape):
    return jax.ShapeDtypeStruct(shape, jnp.float32)


def bf16(*shape):
    return jax.ShapeDtypeStruct(shape, jnp.bfloat16)


def begin_kernel(out_ref):
    out_ref[...] = jnp.zeros(out_ref.shape, out_ref.dtype)


def prepare_kernel(zero_ref, high_ref, wid_ref, taps_ref, act_ref, wide_ref, valid_ref):
    count, chans = taps_ref.shape
    taps = taps_ref[...].astype(jnp.float32)
    for tap in range(count):
        wide_ref[tap] = jnp.broadcast_to(taps[tap : tap + 1], (SUBLANES, chans))
    _, width, lanes = valid_ref.shape
    columns = lax.broadcasted_iota(jnp.int32, (width, lanes), 0) < wid_ref[0]

    @pl.loop(0, valid_ref.shape[0])
    def _(row):
        valid_ref[row] = jnp.where(columns & (row < high_ref[0]), 1.0, 0.0) + zero_ref[0:1, :]


def prepare(heights, widths, taps, act, height):
    count, chans = taps.shape
    outs = [f32(count, SUBLANES, chans), f32(height, act.shape[1], LANES)]
    estimate = cost(VECTOR * 128 * taps.size, 1)
    zero = run(begin_kernel, [f32(SUBLANES, LANES)], (), estimate=estimate, name="begin")[0]
    args = (zero, heights, widths, taps, act)
    return run(prepare_kernel, outs, args, name="prepare")


def clear_sides(source, width):
    sides = jnp.zeros((source.shape[0], 8, LANES), source.dtype)
    source[:, :8, :] = sides
    source[:, 8 + width :, :] = sides


def conv_rows(load, positions, outs, wide_ref, lanes, width, flip):
    stride = width // SUBLANES
    running = {out: [None] * stride for out in outs}
    for row, position in enumerate(positions):
        users = [out for out in outs if 0 <= position - out <= 6]
        if not users:
            continue
        shifted = [load(row, pl.ds(5 + k, SUBLANES, stride=stride)) for k in range(stride + 6)]
        for out in users:
            for along in range(7):
                tap = (position - out) * 7 + along
                weight = wide_ref[48 - tap if flip else tap, :, lanes]
                for i in range(stride):
                    term = weight * shifted[i + along]
                    before = running[out][i]
                    running[out][i] = term if before is None else before + term
    return running


def forward_kernel(bands, indices, fresh, valid_ref, taps_ref, *refs):
    act_refs, (mixed, source) = refs[: len(indices)], refs[-2:]
    rows_dev, width, _ = act_refs[0].shape
    blocks, height = mixed.shape[0], mixed.shape[1] - 6
    stride = width // SUBLANES
    band = lax.axis_index("rows")
    joined = source.shape[0] // rows_dev
    clear_sides(source, width)
    once = fresh and len(indices) == joined
    firsts = [sender(band, index, bands) * rows_dev for index in indices]

    @pl.loop(0, blocks)
    def _(block):
        lanes = pl.ds(pl.multiple_of(block * LANES, LANES), LANES)
        if fresh:
            mixed[block] = jnp.zeros(mixed.shape[1:], mixed.dtype)
        for start in range(0, len(indices), joined):
            base = firsts[start]
            for first in firsts[start : start + joined]:
                base = jnp.minimum(base, first)
            for first, act_ref in zip(firsts[start:], act_refs[start : start + joined]):
                for i in range(rows_dev):
                    row = first + i
                    value = act_ref[i, :, lanes].astype(jnp.float32) * valid_ref[row]
                    source[row - base, 8 : 8 + width, :] = value
            rows = joined * rows_dev
            for low in range(0, rows + 6, TILE):
                outs = range(low, min(low + TILE, rows + 6))
                positions = [i + 6 for i in range(rows)]
                running = conv_rows(
                    lambda row, columns_of: source[row, columns_of, :],
                    positions, outs, taps_ref, lanes, width, False,
                )
                for out, pieces in running.items():
                    for i, value in enumerate(pieces):
                        columns_of = pl.ds(i, SUBLANES, stride=stride)
                        if not once:
                            value = value + mixed[block, base + out, columns_of, :]
                        mixed[block, base + out, columns_of, :] = value


def forward(valid, wide, acts, indices, bands, before=None):
    rows_dev, width, chans = acts[0].shape
    joined = 2 if bands & (bands - 1) == 0 and len(indices) % 2 == 0 else 1
    extra = () if before is None else (before,)
    return run(
        functools.partial(forward_kernel, bands, indices, before is None),
        [f32(chans // LANES, rows_dev * bands + 6, width, LANES)],
        (valid, wide, *acts, *extra),
        [f32(joined * rows_dev, width + 16, LANES)],
        cost(1, 1) if extra else cost(3 * VECTOR * len(acts) * acts[0].size * 49 * 2, 1),
        {2 + len(acts): 0} if extra else {},
        "forward",
    )[0]


def rows_at_once(height):
    return 2 * TILE if height % (2 * TILE) == 0 else TILE


def normalise_kernel(valid_ref, mixed, gain_ref, shift_ref, normed_ref, centres, spreads):
    blocks, height, width, _ = mixed.shape
    height = height - 6
    chans = blocks * LANES
    many = rows_at_once(height)

    @pl.loop(0, height // many)
    def _(step):
        rows = [step * many + i for i in range(many)]
        sums = [sum(mixed[block, row + 3] for block in range(blocks)) for row in rows]
        for row, value in zip(rows, sums):
            centre = jnp.sum(value, axis=-1, keepdims=True) / chans
            centres[row] = jnp.broadcast_to(centre, (width, LANES))

    @pl.loop(0, height // many)
    def _(step):
        rows = [step * many + i for i in range(many)]
        sums = []
        for row in rows:
            centre = centres[row]
            away = [mixed[block, row + 3] - centre for block in range(blocks)]
            sums.append(sum(value * value for value in away))
        for row, value in zip(rows, sums):
            spread = jnp.sum(value, axis=-1, keepdims=True) / chans
            spreads[row] = jnp.broadcast_to(lax.rsqrt(spread + epsilon), (width, LANES))

    @pl.loop(0, height, unroll=2)
    def _(row):
        rows = pl.ds(pl.multiple_of(row * width, width), width)
        centre, inv = centres[row], spreads[row]
        for block in range(blocks):
            lanes = slice(block * LANES, (block + 1) * LANES)
            unit = (mixed[block, row + 3] - centre) * inv
            value = unit * gain_ref[block : block + 1, :] + shift_ref[block : block + 1, :]
            value = value * valid_ref[row]
            normed_ref[rows, lanes] = value.astype(normed_ref.dtype)


def normalise(valid, mixed, gain, shift):
    blocks, height, width, _ = mixed.shape
    height = height - 6
    outs = [bf16(height * width, blocks * LANES)] + [f32(height, width, LANES)] * 2
    return run(normalise_kernel, outs, (valid, mixed, gain, shift), name="normalise")


def project_kernel(valid_ref, grad_ref, mixed, centres, spreads, gain_ref, *refs):
    mine_ref, other_ref, out_ref, whole, result, means, alongs = refs
    steps, band, _ = mine_ref.shape
    blocks, height, width, _ = mixed.shape
    height = height - 6
    chans = blocks * LANES
    parity, place = parity_and_place()
    for ref, core in ((mine_ref, parity), (other_ref, 1 - parity)):
        for index in range(steps):
            step = sender(place, index, steps)
            start = pl.multiple_of((2 * step + core) * band, 16)
            whole[pl.ds(start, band), :] = ref[index]
    result[...] = lax.dot_general(
        grad_ref[...], whole[...], (((1,), (1,)), ((), ())), preferred_element_type=jnp.float32
    )

    def scaled_unit(row, block):
        rows = pl.ds(pl.multiple_of(row * width, width), width)
        lanes = slice(block * LANES, (block + 1) * LANES)
        scaled = result[rows, lanes] * gain_ref[block : block + 1, :]
        return scaled, (mixed[block, row + 3] - centres[row]) * spreads[row]

    many = rows_at_once(height)

    @pl.loop(0, height // many)
    def _(step):
        sums = []
        for i in range(many):
            row = step * many + i
            pairs = [scaled_unit(row, block) for block in range(blocks)]
            sums.append((row, sum(p[0] for p in pairs), sum(p[0] * p[1] for p in pairs)))
        for row, scaled, product in sums:
            mean = jnp.sum(scaled, axis=-1, keepdims=True) / chans
            means[row] = jnp.broadcast_to(mean, (width, LANES))
            along = jnp.sum(product, axis=-1, keepdims=True) / chans
            alongs[row] = jnp.broadcast_to(along, (width, LANES))

    @pl.loop(0, blocks)
    def _(block):
        clear_sides(out_ref.at[block], width)
        empty = jnp.zeros((3,) + out_ref.shape[2:], out_ref.dtype)
        out_ref[block, :3] = empty
        out_ref[block, 3 + height :] = empty

    @pl.loop(0, height, unroll=2)
    def _(row):
        mean, along = means[row], alongs[row]
        inv = spreads[row] * valid_ref[row]
        for block in range(blocks):
            scaled, unit = scaled_unit(row, block)
            out_ref[block, row + 3, 8 : 8 + width, :] = inv * (scaled - mean - unit * along)


def project(valid, grad, mixed, centres, spreads, gain, mine, other):
    blocks, height, width, _ = mixed.shape
    chans = blocks * LANES
    return run(
        project_kernel,
        [f32(blocks, height, width + 16, LANES)],
        (valid, grad, mixed, centres, spreads, gain, mine, other),
        [bf16(chans, grad.shape[1]), f32(grad.shape[0], chans)] + [f32(*centres.shape)] * 2,
        cost(VECTOR * mixed.size * 12, 8 * mixed.size),
        name="project",
    )[0]


def backward_kernel(index, bands, valid_ref, grad_ref, taps_ref, out_ref, result):
    rows_dev, width, chans = out_ref.shape
    stride = width // SUBLANES
    first = partner(lax.axis_index("rows"), index, bands) * rows_dev

    @pl.loop(0, chans // LANES)
    def _(block):
        lanes = pl.ds(pl.multiple_of(block * LANES, LANES), LANES)
        for low in range(0, rows_dev, TILE):
            outs = range(low, min(low + TILE, rows_dev))
            running = conv_rows(
                lambda row, columns_of: grad_ref[block, first + row, columns_of, :],
                list(range(rows_dev + 6)), outs, taps_ref, lanes, width, True,
            )
            for out, pieces in running.items():
                for i, value in enumerate(pieces):
                    result[out, pl.ds(i, SUBLANES, stride=stride), :] = value
        for row in range(rows_dev):
            out_ref[row, :, lanes] = (result[row] * valid_ref[first + row]).astype(out_ref.dtype)


def backward(valid, grad, taps, index, bands):
    blocks, height, width, _ = grad.shape
    rows_dev, width = (height - 6) // bands, width - 16
    shape = (rows_dev, width, blocks * LANES)
    return run(
        functools.partial(backward_kernel, index, bands),
        [bf16(*shape) if index else f32(*shape)],
        (valid, grad, taps),
        [f32(rows_dev, width, LANES)],
        cost(VECTOR * rows_dev * width * blocks * LANES * 49 * 2, 1),
        name="backward",
    )[0]


def outer_kernel(normed_ref, grad_ref, whole_ref, send_ref):
    pieces, band, hidden = whole_ref.shape
    parity, _ = parity_and_place()
    whole_ref[...] = lax.dot_general(
        normed_ref[...], grad_ref[...], (((0,), (0,)), ((), ())), preferred_element_type=jnp.float32
    ).reshape(pieces, band, hidden)
    for piece in range(pieces // 2):
        send_ref[piece] = whole_ref[2 * piece + 1 - parity].astype(send_ref.dtype)


def outer(normed, grad, count):
    chans, hidden = normed.shape[1], grad.shape[1]
    outs = [f32(count, chans // count, hidden), bf16(count // 2, chans // count, hidden)]
    return run(outer_kernel, outs, (normed, grad), name="outer")


def kept(held_ref, got_ref, level, parity, piece):
    held = held_ref[2 * piece + parity] if level == 1 else held_ref[piece]
    return held + got_ref[piece].astype(jnp.float32)


def fold_kernel(level, held_ref, got_ref, keep_ref, send_ref):
    parity, place = parity_and_place()
    bit = lax.rem(place >> level - 1, 2)
    for piece in range(keep_ref.shape[0]):
        keep_ref[piece] = kept(held_ref, got_ref, level, parity, 2 * piece + bit)
        sent = kept(held_ref, got_ref, level, parity, 2 * piece + 1 - bit)
        send_ref[piece] = sent.astype(send_ref.dtype)


def fold(held, got, level):
    pieces, band, hidden = got.shape
    outs = [f32(pieces // 2, band, hidden), bf16(pieces // 2, band, hidden)]
    return run(functools.partial(fold_kernel, level), outs, (held, got), name="fold")


def finish_kernel(count, parts, *refs):
    back_refs, weight_refs, (back_ref, weight_ref) = refs[:parts], refs[parts:-2], refs[-2:]

    def total(values):
        return sum(ref[...].astype(jnp.float32) for ref in values)

    back_ref[...] = total(back_refs).astype(back_ref.dtype)
    weight_ref[...] = total(weight_refs) / count


def finish(backs, weights, count):
    outs = [bf16(*backs[0].shape), f32(*weights[0].shape)]
    kernel = functools.partial(finish_kernel, count, len(backs))
    return run(kernel, outs, (*backs, *weights), name="finish")


def parity_and_place():
    index = lax.axis_index("section")
    return lax.rem(index, 2), index // 2


def partner(place, index, count):
    return place ^ index if count & (count - 1) == 0 else (place + index) % count


def sender(place, index, count):
    return place ^ index if count & (count - 1) == 0 else (place + count - index) % count


def swap_pairs(value):
    count = lax.axis_size("section")
    return lax.ppermute(value, "section", [(i, i ^ 1) for i in range(count)])


def send_rows(value, index):
    if index == 0:
        return value
    count = lax.axis_size("rows")
    return lax.ppermute(value, "rows", [(i, partner(i, index, count)) for i in range(count)])


def send_section(value, index):
    count = lax.axis_size("section")
    way = [(i, partner(i // 2, index, count // 2) * 2 + i % 2) for i in range(count)]
    return lax.ppermute(value, "section", way)


def stack_kernel(*refs):
    for index, ref in enumerate(refs[:-1]):
        refs[-1][index] = ref[...]


def stack(pieces):
    return run(stack_kernel, [bf16(len(pieces), *pieces[0].shape)], pieces, name="stack")[0]


def send_pieces(block):
    steps = lax.axis_size("section") // 2
    if steps & (steps - 1):
        return {index: send_section(block, index) for index in range(1, steps)}
    return {1 << level: send_section(block, 1 << level) for level in range(steps.bit_length() - 1)}


def gather_pairs(block, sent, first):
    steps = lax.axis_size("section") // 2
    pieces = {0: block}
    for index in sorted(sent, reverse=True):
        if steps & (steps - 1):
            pieces[index] = sent[index]
            continue
        passed = {i ^ index: send_section(after(v, first), index) for i, v in pieces.items() if i}
        pieces = pieces | {index: sent[index]} | passed
    return [pieces[index] for index in range(steps)]


def scatter_section(keep, send):
    count = lax.axis_size("section")
    level, sends = 0, [send]
    while True:
        way = [(i, i ^ 1 << level) for i in range(count)]
        got = lax.ppermute(send, "section", way)
        level += 1
        if got.shape[0] % 2:
            break
        keep, send = fold(keep, got, level)
        sends.append(send)
    rest = keep.shape[0]
    if rest == 1:
        return [keep[0], got[0]], sends
    total = keep + got.astype(jnp.float32)
    place = lax.axis_index("section") >> level
    result = lax.dynamic_index_in_dim(total, place, 0, keepdims=False)
    for shift in range(1, rest):
        piece = lax.dynamic_index_in_dim(total, (place + shift) % rest, 0, keepdims=False)
        way = [(i, (i + (shift << level)) % count) for i in range(count)]
        result = result + lax.ppermute(piece.astype(jnp.bfloat16), "section", way).astype(jnp.float32)
    return [result], sends


def after(value, *others):
    return lax.optimization_barrier((value, others))[0]


def local(activations, cotangent, proj_weight, kernel_taps, ln_gain, ln_shift, heights, widths):
    rows_dev, width_dev, chans = activations.shape[1:]
    height_all = cotangent.shape[1]
    hidden_dev = cotangent.shape[3]
    bands = lax.axis_size("rows")
    count = lax.axis_size("section")
    wide, valid = prepare(heights, widths, kernel_taps, activations[0], height_all)
    gain, shift = (value.reshape(chans // LANES, LANES) for value in (ln_gain, ln_shift))
    grad = cotangent.reshape(-1, hidden_dev)

    late = after(activations[0], valid)
    acts = [send_rows(late if i == bands - 1 else activations[0], i) for i in range(bands)]
    half = bands // 2
    mixed = forward(valid, wide, acts[:half], range(half), bands)
    sent = send_pieces(proj_weight)
    proj_mine = stack(gather_pairs(proj_weight, sent, mixed))
    mixed = forward(valid, wide, acts[half:], range(half, bands), bands, mixed)

    normed, centres, spreads = normalise(after(valid, sent[1]), mixed, gain, shift)
    whole, send = outer(normed, grad, count)
    weights, sends = scatter_section(whole, send)

    proj_other = swap_pairs(proj_mine)
    grads = after(grad, sends[min(1, len(sends) - 1)])
    grad_mixed = project(valid, grads, mixed, centres, spreads, gain, proj_mine, proj_other)
    backs = []
    for i in [*range(2, bands), 1, 0]:
        ready = sends[min(1, len(sends) - 1)] if i > 1 else sends[-1]
        backs.append(send_rows(backward(after(valid, ready), grad_mixed, wide, i, bands), i))
    back, weight_grad = finish(backs, weights, count)
    return (back[None], weight_grad)


def solution(mesh):
    in_specs = (
        P("section", "rows", None, None),
        P("section", None, None, "rows"),
        P("section", "rows"),
        P(),
        P(),
        P(),
        P("section"),
        P("section"),
    )
    out_specs = (P("section", "rows", None, None), P("section", "rows"))
    return jax.shard_map(local, mesh=mesh, in_specs=in_specs, out_specs=out_specs, check_vma=False)
```

```python
import functools

import jax
import jax.numpy as jnp
import numpy as np
from jax import lax
from jax.experimental import pallas as pl
from jax.experimental.pallas import tpu as pltpu
from jax.sharding import PartitionSpec as P

epsilon = 1e-06
LANES = 128
VECTOR = 240
SUBLANES = 8


TILE = 4
WIDE_TILE = 7


def cost(operations, moved):
    return pl.CostEstimate(flops=operations, bytes_accessed=moved, transcendentals=0)


def run(kernel, outs, args, scratch=(), estimate=None, aliases=None, name=None):
    held = list(args) + list(outs) + list(scratch)
    taken = sum(int(np.prod(value.shape)) * jnp.dtype(value.dtype).itemsize for value in held)
    vmem = pl.BlockSpec(memory_space=pltpu.VMEM)
    smem = pl.BlockSpec(memory_space=pltpu.SMEM)
    return pl.pallas_call(
        kernel,
        out_shape=tuple(outs),
        in_specs=[smem if arg.dtype == jnp.int32 else vmem for arg in args],
        out_specs=tuple(vmem for _ in outs),
        scratch_shapes=[pltpu.VMEM(value.shape, value.dtype) for value in scratch],
        input_output_aliases=aliases or {},
        compiler_params=pltpu.CompilerParams(vmem_limit_bytes=taken + taken // 8 + (4 << 20)),
        cost_estimate=estimate or cost(1, 1),
        name=name,
    )(*args)


def f32(*shape):
    return jax.ShapeDtypeStruct(shape, jnp.float32)


def bf16(*shape):
    return jax.ShapeDtypeStruct(shape, jnp.bfloat16)


def begin_kernel(out_ref):
    out_ref[...] = jnp.zeros(out_ref.shape, out_ref.dtype)


def prepare_kernel(zero_ref, high_ref, wid_ref, taps_ref, act_ref, wide_ref, valid_ref):
    count, chans = taps_ref.shape
    taps = taps_ref[...].astype(jnp.float32)
    for tap in range(count):
        wide_ref[tap] = jnp.broadcast_to(taps[tap : tap + 1], (SUBLANES, chans))
    _, width, lanes = valid_ref.shape
    columns = lax.broadcasted_iota(jnp.int32, (width, lanes), 0) < wid_ref[0]

    @pl.loop(0, valid_ref.shape[0])
    def _(row):
        valid_ref[row] = jnp.where(columns & (row < high_ref[0]), 1.0, 0.0) + zero_ref[0:1, :]


def prepare(heights, widths, taps, act, height):
    count, chans = taps.shape
    outs = [f32(count, SUBLANES, chans), f32(height, act.shape[1], LANES)]
    estimate = cost(VECTOR * 128 * taps.size, 1)
    zero = run(begin_kernel, [f32(SUBLANES, LANES)], (), estimate=estimate, name="begin")[0]
    args = (zero, heights, widths, taps, act)
    return run(prepare_kernel, outs, args, name="prepare")


def clear_sides(source, width):
    sides = jnp.zeros((source.shape[0], 8, LANES), source.dtype)
    source[:, :8, :] = sides
    source[:, 8 + width :, :] = sides


def conv_rows(load, positions, outs, wide_ref, lanes, width, flip):
    stride = width // SUBLANES
    running = {out: [None] * stride for out in outs}
    for row, position in enumerate(positions):
        users = [out for out in outs if 0 <= position - out <= 6]
        if not users:
            continue
        shifted = [load(row, pl.ds(5 + k, SUBLANES, stride=stride)) for k in range(stride + 6)]
        for out in users:
            for along in range(7):
                tap = (position - out) * 7 + along
                weight = wide_ref[48 - tap if flip else tap, :, lanes]
                for i in range(stride):
                    term = weight * shifted[i + along]
                    before = running[out][i]
                    running[out][i] = term if before is None else before + term
    return running


def forward_kernel(bands, indices, fresh, valid_ref, taps_ref, *refs):
    act_refs, (mixed, source) = refs[: len(indices)], refs[-2:]
    rows_dev, width, _ = act_refs[0].shape
    blocks, height = mixed.shape[0], mixed.shape[1] - 6
    stride = width // SUBLANES
    band = lax.axis_index("rows")
    joined = source.shape[0] // rows_dev
    clear_sides(source, width)
    once = fresh and len(indices) == joined
    firsts = [sender(band, index, bands) * rows_dev for index in indices]

    @pl.loop(0, blocks)
    def _(block):
        lanes = pl.ds(pl.multiple_of(block * LANES, LANES), LANES)
        if fresh:
            mixed[block] = jnp.zeros(mixed.shape[1:], mixed.dtype)
        for start in range(0, len(indices), joined):
            base = firsts[start]
            for first in firsts[start : start + joined]:
                base = jnp.minimum(base, first)
            for first, act_ref in zip(firsts[start:], act_refs[start : start + joined]):
                for i in range(rows_dev):
                    row = first + i
                    value = act_ref[i, :, lanes].astype(jnp.float32) * valid_ref[row]
                    source[row - base, 8 : 8 + width, :] = value
            rows = joined * rows_dev
            for low in range(0, rows + 6, WIDE_TILE):
                outs = range(low, min(low + WIDE_TILE, rows + 6))
                positions = [i + 6 for i in range(rows)]
                running = conv_rows(
                    lambda row, columns_of: source[row, columns_of, :],
                    positions, outs, taps_ref, lanes, width, False,
                )
                for out, pieces in running.items():
                    for i, value in enumerate(pieces):
                        columns_of = pl.ds(i, SUBLANES, stride=stride)
                        if not once:
                            value = value + mixed[block, base + out, columns_of, :]
                        mixed[block, base + out, columns_of, :] = value


def forward(valid, wide, acts, indices, bands, before=None):
    rows_dev, width, chans = acts[0].shape
    joined = 2 if bands & (bands - 1) == 0 and len(indices) % 2 == 0 else 1
    extra = () if before is None else (before,)
    return run(
        functools.partial(forward_kernel, bands, indices, before is None),
        [f32(chans // LANES, rows_dev * bands + 6, width, LANES)],
        (valid, wide, *acts, *extra),
        [f32(joined * rows_dev, width + 16, LANES)],
        cost(1, 1) if extra else cost(3 * VECTOR * len(acts) * acts[0].size * 49 * 2, 1),
        {2 + len(acts): 0} if extra else {},
        "forward",
    )[0]


def rows_at_once(height):
    return 2 * TILE if height % (2 * TILE) == 0 else TILE


def normalise_kernel(valid_ref, mixed, gain_ref, shift_ref, normed_ref, centres, spreads):
    blocks, height, width, _ = mixed.shape
    height = height - 6
    chans = blocks * LANES
    many = rows_at_once(height)

    @pl.loop(0, height // many)
    def _(step):
        rows = [step * many + i for i in range(many)]
        sums = [sum(mixed[block, row + 3] for block in range(blocks)) for row in rows]
        for row, value in zip(rows, sums):
            centre = jnp.sum(value, axis=-1, keepdims=True) / chans
            centres[row] = jnp.broadcast_to(centre, (width, LANES))

    @pl.loop(0, height // many)
    def _(step):
        rows = [step * many + i for i in range(many)]
        sums = []
        for row in rows:
            centre = centres[row]
            away = [mixed[block, row + 3] - centre for block in range(blocks)]
            sums.append(sum(value * value for value in away))
        for row, value in zip(rows, sums):
            spread = jnp.sum(value, axis=-1, keepdims=True) / chans
            spreads[row] = jnp.broadcast_to(lax.rsqrt(spread + epsilon), (width, LANES))

    @pl.loop(0, height, unroll=2)
    def _(row):
        rows = pl.ds(pl.multiple_of(row * width, width), width)
        centre, inv = centres[row], spreads[row]
        for block in range(blocks):
            lanes = slice(block * LANES, (block + 1) * LANES)
            unit = (mixed[block, row + 3] - centre) * inv
            value = unit * gain_ref[block : block + 1, :] + shift_ref[block : block + 1, :]
            value = value * valid_ref[row]
            normed_ref[rows, lanes] = value.astype(normed_ref.dtype)


def normalise(valid, mixed, gain, shift):
    blocks, height, width, _ = mixed.shape
    height = height - 6
    outs = [bf16(height * width, blocks * LANES)] + [f32(height, width, LANES)] * 2
    return run(normalise_kernel, outs, (valid, mixed, gain, shift), name="normalise")


def project_kernel(valid_ref, grad_ref, mixed, centres, spreads, gain_ref, *refs):
    mine_ref, other_ref, out_ref, whole, result, means, alongs = refs
    steps, band, _ = mine_ref.shape
    blocks, height, width, _ = mixed.shape
    height = height - 6
    chans = blocks * LANES
    parity, place = parity_and_place()
    for ref, core in ((mine_ref, parity), (other_ref, 1 - parity)):
        for index in range(steps):
            step = sender(place, index, steps)
            start = pl.multiple_of((2 * step + core) * band, 16)
            whole[pl.ds(start, band), :] = ref[index]
    result[...] = lax.dot_general(
        grad_ref[...], whole[...], (((1,), (1,)), ((), ())), preferred_element_type=jnp.float32
    )

    def scaled_unit(row, block):
        rows = pl.ds(pl.multiple_of(row * width, width), width)
        lanes = slice(block * LANES, (block + 1) * LANES)
        scaled = result[rows, lanes] * gain_ref[block : block + 1, :]
        return scaled, (mixed[block, row + 3] - centres[row]) * spreads[row]

    many = rows_at_once(height)

    @pl.loop(0, height // many)
    def _(step):
        sums = []
        for i in range(many):
            row = step * many + i
            pairs = [scaled_unit(row, block) for block in range(blocks)]
            sums.append((row, sum(p[0] for p in pairs), sum(p[0] * p[1] for p in pairs)))
        for row, scaled, product in sums:
            mean = jnp.sum(scaled, axis=-1, keepdims=True) / chans
            means[row] = jnp.broadcast_to(mean, (width, LANES))
            along = jnp.sum(product, axis=-1, keepdims=True) / chans
            alongs[row] = jnp.broadcast_to(along, (width, LANES))

    @pl.loop(0, blocks)
    def _(block):
        clear_sides(out_ref.at[block], width)
        empty = jnp.zeros((3,) + out_ref.shape[2:], out_ref.dtype)
        out_ref[block, :3] = empty
        out_ref[block, 3 + height :] = empty

    @pl.loop(0, height, unroll=2)
    def _(row):
        mean, along = means[row], alongs[row]
        inv = spreads[row] * valid_ref[row]
        for block in range(blocks):
            scaled, unit = scaled_unit(row, block)
            out_ref[block, row + 3, 8 : 8 + width, :] = inv * (scaled - mean - unit * along)


def project(valid, grad, mixed, centres, spreads, gain, mine, other):
    blocks, height, width, _ = mixed.shape
    chans = blocks * LANES
    return run(
        project_kernel,
        [f32(blocks, height, width + 16, LANES)],
        (valid, grad, mixed, centres, spreads, gain, mine, other),
        [bf16(chans, grad.shape[1]), f32(grad.shape[0], chans)] + [f32(*centres.shape)] * 2,
        cost(VECTOR * mixed.size * 12, 8 * mixed.size),
        name="project",
    )[0]


def backward_kernel(index, bands, valid_ref, grad_ref, taps_ref, out_ref, result):
    rows_dev, width, chans = out_ref.shape
    stride = width // SUBLANES
    first = partner(lax.axis_index("rows"), index, bands) * rows_dev

    @pl.loop(0, chans // LANES)
    def _(block):
        lanes = pl.ds(pl.multiple_of(block * LANES, LANES), LANES)
        for low in range(0, rows_dev, TILE):
            outs = range(low, min(low + TILE, rows_dev))
            running = conv_rows(
                lambda row, columns_of: grad_ref[block, first + row, columns_of, :],
                list(range(rows_dev + 6)), outs, taps_ref, lanes, width, True,
            )
            for out, pieces in running.items():
                for i, value in enumerate(pieces):
                    result[out, pl.ds(i, SUBLANES, stride=stride), :] = value
        for row in range(rows_dev):
            out_ref[row, :, lanes] = (result[row] * valid_ref[first + row]).astype(out_ref.dtype)


def backward(valid, grad, taps, index, bands):
    blocks, height, width, _ = grad.shape
    rows_dev, width = (height - 6) // bands, width - 16
    shape = (rows_dev, width, blocks * LANES)
    return run(
        functools.partial(backward_kernel, index, bands),
        [bf16(*shape) if index else f32(*shape)],
        (valid, grad, taps),
        [f32(rows_dev, width, LANES)],
        cost(VECTOR * rows_dev * width * blocks * LANES * 49 * 2, 1),
        name="backward",
    )[0]


def outer_kernel(normed_ref, grad_ref, whole_ref, send_ref):
    pieces, band, hidden = whole_ref.shape
    parity, _ = parity_and_place()
    whole_ref[...] = lax.dot_general(
        normed_ref[...], grad_ref[...], (((0,), (0,)), ((), ())), preferred_element_type=jnp.float32
    ).reshape(pieces, band, hidden)
    for piece in range(pieces // 2):
        send_ref[piece] = whole_ref[2 * piece + 1 - parity].astype(send_ref.dtype)


def outer(normed, grad, count):
    chans, hidden = normed.shape[1], grad.shape[1]
    outs = [f32(count, chans // count, hidden), bf16(count // 2, chans // count, hidden)]
    return run(outer_kernel, outs, (normed, grad), name="outer")


def kept(held_ref, got_ref, level, parity, piece):
    held = held_ref[2 * piece + parity] if level == 1 else held_ref[piece]
    return held + got_ref[piece].astype(jnp.float32)


def fold_kernel(level, held_ref, got_ref, keep_ref, send_ref):
    parity, place = parity_and_place()
    bit = lax.rem(place >> level - 1, 2)
    for piece in range(keep_ref.shape[0]):
        keep_ref[piece] = kept(held_ref, got_ref, level, parity, 2 * piece + bit)
        sent = kept(held_ref, got_ref, level, parity, 2 * piece + 1 - bit)
        send_ref[piece] = sent.astype(send_ref.dtype)


def fold(held, got, level):
    pieces, band, hidden = got.shape
    outs = [f32(pieces // 2, band, hidden), bf16(pieces // 2, band, hidden)]
    return run(functools.partial(fold_kernel, level), outs, (held, got), name="fold")


def finish_kernel(count, parts, *refs):
    back_refs, weight_refs, (back_ref, weight_ref) = refs[:parts], refs[parts:-2], refs[-2:]

    def total(values):
        return sum(ref[...].astype(jnp.float32) for ref in values)

    back_ref[...] = total(back_refs).astype(back_ref.dtype)
    weight_ref[...] = total(weight_refs) / count


def finish(backs, weights, count):
    outs = [bf16(*backs[0].shape), f32(*weights[0].shape)]
    kernel = functools.partial(finish_kernel, count, len(backs))
    return run(kernel, outs, (*backs, *weights), name="finish")


def parity_and_place():
    index = lax.axis_index("section")
    return lax.rem(index, 2), index // 2


def partner(place, index, count):
    return place ^ index if count & (count - 1) == 0 else (place + index) % count


def sender(place, index, count):
    return place ^ index if count & (count - 1) == 0 else (place + count - index) % count


def swap_pairs(value):
    count = lax.axis_size("section")
    return lax.ppermute(value, "section", [(i, i ^ 1) for i in range(count)])


def send_rows(value, index):
    if index == 0:
        return value
    count = lax.axis_size("rows")
    return lax.ppermute(value, "rows", [(i, partner(i, index, count)) for i in range(count)])


def send_section(value, index):
    count = lax.axis_size("section")
    way = [(i, partner(i // 2, index, count // 2) * 2 + i % 2) for i in range(count)]
    return lax.ppermute(value, "section", way)


def stack_kernel(*refs):
    for index, ref in enumerate(refs[:-1]):
        refs[-1][index] = ref[...]


def stack(pieces):
    return run(stack_kernel, [bf16(len(pieces), *pieces[0].shape)], pieces, name="stack")[0]


def send_pieces(block):
    steps = lax.axis_size("section") // 2
    if steps & (steps - 1):
        return {index: send_section(block, index) for index in range(1, steps)}
    return {1 << level: send_section(block, 1 << level) for level in range(steps.bit_length() - 1)}


def gather_pairs(block, sent, first):
    steps = lax.axis_size("section") // 2
    pieces = {0: block}
    for index in sorted(sent, reverse=True):
        if steps & (steps - 1):
            pieces[index] = sent[index]
            continue
        passed = {i ^ index: send_section(after(v, first), index) for i, v in pieces.items() if i}
        pieces = pieces | {index: sent[index]} | passed
    return [pieces[index] for index in range(steps)]


def scatter_section(keep, send):
    count = lax.axis_size("section")
    level, sends = 0, [send]
    while True:
        way = [(i, i ^ 1 << level) for i in range(count)]
        got = lax.ppermute(send, "section", way)
        level += 1
        if got.shape[0] % 2:
            break
        keep, send = fold(keep, got, level)
        sends.append(send)
    rest = keep.shape[0]
    if rest == 1:
        return [keep[0], got[0]], sends
    total = keep + got.astype(jnp.float32)
    place = lax.axis_index("section") >> level
    result = lax.dynamic_index_in_dim(total, place, 0, keepdims=False)
    for shift in range(1, rest):
        piece = lax.dynamic_index_in_dim(total, (place + shift) % rest, 0, keepdims=False)
        way = [(i, (i + (shift << level)) % count) for i in range(count)]
        result = result + lax.ppermute(piece.astype(jnp.bfloat16), "section", way).astype(jnp.float32)
    return [result], sends


def after(value, *others):
    return lax.optimization_barrier((value, others))[0]


def local(activations, cotangent, proj_weight, kernel_taps, ln_gain, ln_shift, heights, widths):
    rows_dev, width_dev, chans = activations.shape[1:]
    height_all = cotangent.shape[1]
    hidden_dev = cotangent.shape[3]
    bands = lax.axis_size("rows")
    count = lax.axis_size("section")
    wide, valid = prepare(heights, widths, kernel_taps, activations[0], height_all)
    gain, shift = (value.reshape(chans // LANES, LANES) for value in (ln_gain, ln_shift))
    grad = cotangent.reshape(-1, hidden_dev)

    acts = [activations[0]] + [send_rows(activations[0], i) for i in range(1, bands)]
    half = bands // 2
    mixed = forward(valid, wide, acts[:half], range(half), bands)
    sent = send_pieces(proj_weight)
    mixed = forward(valid, wide, acts[half:], range(half, bands), bands, mixed)
    proj_mine = stack(gather_pairs(proj_weight, sent, mixed))

    normed, centres, spreads = normalise(after(valid, sent[1]), mixed, gain, shift)
    whole, send = outer(normed, grad, count)
    weights, sends = scatter_section(whole, send)

    proj_other = swap_pairs(proj_mine)
    grads = after(grad, sends[min(1, len(sends) - 1)])
    grad_mixed = project(valid, grads, mixed, centres, spreads, gain, proj_mine, proj_other)
    backs = []
    for i in [*range(2, bands), 1, 0]:
        ready = sends[min(1, len(sends) - 1)] if i > 1 else sends[-1]
        backs.append(send_rows(backward(after(valid, ready), grad_mixed, wide, i, bands), i))
    back, weight_grad = finish(backs, weights, count)
    return (back[None], weight_grad)


def solution(mesh):
    in_specs = (
        P("section", "rows", None, None),
        P("section", None, None, "rows"),
        P("section", "rows"),
        P(),
        P(),
        P(),
        P("section"),
        P("section"),
    )
    out_specs = (P("section", "rows", None, None), P("section", "rows"))
    return jax.shard_map(local, mesh=mesh, in_specs=in_specs, out_specs=out_specs, check_vma=False)
```

```python
import functools

import jax
import jax.numpy as jnp
import numpy as np
from jax import lax
from jax.experimental import pallas as pl
from jax.experimental.pallas import tpu as pltpu
from jax.sharding import PartitionSpec as P

epsilon = 1e-06
LANES = 128
VECTOR = 240
SUBLANES = 8


TILE = 4


def cost(operations, moved):
    return pl.CostEstimate(flops=operations, bytes_accessed=moved, transcendentals=0)


def run(kernel, outs, args, scratch=(), estimate=None, aliases=None, name=None):
    held = list(args) + list(outs) + list(scratch)
    taken = sum(int(np.prod(value.shape)) * jnp.dtype(value.dtype).itemsize for value in held)
    vmem = pl.BlockSpec(memory_space=pltpu.VMEM)
    smem = pl.BlockSpec(memory_space=pltpu.SMEM)
    return pl.pallas_call(
        kernel,
        out_shape=tuple(outs),
        in_specs=[smem if arg.dtype == jnp.int32 else vmem for arg in args],
        out_specs=tuple(vmem for _ in outs),
        scratch_shapes=[pltpu.VMEM(value.shape, value.dtype) for value in scratch],
        input_output_aliases=aliases or {},
        compiler_params=pltpu.CompilerParams(vmem_limit_bytes=taken + taken // 8 + (4 << 20)),
        cost_estimate=estimate or cost(1, 1),
        name=name,
    )(*args)


def f32(*shape):
    return jax.ShapeDtypeStruct(shape, jnp.float32)


def bf16(*shape):
    return jax.ShapeDtypeStruct(shape, jnp.bfloat16)


def begin_kernel(out_ref):
    out_ref[...] = jnp.zeros(out_ref.shape, out_ref.dtype)


def prepare_kernel(zero_ref, high_ref, wid_ref, taps_ref, act_ref, wide_ref, valid_ref):
    count, chans = taps_ref.shape
    taps = taps_ref[...].astype(jnp.float32)
    for tap in range(count):
        wide_ref[tap] = jnp.broadcast_to(taps[tap : tap + 1], (SUBLANES, chans))
    _, width, lanes = valid_ref.shape
    columns = lax.broadcasted_iota(jnp.int32, (width, lanes), 0) < wid_ref[0]

    @pl.loop(0, valid_ref.shape[0])
    def _(row):
        valid_ref[row] = jnp.where(columns & (row < high_ref[0]), 1.0, 0.0) + zero_ref[0:1, :]


def prepare(heights, widths, taps, act, height):
    count, chans = taps.shape
    outs = [f32(count, SUBLANES, chans), f32(height, act.shape[1], LANES)]
    estimate = cost(VECTOR * 128 * taps.size, 1)
    zero = run(begin_kernel, [f32(SUBLANES, LANES)], (), estimate=estimate, name="begin")[0]
    args = (zero, heights, widths, taps, act)
    return run(prepare_kernel, outs, args, name="prepare")


def clear_sides(source, width):
    sides = jnp.zeros((source.shape[0], 8, LANES), source.dtype)
    source[:, :8, :] = sides
    source[:, 8 + width :, :] = sides


def conv_rows(load, positions, outs, wide_ref, lanes, width, flip):
    stride = width // SUBLANES
    running = {out: [None] * stride for out in outs}
    for row, position in enumerate(positions):
        users = [out for out in outs if 0 <= position - out <= 6]
        if not users:
            continue
        shifted = [load(row, pl.ds(5 + k, SUBLANES, stride=stride)) for k in range(stride + 6)]
        for out in users:
            for along in range(7):
                tap = (position - out) * 7 + along
                weight = wide_ref[48 - tap if flip else tap, :, lanes]
                for i in range(stride):
                    term = weight * shifted[i + along]
                    before = running[out][i]
                    running[out][i] = term if before is None else before + term
    return running


def forward_kernel(bands, indices, fresh, valid_ref, taps_ref, *refs):
    act_refs, (mixed, source) = refs[: len(indices)], refs[-2:]
    rows_dev, width, _ = act_refs[0].shape
    blocks, height = mixed.shape[0], mixed.shape[1] - 6
    stride = width // SUBLANES
    band = lax.axis_index("rows")
    joined = source.shape[0] // rows_dev
    clear_sides(source, width)
    once = fresh and len(indices) == joined
    firsts = [sender(band, index, bands) * rows_dev for index in indices]

    @pl.loop(0, blocks)
    def _(block):
        lanes = pl.ds(pl.multiple_of(block * LANES, LANES), LANES)
        if fresh:
            mixed[block] = jnp.zeros(mixed.shape[1:], mixed.dtype)
        for start in range(0, len(indices), joined):
            base = firsts[start]
            for first in firsts[start : start + joined]:
                base = jnp.minimum(base, first)
            for first, act_ref in zip(firsts[start:], act_refs[start : start + joined]):
                for i in range(rows_dev):
                    row = first + i
                    value = act_ref[i, :, lanes].astype(jnp.float32) * valid_ref[row]
                    source[row - base, 8 : 8 + width, :] = value
            rows = joined * rows_dev
            for low in range(0, rows + 6, TILE):
                outs = range(low, min(low + TILE, rows + 6))
                positions = [i + 6 for i in range(rows)]
                running = conv_rows(
                    lambda row, columns_of: source[row, columns_of, :],
                    positions, outs, taps_ref, lanes, width, False,
                )
                for out, pieces in running.items():
                    for i, value in enumerate(pieces):
                        columns_of = pl.ds(i, SUBLANES, stride=stride)
                        if not once:
                            value = value + mixed[block, base + out, columns_of, :]
                        mixed[block, base + out, columns_of, :] = value


def forward(valid, wide, acts, indices, bands, before=None):
    rows_dev, width, chans = acts[0].shape
    joined = 2 if bands & (bands - 1) == 0 and len(indices) % 2 == 0 else 1
    extra = () if before is None else (before,)
    return run(
        functools.partial(forward_kernel, bands, indices, before is None),
        [f32(chans // LANES, rows_dev * bands + 6, width, LANES)],
        (valid, wide, *acts, *extra),
        [f32(joined * rows_dev, width + 16, LANES)],
        cost(1, 1) if extra else cost(3 * VECTOR * len(acts) * acts[0].size * 49 * 2, 1),
        {2 + len(acts): 0} if extra else {},
        "forward",
    )[0]


def rows_at_once(height):
    return 2 * TILE if height % (2 * TILE) == 0 else TILE


def normalise_kernel(valid_ref, mixed, gain_ref, shift_ref, normed_ref, centres, spreads):
    blocks, height, width, _ = mixed.shape
    height = height - 6
    chans = blocks * LANES
    many = rows_at_once(height)

    @pl.loop(0, height // many)
    def _(step):
        rows = [step * many + i for i in range(many)]
        sums = [sum(mixed[block, row + 3] for block in range(blocks)) for row in rows]
        for row, value in zip(rows, sums):
            centre = jnp.sum(value, axis=-1, keepdims=True) / chans
            centres[row] = jnp.broadcast_to(centre, (width, LANES))

    @pl.loop(0, height // many)
    def _(step):
        rows = [step * many + i for i in range(many)]
        sums = []
        for row in rows:
            centre = centres[row]
            away = [mixed[block, row + 3] - centre for block in range(blocks)]
            sums.append(sum(value * value for value in away))
        for row, value in zip(rows, sums):
            spread = jnp.sum(value, axis=-1, keepdims=True) / chans
            spreads[row] = jnp.broadcast_to(lax.rsqrt(spread + epsilon), (width, LANES))

    @pl.loop(0, height, unroll=2)
    def _(row):
        rows = pl.ds(pl.multiple_of(row * width, width), width)
        centre, inv = centres[row], spreads[row]
        for block in range(blocks):
            lanes = slice(block * LANES, (block + 1) * LANES)
            unit = (mixed[block, row + 3] - centre) * inv
            value = unit * gain_ref[block : block + 1, :] + shift_ref[block : block + 1, :]
            value = value * valid_ref[row]
            normed_ref[rows, lanes] = value.astype(normed_ref.dtype)


def normalise(valid, mixed, gain, shift):
    blocks, height, width, _ = mixed.shape
    height = height - 6
    outs = [bf16(height * width, blocks * LANES)] + [f32(height, width, LANES)] * 2
    return run(normalise_kernel, outs, (valid, mixed, gain, shift), name="normalise")


def project_kernel(valid_ref, grad_ref, mixed, centres, spreads, gain_ref, *refs):
    mine_ref, other_ref, out_ref, whole, result, means, alongs = refs
    steps, band, _ = mine_ref.shape
    blocks, height, width, _ = mixed.shape
    height = height - 6
    chans = blocks * LANES
    parity, place = parity_and_place()
    for ref, core in ((mine_ref, parity), (other_ref, 1 - parity)):
        for index in range(steps):
            step = sender(place, index, steps)
            start = pl.multiple_of((2 * step + core) * band, 16)
            whole[pl.ds(start, band), :] = ref[index]
    result[...] = lax.dot_general(
        grad_ref[...], whole[...], (((1,), (1,)), ((), ())), preferred_element_type=jnp.float32
    )

    def scaled_unit(row, block):
        rows = pl.ds(pl.multiple_of(row * width, width), width)
        lanes = slice(block * LANES, (block + 1) * LANES)
        scaled = result[rows, lanes] * gain_ref[block : block + 1, :]
        return scaled, (mixed[block, row + 3] - centres[row]) * spreads[row]

    many = rows_at_once(height)

    @pl.loop(0, height // many)
    def _(step):
        sums = []
        for i in range(many):
            row = step * many + i
            pairs = [scaled_unit(row, block) for block in range(blocks)]
            sums.append((row, sum(p[0] for p in pairs), sum(p[0] * p[1] for p in pairs)))
        for row, scaled, product in sums:
            mean = jnp.sum(scaled, axis=-1, keepdims=True) / chans
            means[row] = jnp.broadcast_to(mean, (width, LANES))
            along = jnp.sum(product, axis=-1, keepdims=True) / chans
            alongs[row] = jnp.broadcast_to(along, (width, LANES))

    @pl.loop(0, blocks)
    def _(block):
        clear_sides(out_ref.at[block], width)
        empty = jnp.zeros((3,) + out_ref.shape[2:], out_ref.dtype)
        out_ref[block, :3] = empty
        out_ref[block, 3 + height :] = empty

    @pl.loop(0, height, unroll=2)
    def _(row):
        mean, along = means[row], alongs[row]
        inv = spreads[row] * valid_ref[row]
        for block in range(blocks):
            scaled, unit = scaled_unit(row, block)
            out_ref[block, row + 3, 8 : 8 + width, :] = inv * (scaled - mean - unit * along)


def project(valid, grad, mixed, centres, spreads, gain, mine, other):
    blocks, height, width, _ = mixed.shape
    chans = blocks * LANES
    return run(
        project_kernel,
        [f32(blocks, height, width + 16, LANES)],
        (valid, grad, mixed, centres, spreads, gain, mine, other),
        [bf16(chans, grad.shape[1]), f32(grad.shape[0], chans)] + [f32(*centres.shape)] * 2,
        cost(VECTOR * mixed.size * 12, 8 * mixed.size),
        name="project",
    )[0]


def backward_kernel(index, bands, valid_ref, grad_ref, taps_ref, out_ref, result):
    rows_dev, width, chans = out_ref.shape
    stride = width // SUBLANES
    first = partner(lax.axis_index("rows"), index, bands) * rows_dev

    @pl.loop(0, chans // LANES)
    def _(block):
        lanes = pl.ds(pl.multiple_of(block * LANES, LANES), LANES)
        for low in range(0, rows_dev, TILE):
            outs = range(low, min(low + TILE, rows_dev))
            running = conv_rows(
                lambda row, columns_of: grad_ref[block, first + row, columns_of, :],
                list(range(rows_dev + 6)), outs, taps_ref, lanes, width, True,
            )
            for out, pieces in running.items():
                for i, value in enumerate(pieces):
                    result[out, pl.ds(i, SUBLANES, stride=stride), :] = value
        for row in range(rows_dev):
            out_ref[row, :, lanes] = (result[row] * valid_ref[first + row]).astype(out_ref.dtype)


def backward(valid, grad, taps, index, bands):
    blocks, height, width, _ = grad.shape
    rows_dev, width = (height - 6) // bands, width - 16
    shape = (rows_dev, width, blocks * LANES)
    return run(
        functools.partial(backward_kernel, index, bands),
        [bf16(*shape) if index else f32(*shape)],
        (valid, grad, taps),
        [f32(rows_dev, width, LANES)],
        cost(VECTOR * rows_dev * width * blocks * LANES * 49 * 2, 1),
        name="backward",
    )[0]


def outer_kernel(normed_ref, grad_ref, whole_ref, send_ref):
    pieces, band, hidden = whole_ref.shape
    parity, _ = parity_and_place()
    whole_ref[...] = lax.dot_general(
        normed_ref[...], grad_ref[...], (((0,), (0,)), ((), ())), preferred_element_type=jnp.float32
    ).reshape(pieces, band, hidden)
    for piece in range(pieces // 2):
        send_ref[piece] = whole_ref[2 * piece + 1 - parity].astype(send_ref.dtype)


def outer(normed, grad, count):
    chans, hidden = normed.shape[1], grad.shape[1]
    outs = [f32(count, chans // count, hidden), bf16(count // 2, chans // count, hidden)]
    return run(outer_kernel, outs, (normed, grad), name="outer")


def kept(held_ref, got_ref, level, parity, piece):
    held = held_ref[2 * piece + parity] if level == 1 else held_ref[piece]
    return held + got_ref[piece].astype(jnp.float32)


def fold_kernel(level, held_ref, got_ref, keep_ref, send_ref):
    parity, place = parity_and_place()
    bit = lax.rem(place >> level - 1, 2)
    for piece in range(keep_ref.shape[0]):
        keep_ref[piece] = kept(held_ref, got_ref, level, parity, 2 * piece + bit)
        sent = kept(held_ref, got_ref, level, parity, 2 * piece + 1 - bit)
        send_ref[piece] = sent.astype(send_ref.dtype)


def fold(held, got, level):
    pieces, band, hidden = got.shape
    outs = [f32(pieces // 2, band, hidden), bf16(pieces // 2, band, hidden)]
    return run(functools.partial(fold_kernel, level), outs, (held, got), name="fold")


def finish_kernel(count, parts, *refs):
    back_refs, weight_refs, (back_ref, weight_ref) = refs[:parts], refs[parts:-2], refs[-2:]

    def total(values):
        return sum(ref[...].astype(jnp.float32) for ref in values)

    back_ref[...] = total(back_refs).astype(back_ref.dtype)
    weight_ref[...] = total(weight_refs) / count


def finish(backs, weights, count):
    outs = [bf16(*backs[0].shape), f32(*weights[0].shape)]
    kernel = functools.partial(finish_kernel, count, len(backs))
    return run(kernel, outs, (*backs, *weights), name="finish")


def parity_and_place():
    index = lax.axis_index("section")
    return lax.rem(index, 2), index // 2


def partner(place, index, count):
    return place ^ index if count & (count - 1) == 0 else (place + index) % count


def sender(place, index, count):
    return place ^ index if count & (count - 1) == 0 else (place + count - index) % count


def swap_pairs(value):
    count = lax.axis_size("section")
    return lax.ppermute(value, "section", [(i, i ^ 1) for i in range(count)])


def send_rows(value, index):
    if index == 0:
        return value
    count = lax.axis_size("rows")
    return lax.ppermute(value, "rows", [(i, partner(i, index, count)) for i in range(count)])


def send_section(value, index):
    count = lax.axis_size("section")
    way = [(i, partner(i // 2, index, count // 2) * 2 + i % 2) for i in range(count)]
    return lax.ppermute(value, "section", way)


def stack_kernel(*refs):
    for index, ref in enumerate(refs[:-1]):
        refs[-1][index] = ref[...]


def stack(pieces):
    return run(stack_kernel, [bf16(len(pieces), *pieces[0].shape)], pieces, name="stack")[0]


def send_pieces(block):
    steps = lax.axis_size("section") // 2
    if steps & (steps - 1):
        return {index: send_section(block, index) for index in range(1, steps)}
    return {1 << level: send_section(block, 1 << level) for level in range(steps.bit_length() - 1)}


def gather_pairs(block, sent, first):
    steps = lax.axis_size("section") // 2
    pieces = {0: block}
    for index in sorted(sent, reverse=True):
        if steps & (steps - 1):
            pieces[index] = sent[index]
            continue
        passed = {i ^ index: send_section(after(v, first), index) for i, v in pieces.items() if i}
        pieces = pieces | {index: sent[index]} | passed
    return [pieces[index] for index in range(steps)]


def scatter_section(keep, send):
    count = lax.axis_size("section")
    level, sends = 0, [send]
    while True:
        way = [(i, i ^ 1 << level) for i in range(count)]
        got = lax.ppermute(send, "section", way)
        level += 1
        if got.shape[0] % 2:
            break
        keep, send = fold(keep, got, level)
        sends.append(send)
    rest = keep.shape[0]
    if rest == 1:
        return [keep[0], got[0]], sends
    total = keep + got.astype(jnp.float32)
    place = lax.axis_index("section") >> level
    result = lax.dynamic_index_in_dim(total, place, 0, keepdims=False)
    for shift in range(1, rest):
        piece = lax.dynamic_index_in_dim(total, (place + shift) % rest, 0, keepdims=False)
        way = [(i, (i + (shift << level)) % count) for i in range(count)]
        result = result + lax.ppermute(piece.astype(jnp.bfloat16), "section", way).astype(jnp.float32)
    return [result], sends


def after(value, *others):
    return lax.optimization_barrier((value, others))[0]


def local(activations, cotangent, proj_weight, kernel_taps, ln_gain, ln_shift, heights, widths):
    rows_dev, width_dev, chans = activations.shape[1:]
    height_all = cotangent.shape[1]
    hidden_dev = cotangent.shape[3]
    bands = lax.axis_size("rows")
    count = lax.axis_size("section")
    wide, valid = prepare(heights, widths, kernel_taps, activations[0], height_all)
    gain, shift = (value.reshape(chans // LANES, LANES) for value in (ln_gain, ln_shift))
    grad = cotangent.reshape(-1, hidden_dev)

    acts = [activations[0]] + [send_rows(activations[0], i) for i in range(1, bands)]
    half = bands // 2
    mixed = forward(valid, wide, acts[:half], range(half), bands)
    sent = send_pieces(proj_weight)
    proj_mine = stack(gather_pairs(proj_weight, sent, mixed))
    mixed = forward(valid, wide, acts[half:], range(half, bands), bands, mixed)

    normed, centres, spreads = normalise(after(valid, sent[1]), mixed, gain, shift)
    whole, send = outer(normed, grad, count)
    weights, sends = scatter_section(whole, send)

    proj_other = swap_pairs(proj_mine)
    grads = after(grad, sends[min(1, len(sends) - 1)])
    grad_mixed = project(valid, grads, mixed, centres, spreads, gain, proj_mine, proj_other)
    backs = []
    for i in [*range(2, bands), 1, 0]:
        ready = sends[min(1, len(sends) - 1)] if i > 1 else sends[-1]
        backs.append(send_rows(backward(after(valid, ready), grad_mixed, wide, i, bands), i))
    back, weight_grad = finish(backs, weights, count)
    return (back[None], weight_grad)


def solution(mesh):
    in_specs = (
        P("section", "rows", None, None),
        P("section", None, None, "rows"),
        P("section", "rows"),
        P(),
        P(),
        P(),
        P("section"),
        P("section"),
    )
    out_specs = (P("section", "rows", None, None), P("section", "rows"))
    return jax.shard_map(local, mesh=mesh, in_specs=in_specs, out_specs=out_specs, check_vma=False)
```

```python
import functools

import jax
import jax.numpy as jnp
import numpy as np
from jax import lax
from jax.experimental import pallas as pl
from jax.experimental.pallas import tpu as pltpu
from jax.sharding import PartitionSpec as P

epsilon = 1e-06
LANES = 128
VECTOR = 240
SUBLANES = 8


TILE = 4


def cost(operations, moved):
    return pl.CostEstimate(flops=operations, bytes_accessed=moved, transcendentals=0)


def run(kernel, outs, args, scratch=(), estimate=None, aliases=None, name=None):
    held = list(args) + list(outs) + list(scratch)
    taken = sum(int(np.prod(value.shape)) * jnp.dtype(value.dtype).itemsize for value in held)
    vmem = pl.BlockSpec(memory_space=pltpu.VMEM)
    smem = pl.BlockSpec(memory_space=pltpu.SMEM)
    return pl.pallas_call(
        kernel,
        out_shape=tuple(outs),
        in_specs=[smem if arg.dtype == jnp.int32 else vmem for arg in args],
        out_specs=tuple(vmem for _ in outs),
        scratch_shapes=[pltpu.VMEM(value.shape, value.dtype) for value in scratch],
        input_output_aliases=aliases or {},
        compiler_params=pltpu.CompilerParams(vmem_limit_bytes=taken + taken // 8 + (4 << 20)),
        cost_estimate=estimate or cost(1, 1),
        name=name,
    )(*args)


def f32(*shape):
    return jax.ShapeDtypeStruct(shape, jnp.float32)


def bf16(*shape):
    return jax.ShapeDtypeStruct(shape, jnp.bfloat16)


def begin_kernel(out_ref):
    out_ref[...] = jnp.zeros(out_ref.shape, out_ref.dtype)


def prepare_kernel(zero_ref, high_ref, wid_ref, taps_ref, act_ref, wide_ref, valid_ref):
    count, chans = taps_ref.shape
    taps = taps_ref[...].astype(jnp.float32)
    for tap in range(count):
        wide_ref[tap] = jnp.broadcast_to(taps[tap : tap + 1], (SUBLANES, chans))
    _, width, lanes = valid_ref.shape
    columns = lax.broadcasted_iota(jnp.int32, (width, lanes), 0) < wid_ref[0]

    @pl.loop(0, valid_ref.shape[0])
    def _(row):
        valid_ref[row] = jnp.where(columns & (row < high_ref[0]), 1.0, 0.0) + zero_ref[0:1, :]


def prepare(heights, widths, taps, act, height):
    count, chans = taps.shape
    outs = [f32(count, SUBLANES, chans), f32(height, act.shape[1], LANES)]
    estimate = cost(VECTOR * 128 * taps.size, 1)
    zero = run(begin_kernel, [f32(SUBLANES, LANES)], (), estimate=estimate, name="begin")[0]
    args = (zero, heights, widths, taps, act)
    return run(prepare_kernel, outs, args, name="prepare")


def clear_sides(source, width):
    sides = jnp.zeros((source.shape[0], 8, LANES), source.dtype)
    source[:, :8, :] = sides
    source[:, 8 + width :, :] = sides


def conv_rows(load, positions, outs, wide_ref, lanes, width, flip):
    stride = width // SUBLANES
    running = {out: [None] * stride for out in outs}
    for row, position in enumerate(positions):
        users = [out for out in outs if 0 <= position - out <= 6]
        if not users:
            continue
        shifted = [load(row, pl.ds(5 + k, SUBLANES, stride=stride)) for k in range(stride + 6)]
        for out in users:
            for along in range(7):
                tap = (position - out) * 7 + along
                weight = wide_ref[48 - tap if flip else tap, :, lanes]
                for i in range(stride):
                    term = weight * shifted[i + along]
                    before = running[out][i]
                    running[out][i] = term if before is None else before + term
    return running


def forward_kernel(bands, indices, fresh, valid_ref, taps_ref, *refs):
    act_refs, (mixed, source) = refs[: len(indices)], refs[-2:]
    rows_dev, width, _ = act_refs[0].shape
    blocks, height = mixed.shape[0], mixed.shape[1] - 6
    stride = width // SUBLANES
    band = lax.axis_index("rows")
    joined = source.shape[0] // rows_dev
    clear_sides(source, width)
    once = fresh and len(indices) == joined
    firsts = [sender(band, index, bands) * rows_dev for index in indices]

    @pl.loop(0, blocks)
    def _(block):
        lanes = pl.ds(pl.multiple_of(block * LANES, LANES), LANES)
        if fresh:
            mixed[block] = jnp.zeros(mixed.shape[1:], mixed.dtype)
        for start in range(0, len(indices), joined):
            base = firsts[start]
            for first in firsts[start : start + joined]:
                base = jnp.minimum(base, first)
            for first, act_ref in zip(firsts[start:], act_refs[start : start + joined]):
                for i in range(rows_dev):
                    row = first + i
                    value = act_ref[i, :, lanes].astype(jnp.float32) * valid_ref[row]
                    source[row - base, 8 : 8 + width, :] = value
            rows = joined * rows_dev
            for low in range(0, rows + 6, TILE):
                outs = range(low, min(low + TILE, rows + 6))
                positions = [i + 6 for i in range(rows)]
                running = conv_rows(
                    lambda row, columns_of: source[row, columns_of, :],
                    positions, outs, taps_ref, lanes, width, False,
                )
                for out, pieces in running.items():
                    for i, value in enumerate(pieces):
                        columns_of = pl.ds(i, SUBLANES, stride=stride)
                        if not once:
                            value = value + mixed[block, base + out, columns_of, :]
                        mixed[block, base + out, columns_of, :] = value


def forward(valid, wide, acts, indices, bands, before=None):
    rows_dev, width, chans = acts[0].shape
    joined = 2 if bands & (bands - 1) == 0 and len(indices) % 2 == 0 else 1
    extra = () if before is None else (before,)
    return run(
        functools.partial(forward_kernel, bands, indices, before is None),
        [f32(chans // LANES, rows_dev * bands + 6, width, LANES)],
        (valid, wide, *acts, *extra),
        [f32(joined * rows_dev, width + 16, LANES)],
        cost(1, 1) if extra else cost(3 * VECTOR * len(acts) * acts[0].size * 49 * 2, 1),
        {2 + len(acts): 0} if extra else {},
        "forward",
    )[0]


def rows_at_once(height):
    return 2 * TILE if height % (2 * TILE) == 0 else TILE


def normalise_kernel(valid_ref, mixed, gain_ref, shift_ref, normed_ref, centres, spreads):
    blocks, height, width, _ = mixed.shape
    height = height - 6
    chans = blocks * LANES
    many = rows_at_once(height)

    @pl.loop(0, height // many)
    def _(step):
        rows = [step * many + i for i in range(many)]
        sums = [sum(mixed[block, row + 3] for block in range(blocks)) for row in rows]
        for row, value in zip(rows, sums):
            centre = jnp.sum(value, axis=-1, keepdims=True) / chans
            centres[row] = jnp.broadcast_to(centre, (width, LANES))

    @pl.loop(0, height // many)
    def _(step):
        rows = [step * many + i for i in range(many)]
        sums = []
        for row in rows:
            centre = centres[row]
            away = [mixed[block, row + 3] - centre for block in range(blocks)]
            sums.append(sum(value * value for value in away))
        for row, value in zip(rows, sums):
            spread = jnp.sum(value, axis=-1, keepdims=True) / chans
            spreads[row] = jnp.broadcast_to(lax.rsqrt(spread + epsilon), (width, LANES))

    @pl.loop(0, height, unroll=2)
    def _(row):
        rows = pl.ds(pl.multiple_of(row * width, width), width)
        centre, inv = centres[row], spreads[row]
        for block in range(blocks):
            lanes = slice(block * LANES, (block + 1) * LANES)
            unit = (mixed[block, row + 3] - centre) * inv
            value = unit * gain_ref[block : block + 1, :] + shift_ref[block : block + 1, :]
            value = value * valid_ref[row]
            normed_ref[rows, lanes] = value.astype(normed_ref.dtype)


def normalise(valid, mixed, gain, shift):
    blocks, height, width, _ = mixed.shape
    height = height - 6
    outs = [bf16(height * width, blocks * LANES)] + [f32(height, width, LANES)] * 2
    return run(normalise_kernel, outs, (valid, mixed, gain, shift), name="normalise")


def project_kernel(valid_ref, grad_ref, mixed, centres, spreads, gain_ref, *refs):
    mine_ref, other_ref, out_ref, whole, result, means, alongs = refs
    steps, band, _ = mine_ref.shape
    blocks, height, width, _ = mixed.shape
    height = height - 6
    chans = blocks * LANES
    parity, place = parity_and_place()
    for ref, core in ((mine_ref, parity), (other_ref, 1 - parity)):
        for index in range(steps):
            step = sender(place, index, steps)
            start = pl.multiple_of((2 * step + core) * band, 16)
            whole[pl.ds(start, band), :] = ref[index]
    result[...] = lax.dot_general(
        grad_ref[...], whole[...], (((1,), (1,)), ((), ())), preferred_element_type=jnp.float32
    )

    def scaled_unit(row, block):
        rows = pl.ds(pl.multiple_of(row * width, width), width)
        lanes = slice(block * LANES, (block + 1) * LANES)
        scaled = result[rows, lanes] * gain_ref[block : block + 1, :]
        return scaled, (mixed[block, row + 3] - centres[row]) * spreads[row]

    many = rows_at_once(height)

    @pl.loop(0, height // many)
    def _(step):
        sums = []
        for i in range(many):
            row = step * many + i
            pairs = [scaled_unit(row, block) for block in range(blocks)]
            sums.append((row, sum(p[0] for p in pairs), sum(p[0] * p[1] for p in pairs)))
        for row, scaled, product in sums:
            mean = jnp.sum(scaled, axis=-1, keepdims=True) / chans
            means[row] = jnp.broadcast_to(mean, (width, LANES))
            along = jnp.sum(product, axis=-1, keepdims=True) / chans
            alongs[row] = jnp.broadcast_to(along, (width, LANES))

    @pl.loop(0, blocks)
    def _(block):
        clear_sides(out_ref.at[block], width)
        empty = jnp.zeros((3,) + out_ref.shape[2:], out_ref.dtype)
        out_ref[block, :3] = empty
        out_ref[block, 3 + height :] = empty

    @pl.loop(0, height, unroll=2)
    def _(row):
        mean, along = means[row], alongs[row]
        inv = spreads[row] * valid_ref[row]
        for block in range(blocks):
            scaled, unit = scaled_unit(row, block)
            out_ref[block, row + 3, 8 : 8 + width, :] = inv * (scaled - mean - unit * along)


def project(valid, grad, mixed, centres, spreads, gain, mine, other):
    blocks, height, width, _ = mixed.shape
    chans = blocks * LANES
    return run(
        project_kernel,
        [f32(blocks, height, width + 16, LANES)],
        (valid, grad, mixed, centres, spreads, gain, mine, other),
        [bf16(chans, grad.shape[1]), f32(grad.shape[0], chans)] + [f32(*centres.shape)] * 2,
        cost(VECTOR * mixed.size * 12, 8 * mixed.size),
        name="project",
    )[0]


def backward_kernel(index, bands, valid_ref, grad_ref, taps_ref, out_ref, result):
    rows_dev, width, chans = out_ref.shape
    stride = width // SUBLANES
    first = partner(lax.axis_index("rows"), index, bands) * rows_dev

    @pl.loop(0, chans // LANES)
    def _(block):
        lanes = pl.ds(pl.multiple_of(block * LANES, LANES), LANES)
        for low in range(0, rows_dev, TILE):
            outs = range(low, min(low + TILE, rows_dev))
            running = conv_rows(
                lambda row, columns_of: grad_ref[block, first + row, columns_of, :],
                list(range(rows_dev + 6)), outs, taps_ref, lanes, width, True,
            )
            for out, pieces in running.items():
                for i, value in enumerate(pieces):
                    result[out, pl.ds(i, SUBLANES, stride=stride), :] = value
        for row in range(rows_dev):
            out_ref[row, :, lanes] = (result[row] * valid_ref[first + row]).astype(out_ref.dtype)


def backward(valid, grad, taps, index, bands):
    blocks, height, width, _ = grad.shape
    rows_dev, width = (height - 6) // bands, width - 16
    shape = (rows_dev, width, blocks * LANES)
    return run(
        functools.partial(backward_kernel, index, bands),
        [bf16(*shape) if index else f32(*shape)],
        (valid, grad, taps),
        [f32(rows_dev, width, LANES)],
        cost(VECTOR * rows_dev * width * blocks * LANES * 49 * 2, 1),
        name="backward",
    )[0]


def outer_kernel(normed_ref, grad_ref, whole_ref, send_ref):
    pieces, band, hidden = whole_ref.shape
    parity, _ = parity_and_place()
    whole_ref[...] = lax.dot_general(
        normed_ref[...], grad_ref[...], (((0,), (0,)), ((), ())), preferred_element_type=jnp.float32
    ).reshape(pieces, band, hidden)
    for piece in range(pieces // 2):
        send_ref[piece] = whole_ref[2 * piece + 1 - parity].astype(send_ref.dtype)


def outer(normed, grad, count):
    chans, hidden = normed.shape[1], grad.shape[1]
    outs = [f32(count, chans // count, hidden), bf16(count // 2, chans // count, hidden)]
    return run(outer_kernel, outs, (normed, grad), name="outer")


def kept(held_ref, got_ref, level, parity, piece):
    held = held_ref[2 * piece + parity] if level == 1 else held_ref[piece]
    return held + got_ref[piece].astype(jnp.float32)


def fold_kernel(level, held_ref, got_ref, keep_ref, send_ref):
    parity, place = parity_and_place()
    bit = lax.rem(place >> level - 1, 2)
    for piece in range(keep_ref.shape[0]):
        keep_ref[piece] = kept(held_ref, got_ref, level, parity, 2 * piece + bit)
        sent = kept(held_ref, got_ref, level, parity, 2 * piece + 1 - bit)
        send_ref[piece] = sent.astype(send_ref.dtype)


def fold(held, got, level):
    pieces, band, hidden = got.shape
    outs = [f32(pieces // 2, band, hidden), bf16(pieces // 2, band, hidden)]
    return run(functools.partial(fold_kernel, level), outs, (held, got), name="fold")


def finish_kernel(count, *refs):
    total = sum(ref[...].astype(jnp.float32) for ref in refs[:-1])
    refs[-1][...] = (total / count if count > 1 else total).astype(refs[-1].dtype)


def finish(out, parts, count=1):
    return run(functools.partial(finish_kernel, count), [out], parts, name="finish")[0]


def parity_and_place():
    index = lax.axis_index("section")
    return lax.rem(index, 2), index // 2


def partner(place, index, count):
    return place ^ index if count & (count - 1) == 0 else (place + index) % count


def sender(place, index, count):
    return place ^ index if count & (count - 1) == 0 else (place + count - index) % count


def swap_pairs(value):
    count = lax.axis_size("section")
    return lax.ppermute(value, "section", [(i, i ^ 1) for i in range(count)])


def send_rows(value, index):
    if index == 0:
        return value
    count = lax.axis_size("rows")
    return lax.ppermute(value, "rows", [(i, partner(i, index, count)) for i in range(count)])


def send_section(value, index):
    count = lax.axis_size("section")
    way = [(i, partner(i // 2, index, count // 2) * 2 + i % 2) for i in range(count)]
    return lax.ppermute(value, "section", way)


def stack_kernel(*refs):
    for index, ref in enumerate(refs[:-1]):
        refs[-1][index] = ref[...]


def stack(pieces):
    return run(stack_kernel, [bf16(len(pieces), *pieces[0].shape)], pieces, name="stack")[0]


def send_pieces(block):
    steps = lax.axis_size("section") // 2
    if steps & (steps - 1):
        return {index: send_section(block, index) for index in range(1, steps)}
    return {1 << level: send_section(block, 1 << level) for level in range(steps.bit_length() - 1)}


def gather_pairs(block, sent, first):
    steps = lax.axis_size("section") // 2
    pieces = {0: block}
    for index in sorted(sent, reverse=True):
        if steps & (steps - 1):
            pieces[index] = sent[index]
            continue
        passed = {i ^ index: send_section(after(v, first), index) for i, v in pieces.items() if i}
        pieces = pieces | {index: sent[index]} | passed
    return [pieces[index] for index in range(steps)]


def scatter_section(keep, send):
    count = lax.axis_size("section")
    level, sends = 0, [send]
    while True:
        way = [(i, i ^ 1 << level) for i in range(count)]
        got = lax.ppermute(send, "section", way)
        level += 1
        if got.shape[0] % 2:
            break
        keep, send = fold(keep, got, level)
        sends.append(send)
    rest = keep.shape[0]
    if rest == 1:
        return [keep[0], got[0]], sends
    total = keep + got.astype(jnp.float32)
    place = lax.axis_index("section") >> level
    result = lax.dynamic_index_in_dim(total, place, 0, keepdims=False)
    for shift in range(1, rest):
        piece = lax.dynamic_index_in_dim(total, (place + shift) % rest, 0, keepdims=False)
        way = [(i, (i + (shift << level)) % count) for i in range(count)]
        result = result + lax.ppermute(piece.astype(jnp.bfloat16), "section", way).astype(jnp.float32)
    return [result], sends


def after(value, *others):
    return lax.optimization_barrier((value, others))[0]


def local(activations, cotangent, proj_weight, kernel_taps, ln_gain, ln_shift, heights, widths):
    rows_dev, width_dev, chans = activations.shape[1:]
    height_all = cotangent.shape[1]
    hidden_dev = cotangent.shape[3]
    bands = lax.axis_size("rows")
    count = lax.axis_size("section")
    wide, valid = prepare(heights, widths, kernel_taps, activations[0], height_all)
    gain, shift = (value.reshape(chans // LANES, LANES) for value in (ln_gain, ln_shift))
    grad = cotangent.reshape(-1, hidden_dev)

    acts = [activations[0]] + [send_rows(activations[0], i) for i in range(1, bands)]
    half = bands // 2
    mixed = forward(valid, wide, acts[:half], range(half), bands)
    sent = send_pieces(proj_weight)
    mixed = forward(valid, wide, acts[half:], range(half, bands), bands, mixed)
    proj_mine = stack(gather_pairs(proj_weight, sent, mixed))

    normed, centres, spreads = normalise(after(valid, sent[1]), mixed, gain, shift)
    whole, send = outer(normed, grad, count)
    weights, sends = scatter_section(whole, send)

    proj_other = swap_pairs(proj_mine)
    grads = after(grad, sends[min(1, len(sends) - 1)])
    grad_mixed = project(valid, grads, mixed, centres, spreads, gain, proj_mine, proj_other)
    backs = []
    for i in [*range(2, bands), 1, 0]:
        ready = sends[min(1, len(sends) - 1)] if i > 1 else sends[-1]
        backs.append(send_rows(backward(after(valid, ready), grad_mixed, wide, i, bands), i))
    weight_grad = finish(f32(*weights[0].shape), weights, count)
    backs[-2] = after(backs[-2], weight_grad)
    back = finish(bf16(*backs[0].shape), backs)
    return (back[None], weight_grad)


def solution(mesh):
    in_specs = (
        P("section", "rows", None, None),
        P("section", None, None, "rows"),
        P("section", "rows"),
        P(),
        P(),
        P(),
        P("section"),
        P("section"),
    )
    out_specs = (P("section", "rows", None, None), P("section", "rows"))
    return jax.shard_map(local, mesh=mesh, in_specs=in_specs, out_specs=out_specs, check_vma=False)
```

```python
import functools

import jax
import jax.numpy as jnp
import numpy as np
from jax import lax
from jax.experimental import pallas as pl
from jax.experimental.pallas import tpu as pltpu
from jax.sharding import PartitionSpec as P

epsilon = 1e-06
LANES = 128
VECTOR = 240
SUBLANES = 8


TILE = 4


def cost(operations, moved):
    return pl.CostEstimate(flops=operations, bytes_accessed=moved, transcendentals=0)


def run(kernel, outs, args, scratch=(), estimate=None, aliases=None, name=None):
    held = list(args) + list(outs) + list(scratch)
    taken = sum(int(np.prod(value.shape)) * jnp.dtype(value.dtype).itemsize for value in held)
    vmem = pl.BlockSpec(memory_space=pltpu.VMEM)
    smem = pl.BlockSpec(memory_space=pltpu.SMEM)
    return pl.pallas_call(
        kernel,
        out_shape=tuple(outs),
        in_specs=[smem if arg.dtype == jnp.int32 else vmem for arg in args],
        out_specs=tuple(vmem for _ in outs),
        scratch_shapes=[pltpu.VMEM(value.shape, value.dtype) for value in scratch],
        input_output_aliases=aliases or {},
        compiler_params=pltpu.CompilerParams(vmem_limit_bytes=taken + taken // 8 + (4 << 20)),
        cost_estimate=estimate or cost(1, 1),
        name=name,
    )(*args)


def f32(*shape):
    return jax.ShapeDtypeStruct(shape, jnp.float32)


def bf16(*shape):
    return jax.ShapeDtypeStruct(shape, jnp.bfloat16)


def begin_kernel(out_ref):
    out_ref[...] = jnp.zeros(out_ref.shape, out_ref.dtype)


def prepare_kernel(zero_ref, high_ref, wid_ref, taps_ref, act_ref, wide_ref, valid_ref):
    count, chans = taps_ref.shape
    taps = taps_ref[...].astype(jnp.float32)
    for tap in range(count):
        wide_ref[tap] = jnp.broadcast_to(taps[tap : tap + 1], (SUBLANES, chans))
    _, width, lanes = valid_ref.shape
    columns = lax.broadcasted_iota(jnp.int32, (width, lanes), 0) < wid_ref[0]

    @pl.loop(0, valid_ref.shape[0])
    def _(row):
        valid_ref[row] = jnp.where(columns & (row < high_ref[0]), 1.0, 0.0) + zero_ref[0:1, :]


def prepare(heights, widths, taps, act, height):
    count, chans = taps.shape
    outs = [f32(count, SUBLANES, chans), f32(height, act.shape[1], LANES)]
    estimate = cost(VECTOR * 128 * taps.size, 1)
    zero = run(begin_kernel, [f32(SUBLANES, LANES)], (), estimate=estimate, name="begin")[0]
    args = (zero, heights, widths, taps, act)
    return run(prepare_kernel, outs, args, name="prepare")


def clear_sides(source, width):
    sides = jnp.zeros((source.shape[0], 8, LANES), source.dtype)
    source[:, :8, :] = sides
    source[:, 8 + width :, :] = sides


def conv_rows(load, positions, outs, wide_ref, lanes, width, flip):
    stride = width // SUBLANES
    running = {out: [None] * stride for out in outs}
    for row, position in enumerate(positions):
        users = [out for out in outs if 0 <= position - out <= 6]
        if not users:
            continue
        shifted = [load(row, pl.ds(5 + k, SUBLANES, stride=stride)) for k in range(stride + 6)]
        for out in users:
            for along in range(7):
                tap = (position - out) * 7 + along
                weight = wide_ref[48 - tap if flip else tap, :, lanes]
                for i in range(stride):
                    term = weight * shifted[i + along]
                    before = running[out][i]
                    running[out][i] = term if before is None else before + term
    return running


def forward_kernel(bands, indices, fresh, valid_ref, taps_ref, *refs):
    act_refs, (mixed, source) = refs[: len(indices)], refs[-2:]
    rows_dev, width, _ = act_refs[0].shape
    blocks, height = mixed.shape[0], mixed.shape[1] - 6
    stride = width // SUBLANES
    band = lax.axis_index("rows")
    joined = source.shape[0] // rows_dev
    clear_sides(source, width)
    once = fresh and len(indices) == joined
    firsts = [sender(band, index, bands) * rows_dev for index in indices]

    @pl.loop(0, blocks)
    def _(block):
        lanes = pl.ds(pl.multiple_of(block * LANES, LANES), LANES)
        if fresh:
            mixed[block] = jnp.zeros(mixed.shape[1:], mixed.dtype)
        for start in range(0, len(indices), joined):
            base = firsts[start]
            for first in firsts[start : start + joined]:
                base = jnp.minimum(base, first)
            for first, act_ref in zip(firsts[start:], act_refs[start : start + joined]):
                for i in range(rows_dev):
                    row = first + i
                    value = act_ref[i, :, lanes].astype(jnp.float32) * valid_ref[row]
                    source[row - base, 8 : 8 + width, :] = value
            rows = joined * rows_dev
            for low in range(0, rows + 6, TILE):
                outs = range(low, min(low + TILE, rows + 6))
                positions = [i + 6 for i in range(rows)]
                running = conv_rows(
                    lambda row, columns_of: source[row, columns_of, :],
                    positions, outs, taps_ref, lanes, width, False,
                )
                for out, pieces in running.items():
                    for i, value in enumerate(pieces):
                        columns_of = pl.ds(i, SUBLANES, stride=stride)
                        if not once:
                            value = value + mixed[block, base + out, columns_of, :]
                        mixed[block, base + out, columns_of, :] = value


def forward(valid, wide, acts, indices, bands, before=None):
    rows_dev, width, chans = acts[0].shape
    joined = 2 if bands & (bands - 1) == 0 and len(indices) % 2 == 0 else 1
    extra = () if before is None else (before,)
    return run(
        functools.partial(forward_kernel, bands, indices, before is None),
        [f32(chans // LANES, rows_dev * bands + 6, width, LANES)],
        (valid, wide, *acts, *extra),
        [f32(joined * rows_dev, width + 16, LANES)],
        cost(1, 1) if extra else cost(3 * VECTOR * len(acts) * acts[0].size * 49 * 2, 1),
        {2 + len(acts): 0} if extra else {},
        "forward",
    )[0]


def rows_at_once(height):
    return 2 * TILE if height % (2 * TILE) == 0 else TILE


def normalise_kernel(valid_ref, mixed, gain_ref, shift_ref, normed_ref, centres, spreads):
    blocks, height, width, _ = mixed.shape
    height = height - 6
    chans = blocks * LANES
    many = rows_at_once(height)

    @pl.loop(0, height // many)
    def _(step):
        rows = [step * many + i for i in range(many)]
        sums = [sum(mixed[block, row + 3] for block in range(blocks)) for row in rows]
        for row, value in zip(rows, sums):
            centre = jnp.sum(value, axis=-1, keepdims=True) / chans
            centres[row] = jnp.broadcast_to(centre, (width, LANES))

    @pl.loop(0, height // many)
    def _(step):
        rows = [step * many + i for i in range(many)]
        sums = []
        for row in rows:
            centre = centres[row]
            away = [mixed[block, row + 3] - centre for block in range(blocks)]
            sums.append(sum(value * value for value in away))
        for row, value in zip(rows, sums):
            spread = jnp.sum(value, axis=-1, keepdims=True) / chans
            spreads[row] = jnp.broadcast_to(lax.rsqrt(spread + epsilon), (width, LANES))

    @pl.loop(0, height, unroll=2)
    def _(row):
        rows = pl.ds(pl.multiple_of(row * width, width), width)
        centre, inv = centres[row], spreads[row]
        for block in range(blocks):
            lanes = slice(block * LANES, (block + 1) * LANES)
            unit = (mixed[block, row + 3] - centre) * inv
            value = unit * gain_ref[block : block + 1, :] + shift_ref[block : block + 1, :]
            value = value * valid_ref[row]
            normed_ref[rows, lanes] = value.astype(normed_ref.dtype)


def normalise(valid, mixed, gain, shift):
    blocks, height, width, _ = mixed.shape
    height = height - 6
    outs = [bf16(height * width, blocks * LANES)] + [f32(height, width, LANES)] * 2
    return run(normalise_kernel, outs, (valid, mixed, gain, shift), name="normalise")


def project_kernel(valid_ref, grad_ref, mixed, centres, spreads, gain_ref, *refs):
    mine_ref, other_ref, out_ref, whole, result, means, alongs = refs
    steps, band, _ = mine_ref.shape
    blocks, height, width, _ = mixed.shape
    height = height - 6
    chans = blocks * LANES
    parity, place = parity_and_place()
    for ref, core in ((mine_ref, parity), (other_ref, 1 - parity)):
        for index in range(steps):
            step = sender(place, index, steps)
            start = pl.multiple_of((2 * step + core) * band, 16)
            whole[pl.ds(start, band), :] = ref[index]
    result[...] = lax.dot_general(
        grad_ref[...], whole[...], (((1,), (1,)), ((), ())), preferred_element_type=jnp.float32
    )

    def scaled_unit(row, block):
        rows = pl.ds(pl.multiple_of(row * width, width), width)
        lanes = slice(block * LANES, (block + 1) * LANES)
        scaled = result[rows, lanes] * gain_ref[block : block + 1, :]
        return scaled, (mixed[block, row + 3] - centres[row]) * spreads[row]

    many = rows_at_once(height)

    @pl.loop(0, height // many)
    def _(step):
        sums = []
        for i in range(many):
            row = step * many + i
            pairs = [scaled_unit(row, block) for block in range(blocks)]
            sums.append((row, sum(p[0] for p in pairs), sum(p[0] * p[1] for p in pairs)))
        for row, scaled, product in sums:
            mean = jnp.sum(scaled, axis=-1, keepdims=True) / chans
            means[row] = jnp.broadcast_to(mean, (width, LANES))
            along = jnp.sum(product, axis=-1, keepdims=True) / chans
            alongs[row] = jnp.broadcast_to(along, (width, LANES))

    @pl.loop(0, blocks)
    def _(block):
        clear_sides(out_ref.at[block], width)
        empty = jnp.zeros((3,) + out_ref.shape[2:], out_ref.dtype)
        out_ref[block, :3] = empty
        out_ref[block, 3 + height :] = empty

    @pl.loop(0, height, unroll=2)
    def _(row):
        mean, along = means[row], alongs[row]
        inv = spreads[row] * valid_ref[row]
        for block in range(blocks):
            scaled, unit = scaled_unit(row, block)
            out_ref[block, row + 3, 8 : 8 + width, :] = inv * (scaled - mean - unit * along)


def project(valid, grad, mixed, centres, spreads, gain, mine, other):
    blocks, height, width, _ = mixed.shape
    chans = blocks * LANES
    return run(
        project_kernel,
        [f32(blocks, height, width + 16, LANES)],
        (valid, grad, mixed, centres, spreads, gain, mine, other),
        [bf16(chans, grad.shape[1]), f32(grad.shape[0], chans)] + [f32(*centres.shape)] * 2,
        cost(VECTOR * mixed.size * 12, 8 * mixed.size),
        name="project",
    )[0]


def backward_kernel(index, bands, valid_ref, grad_ref, taps_ref, out_ref, result):
    rows_dev, width, chans = out_ref.shape
    stride = width // SUBLANES
    first = partner(lax.axis_index("rows"), index, bands) * rows_dev

    @pl.loop(0, chans // LANES)
    def _(block):
        lanes = pl.ds(pl.multiple_of(block * LANES, LANES), LANES)
        for low in range(0, rows_dev, TILE):
            outs = range(low, min(low + TILE, rows_dev))
            running = conv_rows(
                lambda row, columns_of: grad_ref[block, first + row, columns_of, :],
                list(range(rows_dev + 6)), outs, taps_ref, lanes, width, True,
            )
            for out, pieces in running.items():
                for i, value in enumerate(pieces):
                    result[out, pl.ds(i, SUBLANES, stride=stride), :] = value
        for row in range(rows_dev):
            out_ref[row, :, lanes] = (result[row] * valid_ref[first + row]).astype(out_ref.dtype)


def backward(valid, grad, taps, index, bands):
    blocks, height, width, _ = grad.shape
    rows_dev, width = (height - 6) // bands, width - 16
    shape = (rows_dev, width, blocks * LANES)
    return run(
        functools.partial(backward_kernel, index, bands),
        [bf16(*shape) if index else f32(*shape)],
        (valid, grad, taps),
        [f32(rows_dev, width, LANES)],
        cost(VECTOR * rows_dev * width * blocks * LANES * 49 * 2, 1),
        name="backward",
    )[0]


def outer_kernel(normed_ref, grad_ref, whole_ref, send_ref):
    pieces, band, hidden = whole_ref.shape
    parity, _ = parity_and_place()
    whole_ref[...] = lax.dot_general(
        normed_ref[...], grad_ref[...], (((0,), (0,)), ((), ())), preferred_element_type=jnp.float32
    ).reshape(pieces, band, hidden)
    for piece in range(pieces // 2):
        send_ref[piece] = whole_ref[2 * piece + 1 - parity].astype(send_ref.dtype)


def outer(normed, grad, count):
    chans, hidden = normed.shape[1], grad.shape[1]
    outs = [f32(count, chans // count, hidden), bf16(count // 2, chans // count, hidden)]
    return run(outer_kernel, outs, (normed, grad), name="outer")


def kept(held_ref, got_ref, level, parity, piece):
    held = held_ref[2 * piece + parity] if level == 1 else held_ref[piece]
    return held + got_ref[piece].astype(jnp.float32)


def fold_kernel(level, held_ref, got_ref, keep_ref, send_ref):
    parity, place = parity_and_place()
    bit = lax.rem(place >> level - 1, 2)
    for piece in range(keep_ref.shape[0]):
        keep_ref[piece] = kept(held_ref, got_ref, level, parity, 2 * piece + bit)
        sent = kept(held_ref, got_ref, level, parity, 2 * piece + 1 - bit)
        send_ref[piece] = sent.astype(send_ref.dtype)


def fold(held, got, level):
    pieces, band, hidden = got.shape
    outs = [f32(pieces // 2, band, hidden), bf16(pieces // 2, band, hidden)]
    return run(functools.partial(fold_kernel, level), outs, (held, got), name="fold")


def finish_kernel(count, *refs):
    total = sum(ref[...].astype(jnp.float32) for ref in refs[:-1])
    refs[-1][...] = (total / count if count > 1 else total).astype(refs[-1].dtype)


def finish(out, parts, count=1):
    return run(functools.partial(finish_kernel, count), [out], parts, name="finish")[0]


def parity_and_place():
    index = lax.axis_index("section")
    return lax.rem(index, 2), index // 2


def partner(place, index, count):
    return place ^ index if count & (count - 1) == 0 else (place + index) % count


def sender(place, index, count):
    return place ^ index if count & (count - 1) == 0 else (place + count - index) % count


def swap_pairs(value):
    count = lax.axis_size("section")
    return lax.ppermute(value, "section", [(i, i ^ 1) for i in range(count)])


def send_rows(value, index):
    if index == 0:
        return value
    count = lax.axis_size("rows")
    return lax.ppermute(value, "rows", [(i, partner(i, index, count)) for i in range(count)])


def send_section(value, index):
    count = lax.axis_size("section")
    way = [(i, partner(i // 2, index, count // 2) * 2 + i % 2) for i in range(count)]
    return lax.ppermute(value, "section", way)


def stack_kernel(*refs):
    for index, ref in enumerate(refs[:-1]):
        refs[-1][index] = ref[...]


def stack(pieces):
    return run(stack_kernel, [bf16(len(pieces), *pieces[0].shape)], pieces, name="stack")[0]


def send_pieces(block):
    steps = lax.axis_size("section") // 2
    if steps & (steps - 1):
        return {index: send_section(block, index) for index in range(1, steps)}
    return {1 << level: send_section(block, 1 << level) for level in range(steps.bit_length() - 1)}


def gather_pairs(block, sent, first):
    steps = lax.axis_size("section") // 2
    pieces = {0: block}
    for index in sorted(sent, reverse=True):
        if steps & (steps - 1):
            pieces[index] = sent[index]
            continue
        passed = {i ^ index: send_section(after(v, first), index) for i, v in pieces.items() if i}
        pieces = pieces | {index: sent[index]} | passed
    return [pieces[index] for index in range(steps)]


def scatter_section(keep, send):
    count = lax.axis_size("section")
    level, sends = 0, [send]
    while True:
        way = [(i, i ^ 1 << level) for i in range(count)]
        got = lax.ppermute(send, "section", way)
        level += 1
        if got.shape[0] % 2:
            break
        keep, send = fold(keep, got, level)
        sends.append(send)
    rest = keep.shape[0]
    if rest == 1:
        return [keep[0], got[0]], sends
    total = keep + got.astype(jnp.float32)
    place = lax.axis_index("section") >> level
    result = lax.dynamic_index_in_dim(total, place, 0, keepdims=False)
    for shift in range(1, rest):
        piece = lax.dynamic_index_in_dim(total, (place + shift) % rest, 0, keepdims=False)
        way = [(i, (i + (shift << level)) % count) for i in range(count)]
        result = result + lax.ppermute(piece.astype(jnp.bfloat16), "section", way).astype(jnp.float32)
    return [result], sends


def after(value, *others):
    return lax.optimization_barrier((value, others))[0]


def local(activations, cotangent, proj_weight, kernel_taps, ln_gain, ln_shift, heights, widths):
    rows_dev, width_dev, chans = activations.shape[1:]
    height_all = cotangent.shape[1]
    hidden_dev = cotangent.shape[3]
    bands = lax.axis_size("rows")
    count = lax.axis_size("section")
    wide, valid = prepare(heights, widths, kernel_taps, activations[0], height_all)
    gain, shift = (value.reshape(chans // LANES, LANES) for value in (ln_gain, ln_shift))
    grad = cotangent.reshape(-1, hidden_dev)

    acts = [activations[0]] + [send_rows(activations[0], i) for i in range(1, bands)]
    half = bands // 2
    mixed = forward(valid, wide, acts[:half], range(half), bands)
    sent = send_pieces(proj_weight)
    mixed = forward(valid, wide, acts[half:], range(half, bands), bands, mixed)
    proj_mine = stack(gather_pairs(proj_weight, sent, mixed))

    normed, centres, spreads = normalise(after(valid, sent[1]), mixed, gain, shift)
    whole, send = outer(normed, grad, count)
    weights, sends = scatter_section(whole, send)

    proj_other = swap_pairs(proj_mine)
    grads = after(grad, sends[min(1, len(sends) - 1)])
    grad_mixed = project(valid, grads, mixed, centres, spreads, gain, proj_mine, proj_other)
    backs = []
    for i in [*range(bands - 1, 1, -1), 1, 0]:
        ready = sends[min(1, len(sends) - 1)] if i > 1 else sends[-1]
        backs.append(send_rows(backward(after(valid, ready), grad_mixed, wide, i, bands), i))
    weight_grad = finish(f32(*weights[0].shape), weights, count)
    backs[-2] = after(backs[-2], weight_grad)
    back = finish(bf16(*backs[0].shape), backs)
    return (back[None], weight_grad)


def solution(mesh):
    in_specs = (
        P("section", "rows", None, None),
        P("section", None, None, "rows"),
        P("section", "rows"),
        P(),
        P(),
        P(),
        P("section"),
        P("section"),
    )
    out_specs = (P("section", "rows", None, None), P("section", "rows"))
    return jax.shard_map(local, mesh=mesh, in_specs=in_specs, out_specs=out_specs, check_vma=False)
```
